32 devices in a mesh: seq: 2 (over core), fsdp: 16 (over z, y, x).
Axes of the slice: x: 2, y: 2, z: 4, core: 2. Of those that a mesh axis runs over, the one named last changes fastest.
Arguments:
- tokens: bfloat16 [4096, 2, 1536], P(('seq', 'fsdp')), may hold values from -6 to 6
- routes: int32 [4096, 2, 6], P(('seq', 'fsdp')), may hold values from 0 to 15, all different within a row; in each aligned block of 256 rows (0 to 255, 256 to 511, ..., all dimensions but the last counted through in order) at most 144 rows name the same one
- out_grad: bfloat16 [4096, 2, 1536], P(('seq', 'fsdp')), may hold values from -6 to 6
- attn_gain: bfloat16 [1536], P(('seq', 'fsdp')), may hold values from 0.5 to 1.5
- ffn_gain: bfloat16 [1536], P(('seq', 'fsdp')), may hold values from 0.5 to 1.5
- query_projection: bfloat16 [1536, 1536], P(('seq', 'fsdp')), may hold values from -0.15625 to 0.15625
- key_projection: bfloat16 [1536, 512], P(('seq', 'fsdp')), may hold values from -0.15625 to 0.15625
- value_projection: bfloat16 [1536, 512], P(('seq', 'fsdp')), may hold values from -0.15625 to 0.15625
- w_out: bfloat16 [1536, 1536], P(('seq', 'fsdp')), may hold values from -3.59375 to 3.59375
- w_router: bfloat16 [1536, 16], P(('seq', 'fsdp')), may hold values from -0.078125 to 0.078125
- shared_gate: bfloat16 [1536, 1024], P(('seq', 'fsdp')), may hold values from -0.15625 to 0.15625
- shared_up: bfloat16 [1536, 1024], P(('seq', 'fsdp')), may hold values from -0.15625 to 0.15625
- shared_down: bfloat16 [1024, 1536], P(('seq', 'fsdp')), may hold values from -0.1875 to 0.1875
- expert_gate: bfloat16 [16, 1536, 512], P('fsdp'), may hold values from -0.15625 to 0.15625
- expert_up: bfloat16 [16, 1536, 512], P('fsdp'), may hold values from -0.15625 to 0.15625
- expert_down: bfloat16 [16, 512, 1536], P('fsdp'), may hold values from -1 to 1
Outputs:
- out: bfloat16 [4096, 2, 1536], P(('seq', 'fsdp'))
- tokens_grad: float32 [4096, 2, 1536], P(('seq', 'fsdp'))
- attn_gain_grad: float32 [1536], P(('seq', 'fsdp'))
- ffn_gain_grad: float32 [1536], P(('seq', 'fsdp'))
- query_grad: float32 [1536, 1536], P(('seq', 'fsdp'))
- key_grad: float32 [1536, 512], P(('seq', 'fsdp'))
- value_grad: float32 [1536, 512], P(('seq', 'fsdp'))
- out_proj_grad: float32 [1536, 1536], P(('seq', 'fsdp'))
- router_grad: float32 [1536, 16], P(('seq', 'fsdp'))
- shared_gate_grad: float32 [1536, 1024], P(('seq', 'fsdp'))
- shared_up_grad: float32 [1536, 1024], P(('seq', 'fsdp'))
- shared_down_grad: float32 [1024, 1536], P(('seq', 'fsdp'))
- expert_gate_grad: float32 [16, 1536, 512], P('fsdp')
- expert_up_grad: float32 [16, 1536, 512], P('fsdp')
- expert_down_grad: float32 [16, 512, 1536], P('fsdp')
The draws below stay inside these ranges and needn't reach their ends.
Inputs may be any that keep to these rules, and one draw needn't show every extreme that they name: `routes`: each row names 6 different experts. In each aligned block of 256 rows of the first two dimensions taken together (the rows of one device) no expert is named by more than 144 rows, a bound that some block reaches.
All inputs are finite; a program needn't handle non-finite values.
Results may differ from the reference program's by a relative error of at most 0.023.
Values may be sent and summed in bfloat16 or wider, within the bound.
A program may use at most 384 MiB of HBM per device.

```python
import math
import jax
import jax.numpy as jnp
import numpy as np
from jax import lax

MODEL_DIM = 1536
QUERY_HEADS = 12
KEY_VALUE_HEADS = 4
HEAD_SIZE = 128
EXP_FF = 512
SH_FF = 1024
TOPK = 6
SEQUENCE_COUNT = 2
EXPERTS = 16
SEQUENCE_LENGTH = 4096
TOK_DEV = 256
MOST = 144


def levels(own_key, extent, cuts, smallest, high):
    def one(position, blocks):
        steps = jax.random.uniform(jax.random.fold_in(jax.random.fold_in(own_key, 6), position), (blocks,), jnp.float32, smallest / len(cuts), high / len(cuts))
        return jnp.repeat(jnp.exp(steps), extent[position] // blocks).reshape((-1,) + (1,) * (len(extent) - position - 1))

    gain = one(*cuts[0])
    for cut in cuts[1:]:
        gain = gain * one(*cut)
    return gain


def deal_out(key, own, number, rows, amount, top, bound, slope):
    ranking = jax.random.permutation(key, amount)
    crowded, ordinary = portions_of(amount, rows * top, bound, slope, True), portions_of(amount, rows * top, bound, slope, False)
    places = jnp.arange(amount)

    def named(sizes, offset_by):
        used = int((sizes > 0).sum())
        fixed = max(1, used // 4)
        passed = fixed + (places - fixed + offset_by * (used - fixed)) % max(1, amount - fixed)
        return jnp.zeros((amount,), jnp.int32).at[ranking[jnp.where(places < fixed, places, passed)]].set(jnp.asarray(sizes, jnp.int32))

    sizes = jnp.where(number % 4 == 0, named(crowded, number // 4), named(ordinary, number - number // 4 - 1))
    mixed = jax.random.permutation(jax.random.fold_in(own, 3), amount)
    giver, taker = mixed[0:amount // 2 * 2:2], mixed[1:amount // 2 * 2:2]
    room = jnp.minimum(sizes[giver] - 1, bound - sizes[taker]) // 2
    room = jnp.where((giver == ranking[0]) | (taker == ranking[0]) | (sizes[taker] == 0), 0, jnp.maximum(room, 0))
    passed = jax.random.randint(jax.random.fold_in(own, 4), (amount // 2,), 0, 1 << 20) % (room + 1)
    sizes = sizes.at[giver].add(-passed).at[taker].add(passed)
    items = jnp.searchsorted(jnp.cumsum(sizes), jnp.arange(rows * top), side="right").astype(jnp.int32)
    grid = items.reshape(top, rows).T
    grid = grid[jax.random.permutation(jax.random.fold_in(own, 1), rows)]
    offset_by = jax.random.randint(jax.random.fold_in(own, 2), (rows, 1), 0, top)
    return jnp.take_along_axis(grid, (jnp.arange(top)[None, :] + offset_by) % top, axis=1)


def portions_of(number_of, total, reach, lean, full):
    weights = [(1 << 20) // math.isqrt(standing ** lean) + 1 for standing in range(1, number_of + 1)]
    largest = reach if full else min(reach, max(-(-total // number_of), total * weights[0] // sum(weights)))
    least = 1 if total - largest >= number_of - 1 else 0
    counts, surplus = [largest] + [least] * (number_of - 1), total - largest - least * (number_of - 1)
    while surplus > 0:
        movable = [i for i in range(1, number_of) if counts[i] < largest] or [i for i in range(1, number_of) if counts[i] < reach]
        pool, budget = sum([weights[i] for i in movable]), surplus
        for i in movable:
            more = min(reach - counts[i], max(1, budget * weights[i] // pool), surplus)
            counts[i] = counts[i] + more
            surplus = surplus - more
    return np.array(counts)


def noise(own_key, shape, deviation, limit, pieces=(), kind=jnp.bfloat16):
    level = levels(own_key, shape, pieces, -0.22, 0.18) if pieces else 1.0
    drawn = jax.random.normal(own_key, shape, jnp.float32) * deviation * level
    return jnp.minimum(jnp.maximum(drawn, -limit), limit).astype(kind)


def setup_inputs(seed: int = 0) -> dict:
    key_of = jax.random.split(jax.random.key(seed), 17)
    tokens = noise(key_of[0], (SEQUENCE_LENGTH, SEQUENCE_COUNT, MODEL_DIM), 1.0, 6.0, ((0, 32),))
    routes_keys = jax.random.split(jax.random.fold_in(key_of[1], 1), SEQUENCE_LENGTH * SEQUENCE_COUNT // TOK_DEV)
    routes_turns = jax.random.permutation(jax.random.fold_in(key_of[1], 3), SEQUENCE_LENGTH * SEQUENCE_COUNT // TOK_DEV)
    routes = jax.vmap(lambda own, number: deal_out(jax.random.fold_in(key_of[1], 2), own, number, TOK_DEV, EXPERTS, TOPK, MOST, 1))(routes_keys, routes_turns).reshape((SEQUENCE_LENGTH, SEQUENCE_COUNT, TOPK))
    out_grad = noise(key_of[2], (SEQUENCE_LENGTH, SEQUENCE_COUNT, MODEL_DIM), 1.0, 6.0, ((0, 32),))
    attn_gain = jnp.clip(1.0 + 0.1 * jax.random.normal(key_of[3], (MODEL_DIM,), jnp.float32), 0.5, 1.5).astype(jnp.bfloat16)
    ffn_gain = jnp.clip(1.0 + 0.1 * jax.random.normal(key_of[4], (MODEL_DIM,), jnp.float32), 0.5, 1.5).astype(jnp.bfloat16)
    query_projection = noise(key_of[5], (MODEL_DIM, QUERY_HEADS * HEAD_SIZE), MODEL_DIM ** -0.5, 0.15625, ((0, 32),))
    key_projection = noise(key_of[6], (MODEL_DIM, KEY_VALUE_HEADS * HEAD_SIZE), MODEL_DIM ** -0.5, 0.15625, ((0, 32),))
    value_projection = noise(key_of[7], (MODEL_DIM, KEY_VALUE_HEADS * HEAD_SIZE), MODEL_DIM ** -0.5, 0.15625, ((0, 32),))
    w_out = noise(key_of[8], (QUERY_HEADS * HEAD_SIZE, MODEL_DIM), 0.6, 3.59375, ((0, 32),))
    w_router = noise(key_of[9], (MODEL_DIM, EXPERTS), (4 * MODEL_DIM) ** -0.5, 0.078125, ((0, 32),))
    shared_gate = noise(key_of[10], (MODEL_DIM, SH_FF), MODEL_DIM ** -0.5, 0.15625, ((0, 32),))
    shared_up = noise(key_of[11], (MODEL_DIM, SH_FF), MODEL_DIM ** -0.5, 0.15625, ((0, 32),))
    shared_down = noise(key_of[12], (SH_FF, MODEL_DIM), SH_FF ** -0.5, 0.1875, ((0, 32),))
    expert_gate = noise(key_of[13], (EXPERTS, MODEL_DIM, EXP_FF), MODEL_DIM ** -0.5, 0.15625, ((0, 16),))
    expert_up = noise(key_of[14], (EXPERTS, MODEL_DIM, EXP_FF), MODEL_DIM ** -0.5, 0.15625, ((0, 16),))
    expert_down = noise(key_of[15], (EXPERTS, EXP_FF, MODEL_DIM), (EXP_FF // 16) ** -0.5, 1.0, ((0, 16),))
    return dict(tokens=tokens, routes=routes, out_grad=out_grad, attn_gain=attn_gain, ffn_gain=ffn_gain, query_projection=query_projection, key_projection=key_projection, value_projection=value_projection, w_out=w_out, w_router=w_router, shared_gate=shared_gate, shared_up=shared_up, shared_down=shared_down, expert_gate=expert_gate, expert_up=expert_up, expert_down=expert_down)


@jax.custom_vjp
def lowered_precision(v):
    return lax.optimization_barrier(v.astype(jnp.bfloat16)).astype(jnp.float32)

@jax.custom_vjp
def lowered_backward(v):
    return v

def low_keep(v):
    return (lowered_precision(v), None)

def low_pass(kept, grad):
    return (grad,)

def back_keep(v):
    return (v, None)

def back_low(kept, grad):
    return (lowered_precision(grad),)
lowered_precision.defvjp(low_keep, low_pass)
lowered_backward.defvjp(back_keep, back_low)
epsilon = 1e-06
masked_score = -1e+30

def matrix_multiply(left_matrix, right_matrix):
    return jnp.dot(left_matrix, right_matrix, precision=lax.Precision.HIGHEST, preferred_element_type=jnp.float32)

def rms_scale(values, gain_vector):
    inverse = lax.rsqrt(lax.optimization_barrier(jnp.mean(values * values, axis=-1, keepdims=True)) + epsilon)
    return values * inverse * gain_vector

def swiglu(gate_part, up_part):
    return gate_part * jax.nn.sigmoid(gate_part) * up_part

def attend_sequence(query_data, key_tensor, value_tensor):
    length = query_data.shape[0]
    block_rows = min(512, length)
    score_scale = HEAD_SIZE ** (-0.5)
    key_place = jnp.arange(length, dtype=jnp.int32)

    def one_block(block_start):
        block_query = lax.dynamic_slice_in_dim(query_data, block_start, block_rows, 0)
        scores = jnp.einsum('rgcd,jgd->gcrj', block_query, key_tensor, precision=lax.Precision.HIGHEST)
        scores = lowered_backward(scores * score_scale)
        query_place = block_start + jnp.arange(block_rows, dtype=jnp.int32)
        allowed = key_place[None, :] <= query_place[:, None]
        scores = jnp.where(allowed, scores, masked_score)
        top_score = lax.optimization_barrier(jnp.max(scores, axis=-1, keepdims=True))
        exponent = jnp.exp(scores - top_score)
        weights = exponent / lax.optimization_barrier(jnp.sum(exponent, axis=-1, keepdims=True))
        return jnp.einsum('gcrj,jgd->rgcd', lowered_precision(weights), value_tensor, precision=lax.Precision.HIGHEST)
    starts = jnp.arange(length // block_rows, dtype=jnp.int32) * block_rows
    mixed_blocks = lax.map(jax.checkpoint(one_block), starts)
    return mixed_blocks.reshape(query_data.shape)

def expert_slots(routes):
    flat_routes = routes.reshape(-1).astype(jnp.int32)
    per_block = TOK_DEV * TOPK
    blocks = flat_routes.shape[0] // per_block
    grouped = flat_routes.reshape(blocks, per_block)
    onehot = (grouped[:, :, None] == jnp.arange(EXPERTS, dtype=jnp.int32)).astype(jnp.int32)
    running_count = jnp.cumsum(onehot, axis=1).astype(jnp.int32)
    earlier = lax.optimization_barrier(jnp.sum((running_count - onehot) * onehot, axis=2)).astype(jnp.int32)
    slot_place = (jnp.arange(blocks, dtype=jnp.int32)[:, None] * MOST + earlier).reshape(-1).astype(jnp.int32)
    pair_ids = jnp.arange(flat_routes.shape[0], dtype=jnp.int32)
    slot_table = jnp.zeros((EXPERTS, blocks * MOST), jnp.int32).at[flat_routes, slot_place].set(pair_ids)
    filled = jnp.zeros((EXPERTS, blocks * MOST), jnp.float32).at[flat_routes, slot_place].set(1.0)
    return (slot_table, filled)

def block_forward(params, routes, slot_table, filled):
    tokens, attn_gain, ffn_gain, query_projection, key_projection, value_projection, w_out, w_router, shared_gate, shared_up, shared_down, expert_gate, expert_up, expert_down = params
    row_count = SEQUENCE_LENGTH * SEQUENCE_COUNT
    group_members = QUERY_HEADS // KEY_VALUE_HEADS
    hidden_in = tokens.reshape(row_count, MODEL_DIM)
    first_normalized = lowered_precision(rms_scale(hidden_in, attn_gain))
    query_rows = lowered_backward(lowered_precision(matrix_multiply(first_normalized, query_projection))).reshape(SEQUENCE_LENGTH, SEQUENCE_COUNT, KEY_VALUE_HEADS, group_members, HEAD_SIZE)
    key_tensor = lowered_backward(lowered_precision(matrix_multiply(first_normalized, key_projection))).reshape(SEQUENCE_LENGTH, SEQUENCE_COUNT, KEY_VALUE_HEADS, HEAD_SIZE)
    value_tensor = lowered_backward(lowered_precision(matrix_multiply(first_normalized, value_projection))).reshape(SEQUENCE_LENGTH, SEQUENCE_COUNT, KEY_VALUE_HEADS, HEAD_SIZE)
    mixed_all = lax.map(lambda scan_items: attend_sequence(*scan_items), (query_rows.transpose(1, 0, 2, 3, 4), key_tensor.transpose(1, 0, 2, 3), value_tensor.transpose(1, 0, 2, 3)))
    mixed_all = mixed_all.transpose(1, 0, 2, 3, 4).reshape(row_count, QUERY_HEADS * HEAD_SIZE)
    mixed_all = lowered_backward(lowered_precision(mixed_all))
    residual = hidden_in + lowered_backward(matrix_multiply(mixed_all, w_out))
    normed_two = lowered_precision(rms_scale(residual, ffn_gain))
    logits = matrix_multiply(normed_two, w_router)
    flat_routes = routes.reshape(row_count, TOPK)
    onehot = (flat_routes[:, :, None] == jnp.arange(EXPERTS, dtype=jnp.int32)).astype(jnp.float32)
    chosen = lax.optimization_barrier(jnp.sum(onehot * logits[:, None, :], axis=-1))
    top_logit = lax.optimization_barrier(jnp.max(chosen, axis=-1, keepdims=True))
    exponent = jnp.exp(chosen - top_logit)
    gate_probs = exponent / lax.optimization_barrier(jnp.sum(exponent, axis=-1, keepdims=True))
    shared_hidden = lowered_precision(swiglu(lowered_backward(matrix_multiply(normed_two, shared_gate)), lowered_backward(matrix_multiply(normed_two, shared_up))))
    shared_result = matrix_multiply(shared_hidden, shared_down)
    pair_gates = gate_probs.reshape(-1)

    def one_expert(scan_items):
        slot_pairs, slot_filled, gate_weight, up_weight, down_weight = scan_items
        token_rows = slot_pairs // TOPK
        expert_input = lowered_backward(normed_two[token_rows])
        gate_part = lowered_backward(matrix_multiply(expert_input, gate_weight))
        up_part = lowered_backward(matrix_multiply(expert_input, up_weight))
        expert_hidden = lowered_precision(swiglu(gate_part, up_part))
        result = lowered_backward(lowered_precision(matrix_multiply(expert_hidden, down_weight)))
        return result * (pair_gates[slot_pairs] * slot_filled)[:, None]
    weighted = lax.map(jax.checkpoint(one_expert), (slot_table, filled, expert_gate, expert_up, expert_down))
    target_rows = (slot_table // TOPK).reshape(-1)
    mixture = jnp.zeros((row_count, MODEL_DIM), jnp.float32).at[target_rows].add(weighted.reshape(-1, MODEL_DIM))
    return lowered_precision(residual + shared_result + mixture)

def reference(tokens, routes, out_grad, attn_gain, ffn_gain, query_projection, key_projection, value_projection, w_out, w_router, shared_gate, shared_up, shared_down, expert_gate, expert_up, expert_down):
    slot_table, filled = expert_slots(routes)
    params = tuple((array.astype(jnp.float32) for array in (tokens, attn_gain, ffn_gain, query_projection, key_projection, value_projection, w_out, w_router, shared_gate, shared_up, shared_down, expert_gate, expert_up, expert_down)))
    result, pullback = jax.vjp(lambda *params_in: block_forward(params_in, routes, slot_table, filled), *params)
    grads = pullback(out_grad.reshape(SEQUENCE_LENGTH * SEQUENCE_COUNT, MODEL_DIM).astype(jnp.float32))
    return (result.reshape(SEQUENCE_LENGTH, SEQUENCE_COUNT, MODEL_DIM).astype(jnp.bfloat16), grads[0].reshape(SEQUENCE_LENGTH, SEQUENCE_COUNT, MODEL_DIM), grads[1], grads[2], grads[3], grads[4], grads[5], grads[6], grads[7], grads[8], grads[9], grads[10], grads[11], grads[12], grads[13])
```

```python
import functools
import math

import jax
import jax.numpy as jnp
from jax import lax
from jax.experimental import pallas as pl
from jax.experimental.pallas import tpu as pltpu
from jax.sharding import PartitionSpec as P

QUERY_HEADS = 12
KEY_VALUE_HEADS = 4
HEAD_SIZE = 128
GROUP_MEMBERS = QUERY_HEADS // KEY_VALUE_HEADS

epsilon = 1e-06
masked_score = -1e30
MESH = pl.DeviceIdType.MESH
VMEM_LIMIT = 63 * 1024 * 1024
f32 = jnp.float32
bf16 = jnp.bfloat16


def round_up(number, step):
    return -(-number // step) * step


def nn(left, right):
    return lax.dot_general(left, right, (((1,), (0,)), ((), ())), preferred_element_type=f32)


def nt(left, right):
    return lax.dot_general(left, right, (((1,), (1,)), ((), ())), preferred_element_type=f32)


def tn(left, right):
    return lax.dot_general(left, right, (((0,), (0,)), ((), ())), preferred_element_type=f32)


def place():
    core = lax.axis_index("seq")
    chip = lax.axis_index("fsdp")
    return core, chip, chip // KEY_VALUE_HEADS, lax.rem(chip, KEY_VALUE_HEADS)


def group(kind, shards):
    core, chip, outer, inner = place()
    if kind == "plane":
        size = 2 * KEY_VALUE_HEADS
        return (
            size,
            core * KEY_VALUE_HEADS + inner,
            lambda r: (r // KEY_VALUE_HEADS, outer * KEY_VALUE_HEADS + lax.rem(r, KEY_VALUE_HEADS)),
        )
    if kind == "inner":
        return KEY_VALUE_HEADS, inner, lambda r: (core, outer * KEY_VALUE_HEADS + r)
    if kind == "outer":
        return shards // KEY_VALUE_HEADS, outer, lambda r: (core, r * KEY_VALUE_HEADS + inner)
    if kind == "chips":
        return shards, chip, lambda r: (core, r)
    if kind == "all":
        return 2 * shards, core * shards + chip, lambda r: (r // shards, lax.rem(r, shards))
    return 2, core, lambda r: (r, chip)


def repeat(first, last, step):
    if last - first <= 16:
        for index in range(first, last):
            step(index)
    else:

        def one(index, carry):
            step(index)
            return carry

        lax.fori_loop(first, last, one, 0)


class Wires:
    def __init__(self, shards, send_sems, recv_sems, local_sems):
        self.shards = shards
        self.send_sems, self.recv_sems, self.local_sems = send_sems, recv_sems, local_sems
        self.used = 0
        self.leaving = []

    def greet(self, kinds):
        barrier = pltpu.get_barrier_semaphore()
        total = 0
        for kind in kinds:
            size, me, device = group(kind, self.shards)

            def signal(d, size=size, me=me, device=device):
                pl.semaphore_signal(
                    barrier, inc=1, device_id=device(lax.rem(me + d, size)), device_id_type=MESH
                )

            repeat(1, size, signal)
            total += size - 1
        pl.semaphore_wait(barrier, total)

    def take(self, count):
        base = self.used
        self.used += count
        return base

    def remote(self, source, target, index, device):
        return pltpu.make_async_remote_copy(
            src_ref=source,
            dst_ref=target,
            send_sem=self.send_sems.at[index],
            recv_sem=self.recv_sems.at[index],
            device_id=device,
            device_id_type=MESH,
        )

    def local(self, source, target, index):
        return pltpu.make_async_copy(source, target, self.local_sems.at[index])

    def exchange(self, kind, source_for, target_from, own=True):
        size, me, device = group(kind, self.shards)
        base = self.take(size)

        def copy(d):
            to = lax.rem(me + d, size)
            return self.remote(source_for(to), target_from(me), base + d, device(to))

        repeat(1, size, lambda d: copy(d).start())
        if own:
            self.local(source_for(me), target_from(me), base).start()
        self.leaving.append(lambda: repeat(1, size, lambda d: copy(d).wait_send()))

        def arrive(then=None):
            def one(d):
                came = lax.rem(me - d + size, size)
                place_of = target_from(came)
                self.remote(place_of, place_of, base + d, device(came)).wait_recv()
                if then is not None:
                    then(came)

            repeat(1, size, one)
            if own:
                self.local(source_for(me), target_from(me), base).wait()

        return arrive

    def sibling(self, source, target, comes):
        core, chip, _, _ = place()
        device = (1 - core, chip)
        index = self.take(1)
        copy = self.remote(source, target, index, device)
        copy.start()
        self.leaving.append(copy.wait_send)
        return self.remote(comes, comes, index, device).wait_recv

    def finish(self):
        for leave in self.leaving:
            leave()


def transfer(name, collective, shards, kinds, sems, body, operands, outs):
    count = len(operands)

    def kernel(*refs):
        ins, results = refs[:count], refs[count : count + len(outs)]
        wires = Wires(shards, *refs[count + len(outs) :])
        wires.greet(kinds)
        body(wires, ins, results)
        wires.finish()

    return pl.pallas_call(
        kernel,
        out_shape=[jax.ShapeDtypeStruct(shape, kind) for shape, kind in outs],
        in_specs=[pl.BlockSpec(memory_space=pl.ANY)] * count,
        out_specs=[pl.BlockSpec(memory_space=pl.ANY)] * len(outs),
        scratch_shapes=[pltpu.SemaphoreType.DMA((sems,))] * 3,
        compiler_params=pltpu.CompilerParams(collective_id=collective, has_side_effects=True),
        name=name,
    )(*operands)


def attend_kernel(chunk, n_out, q_ref, kv_ref, mixed_ref, log_ref):
    outer = lax.axis_index("fsdp") // KEY_VALUE_HEADS
    factor = HEAD_SIZE**-0.5 * math.log2(math.e)
    for half in range(2):
        query = q_ref[pl.ds(half * chunk, chunk), :]

        def fold(block, carry, masked, query=query):
            largest, total, summed = carry
            rows = pl.ds(pl.multiple_of((block // n_out) * chunk, chunk), chunk)
            key = kv_ref[lax.rem(block, n_out), rows, 0:HEAD_SIZE]
            value = kv_ref[lax.rem(block, n_out), rows, HEAD_SIZE : 2 * HEAD_SIZE]
            scores = nt(key, query)
            if masked:
                key_at = lax.broadcasted_iota(jnp.int32, scores.shape, 0)
                query_at = lax.broadcasted_iota(jnp.int32, scores.shape, 1)
                scores = jnp.where(key_at <= query_at, scores, masked_score)
            new = jnp.maximum(largest, jnp.max(scores, axis=0, keepdims=True))
            weights = jnp.exp2((scores - new) * factor)
            shrink = jnp.exp2((largest - new) * factor)
            total = total * shrink + jnp.sum(weights, axis=0, keepdims=True)
            summed = summed * shrink + tn(value, weights.astype(bf16))
            return new, total, summed

        start = (
            jnp.full((1, chunk), masked_score, f32),
            jnp.zeros((1, chunk), f32),
            jnp.zeros((HEAD_SIZE, chunk), f32),
        )
        own = half * n_out + outer
        carry = fold(own, start, True)
        largest, total, summed = lax.fori_loop(
            0, own, lambda block, carry: fold(block, carry, False), carry
        )
        mixed_ref[pl.ds(half * chunk, chunk), :] = (summed / total).T
        log_ref[0, half : half + 1, :] = largest * factor + jnp.log2(total)


def attend(chunk, n_out, qkv, kv_all):
    rows = 2 * chunk
    return pl.pallas_call(
        functools.partial(attend_kernel, chunk, n_out),
        grid=(GROUP_MEMBERS,),
        in_specs=[
            pl.BlockSpec((rows, HEAD_SIZE), lambda h: (0, h)),
            pl.BlockSpec(kv_all.shape, lambda h: (0, 0, 0), pipeline_mode=pl.Buffered(1)),
        ],
        out_specs=[
            pl.BlockSpec((rows, HEAD_SIZE), lambda h: (0, h)),
            pl.BlockSpec((1, 2, chunk), lambda h: (h, 0, 0)),
        ],
        out_shape=[
            jax.ShapeDtypeStruct((rows, GROUP_MEMBERS * HEAD_SIZE), f32),
            jax.ShapeDtypeStruct((GROUP_MEMBERS, 2, chunk), f32),
        ],
        compiler_params=pltpu.CompilerParams(vmem_limit_bytes=VMEM_LIMIT),
        name="attend",
    )(qkv, kv_all)


def attend_back_kernel(
    chunk, n_out, q_ref, kv_ref, grad_ref, log_ref, delta_ref, dq_ref, dkv_ref, sums
):
    head = pl.program_id(0)
    outer = lax.axis_index("fsdp") // KEY_VALUE_HEADS
    scale = HEAD_SIZE**-0.5
    factor = scale * math.log2(math.e)

    @pl.when(head == 0)
    def _():
        sums[...] = jnp.zeros_like(sums)

    for half in range(2):
        mine = pl.ds(half * chunk, chunk)
        query = q_ref[mine, :]
        grad = grad_ref[mine, :]
        log_row = log_ref[0, half : half + 1, :]
        delta_row = delta_ref[0, half : half + 1, :]

        def fold(block, dq, masked, query=query, grad=grad, log_row=log_row, delta_row=delta_row):
            at = lax.rem(block, n_out)
            rows = pl.ds(pl.multiple_of((block // n_out) * chunk, chunk), chunk)
            key = kv_ref[at, rows, 0:HEAD_SIZE]
            value = kv_ref[at, rows, HEAD_SIZE : 2 * HEAD_SIZE]
            scores = nt(key, query)
            if masked:
                key_at = lax.broadcasted_iota(jnp.int32, scores.shape, 0)
                query_at = lax.broadcasted_iota(jnp.int32, scores.shape, 1)
                scores = jnp.where(key_at <= query_at, scores, masked_score)
            weights = jnp.exp2(scores * factor - log_row)
            grad_scores = (weights * (nt(value, grad) - delta_row)).astype(bf16)
            sums[at, rows, 0:HEAD_SIZE] += nn(grad_scores, query)
            sums[at, rows, HEAD_SIZE : 2 * HEAD_SIZE] += nn(weights.astype(bf16), grad)
            return dq + tn(grad_scores, key)

        own = half * n_out + outer
        dq = fold(own, jnp.zeros((chunk, HEAD_SIZE), f32), True)
        dq = lax.fori_loop(0, own, lambda block, dq: fold(block, dq, False), dq)
        dq_ref[mine, :] = (dq * scale).astype(bf16)

    @pl.when(head == GROUP_MEMBERS - 1)
    def _():
        dkv_ref[...] = sums[...].astype(bf16)


def attend_back(chunk, n_out, qkv, kv_all, grad_mixed, log_rows, delta_rows):
    rows = 2 * chunk
    per_head = pl.BlockSpec((rows, HEAD_SIZE), lambda h: (0, h))
    per_row = pl.BlockSpec((1, 2, chunk), lambda h: (h, 0, 0))
    whole = pl.BlockSpec(kv_all.shape, lambda h: (0, 0, 0), pipeline_mode=pl.Buffered(1))
    return pl.pallas_call(
        functools.partial(attend_back_kernel, chunk, n_out),
        grid=(GROUP_MEMBERS,),
        in_specs=[per_head, whole, per_head, per_row, per_row],
        out_specs=[per_head, whole],
        out_shape=[
            jax.ShapeDtypeStruct((rows, GROUP_MEMBERS * HEAD_SIZE), bf16),
            jax.ShapeDtypeStruct(kv_all.shape, bf16),
        ],
        scratch_shapes=[pltpu.VMEM(kv_all.shape, f32)],
        compiler_params=pltpu.CompilerParams(vmem_limit_bytes=VMEM_LIMIT),
        name="attend_back",
    )(qkv, kv_all, grad_mixed, log_rows, delta_rows)


def swiglu_parts(gate_part, up_part):
    sigmoid = jax.nn.sigmoid(gate_part)
    active = gate_part * sigmoid
    slope = up_part * sigmoid * (1.0 + gate_part * (1.0 - sigmoid))
    return active * up_part, active, slope


def experts_kernel(
    room,
    hidden,
    h_ref,
    c_ref,
    meta_ref,
    wg_ref,
    wu_ref,
    wd_ref,
    sgu_ref,
    sd_ref,
    out_ref,
    dh_ref,
    dgate_ref,
    dwg_ref,
    dwu_ref,
    dwd_ref,
    dsgu_ref,
    dsd_ref,
    sum_out,
    sum_dh,
    h_rows,
    c_rows,
    picks,
    gate_col,
):
    expert = pl.program_id(0)
    blocks, rows, width = h_ref.shape

    @pl.when(expert == 0)
    def _():
        dgate_ref[...] = jnp.zeros_like(dgate_ref)
        hid = h_ref[...].reshape(blocks * rows, width)
        cot = c_ref[...].reshape(blocks * rows, width)
        gate_w, up_w, down_w = sgu_ref[:, 0:hidden], sgu_ref[:, hidden : 2 * hidden], sd_ref[...]
        both, active, slope = swiglu_parts(nn(hid, gate_w), nn(hid, up_w))
        act = both.astype(bf16)
        d_act = nt(cot, down_w)
        d_gate = (d_act * slope).astype(bf16)
        d_up = (d_act * active).astype(bf16)
        sum_out[...] = nn(act, down_w)
        sum_dh[...] = nt(d_gate, gate_w) + nt(d_up, up_w)
        dsgu_ref[:, 0:hidden] = tn(hid, d_gate).astype(bf16)
        dsgu_ref[:, hidden : 2 * hidden] = tn(hid, d_up).astype(bf16)
        dsd_ref[...] = tn(act, cot).astype(bf16)

    slots = lax.broadcasted_iota(jnp.int32, (room, rows), 0).astype(f32)
    for block in range(blocks):
        part = pl.ds(block * room, room)
        gate_row = meta_ref[block, pl.ds(expert, 1), :]
        slot_row = meta_ref[block, pl.ds(expert + KEY_VALUE_HEADS, 1), :]
        pick = (slots == slot_row).astype(f32)
        gate_col[part, :] = jnp.broadcast_to(
            jnp.sum(pick * gate_row, axis=1, keepdims=True), (room, gate_col.shape[1])
        )
        pick = pick.astype(bf16)
        picks[block] = pick
        h_rows[part, :] = nn(pick, h_ref[block]).astype(bf16)
        c_rows[part, :] = nn(pick, c_ref[block]).astype(bf16)
    gate = gate_col[:, 0:1]
    gate_w, up_w, down_w = wg_ref[0], wu_ref[0], wd_ref[0]
    both, active, slope = swiglu_parts(nn(h_rows[...], gate_w), nn(h_rows[...], up_w))
    act = both.astype(bf16)
    d_act = nt(c_rows[...], down_w)
    d_gates = jnp.sum(d_act * act.astype(f32), axis=1, keepdims=True)
    d_act = d_act * gate
    act = (act.astype(f32) * gate).astype(bf16)
    d_gate = (d_act * slope).astype(bf16)
    d_up = (d_act * active).astype(bf16)
    dwd_ref[0] = tn(act, c_rows[...]).astype(bf16)
    dwg_ref[0] = tn(h_rows[...], d_gate).astype(bf16)
    dwu_ref[0] = tn(h_rows[...], d_up).astype(bf16)
    result = nn(act, down_w).astype(bf16)
    d_rows = (nt(d_gate, gate_w) + nt(d_up, up_w)).astype(bf16)
    for block in range(blocks):
        pick = picks[block]
        part = slice(block * room, (block + 1) * room)
        here = pl.ds(block * rows, rows)
        sum_out[here, :] += tn(pick, result[part])
        sum_dh[here, :] += tn(pick, d_rows[part])
        dgate_ref[block, pl.ds(expert, 1), :] = jnp.sum(
            pick.astype(f32) * d_gates[part], axis=0, keepdims=True
        )

    @pl.when(expert == pl.num_programs(0) - 1)
    def _():
        out_ref[...] = sum_out[...].astype(bf16).reshape(out_ref.shape)
        dh_ref[...] = sum_dh[...].astype(bf16).reshape(dh_ref.shape)


def experts(room, hidden, h_all, c_all, meta, wg, wu, wd, sgu, sd):
    blocks, rows, width = h_all.shape
    n_experts, _, inner = wg.shape

    def once(shape):
        return pl.BlockSpec(shape, lambda e: (0,) * len(shape), pipeline_mode=pl.Buffered(1))

    def each(shape, **kind):
        return pl.BlockSpec((1,) + shape[1:], lambda e: (e, 0, 0), **kind)

    single = dict(pipeline_mode=pl.Buffered(1))
    return pl.pallas_call(
        functools.partial(experts_kernel, room, hidden),
        grid=(n_experts,),
        in_specs=[
            once(h_all.shape),
            once(c_all.shape),
            once(meta.shape),
            each(wg.shape),
            each(wu.shape),
            each(wd.shape),
            once(sgu.shape),
            once(sd.shape),
        ],
        out_specs=[
            once(h_all.shape),
            once(h_all.shape),
            once(meta.shape),
            each(wg.shape, **single),
            each(wu.shape, **single),
            each(wd.shape, **single),
            once(sgu.shape),
            once(sd.shape),
        ],
        out_shape=[
            jax.ShapeDtypeStruct(h_all.shape, bf16),
            jax.ShapeDtypeStruct(h_all.shape, bf16),
            jax.ShapeDtypeStruct(meta.shape, f32),
            jax.ShapeDtypeStruct(wg.shape, bf16),
            jax.ShapeDtypeStruct(wu.shape, bf16),
            jax.ShapeDtypeStruct(wd.shape, bf16),
            jax.ShapeDtypeStruct(sgu.shape, bf16),
            jax.ShapeDtypeStruct(sd.shape, bf16),
        ],
        scratch_shapes=[
            pltpu.VMEM((blocks * rows, width), f32),
            pltpu.VMEM((blocks * rows, width), f32),
            pltpu.VMEM((blocks * room, width), bf16),
            pltpu.VMEM((blocks * room, width), bf16),
            pltpu.VMEM((blocks, room, rows), bf16),
            pltpu.VMEM((blocks * room, 128), f32),
        ],
        compiler_params=pltpu.CompilerParams(vmem_limit_bytes=VMEM_LIMIT),
        name="experts",
    )(h_all, c_all, meta, wg, wu, wd, sgu, sd)


def norm_rows(values, gain_vector):
    inverse = lax.rsqrt(jnp.mean(values * values, axis=-1, keepdims=True) + epsilon)
    normed = values * inverse
    return (normed, inverse, normed * gain_vector)


def norm_back(grad_hidden, normed, inverse, gain_vector):
    grad_normed = grad_hidden * gain_vector
    gain_grad = jnp.sum(grad_hidden * normed, axis=(0, 1))
    inner_mean = jnp.mean(grad_normed * normed, axis=-1, keepdims=True)
    return (inverse * (grad_normed - normed * inner_mean), gain_grad)


def pad_rows(array, axis):
    size = array.shape[axis]
    widths = [(0, 0)] * array.ndim
    widths[axis] = (0, round_up(size, 16) - size)
    return jnp.pad(array, widths) if widths[axis][1] else array


def pad_to(array, axis, size):
    widths = [(0, 0)] * array.ndim
    widths[axis] = (0, size - array.shape[axis])
    return jnp.pad(array, widths) if widths[axis][1] else array


def body(
    tokens,
    routes,
    out_grad,
    attn_gain,
    ffn_gain,
    query_projection,
    key_projection,
    value_projection,
    w_out,
    w_router,
    shared_gate,
    shared_up,
    shared_down,
    expert_gate,
    expert_up,
    expert_down,
):
    shards = lax.axis_size("fsdp")
    n_in = KEY_VALUE_HEADS
    n_out = shards // n_in
    core, chip, outer, inner = place()
    seg, seqs, width = tokens.shape
    rows = seg * seqs
    topk = routes.shape[2]
    n_experts = w_router.shape[1]
    w_rows = query_projection.shape[0]
    w_pad = round_up(w_rows, 16)
    d_rows = shared_down.shape[0]
    d_pad = round_up(d_rows, 16)
    half_chips = shards // 2
    q_cols = GROUP_MEMBERS * HEAD_SIZE
    cols = q_cols + 2 * HEAD_SIZE
    ff = expert_gate.shape[2]
    hid_core = n_in * d_rows
    hid = 2 * hid_core
    hid_pad = round_up(hid, 128)
    small = round_up(n_experts + 2, 128)
    gu_cols = 2 * hid_pad + small
    chunk = n_in * seg
    half_width, half_ff = width // 2, ff // 2
    room = round_up(max(2, (3 * rows * topk + 2 * n_experts - 1) // (2 * n_experts)), 16)

    q_pieces = pad_rows(
        jnp.concatenate(
            [
                query_projection.reshape(w_rows, n_in, q_cols),
                key_projection.reshape(w_rows, n_in, HEAD_SIZE),
                value_projection.reshape(w_rows, n_in, HEAD_SIZE),
            ],
            axis=2,
        ).transpose(1, 0, 2),
        1,
    )

    def hidden_piece(weight):
        piece = weight.reshape(w_rows, 2, n_out, hid_core).transpose(2, 0, 1, 3)
        return pad_to(piece.reshape(n_out, w_rows, hid), 2, hid_pad)

    small_piece = pad_to(
        jnp.concatenate([w_router, attn_gain[:, None], ffn_gain[:, None]], axis=1), 1, small
    )
    gu_pieces = pad_rows(
        jnp.concatenate(
            [
                hidden_piece(shared_gate),
                hidden_piece(shared_up),
                jnp.broadcast_to(small_piece[None], (n_out, w_rows, small)),
            ],
            axis=2,
        ),
        1,
    )
    out_piece = pad_rows(w_out, 0)
    down_piece = pad_rows(shared_down, 0)
    x_own = tokens.transpose(1, 0, 2)
    c_own = out_grad.transpose(1, 0, 2)
    cot = c_own.reshape(rows, width)

    def fetch(wires, ins, outs):
        x_ref, c_ref, q_ref, gu_ref, o_ref, s_ref, eg_ref, eu_ref, ed_ref = ins
        xs_ref, cs_ref, wq_ref, wgu_ref, wo_ref, ws_ref, ag_ref, au_ref, ad_ref = outs
        core, chip, outer, inner = place()
        x_in = wires.exchange("plane", lambda r: x_ref.at[r // n_in], lambda r: xs_ref.at[r])
        q_in = wires.exchange(
            "chips", lambda r: q_ref.at[lax.rem(r, n_in)], lambda r: wq_ref.at[core, r]
        )
        gu_in = wires.exchange(
            "chips", lambda r: gu_ref.at[r // n_in], lambda r: wgu_ref.at[core, r]
        )
        s_in = wires.exchange("inner", lambda r: s_ref, lambda r: ws_ref.at[core, r])
        o_in = out_rows(wires, o_ref, wo_ref)
        halves = (
            (eg_ref, ag_ref, pl.ds(core * half_width, half_width)),
            (eu_ref, au_ref, pl.ds(core * half_width, half_width)),
            (ed_ref, ad_ref, pl.ds(core * half_ff, half_ff)),
        )
        others = (
            pl.ds((1 - core) * half_width, half_width),
            pl.ds((1 - core) * half_width, half_width),
            pl.ds((1 - core) * half_ff, half_ff),
        )
        e_in = [
            wires.exchange(
                "inner",
                lambda r, mine=mine, part=part: mine.at[0, part],
                lambda r, every=every, part=part: every.at[r, part],
                own=False,
            )
            for mine, every, part in halves
        ]
        c_in = wires.exchange("outer", lambda r: c_ref, lambda r: cs_ref.at[r])
        later = [
            wires.sibling(mine.at[0], every.at[inner], every.at[inner])
            for mine, every, part in halves
        ]
        q_in()
        later.append(wires.sibling(wq_ref.at[core], wq_ref.at[core], wq_ref.at[1 - core]))
        gu_in()
        later.append(wires.sibling(wgu_ref.at[core], wgu_ref.at[core], wgu_ref.at[1 - core]))
        s_in()
        later.append(wires.sibling(ws_ref.at[core], ws_ref.at[core], ws_ref.at[1 - core]))
        x_in()
        o_in()
        for (mine, every, part), other, arrive in zip(halves, others, e_in):
            base = wires.take(n_in)
            device = (1 - core, chip)

            def forward(r, every=every, part=part, base=base):
                wires.remote(every.at[r, part], every.at[r, part], base + r, device).start()

            arrive(forward)

            def settle(every=every, part=part, other=other, base=base):
                def one(d):
                    r = lax.rem(inner + d, n_in)
                    copy = wires.remote(every.at[r, part], every.at[r, part], base + r, device)
                    copy.wait_send()
                    wires.remote(
                        every.at[r, other], every.at[r, other], base + r, device
                    ).wait_recv()

                repeat(1, n_in, one)

            later.append(settle)
        c_in()
        for wait in later:
            wait()

    def out_rows(wires, o_ref, wo_ref):
        core, chip, outer, inner = place()
        to_inner = 2 * core + chip // half_chips
        slot = lax.rem(chip, half_chips)
        base = wires.take(half_chips)
        sends = wires.take(2 * n_out)

        def copy(k):
            to = (k // n_out, lax.rem(k, n_out) * n_in + to_inner)
            here = (to[0] == core) & (to[1] == chip)
            return here, pltpu.make_async_remote_copy(
                src_ref=o_ref,
                dst_ref=wo_ref.at[slot],
                send_sem=wires.send_sems.at[sends + k],
                recv_sem=wires.recv_sems.at[base + slot],
                device_id=to,
                device_id_type=MESH,
            )

        def start(k):
            here, send = copy(k)
            pl.when(jnp.logical_not(here))(send.start)
            pl.when(here)(lambda: wires.local(o_ref, wo_ref.at[slot], base).start())

        def leave(k):
            here, send = copy(k)
            pl.when(jnp.logical_not(here))(send.wait_send)

        def come(i):
            origin = (inner // 2, half_chips * lax.rem(inner, 2) + i)
            here = (origin[0] == core) & (origin[1] == chip)
            place_of = wo_ref.at[i]
            pl.when(jnp.logical_not(here))(
                wires.remote(place_of, place_of, base + i, origin).wait_recv
            )
            pl.when(here)(lambda: wires.local(o_ref, place_of, base).wait())

        repeat(0, 2 * n_out, start)
        wires.leaving.append(lambda: repeat(0, 2 * n_out, leave))
        return lambda: repeat(0, half_chips, come)

    def out_rows_back(wires, grad_ref, sums_ref):
        core, chip, outer, inner = place()
        from_inner = 2 * core + chip // half_chips
        slot = core * n_out + outer
        sends = wires.take(half_chips)
        base = wires.take(2 * n_out)

        def copy(i):
            to = (inner // 2, half_chips * lax.rem(inner, 2) + i)
            here = (to[0] == core) & (to[1] == chip)
            return here, pltpu.make_async_remote_copy(
                src_ref=grad_ref.at[i],
                dst_ref=sums_ref.at[slot],
                send_sem=wires.send_sems.at[sends + i],
                recv_sem=wires.recv_sems.at[base + slot],
                device_id=to,
                device_id_type=MESH,
            )

        def start(i):
            here, send = copy(i)
            pl.when(jnp.logical_not(here))(send.start)
            pl.when(here)(lambda: wires.local(grad_ref.at[i], sums_ref.at[slot], base).start())

        def leave(i):
            here, send = copy(i)
            pl.when(jnp.logical_not(here))(send.wait_send)

        def come(k):
            origin = (k // n_out, lax.rem(k, n_out) * n_in + from_inner)
            here = (origin[0] == core) & (origin[1] == chip)
            place_of = sums_ref.at[k]
            pl.when(jnp.logical_not(here))(
                wires.remote(place_of, place_of, base + k, origin).wait_recv
            )
            pl.when(here)(lambda: wires.local(place_of, place_of, base).wait())

        repeat(0, half_chips, start)
        wires.leaving.append(lambda: repeat(0, half_chips, leave))
        return lambda: repeat(0, 2 * n_out, come)

    xs, c_all, wq, wgu, wo, ws, e_gate, e_up, e_down = transfer(
        "fetch",
        0,
        shards,
        ["all"],
        4 * shards + 64,
        fetch,
        [
            x_own,
            cot,
            q_pieces,
            gu_pieces,
            out_piece,
            down_piece,
            expert_gate,
            expert_up,
            expert_down,
        ],
        [
            ((2 * n_in, seg, width), bf16),
            ((n_out, rows, width), bf16),
            ((2, shards, w_pad, cols), bf16),
            ((2, shards, w_pad, gu_cols), bf16),
            ((half_chips, w_pad, width), bf16),
            ((2, n_in, d_pad, width), bf16),
            ((n_in, width, ff), bf16),
            ((n_in, width, ff), bf16),
            ((n_in, ff, width), bf16),
        ],
    )
    wq = wq[:, :, :w_rows].reshape(width, cols)
    wgu = wgu[:, :, :w_rows].reshape(width, gu_cols)
    wo = wo[:, :w_rows].reshape(q_cols, width)
    ws = pad_to(ws[:, :, :d_rows].reshape(hid, width), 0, hid_pad)
    small_w = wgu[:, 2 * hid_pad :]
    router_w = small_w[:, :n_experts]
    gain_one = small_w[:, n_experts].astype(f32)
    gain_two = small_w[:, n_experts + 1].astype(f32)

    h1 = norm_rows(xs.reshape(2 * chunk, width).astype(f32), gain_one)[2].astype(bf16)
    qkv = nn(h1, wq).astype(bf16)

    def spread_kv(wires, ins, outs):
        wires.exchange("outer", lambda r: ins[0], lambda r: outs[0].at[r])()

    (kv_all,) = transfer(
        "spread_kv",
        1,
        shards,
        ["outer"],
        n_out,
        spread_kv,
        [qkv[:, q_cols:]],
        [((n_out, 2 * chunk, 2 * HEAD_SIZE), bf16)],
    )
    mixed, log_rows = attend(chunk, n_out, qkv, kv_all)
    mixed_low = mixed.astype(bf16)
    out_part = nn(mixed_low, wo).astype(bf16).reshape(2 * n_in, seg, width)

    def sum_plane(wires, ins, outs):
        wires.exchange("plane", lambda r: ins[0].at[r], lambda r: outs[0].at[r])()

    (out_parts,) = transfer(
        "sum_out",
        2,
        shards,
        ["plane"],
        2 * n_in,
        sum_plane,
        [out_part],
        [((2 * n_in, seg, width), bf16)],
    )
    inputs = x_own.astype(f32)
    residual = inputs + jnp.sum(out_parts.astype(f32).reshape(2, n_in, seg, width), axis=1)

    normed_two, inverse_two, scaled_two = norm_rows(residual, gain_two)
    hidden_two = scaled_two.astype(bf16).reshape(rows, width)
    logits = nn(hidden_two, router_w)
    flat_routes = routes.transpose(1, 0, 2).reshape(rows, topk)
    chooser = (flat_routes[:, :, None] == jnp.arange(n_experts, dtype=jnp.int32)).astype(f32)
    taken = jnp.sum(chooser, axis=1)
    chosen = jnp.where(taken > 0, logits, masked_score)
    exponent = jnp.where(
        taken > 0, jnp.exp(chosen - jnp.max(chosen, axis=-1, keepdims=True)), 0.0
    )
    gates = exponent / jnp.sum(exponent, axis=-1, keepdims=True)
    before = (
        lax.broadcasted_iota(jnp.int32, (rows, rows), 0)
        < lax.broadcasted_iota(jnp.int32, (rows, rows), 1)
    ).astype(bf16)
    slots = jnp.where(taken.T > 0, nn(taken.T.astype(bf16), before), -1.0)
    meta = jnp.concatenate(
        [gates.T.reshape(n_out, n_in, rows), slots.reshape(n_out, n_in, rows)], axis=1
    )

    def spread_hidden(wires, ins, outs):
        first = wires.exchange("outer", lambda r: ins[0], lambda r: outs[0].at[r])
        second = wires.exchange("outer", lambda r: ins[1].at[r], lambda r: outs[1].at[r])
        first()
        second()

    h_all, meta_all = transfer(
        "spread_hidden",
        3,
        shards,
        ["outer"],
        2 * n_out,
        spread_hidden,
        [hidden_two, meta],
        [((n_out, rows, width), bf16), ((n_out, 2 * n_in, rows), f32)],
    )

    sgu = wgu[:, : 2 * hid_pad]
    at_once = math.gcd(n_out, 4)
    parts = [
        experts(
            room,
            hid_pad,
            h_all[i : i + at_once],
            c_all[i : i + at_once],
            meta_all[i : i + at_once],
            e_gate,
            e_up,
            e_down,
            sgu,
            ws,
        )
        for i in range(0, n_out, at_once)
    ]
    mix_part, dh_part, dgate_part = (
        jnp.concatenate([part[k] for part in parts], axis=0) if len(parts) > 1 else parts[0][k]
        for k in range(3)
    )
    eg_grad, eu_grad, ed_grad, sgu_grad, sd_grad = (
        sum(part[k].astype(f32) for part in parts).astype(bf16) if len(parts) > 1 else parts[0][k]
        for k in range(3, 8)
    )

    def sum_hidden(wires, ins, outs):
        core, chip, outer, inner = place()
        mix_ref, dh_ref, dg_ref, eg_ref, eu_ref, ed_ref, gu_ref = ins
        mixes, dhs, dgs, egs, eus, eds, gus = outs
        waits = [
            wires.exchange("outer", lambda r: dh_ref.at[r], lambda r: dhs.at[r]),
            wires.exchange("outer", lambda r: dg_ref.at[r], lambda r: dgs.at[r]),
            wires.exchange("outer", lambda r: mix_ref.at[r], lambda r: mixes.at[r]),
        ]
        wide = pl.ds((1 - core) * half_width, half_width)
        deep = pl.ds((1 - core) * half_ff, half_ff)
        waits += [
            wires.sibling(eg_ref.at[:, wide], egs, egs),
            wires.sibling(eu_ref.at[:, wide], eus, eus),
            wires.sibling(ed_ref.at[:, deep], eds, eds),
            wires.sibling(gu_ref.at[wide], gus, gus),
        ]
        for wait in waits:
            wait()

    mixes, dhs, dgs, egs, eus, eds, gus = transfer(
        "sum_hidden",
        4,
        shards,
        ["outer", "core"],
        3 * n_out + 8,
        sum_hidden,
        [mix_part, dh_part, dgate_part, eg_grad, eu_grad, ed_grad, sgu_grad],
        [
            ((n_out, rows, width), bf16),
            ((n_out, rows, width), bf16),
            ((n_out, 2 * n_in, rows), f32),
            ((n_in, half_width, ff), bf16),
            ((n_in, half_width, ff), bf16),
            ((n_in, half_ff, width), bf16),
            ((half_width, 2 * hid_pad), bf16),
        ],
    )

    def with_sibling(own, came, axis):
        size = came.shape[axis]
        mine = lax.dynamic_slice_in_dim(own, core * size, size, axis)
        return (mine.astype(f32) + came.astype(f32)).astype(bf16)

    eg_half = with_sibling(eg_grad, egs, 1)
    eu_half = with_sibling(eu_grad, eus, 1)
    ed_half = with_sibling(ed_grad, eds, 1)
    gu_half = pad_rows(with_sibling(sgu_grad, gus, 0).reshape(shards, w_rows, 2 * hid_pad), 1)
    sd_send = pad_rows(sd_grad[:hid].reshape(2 * n_in, d_rows, width), 1)

    total_out = residual + jnp.sum(mixes.astype(f32), axis=0).reshape(seqs, seg, width)
    grad_float = c_own.astype(f32)
    grad_gates = dgs[:, :n_in].reshape(n_experts, rows).T
    grad_logits = gates * (grad_gates - jnp.sum(gates * grad_gates, axis=-1, keepdims=True))
    router_grad = lax.dot_general(
        hidden_two.astype(f32),
        grad_logits,
        (((0,), (0,)), ((), ())),
        precision=lax.Precision.HIGHEST,
        preferred_element_type=f32,
    )
    grad_hidden_two = jnp.sum(dhs.astype(f32), axis=0) + lax.dot_general(
        grad_logits,
        router_w.astype(f32),
        (((1,), (1,)), ((), ())),
        precision=lax.Precision.HIGHEST,
        preferred_element_type=f32,
    )
    grad_norm_two, gain_two_grad = norm_back(
        grad_hidden_two.reshape(seqs, seg, width), normed_two, inverse_two, gain_two
    )
    grad_residual = grad_float + grad_norm_two
    grad_attn = grad_residual.astype(bf16)

    def spread_grad(wires, ins, outs):
        wires.exchange("plane", lambda r: ins[0].at[r // n_in], lambda r: outs[0].at[r])()

    (grad_all,) = transfer(
        "spread_grad",
        5,
        shards,
        ["plane"],
        2 * n_in,
        spread_grad,
        [grad_attn],
        [((2 * n_in, seg, width), bf16)],
    )
    grad_all = grad_all.reshape(2 * chunk, width)
    grad_mixed = nt(grad_all, wo).astype(bf16)
    wo_grad = pad_rows(tn(mixed_low, grad_all).astype(bf16).reshape(half_chips, w_rows, width), 1)
    delta_rows = jnp.sum(
        (grad_mixed.astype(f32) * mixed).reshape(2, chunk, GROUP_MEMBERS, HEAD_SIZE), axis=-1
    ).transpose(2, 0, 1)

    dq, dkv_part = attend_back(chunk, n_out, qkv, kv_all, grad_mixed, log_rows, delta_rows)

    def sum_kv(wires, ins, outs):
        kv_ref, eg_ref, eu_ref, ed_ref, gu_ref, s_ref, o_ref = ins
        kvs, egs, eus, eds, gus, sds, wos = outs
        waits = [
            wires.exchange("outer", lambda r: kv_ref.at[r], lambda r: kvs.at[r]),
            wires.exchange("plane", lambda r: s_ref.at[r], lambda r: sds.at[r]),
            wires.exchange("chips", lambda r: gu_ref.at[r], lambda r: gus.at[r]),
            out_rows_back(wires, o_ref, wos),
        ]
        waits += [
            wires.exchange(
                "inner",
                lambda r, mine=mine: mine.at[r],
                lambda r, every=every: every.at[r],
                own=False,
            )
            for mine, every in ((eg_ref, egs), (eu_ref, eus), (ed_ref, eds))
        ]
        for wait in waits:
            wait()

    kvs, egs, eus, eds, gus, sds, wos = transfer(
        "sum_kv",
        6,
        shards,
        ["all"],
        4 * shards + 64,
        sum_kv,
        [dkv_part, eg_half, eu_half, ed_half, gu_half, sd_send, wo_grad],
        [
            (kv_all.shape, bf16),
            ((n_in, half_width, ff), bf16),
            ((n_in, half_width, ff), bf16),
            ((n_in, half_ff, width), bf16),
            ((shards, w_pad, 2 * hid_pad), bf16),
            ((2 * n_in, d_pad, width), bf16),
            ((2 * n_out, w_pad, width), bf16),
        ],
    )

    def over_inner(own, came):
        mine = lax.dynamic_index_in_dim(own, inner, 0, keepdims=False).astype(f32)
        total = mine
        for r in range(n_in):
            total = total + jnp.where(inner == r, 0.0, came[r].astype(f32))
        return total.astype(bf16)

    eg_sum, eu_sum, ed_sum = (
        over_inner(eg_half, egs),
        over_inner(eu_half, eus),
        over_inner(ed_half, eds),
    )
    dkv = jnp.sum(kvs.astype(f32), axis=0)
    key_scale = jnp.concatenate(
        [jnp.full((HEAD_SIZE,), HEAD_SIZE**-0.5, f32), jnp.ones((HEAD_SIZE,), f32)]
    )
    dqkv = jnp.concatenate([dq, (dkv * key_scale).astype(bf16)], axis=1)
    dh1_part = nt(dqkv, wq).astype(bf16).reshape(2 * n_in, seg, width)
    wq_grad = tn(h1, dqkv).astype(bf16)

    def sum_first(wires, ins, outs):
        core, chip, outer, inner = place()
        dh_ref, wq_ref, eg_ref, eu_ref, ed_ref = ins
        dhs, wqs, egs, eus, eds = outs
        wide = pl.ds((1 - core) * half_width, half_width)
        waits = [
            wires.exchange("plane", lambda r: dh_ref.at[r], lambda r: dhs.at[r]),
            wires.sibling(wq_ref.at[wide], wqs, wqs),
            wires.sibling(eg_ref, egs, egs),
            wires.sibling(eu_ref, eus, eus),
            wires.sibling(ed_ref, eds, eds),
        ]
        for wait in waits:
            wait()

    dh1s, wqs, eg_other, eu_other, ed_other = transfer(
        "sum_first",
        7,
        shards,
        ["plane"],
        2 * n_in + 8,
        sum_first,
        [dh1_part, wq_grad, eg_sum, eu_sum, ed_sum],
        [
            ((2 * n_in, seg, width), bf16),
            ((half_width, cols), bf16),
            (eg_sum.shape, bf16),
            (eu_sum.shape, bf16),
            (ed_sum.shape, bf16),
        ],
    )
    wq_half = pad_rows(with_sibling(wq_grad, wqs, 0).reshape(shards, w_rows, cols), 1)
    grad_hidden_one = jnp.sum(dh1s.astype(f32).reshape(2, n_in, seg, width), axis=1)
    normed_one, inverse_one, _ = norm_rows(inputs, gain_one)
    grad_norm_one, gain_one_grad = norm_back(grad_hidden_one, normed_one, inverse_one, gain_one)
    tokens_grad = grad_residual + grad_norm_one
    small_grad = pad_to(
        jnp.concatenate([router_grad, gain_one_grad[:, None], gain_two_grad[:, None]], axis=1),
        1,
        small,
    )
    small_send = pad_rows(small_grad.astype(bf16).reshape(2 * shards, w_rows, small), 1)

    def sum_weights(wires, ins, outs):
        first = wires.exchange("chips", lambda r: ins[0].at[r], lambda r: outs[0].at[r])
        second = wires.exchange("all", lambda r: ins[1].at[r], lambda r: outs[1].at[r])
        first()
        second()

    wq_parts, small_parts = transfer(
        "sum_weights",
        8,
        shards,
        ["all"],
        3 * shards,
        sum_weights,
        [wq_half, small_send],
        [((shards, w_pad, cols), bf16), ((2 * shards, w_pad, small), bf16)],
    )

    wq_total = jnp.sum(
        wq_parts[:, :w_rows].astype(f32).reshape(n_out, n_in, w_rows, cols), axis=0
    ).transpose(1, 0, 2)
    query_grad = wq_total[:, :, :q_cols].reshape(w_rows, n_in * q_cols)
    key_grad = wq_total[:, :, q_cols : q_cols + HEAD_SIZE].reshape(w_rows, n_in * HEAD_SIZE)
    value_grad = wq_total[:, :, q_cols + HEAD_SIZE :].reshape(w_rows, n_in * HEAD_SIZE)
    gu_total = jnp.sum(
        gus[:, :w_rows].astype(f32).reshape(n_out, n_in, w_rows, 2 * hid_pad), axis=1
    )

    def hidden_whole(piece):
        piece = piece[:, :, :hid].reshape(n_out, w_rows, 2, hid_core)
        return piece.transpose(1, 2, 0, 3).reshape(w_rows, n_out * hid)

    gate_w_grad = hidden_whole(gu_total[:, :, :hid_pad])
    up_w_grad = hidden_whole(gu_total[:, :, hid_pad:])
    down_w_grad = jnp.sum(sds[:, :d_rows].astype(f32), axis=0)
    out_w_grad = jnp.sum(wos[:, :w_rows].astype(f32), axis=0)
    small_total = jnp.sum(small_parts[:, :w_rows].astype(f32), axis=0)

    def both_halves(own, came):
        own, came = own.astype(f32), came.astype(f32)
        first = jnp.where(core == 0, own, came)
        second = jnp.where(core == 0, came, own)
        return jnp.concatenate([first, second], axis=0)[None]

    return (
        total_out.astype(bf16).transpose(1, 0, 2),
        tokens_grad.transpose(1, 0, 2),
        small_total[:, n_experts],
        small_total[:, n_experts + 1],
        query_grad,
        key_grad,
        value_grad,
        out_w_grad,
        small_total[:, :n_experts],
        gate_w_grad,
        up_w_grad,
        down_w_grad,
        both_halves(eg_sum, eg_other),
        both_halves(eu_sum, eu_other),
        both_halves(ed_sum, ed_other),
    )


def solution(mesh):
    rows = P(("seq", "fsdp"), None, None)
    matrix = P(("seq", "fsdp"), None)
    vector = P(("seq", "fsdp"))
    expert = P("fsdp", None, None)
    return jax.shard_map(
        body,
        mesh=mesh,
        in_specs=(rows,) * 3 + (vector,) * 2 + (matrix,) * 8 + (expert,) * 3,
        out_specs=(rows,) * 2 + (vector,) * 2 + (matrix,) * 8 + (expert,) * 3,
        check_vma=False,
    )
```

```python
import functools
import math

import jax
import jax.numpy as jnp
from jax import lax
from jax.experimental import pallas as pl
from jax.experimental.pallas import tpu as pltpu
from jax.sharding import PartitionSpec as P

QUERY_HEADS = 12
KEY_VALUE_HEADS = 4
HEAD_SIZE = 128
GROUP_MEMBERS = QUERY_HEADS // KEY_VALUE_HEADS

epsilon = 1e-06
masked_score = -1e30
MESH = pl.DeviceIdType.MESH
VMEM_LIMIT = 63 * 1024 * 1024
f32 = jnp.float32
bf16 = jnp.bfloat16


def round_up(number, step):
    return -(-number // step) * step


def nn(left, right):
    return lax.dot_general(left, right, (((1,), (0,)), ((), ())), preferred_element_type=f32)


def nt(left, right):
    return lax.dot_general(left, right, (((1,), (1,)), ((), ())), preferred_element_type=f32)


def tn(left, right):
    return lax.dot_general(left, right, (((0,), (0,)), ((), ())), preferred_element_type=f32)


def place():
    core = lax.axis_index("seq")
    chip = lax.axis_index("fsdp")
    return core, chip, chip // KEY_VALUE_HEADS, lax.rem(chip, KEY_VALUE_HEADS)


def group(kind, shards):
    core, chip, outer, inner = place()
    if kind == "plane":
        size = 2 * KEY_VALUE_HEADS
        return (
            size,
            core * KEY_VALUE_HEADS + inner,
            lambda r: (r // KEY_VALUE_HEADS, outer * KEY_VALUE_HEADS + lax.rem(r, KEY_VALUE_HEADS)),
        )
    if kind == "inner":
        return KEY_VALUE_HEADS, inner, lambda r: (core, outer * KEY_VALUE_HEADS + r)
    if kind == "outer":
        return shards // KEY_VALUE_HEADS, outer, lambda r: (core, r * KEY_VALUE_HEADS + inner)
    if kind == "chips":
        return shards, chip, lambda r: (core, r)
    if kind == "all":
        return 2 * shards, core * shards + chip, lambda r: (r // shards, lax.rem(r, shards))
    return 2, core, lambda r: (r, chip)


def repeat(first, last, step):
    if last - first <= 16:
        for index in range(first, last):
            step(index)
    else:

        def one(index, carry):
            step(index)
            return carry

        lax.fori_loop(first, last, one, 0)


class Wires:
    def __init__(self, shards, send_sems, recv_sems, local_sems):
        self.shards = shards
        self.send_sems, self.recv_sems, self.local_sems = send_sems, recv_sems, local_sems
        self.used = 0
        self.leaving = []

    def greet(self, kinds):
        barrier = pltpu.get_barrier_semaphore()
        total = 0
        for kind in kinds:
            size, me, device = group(kind, self.shards)

            def signal(d, size=size, me=me, device=device):
                pl.semaphore_signal(
                    barrier, inc=1, device_id=device(lax.rem(me + d, size)), device_id_type=MESH
                )

            repeat(1, size, signal)
            total += size - 1
        pl.semaphore_wait(barrier, total)

    def take(self, count):
        base = self.used
        self.used += count
        return base

    def remote(self, source, target, index, device):
        return pltpu.make_async_remote_copy(
            src_ref=source,
            dst_ref=target,
            send_sem=self.send_sems.at[index],
            recv_sem=self.recv_sems.at[index],
            device_id=device,
            device_id_type=MESH,
        )

    def local(self, source, target, index):
        return pltpu.make_async_copy(source, target, self.local_sems.at[index])

    def exchange(self, kind, source_for, target_from, own=True):
        size, me, device = group(kind, self.shards)
        base = self.take(size)

        def copy(d):
            to = lax.rem(me + d, size)
            return self.remote(source_for(to, d), target_from(me, d), base + d, device(to))

        repeat(1, size, lambda d: copy(d).start())
        if own:
            self.local(source_for(me, 0), target_from(me, 0), base).start()
        self.leaving.append(lambda: repeat(1, size, lambda d: copy(d).wait_send()))

        def arrive(then=None):
            def one(d):
                came = lax.rem(me - d + size, size)
                place_of = target_from(came, d)
                self.remote(place_of, place_of, base + d, device(came)).wait_recv()
                if then is not None:
                    then(d)

            repeat(1, size, one)
            if own:
                self.local(source_for(me, 0), target_from(me, 0), base).wait()

        return arrive

    def sibling(self, source, target, comes):
        core, chip, _, _ = place()
        device = (1 - core, chip)
        index = self.take(1)
        copy = self.remote(source, target, index, device)
        copy.start()
        self.leaving.append(copy.wait_send)
        return self.remote(comes, comes, index, device).wait_recv

    def finish(self):
        for leave in self.leaving:
            leave()


def transfer(name, collective, shards, kinds, sems, body, operands, outs):
    count = len(operands)

    def kernel(*refs):
        ins, results = refs[:count], refs[count : count + len(outs)]
        wires = Wires(shards, *refs[count + len(outs) :])
        wires.greet(kinds)
        body(wires, ins, results)
        wires.finish()

    return pl.pallas_call(
        kernel,
        out_shape=[jax.ShapeDtypeStruct(shape, kind) for shape, kind in outs],
        in_specs=[pl.BlockSpec(memory_space=pl.ANY)] * count,
        out_specs=[pl.BlockSpec(memory_space=pl.ANY)] * len(outs),
        scratch_shapes=[pltpu.SemaphoreType.DMA((sems,))] * 3,
        compiler_params=pltpu.CompilerParams(collective_id=collective, has_side_effects=True),
        name=name,
    )(*operands)


def attend_kernel(chunk, n_out, q_ref, kv_ref, mixed_ref, log_ref):
    outer = lax.axis_index("fsdp") // KEY_VALUE_HEADS
    factor = HEAD_SIZE**-0.5 * math.log2(math.e)
    for half in range(2):
        query = q_ref[pl.ds(half * chunk, chunk), :]

        def fold(block, carry, masked, query=query):
            largest, total, summed = carry
            rows = pl.ds(pl.multiple_of((block // n_out) * chunk, chunk), chunk)
            key = kv_ref[lax.rem(block, n_out), rows, 0:HEAD_SIZE]
            value = kv_ref[lax.rem(block, n_out), rows, HEAD_SIZE : 2 * HEAD_SIZE]
            scores = nt(key, query)
            if masked:
                key_at = lax.broadcasted_iota(jnp.int32, scores.shape, 0)
                query_at = lax.broadcasted_iota(jnp.int32, scores.shape, 1)
                scores = jnp.where(key_at <= query_at, scores, masked_score)
            new = jnp.maximum(largest, jnp.max(scores, axis=0, keepdims=True))
            weights = jnp.exp2((scores - new) * factor)
            shrink = jnp.exp2((largest - new) * factor)
            total = total * shrink + jnp.sum(weights, axis=0, keepdims=True)
            summed = summed * shrink + tn(value, weights.astype(bf16))
            return new, total, summed

        start = (
            jnp.full((1, chunk), masked_score, f32),
            jnp.zeros((1, chunk), f32),
            jnp.zeros((HEAD_SIZE, chunk), f32),
        )
        own = half * n_out + outer
        carry = fold(own, start, True)
        largest, total, summed = lax.fori_loop(
            0, own, lambda block, carry: fold(block, carry, False), carry
        )
        mixed_ref[pl.ds(half * chunk, chunk), :] = (summed / total).T
        log_ref[0, half : half + 1, :] = largest * factor + jnp.log2(total)


def attend(chunk, n_out, qkv, kv_all):
    rows = 2 * chunk
    return pl.pallas_call(
        functools.partial(attend_kernel, chunk, n_out),
        grid=(GROUP_MEMBERS,),
        in_specs=[
            pl.BlockSpec((rows, HEAD_SIZE), lambda h: (0, h)),
            pl.BlockSpec(kv_all.shape, lambda h: (0, 0, 0), pipeline_mode=pl.Buffered(1)),
        ],
        out_specs=[
            pl.BlockSpec((rows, HEAD_SIZE), lambda h: (0, h)),
            pl.BlockSpec((1, 2, chunk), lambda h: (h, 0, 0)),
        ],
        out_shape=[
            jax.ShapeDtypeStruct((rows, GROUP_MEMBERS * HEAD_SIZE), f32),
            jax.ShapeDtypeStruct((GROUP_MEMBERS, 2, chunk), f32),
        ],
        compiler_params=pltpu.CompilerParams(vmem_limit_bytes=VMEM_LIMIT),
        name="attend",
    )(qkv, kv_all)


def attend_back_kernel(
    chunk, n_out, q_ref, kv_ref, grad_ref, log_ref, delta_ref, dq_ref, dkv_ref, sums
):
    head = pl.program_id(0)
    outer = lax.axis_index("fsdp") // KEY_VALUE_HEADS
    scale = HEAD_SIZE**-0.5
    factor = scale * math.log2(math.e)

    @pl.when(head == 0)
    def _():
        sums[...] = jnp.zeros_like(sums)

    for half in range(2):
        mine = pl.ds(half * chunk, chunk)
        query = q_ref[mine, :]
        grad = grad_ref[mine, :]
        log_row = log_ref[0, half : half + 1, :]
        delta_row = delta_ref[0, half : half + 1, :]

        def fold(block, dq, masked, query=query, grad=grad, log_row=log_row, delta_row=delta_row):
            at = lax.rem(block, n_out)
            rows = pl.ds(pl.multiple_of((block // n_out) * chunk, chunk), chunk)
            key = kv_ref[at, rows, 0:HEAD_SIZE]
            value = kv_ref[at, rows, HEAD_SIZE : 2 * HEAD_SIZE]
            scores = nt(key, query)
            if masked:
                key_at = lax.broadcasted_iota(jnp.int32, scores.shape, 0)
                query_at = lax.broadcasted_iota(jnp.int32, scores.shape, 1)
                scores = jnp.where(key_at <= query_at, scores, masked_score)
            weights = jnp.exp2(scores * factor - log_row)
            grad_scores = (weights * (nt(value, grad) - delta_row)).astype(bf16)
            sums[at, rows, 0:HEAD_SIZE] += nn(grad_scores, query)
            sums[at, rows, HEAD_SIZE : 2 * HEAD_SIZE] += nn(weights.astype(bf16), grad)
            return dq + tn(grad_scores, key)

        own = half * n_out + outer
        dq = fold(own, jnp.zeros((chunk, HEAD_SIZE), f32), True)
        dq = lax.fori_loop(0, own, lambda block, dq: fold(block, dq, False), dq)
        dq_ref[mine, :] = (dq * scale).astype(bf16)

    @pl.when(head == GROUP_MEMBERS - 1)
    def _():
        dkv_ref[...] = sums[...].astype(bf16)


def attend_back(chunk, n_out, qkv, kv_all, grad_mixed, log_rows, delta_rows):
    rows = 2 * chunk
    per_head = pl.BlockSpec((rows, HEAD_SIZE), lambda h: (0, h))
    per_row = pl.BlockSpec((1, 2, chunk), lambda h: (h, 0, 0))
    whole = pl.BlockSpec(kv_all.shape, lambda h: (0, 0, 0), pipeline_mode=pl.Buffered(1))
    return pl.pallas_call(
        functools.partial(attend_back_kernel, chunk, n_out),
        grid=(GROUP_MEMBERS,),
        in_specs=[per_head, whole, per_head, per_row, per_row],
        out_specs=[per_head, whole],
        out_shape=[
            jax.ShapeDtypeStruct((rows, GROUP_MEMBERS * HEAD_SIZE), bf16),
            jax.ShapeDtypeStruct(kv_all.shape, bf16),
        ],
        scratch_shapes=[pltpu.VMEM(kv_all.shape, f32)],
        compiler_params=pltpu.CompilerParams(vmem_limit_bytes=VMEM_LIMIT),
        name="attend_back",
    )(qkv, kv_all, grad_mixed, log_rows, delta_rows)


def swiglu_parts(gate_part, up_part):
    sigmoid = jax.nn.sigmoid(gate_part)
    active = gate_part * sigmoid
    slope = up_part * sigmoid * (1.0 + gate_part * (1.0 - sigmoid))
    return active * up_part, active, slope


def experts_kernel(
    room,
    hidden,
    h_ref,
    c_ref,
    meta_ref,
    wg_ref,
    wu_ref,
    wd_ref,
    sgu_ref,
    sd_ref,
    out_ref,
    dh_ref,
    dgate_ref,
    dw_ref,
    dsgu_ref,
    dsd_ref,
    sum_out,
    sum_dh,
    h_rows,
    c_rows,
    picks,
    gate_col,
):
    expert = pl.program_id(0)
    inner = lax.rem(lax.axis_index("fsdp"), KEY_VALUE_HEADS)
    at = lax.rem(inner - expert + KEY_VALUE_HEADS, KEY_VALUE_HEADS)
    blocks, rows, width = h_ref.shape

    @pl.when(expert == 0)
    def _():
        dgate_ref[...] = jnp.zeros_like(dgate_ref)
        hid = h_ref[...].reshape(blocks * rows, width)
        cot = c_ref[...].reshape(blocks * rows, width)
        gate_w, up_w, down_w = sgu_ref[:, 0:hidden], sgu_ref[:, hidden : 2 * hidden], sd_ref[...]
        both, active, slope = swiglu_parts(nn(hid, gate_w), nn(hid, up_w))
        act = both.astype(bf16)
        d_act = nt(cot, down_w)
        d_gate = (d_act * slope).astype(bf16)
        d_up = (d_act * active).astype(bf16)
        sum_out[...] = nn(act, down_w)
        sum_dh[...] = nt(d_gate, gate_w) + nt(d_up, up_w)
        dsgu_ref[:, 0:hidden] = tn(hid, d_gate).astype(bf16)
        dsgu_ref[:, hidden : 2 * hidden] = tn(hid, d_up).astype(bf16)
        dsd_ref[...] = tn(act, cot).astype(bf16)

    slots = lax.broadcasted_iota(jnp.int32, (room, rows), 0).astype(f32)
    for block in range(blocks):
        part = pl.ds(block * room, room)
        gate_row = meta_ref[block, pl.ds(at, 1), :]
        slot_row = meta_ref[block, pl.ds(at + KEY_VALUE_HEADS, 1), :]
        pick = (slots == slot_row).astype(f32)
        gate_col[part, :] = jnp.broadcast_to(
            jnp.sum(pick * gate_row, axis=1, keepdims=True), (room, gate_col.shape[1])
        )
        pick = pick.astype(bf16)
        picks[block] = pick
        h_rows[part, :] = nn(pick, h_ref[block]).astype(bf16)
        c_rows[part, :] = nn(pick, c_ref[block]).astype(bf16)
    gate = gate_col[:, 0:1]
    gate_w, up_w, down_w = wg_ref[0], wu_ref[0], wd_ref[0]
    both, active, slope = swiglu_parts(nn(h_rows[...], gate_w), nn(h_rows[...], up_w))
    act = both.astype(bf16)
    d_act = nt(c_rows[...], down_w)
    d_gates = jnp.sum(d_act * act.astype(f32), axis=1, keepdims=True)
    d_act = d_act * gate
    act = (act.astype(f32) * gate).astype(bf16)
    d_gate = (d_act * slope).astype(bf16)
    d_up = (d_act * active).astype(bf16)
    dw_ref[0, 0] = tn(h_rows[...], d_gate).astype(bf16)
    dw_ref[0, 1] = tn(h_rows[...], d_up).astype(bf16)
    dw_ref[0, 2] = tn(c_rows[...], act).astype(bf16)
    result = nn(act, down_w).astype(bf16)
    d_rows = (nt(d_gate, gate_w) + nt(d_up, up_w)).astype(bf16)
    for block in range(blocks):
        pick = picks[block]
        part = slice(block * room, (block + 1) * room)
        here = pl.ds(block * rows, rows)
        sum_out[here, :] += tn(pick, result[part])
        sum_dh[here, :] += tn(pick, d_rows[part])
        dgate_ref[block, pl.ds(at, 1), :] = jnp.sum(
            pick.astype(f32) * d_gates[part], axis=0, keepdims=True
        )

    @pl.when(expert == pl.num_programs(0) - 1)
    def _():
        out_ref[...] = sum_out[...].astype(bf16).reshape(out_ref.shape)
        dh_ref[...] = sum_dh[...].astype(bf16).reshape(dh_ref.shape)


def experts(room, hidden, h_all, c_all, meta, wg, wu, wd, sgu, sd):
    blocks, rows, width = h_all.shape
    n_experts, _, inner = wg.shape

    def once(shape):
        return pl.BlockSpec(shape, lambda e: (0,) * len(shape), pipeline_mode=pl.Buffered(1))

    def each(shape, **kind):
        return pl.BlockSpec((1,) + shape[1:], lambda e: (e, 0, 0), **kind)

    single = dict(pipeline_mode=pl.Buffered(1))
    return pl.pallas_call(
        functools.partial(experts_kernel, room, hidden),
        grid=(n_experts,),
        in_specs=[
            once(h_all.shape),
            once(c_all.shape),
            once(meta.shape),
            each(wg.shape),
            each(wu.shape),
            each(wd.shape),
            once(sgu.shape),
            once(sd.shape),
        ],
        out_specs=[
            once(h_all.shape),
            once(h_all.shape),
            once(meta.shape),
            pl.BlockSpec((1, 3, width, inner), lambda e: (e, 0, 0, 0), **single),
            once(sgu.shape),
            once(sd.shape),
        ],
        out_shape=[
            jax.ShapeDtypeStruct(h_all.shape, bf16),
            jax.ShapeDtypeStruct(h_all.shape, bf16),
            jax.ShapeDtypeStruct(meta.shape, f32),
            jax.ShapeDtypeStruct((n_experts, 3, width, inner), bf16),
            jax.ShapeDtypeStruct(sgu.shape, bf16),
            jax.ShapeDtypeStruct(sd.shape, bf16),
        ],
        scratch_shapes=[
            pltpu.VMEM((blocks * rows, width), f32),
            pltpu.VMEM((blocks * rows, width), f32),
            pltpu.VMEM((blocks * room, width), bf16),
            pltpu.VMEM((blocks * room, width), bf16),
            pltpu.VMEM((blocks, room, rows), bf16),
            pltpu.VMEM((blocks * room, 128), f32),
        ],
        compiler_params=pltpu.CompilerParams(vmem_limit_bytes=VMEM_LIMIT),
        name="experts",
    )(h_all, c_all, meta, wg, wu, wd, sgu, sd)


def norm_rows(values, gain_vector):
    inverse = lax.rsqrt(jnp.mean(values * values, axis=-1, keepdims=True) + epsilon)
    normed = values * inverse
    return (normed, inverse, normed * gain_vector)


def norm_back(grad_hidden, normed, inverse, gain_vector):
    grad_normed = grad_hidden * gain_vector
    gain_grad = jnp.sum(grad_hidden * normed, axis=(0, 1))
    inner_mean = jnp.mean(grad_normed * normed, axis=-1, keepdims=True)
    return (inverse * (grad_normed - normed * inner_mean), gain_grad)


def pad_rows(array, axis):
    size = array.shape[axis]
    widths = [(0, 0)] * array.ndim
    widths[axis] = (0, round_up(size, 16) - size)
    return jnp.pad(array, widths) if widths[axis][1] else array


def pad_to(array, axis, size):
    widths = [(0, 0)] * array.ndim
    widths[axis] = (0, size - array.shape[axis])
    return jnp.pad(array, widths) if widths[axis][1] else array


def body(
    tokens,
    routes,
    out_grad,
    attn_gain,
    ffn_gain,
    query_projection,
    key_projection,
    value_projection,
    w_out,
    w_router,
    shared_gate,
    shared_up,
    shared_down,
    expert_gate,
    expert_up,
    expert_down,
):
    shards = lax.axis_size("fsdp")
    n_in = KEY_VALUE_HEADS
    n_out = shards // n_in
    core, chip, outer, inner = place()
    seg, seqs, width = tokens.shape
    rows = seg * seqs
    topk = routes.shape[2]
    n_experts = w_router.shape[1]
    w_rows = query_projection.shape[0]
    w_pad = round_up(w_rows, 16)
    d_rows = shared_down.shape[0]
    d_pad = round_up(d_rows, 16)
    half_chips = shards // 2
    q_cols = GROUP_MEMBERS * HEAD_SIZE
    cols = q_cols + 2 * HEAD_SIZE
    ff = expert_gate.shape[2]
    hid_core = n_in * d_rows
    hid = 2 * hid_core
    hid_pad = round_up(hid, 128)
    small = round_up(n_experts + 2, 128)
    chunk = n_in * seg
    half_width, half_ff = width // 2, ff // 2
    room = round_up(max(2, (3 * rows * topk + 2 * n_experts - 1) // (2 * n_experts)), 16)

    small_piece = pad_to(
        jnp.concatenate([w_router, attn_gain[:, None], ffn_gain[:, None]], axis=1), 1, small
    )
    q_pieces = pad_rows(
        jnp.concatenate(
            [
                query_projection.reshape(w_rows, n_in, q_cols),
                key_projection.reshape(w_rows, n_in, HEAD_SIZE),
                value_projection.reshape(w_rows, n_in, HEAD_SIZE),
                jnp.broadcast_to(small_piece[:, None], (w_rows, n_in, small)),
            ],
            axis=2,
        ).transpose(1, 0, 2),
        1,
    )

    def hidden_piece(weight):
        piece = weight.reshape(w_rows, 2, n_out, hid_core).transpose(2, 0, 1, 3)
        return pad_to(piece.reshape(n_out, w_rows, hid), 2, hid_pad)

    gu_pieces = pad_rows(
        jnp.concatenate([hidden_piece(shared_gate), hidden_piece(shared_up)], axis=2), 1
    )
    out_piece = pad_rows(w_out, 0)
    down_piece = pad_rows(shared_down, 0)
    x_own = tokens.transpose(1, 0, 2)
    c_own = out_grad.transpose(1, 0, 2)
    cot = c_own.reshape(rows, width)

    def shift(block, step):
        axis, amount = step
        if axis == "outer":
            pairs = [(f, (f + amount * n_in) % shards) for f in range(shards)]
        else:
            pairs = [(f, f // n_in * n_in + (f + amount) % n_in) for f in range(shards)]
        return lax.ppermute(block, "fsdp", pairs)

    def gather_expert(wires, mine, every, size):
        core, chip, outer, inner = place()
        part, other = pl.ds(core * size, size), pl.ds((1 - core) * size, size)
        device = (1 - core, chip)
        arrive = wires.exchange(
            "inner", lambda r, d: mine.at[0, part], lambda r, d: every.at[d, part], own=False
        )
        own = wires.sibling(mine.at[0], every.at[0], every.at[0])
        base = wires.take(n_in)

        def hand_on(d):
            wires.remote(every.at[d, part], every.at[d, part], base + d, device).start()

        def settle():
            arrive(hand_on)
            own()
            for d in range(1, n_in):
                wires.remote(every.at[d, part], every.at[d, part], base + d, device).wait_send()
                wires.remote(every.at[d, other], every.at[d, other], base + d, device).wait_recv()

        return settle

    def out_rows(wires, o_ref, wo_ref):
        core, chip, outer, inner = place()
        to_inner = 2 * core + chip // half_chips
        slot = lax.rem(chip, half_chips)
        base = wires.take(half_chips)
        sends = wires.take(2 * n_out)

        def copy(k):
            to = (k // n_out, lax.rem(k, n_out) * n_in + to_inner)
            here = (to[0] == core) & (to[1] == chip)
            return here, pltpu.make_async_remote_copy(
                src_ref=o_ref,
                dst_ref=wo_ref.at[slot],
                send_sem=wires.send_sems.at[sends + k],
                recv_sem=wires.recv_sems.at[base + slot],
                device_id=to,
                device_id_type=MESH,
            )

        def start(k):
            here, send = copy(k)
            pl.when(jnp.logical_not(here))(send.start)
            pl.when(here)(lambda: wires.local(o_ref, wo_ref.at[slot], base).start())

        def leave(k):
            here, send = copy(k)
            pl.when(jnp.logical_not(here))(send.wait_send)

        def come(i):
            origin = (inner // 2, half_chips * lax.rem(inner, 2) + i)
            here = (origin[0] == core) & (origin[1] == chip)
            place_of = wo_ref.at[i]
            pl.when(jnp.logical_not(here))(
                wires.remote(place_of, place_of, base + i, origin).wait_recv
            )
            pl.when(here)(lambda: wires.local(o_ref, place_of, base).wait())

        repeat(0, 2 * n_out, start)
        wires.leaving.append(lambda: repeat(0, 2 * n_out, leave))
        return lambda: repeat(0, half_chips, come)

    own_rows = half_chips // 2

    def out_rows_back(wires, grad_ref, sums_ref):
        core, chip, outer, inner = place()
        from_inner = 2 * core + chip // half_chips
        from_core = lax.rem(chip, half_chips) // own_rows
        sends = wires.take(own_rows)
        base = wires.take(n_out)

        def copy(i):
            to = (inner // 2, half_chips * lax.rem(inner, 2) + core * own_rows + i)
            here = (to[0] == core) & (to[1] == chip)
            return here, pltpu.make_async_remote_copy(
                src_ref=grad_ref.at[i],
                dst_ref=sums_ref.at[outer],
                send_sem=wires.send_sems.at[sends + i],
                recv_sem=wires.recv_sems.at[base + outer],
                device_id=to,
                device_id_type=MESH,
            )

        def start(i):
            here, send = copy(i)
            pl.when(jnp.logical_not(here))(send.start)
            pl.when(here)(lambda: wires.local(grad_ref.at[i], sums_ref.at[outer], base).start())

        def leave(i):
            here, send = copy(i)
            pl.when(jnp.logical_not(here))(send.wait_send)

        def come(k):
            origin = (from_core, k * n_in + from_inner)
            here = (origin[0] == core) & (origin[1] == chip)
            place_of = sums_ref.at[k]
            pl.when(jnp.logical_not(here))(
                wires.remote(place_of, place_of, base + k, origin).wait_recv
            )
            pl.when(here)(lambda: wires.local(place_of, place_of, base).wait())

        repeat(0, own_rows, start)
        wires.leaving.append(lambda: repeat(0, own_rows, leave))
        return lambda: repeat(0, n_out, come)

    def fetch(wires, ins, outs):
        x_ref, q_ref, o_ref = ins
        xs_ref, wq_ref, wo_ref = outs
        core, chip, outer, inner = place()
        x_in = wires.exchange("plane", lambda r, d: x_ref.at[r // n_in], lambda r, d: xs_ref.at[r])
        q_in = wires.exchange(
            "chips", lambda r, d: q_ref.at[lax.rem(r, n_in)], lambda r, d: wq_ref.at[core, r]
        )
        o_in = out_rows(wires, o_ref, wo_ref)
        q_in()
        q_other = wires.sibling(wq_ref.at[core], wq_ref.at[core], wq_ref.at[1 - core])
        x_in()
        o_in()
        q_other()

    xs, wq, wo = transfer(
        "fetch",
        0,
        shards,
        ["all"],
        4 * shards + 16,
        fetch,
        [x_own, q_pieces, out_piece],
        [
            ((2 * n_in, seg, width), bf16),
            ((2, shards, w_pad, cols + small), bf16),
            ((half_chips, w_pad, width), bf16),
        ],
    )
    wq = wq[:, :, :w_rows].reshape(width, cols + small)
    wo = wo[:, :w_rows].reshape(q_cols, width)
    wq, small_w = wq[:, :cols], wq[:, cols:]
    router_w = small_w[:, :n_experts]
    gain_one = small_w[:, n_experts].astype(f32)
    gain_two = small_w[:, n_experts + 1].astype(f32)

    normed_all, _, h1 = norm_rows(xs.reshape(2 * chunk, width).astype(f32), gain_one)
    h1 = h1.astype(bf16)
    qkv = nn(h1, wq).astype(bf16)

    def spread_kv(wires, ins, outs):
        kv_in = wires.exchange("outer", lambda r, d: ins[0], lambda r, d: outs[0].at[r])
        e_in = gather_expert(wires, ins[1], outs[1], half_width)
        kv_in()
        e_in()

    kv_all, e_gate = transfer(
        "spread_kv",
        1,
        shards,
        ["outer", "plane"],
        n_out + 4 * n_in,
        spread_kv,
        [qkv[:, q_cols:], expert_gate],
        [((n_out, 2 * chunk, 2 * HEAD_SIZE), bf16), ((n_in, width, ff), bf16)],
    )
    kv_all, cot_late = lax.optimization_barrier((kv_all, cot))
    c_all = jnp.stack([cot] + [shift(cot_late, ("outer", d)) for d in range(1, n_out)])
    mixed, log_rows = attend(chunk, n_out, qkv, kv_all)
    mixed_low = mixed.astype(bf16)
    out_part = nn(mixed_low, wo).astype(bf16).reshape(2 * n_in, seg, width)

    def sum_out(wires, ins, outs):
        core, chip, outer, inner = place()
        part_ref, gu_ref, s_ref = ins
        parts_ref, wgu_ref, ws_ref = outs
        part_in = wires.exchange("plane", lambda r, d: part_ref.at[r], lambda r, d: parts_ref.at[r])
        gu_in = wires.exchange(
            "chips", lambda r, d: gu_ref.at[r // n_in], lambda r, d: wgu_ref.at[core, r]
        )
        s_in = wires.exchange("inner", lambda r, d: s_ref, lambda r, d: ws_ref.at[core, r])
        gu_in()
        gu_other = wires.sibling(wgu_ref.at[core], wgu_ref.at[core], wgu_ref.at[1 - core])
        s_in()
        s_other = wires.sibling(ws_ref.at[core], ws_ref.at[core], ws_ref.at[1 - core])
        part_in()
        gu_other()
        s_other()

    out_parts, sgu, ws = transfer(
        "sum_out",
        2,
        shards,
        ["all"],
        shards + 4 * n_in + 16,
        sum_out,
        [out_part, gu_pieces, down_piece],
        [
            ((2 * n_in, seg, width), bf16),
            ((2, shards, w_pad, 2 * hid_pad), bf16),
            ((2, n_in, d_pad, width), bf16),
        ],
    )
    sgu = sgu[:, :, :w_rows].reshape(width, 2 * hid_pad)
    ws = pad_to(ws[:, :, :d_rows].reshape(hid, width), 0, hid_pad)
    inputs = x_own.astype(f32)
    residual = inputs + jnp.sum(out_parts.astype(f32).reshape(2, n_in, seg, width), axis=1)

    normed_two, inverse_two, scaled_two = norm_rows(residual, gain_two)
    hidden_two = scaled_two.astype(bf16).reshape(rows, width)
    logits = nn(hidden_two, router_w)
    flat_routes = routes.transpose(1, 0, 2).reshape(rows, topk)
    chooser = (flat_routes[:, :, None] == jnp.arange(n_experts, dtype=jnp.int32)).astype(f32)
    taken = jnp.sum(chooser, axis=1)
    chosen = jnp.where(taken > 0, logits, masked_score)
    exponent = jnp.where(
        taken > 0, jnp.exp(chosen - jnp.max(chosen, axis=-1, keepdims=True)), 0.0
    )
    gates = exponent / jnp.sum(exponent, axis=-1, keepdims=True)
    before = (
        lax.broadcasted_iota(jnp.int32, (rows, rows), 0)
        < lax.broadcasted_iota(jnp.int32, (rows, rows), 1)
    ).astype(bf16)
    slots = jnp.where(taken.T > 0, nn(taken.T.astype(bf16), before), -1.0)
    meta = jnp.concatenate(
        [gates.T.reshape(n_out, n_in, rows), slots.reshape(n_out, n_in, rows)], axis=1
    )

    def spread_hidden(wires, ins, outs):
        h_ref, meta_ref, eu_ref, ed_ref = ins
        hs_ref, metas_ref, au_ref, ad_ref = outs
        waits = [
            wires.exchange("outer", lambda r, d: h_ref, lambda r, d: hs_ref.at[d]),
            wires.exchange("outer", lambda r, d: meta_ref.at[r], lambda r, d: metas_ref.at[d]),
            gather_expert(wires, eu_ref, au_ref, half_width),
            gather_expert(wires, ed_ref, ad_ref, half_ff),
        ]
        for wait in waits:
            wait()

    h_all, meta_all, e_up, e_down = transfer(
        "spread_hidden",
        3,
        shards,
        ["outer", "plane"],
        2 * n_out + 8 * n_in,
        spread_hidden,
        [hidden_two, meta, expert_up, expert_down],
        [
            ((n_out, rows, width), bf16),
            ((n_out, 2 * n_in, rows), f32),
            ((n_in, width, ff), bf16),
            ((n_in, ff, width), bf16),
        ],
    )

    at_once = math.gcd(n_out, 4)
    parts = [
        experts(
            room,
            hid_pad,
            h_all[i : i + at_once],
            c_all[i : i + at_once],
            meta_all[i : i + at_once],
            e_gate,
            e_up,
            e_down,
            sgu,
            ws,
        )
        for i in range(0, n_out, at_once)
    ]
    mix_part, dh_part, dgate_part = (
        jnp.concatenate([part[k] for part in parts], axis=0) if len(parts) > 1 else parts[0][k]
        for k in range(3)
    )
    e_grad, sgu_grad, sd_grad = (
        sum(part[k].astype(f32) for part in parts).astype(bf16) if len(parts) > 1 else parts[0][k]
        for k in range(3, 6)
    )

    def sum_hidden(wires, ins, outs):
        core, chip, outer, inner = place()
        dh_ref, dg_ref, e_ref, gu_ref = ins
        dhs, dgs, es, gus = outs
        waits = [
            wires.exchange(
                "outer", lambda r, d: dh_ref.at[(n_out - d) % n_out], lambda r, d: dhs.at[d]
            ),
            wires.exchange(
                "outer", lambda r, d: dg_ref.at[(n_out - d) % n_out], lambda r, d: dgs.at[r]
            ),
        ]
        wide = pl.ds((1 - core) * half_width, half_width)
        waits += [
            wires.sibling(e_ref.at[:, :, wide], es, es),
            wires.sibling(gu_ref.at[wide], gus, gus),
        ]
        for wait in waits:
            wait()

    dhs, dgs, es, gus = transfer(
        "sum_hidden",
        4,
        shards,
        ["outer", "core"],
        2 * n_out + 8,
        sum_hidden,
        [dh_part, dgate_part, e_grad, sgu_grad],
        [
            ((n_out, rows, width), bf16),
            ((n_out, 2 * n_in, rows), f32),
            ((n_in, 3, half_width, ff), bf16),
            ((half_width, 2 * hid_pad), bf16),
        ],
    )
    dhs, mix_late = lax.optimization_barrier((dhs, mix_part))
    mixes = [mix_late[0]] + [
        shift(mix_late[n_out - d], ("outer", d)) for d in range(1, n_out)
    ]

    def with_sibling(own, came, axis):
        size = came.shape[axis]
        mine = lax.dynamic_slice_in_dim(own, core * size, size, axis)
        return (mine.astype(f32) + came.astype(f32)).astype(bf16)

    gu_half = pad_rows(with_sibling(sgu_grad, gus, 0).reshape(shards, w_rows, 2 * hid_pad), 1)
    sd_send = pad_rows(sd_grad[:hid].reshape(2 * n_in, d_rows, width), 1)

    grad_float = c_own.astype(f32)
    grad_gates = dgs[:, :n_in].reshape(n_experts, rows).T
    grad_logits = gates * (grad_gates - jnp.sum(gates * grad_gates, axis=-1, keepdims=True))
    router_grad = lax.dot_general(
        hidden_two.astype(f32),
        grad_logits,
        (((0,), (0,)), ((), ())),
        precision=lax.Precision.HIGHEST,
        preferred_element_type=f32,
    )
    grad_hidden_two = jnp.sum(dhs.astype(f32), axis=0) + lax.dot_general(
        grad_logits,
        router_w.astype(f32),
        (((1,), (1,)), ((), ())),
        precision=lax.Precision.HIGHEST,
        preferred_element_type=f32,
    )
    grad_norm_two, gain_two_grad = norm_back(
        grad_hidden_two.reshape(seqs, seg, width), normed_two, inverse_two, gain_two
    )
    grad_residual = grad_float + grad_norm_two
    grad_attn = grad_residual.astype(bf16)

    def spread_grad(wires, ins, outs):
        first = wires.exchange("plane", lambda r, d: ins[0].at[r // n_in], lambda r, d: outs[0].at[r])
        second = wires.exchange("chips", lambda r, d: ins[1].at[r], lambda r, d: outs[1].at[r])
        first()
        second()

    grad_all, gus = transfer(
        "spread_grad",
        5,
        shards,
        ["all"],
        shards + 2 * n_in,
        spread_grad,
        [grad_attn, gu_half],
        [((2 * n_in, seg, width), bf16), ((shards, w_pad, 2 * hid_pad), bf16)],
    )
    grad_all, es = lax.optimization_barrier((grad_all, es))

    e_mine = lax.dynamic_slice_in_dim(e_grad, core * half_width, half_width, 2)
    e_halves = [(e_mine[d].astype(f32) + es[d].astype(f32)).astype(bf16) for d in range(n_in)]
    e_parts = [e_halves[0]] + [shift(e_halves[n_in - d], ("inner", d)) for d in range(1, n_in)]
    grad_all = grad_all.reshape(2 * chunk, width)
    grad_mixed = nt(grad_all, wo).astype(bf16)
    wo_grad = pad_rows(tn(mixed_low, grad_all).astype(bf16).reshape(half_chips, w_rows, width), 1)
    delta_rows = jnp.sum(
        (grad_mixed.astype(f32) * mixed).reshape(2, chunk, GROUP_MEMBERS, HEAD_SIZE), axis=-1
    ).transpose(2, 0, 1)

    dq, dkv_part = attend_back(chunk, n_out, qkv, kv_all, grad_mixed, log_rows, delta_rows)

    dkv_part, mixes = lax.optimization_barrier((dkv_part, mixes))
    total_out = residual + sum(mix.astype(f32) for mix in mixes).reshape(seqs, seg, width)

    def sum_kv(wires, ins, outs):
        core, chip, outer, inner = place()
        wo_part = ins[1].at[pl.ds((1 - core) * own_rows, own_rows)]
        waits = [
            wires.exchange("outer", lambda r, d: ins[0].at[r], lambda r, d: outs[0].at[r]),
            wires.sibling(wo_part, outs[1], outs[1]),
        ]
        for wait in waits:
            wait()

    kvs, wos = transfer(
        "sum_kv",
        6,
        shards,
        ["outer", "core"],
        n_out + 1,
        sum_kv,
        [dkv_part, wo_grad],
        [(kv_all.shape, bf16), ((own_rows, w_pad, width), bf16)],
    )
    wo_half = with_sibling(wo_grad, wos, 0)
    dkv = jnp.sum(kvs.astype(f32), axis=0)
    key_scale = jnp.concatenate(
        [jnp.full((HEAD_SIZE,), HEAD_SIZE**-0.5, f32), jnp.ones((HEAD_SIZE,), f32)]
    )
    dqkv = jnp.concatenate([dq, (dkv * key_scale).astype(bf16)], axis=1)
    dh1_part = nt(dqkv, wq).astype(bf16).reshape(2 * n_in, seg, width)
    wq_send = pad_rows(tn(h1, dqkv).astype(bf16).reshape(2 * shards, w_rows, cols), 1)
    e_sum = sum(part.astype(f32) for part in e_parts).astype(bf16)
    gain_one_grad = jnp.sum(
        dh1_part.reshape(2 * chunk, width).astype(f32) * normed_all, axis=0
    )
    small_grad = pad_to(
        jnp.concatenate([router_grad, gain_one_grad[:, None], gain_two_grad[:, None]], axis=1),
        1,
        small,
    )
    small_send = pad_rows(small_grad.astype(bf16).reshape(2 * shards, w_rows, small), 1)

    def sum_first(wires, ins, outs):
        dh_ref, wq_ref, small_ref, s_ref, o_ref, e_ref = ins
        dhs, wqs, smalls, sds, wos, es = outs
        waits = [
            wires.exchange("plane", lambda r, d: dh_ref.at[r], lambda r, d: dhs.at[r]),
            wires.exchange("all", lambda r, d: wq_ref.at[r], lambda r, d: wqs.at[r]),
            wires.exchange("all", lambda r, d: small_ref.at[r], lambda r, d: smalls.at[r]),
            wires.exchange("plane", lambda r, d: s_ref.at[r], lambda r, d: sds.at[r]),
            out_rows_back(wires, o_ref, wos),
            wires.sibling(e_ref, es, es),
        ]
        for wait in waits:
            wait()

    dh1s, wq_parts, small_parts, sds, wos, e_other = transfer(
        "sum_first",
        7,
        shards,
        ["all"],
        4 * n_in + 6 * shards + 16,
        sum_first,
        [dh1_part, wq_send, small_send, sd_send, wo_half, e_sum],
        [
            ((2 * n_in, seg, width), bf16),
            ((2 * shards, w_pad, cols), bf16),
            ((2 * shards, w_pad, small), bf16),
            ((2 * n_in, d_pad, width), bf16),
            ((n_out, w_pad, width), bf16),
            (e_sum.shape, bf16),
        ],
    )
    grad_hidden_one = jnp.sum(dh1s.astype(f32).reshape(2, n_in, seg, width), axis=1)
    normed_one, inverse_one, _ = norm_rows(inputs, gain_one)
    grad_norm_one = norm_back(grad_hidden_one, normed_one, inverse_one, gain_one)[0]
    tokens_grad = grad_residual + grad_norm_one

    wq_total = jnp.sum(
        wq_parts[:, :w_rows].astype(f32).reshape(2 * n_out, n_in, w_rows, cols), axis=0
    ).transpose(1, 0, 2)
    query_grad = wq_total[:, :, :q_cols].reshape(w_rows, n_in * q_cols)
    key_grad = wq_total[:, :, q_cols : q_cols + HEAD_SIZE].reshape(w_rows, n_in * HEAD_SIZE)
    value_grad = wq_total[:, :, q_cols + HEAD_SIZE :].reshape(w_rows, n_in * HEAD_SIZE)
    gu_total = jnp.sum(
        gus[:, :w_rows].astype(f32).reshape(n_out, n_in, w_rows, 2 * hid_pad), axis=1
    )

    def hidden_whole(piece):
        piece = piece[:, :, :hid].reshape(n_out, w_rows, 2, hid_core)
        return piece.transpose(1, 2, 0, 3).reshape(w_rows, n_out * hid)

    gate_w_grad = hidden_whole(gu_total[:, :, :hid_pad])
    up_w_grad = hidden_whole(gu_total[:, :, hid_pad:])
    down_w_grad = jnp.sum(sds[:, :d_rows].astype(f32), axis=0)
    out_w_grad = jnp.sum(wos[:, :w_rows].astype(f32), axis=0)
    small_total = jnp.sum(small_parts[:, :w_rows].astype(f32), axis=0)

    own, came = e_sum.astype(f32), e_other.astype(f32)
    e_total = jnp.concatenate(
        [jnp.where(core == 0, own, came), jnp.where(core == 0, came, own)], axis=1
    )

    return (
        total_out.astype(bf16).transpose(1, 0, 2),
        tokens_grad.transpose(1, 0, 2),
        small_total[:, n_experts],
        small_total[:, n_experts + 1],
        query_grad,
        key_grad,
        value_grad,
        out_w_grad,
        small_total[:, :n_experts],
        gate_w_grad,
        up_w_grad,
        down_w_grad,
        e_total[0][None],
        e_total[1][None],
        e_total[2].T[None],
    )


def solution(mesh):
    rows = P(("seq", "fsdp"), None, None)
    matrix = P(("seq", "fsdp"), None)
    vector = P(("seq", "fsdp"))
    expert = P("fsdp", None, None)
    return jax.shard_map(
        body,
        mesh=mesh,
        in_specs=(rows,) * 3 + (vector,) * 2 + (matrix,) * 8 + (expert,) * 3,
        out_specs=(rows,) * 2 + (vector,) * 2 + (matrix,) * 8 + (expert,) * 3,
        check_vma=False,
    )
```

```python
import functools
import math

import jax
import jax.numpy as jnp
from jax import lax
from jax.experimental import pallas as pl
from jax.experimental.pallas import tpu as pltpu
from jax.sharding import PartitionSpec as P

QUERY_HEADS = 12
KEY_VALUE_HEADS = 4
HEAD_SIZE = 128
GROUP_MEMBERS = QUERY_HEADS // KEY_VALUE_HEADS

epsilon = 1e-06
masked_score = -1e30
MESH = pl.DeviceIdType.MESH
VMEM_LIMIT = 63 * 1024 * 1024
f32 = jnp.float32
bf16 = jnp.bfloat16


def round_up(number, step):
    return -(-number // step) * step


def nn(left, right):
    return lax.dot_general(left, right, (((1,), (0,)), ((), ())), preferred_element_type=f32)


def nt(left, right):
    return lax.dot_general(left, right, (((1,), (1,)), ((), ())), preferred_element_type=f32)


def tn(left, right):
    return lax.dot_general(left, right, (((0,), (0,)), ((), ())), preferred_element_type=f32)


def place():
    core = lax.axis_index("seq")
    chip = lax.axis_index("fsdp")
    return core, chip, chip // KEY_VALUE_HEADS, lax.rem(chip, KEY_VALUE_HEADS)


def group(kind, shards):
    core, chip, outer, inner = place()
    if kind == "plane":
        size = 2 * KEY_VALUE_HEADS
        return (
            size,
            core * KEY_VALUE_HEADS + inner,
            lambda r: (r // KEY_VALUE_HEADS, outer * KEY_VALUE_HEADS + lax.rem(r, KEY_VALUE_HEADS)),
        )
    if kind == "inner":
        return KEY_VALUE_HEADS, inner, lambda r: (core, outer * KEY_VALUE_HEADS + r)
    if kind == "outer":
        return shards // KEY_VALUE_HEADS, outer, lambda r: (core, r * KEY_VALUE_HEADS + inner)
    if kind == "chips":
        return shards, chip, lambda r: (core, r)
    if kind == "all":
        return 2 * shards, core * shards + chip, lambda r: (r // shards, lax.rem(r, shards))
    return 2, core, lambda r: (r, chip)


def repeat(first, last, step):
    if last - first <= 16:
        for index in range(first, last):
            step(index)
    else:

        def one(index, carry):
            step(index)
            return carry

        lax.fori_loop(first, last, one, 0)


class Wires:
    def __init__(self, shards, send_sems, recv_sems, local_sems):
        self.shards = shards
        self.send_sems, self.recv_sems, self.local_sems = send_sems, recv_sems, local_sems
        self.used = 0
        self.leaving = []

    def greet(self, kinds):
        barrier = pltpu.get_barrier_semaphore()
        total = 0
        for kind in kinds:
            size, me, device = group(kind, self.shards)

            def signal(d, size=size, me=me, device=device):
                pl.semaphore_signal(
                    barrier, inc=1, device_id=device(lax.rem(me + d, size)), device_id_type=MESH
                )

            repeat(1, size, signal)
            total += size - 1
        pl.semaphore_wait(barrier, total)

    def take(self, count):
        base = self.used
        self.used += count
        return base

    def remote(self, source, target, index, device):
        return pltpu.make_async_remote_copy(
            src_ref=source,
            dst_ref=target,
            send_sem=self.send_sems.at[index],
            recv_sem=self.recv_sems.at[index],
            device_id=device,
            device_id_type=MESH,
        )

    def local(self, source, target, index):
        return pltpu.make_async_copy(source, target, self.local_sems.at[index])

    def exchange(self, kind, source_for, target_from, own=True):
        size, me, device = group(kind, self.shards)
        base = self.take(size)

        def copy(d):
            to = lax.rem(me + d, size)
            return self.remote(source_for(to, d), target_from(me, d), base + d, device(to))

        repeat(1, size, lambda d: copy(d).start())
        if own:
            self.local(source_for(me, 0), target_from(me, 0), base).start()
        self.leaving.append(lambda: repeat(1, size, lambda d: copy(d).wait_send()))

        def arrive(then=None):
            def one(d):
                came = lax.rem(me - d + size, size)
                place_of = target_from(came, d)
                self.remote(place_of, place_of, base + d, device(came)).wait_recv()
                if then is not None:
                    then(d)

            repeat(1, size, one)
            if own:
                self.local(source_for(me, 0), target_from(me, 0), base).wait()

        return arrive

    def sibling(self, source, target, comes):
        core, chip, _, _ = place()
        device = (1 - core, chip)
        index = self.take(1)
        copy = self.remote(source, target, index, device)
        copy.start()
        self.leaving.append(copy.wait_send)
        return self.remote(comes, comes, index, device).wait_recv

    def finish(self):
        for leave in self.leaving:
            leave()


def transfer(name, collective, shards, kinds, sems, body, operands, outs):
    count = len(operands)

    def kernel(*refs):
        ins, results = refs[:count], refs[count : count + len(outs)]
        wires = Wires(shards, *refs[count + len(outs) :])
        wires.greet(kinds)
        body(wires, ins, results)
        wires.finish()

    return pl.pallas_call(
        kernel,
        out_shape=[jax.ShapeDtypeStruct(shape, kind) for shape, kind in outs],
        in_specs=[pl.BlockSpec(memory_space=pl.ANY)] * count,
        out_specs=[pl.BlockSpec(memory_space=pl.ANY)] * len(outs),
        scratch_shapes=[pltpu.SemaphoreType.DMA((sems,))] * 3,
        compiler_params=pltpu.CompilerParams(collective_id=collective, has_side_effects=True),
        name=name,
    )(*operands)


def attend_kernel(chunk, n_out, q_ref, kv_ref, mixed_ref, log_ref):
    outer = lax.axis_index("fsdp") // KEY_VALUE_HEADS
    factor = HEAD_SIZE**-0.5 * math.log2(math.e)
    for half in range(2):
        query = q_ref[pl.ds(half * chunk, chunk), :]

        def fold(block, carry, masked, query=query):
            largest, total, summed = carry
            rows = pl.ds(pl.multiple_of((block // n_out) * chunk, chunk), chunk)
            key = kv_ref[lax.rem(block, n_out), rows, 0:HEAD_SIZE]
            value = kv_ref[lax.rem(block, n_out), rows, HEAD_SIZE : 2 * HEAD_SIZE]
            scores = nt(key, query)
            if masked:
                key_at = lax.broadcasted_iota(jnp.int32, scores.shape, 0)
                query_at = lax.broadcasted_iota(jnp.int32, scores.shape, 1)
                scores = jnp.where(key_at <= query_at, scores, masked_score)
            new = jnp.maximum(largest, jnp.max(scores, axis=0, keepdims=True))
            weights = jnp.exp2((scores - new) * factor)
            shrink = jnp.exp2((largest - new) * factor)
            total = total * shrink + jnp.sum(weights, axis=0, keepdims=True)
            summed = summed * shrink + tn(value, weights.astype(bf16))
            return new, total, summed

        start = (
            jnp.full((1, chunk), masked_score, f32),
            jnp.zeros((1, chunk), f32),
            jnp.zeros((HEAD_SIZE, chunk), f32),
        )
        own = half * n_out + outer
        carry = fold(own, start, True)
        largest, total, summed = lax.fori_loop(
            0, own, lambda block, carry: fold(block, carry, False), carry
        )
        mixed_ref[pl.ds(half * chunk, chunk), :] = (summed / total).T
        log_ref[0, half : half + 1, :] = largest * factor + jnp.log2(total)


def attend(chunk, n_out, qkv, kv_all):
    rows = 2 * chunk
    return pl.pallas_call(
        functools.partial(attend_kernel, chunk, n_out),
        grid=(GROUP_MEMBERS,),
        in_specs=[
            pl.BlockSpec((rows, HEAD_SIZE), lambda h: (0, h)),
            pl.BlockSpec(kv_all.shape, lambda h: (0, 0, 0), pipeline_mode=pl.Buffered(1)),
        ],
        out_specs=[
            pl.BlockSpec((rows, HEAD_SIZE), lambda h: (0, h)),
            pl.BlockSpec((1, 2, chunk), lambda h: (h, 0, 0)),
        ],
        out_shape=[
            jax.ShapeDtypeStruct((rows, GROUP_MEMBERS * HEAD_SIZE), f32),
            jax.ShapeDtypeStruct((GROUP_MEMBERS, 2, chunk), f32),
        ],
        compiler_params=pltpu.CompilerParams(vmem_limit_bytes=VMEM_LIMIT),
        name="attend",
    )(qkv, kv_all)


def attend_back_kernel(
    chunk, n_out, q_ref, kv_ref, grad_ref, log_ref, delta_ref, dq_ref, dkv_ref, sums
):
    head = pl.program_id(0)
    outer = lax.axis_index("fsdp") // KEY_VALUE_HEADS
    scale = HEAD_SIZE**-0.5
    factor = scale * math.log2(math.e)

    @pl.when(head == 0)
    def _():
        sums[...] = jnp.zeros_like(sums)

    for half in range(2):
        mine = pl.ds(half * chunk, chunk)
        query = q_ref[mine, :]
        grad = grad_ref[mine, :]
        log_row = log_ref[0, half : half + 1, :]
        delta_row = delta_ref[0, half : half + 1, :]

        def fold(block, dq, masked, query=query, grad=grad, log_row=log_row, delta_row=delta_row):
            at = lax.rem(block, n_out)
            rows = pl.ds(pl.multiple_of((block // n_out) * chunk, chunk), chunk)
            key = kv_ref[at, rows, 0:HEAD_SIZE]
            value = kv_ref[at, rows, HEAD_SIZE : 2 * HEAD_SIZE]
            scores = nt(key, query)
            if masked:
                key_at = lax.broadcasted_iota(jnp.int32, scores.shape, 0)
                query_at = lax.broadcasted_iota(jnp.int32, scores.shape, 1)
                scores = jnp.where(key_at <= query_at, scores, masked_score)
            weights = jnp.exp2(scores * factor - log_row)
            grad_scores = (weights * (nt(value, grad) - delta_row)).astype(bf16)
            sums[at, rows, 0:HEAD_SIZE] += nn(grad_scores, query)
            sums[at, rows, HEAD_SIZE : 2 * HEAD_SIZE] += nn(weights.astype(bf16), grad)
            return dq + tn(grad_scores, key)

        own = half * n_out + outer
        dq = fold(own, jnp.zeros((chunk, HEAD_SIZE), f32), True)
        dq = lax.fori_loop(0, own, lambda block, dq: fold(block, dq, False), dq)
        dq_ref[mine, :] = (dq * scale).astype(bf16)

    @pl.when(head == GROUP_MEMBERS - 1)
    def _():
        dkv_ref[...] = sums[...].astype(bf16)


def attend_back(chunk, n_out, qkv, kv_all, grad_mixed, log_rows, delta_rows):
    rows = 2 * chunk
    per_head = pl.BlockSpec((rows, HEAD_SIZE), lambda h: (0, h))
    per_row = pl.BlockSpec((1, 2, chunk), lambda h: (h, 0, 0))
    whole = pl.BlockSpec(kv_all.shape, lambda h: (0, 0, 0), pipeline_mode=pl.Buffered(1))
    return pl.pallas_call(
        functools.partial(attend_back_kernel, chunk, n_out),
        grid=(GROUP_MEMBERS,),
        in_specs=[per_head, whole, per_head, per_row, per_row],
        out_specs=[per_head, whole],
        out_shape=[
            jax.ShapeDtypeStruct((rows, GROUP_MEMBERS * HEAD_SIZE), bf16),
            jax.ShapeDtypeStruct(kv_all.shape, bf16),
        ],
        scratch_shapes=[pltpu.VMEM(kv_all.shape, f32)],
        compiler_params=pltpu.CompilerParams(vmem_limit_bytes=VMEM_LIMIT),
        name="attend_back",
    )(qkv, kv_all, grad_mixed, log_rows, delta_rows)


def swiglu_parts(gate_part, up_part):
    sigmoid = jax.nn.sigmoid(gate_part)
    active = gate_part * sigmoid
    slope = up_part * sigmoid * (1.0 + gate_part * (1.0 - sigmoid))
    return active * up_part, active, slope


def experts_kernel(
    room,
    hidden,
    h_ref,
    c_ref,
    meta_ref,
    wg_ref,
    wu_ref,
    wd_ref,
    sgu_ref,
    sd_ref,
    out_ref,
    dh_ref,
    dgate_ref,
    dw_ref,
    dsgu_ref,
    dsd_ref,
    sum_out,
    sum_dh,
    h_rows,
    c_rows,
    picks,
    gate_col,
):
    expert = pl.program_id(0)
    inner = lax.rem(lax.axis_index("fsdp"), KEY_VALUE_HEADS)
    at = lax.rem(inner - expert + KEY_VALUE_HEADS, KEY_VALUE_HEADS)
    blocks, rows, width = h_ref.shape

    @pl.when(expert == 0)
    def _():
        dgate_ref[...] = jnp.zeros_like(dgate_ref)
        hid = h_ref[...].reshape(blocks * rows, width)
        cot = c_ref[...].reshape(blocks * rows, width)
        gate_w, up_w, down_w = sgu_ref[:, 0:hidden], sgu_ref[:, hidden : 2 * hidden], sd_ref[...]
        both, active, slope = swiglu_parts(nn(hid, gate_w), nn(hid, up_w))
        act = both.astype(bf16)
        d_act = nt(cot, down_w)
        d_gate = (d_act * slope).astype(bf16)
        d_up = (d_act * active).astype(bf16)
        sum_out[...] = nn(act, down_w)
        sum_dh[...] = nt(d_gate, gate_w) + nt(d_up, up_w)
        dsgu_ref[:, 0:hidden] = tn(hid, d_gate).astype(bf16)
        dsgu_ref[:, hidden : 2 * hidden] = tn(hid, d_up).astype(bf16)
        dsd_ref[...] = tn(act, cot).astype(bf16)

    slots = lax.broadcasted_iota(jnp.int32, (room, rows), 0).astype(f32)
    for block in range(blocks):
        part = pl.ds(block * room, room)
        gate_row = meta_ref[block, pl.ds(at, 1), :]
        slot_row = meta_ref[block, pl.ds(at + KEY_VALUE_HEADS, 1), :]
        pick = (slots == slot_row).astype(f32)
        gate_col[part, :] = jnp.broadcast_to(
            jnp.sum(pick * gate_row, axis=1, keepdims=True), (room, gate_col.shape[1])
        )
        pick = pick.astype(bf16)
        picks[block] = pick
        h_rows[part, :] = nn(pick, h_ref[block]).astype(bf16)
        c_rows[part, :] = nn(pick, c_ref[block]).astype(bf16)
    gate = gate_col[:, 0:1]
    gate_w, up_w, down_w = wg_ref[0], wu_ref[0], wd_ref[0]
    both, active, slope = swiglu_parts(nn(h_rows[...], gate_w), nn(h_rows[...], up_w))
    act = both.astype(bf16)
    d_act = nt(c_rows[...], down_w)
    d_gates = jnp.sum(d_act * act.astype(f32), axis=1, keepdims=True)
    d_act = d_act * gate
    act = (act.astype(f32) * gate).astype(bf16)
    d_gate = (d_act * slope).astype(bf16)
    d_up = (d_act * active).astype(bf16)
    ff = act.shape[1]
    dw_ref[0, :, 0:ff] = tn(h_rows[...], d_gate).astype(bf16)
    dw_ref[0, :, ff : 2 * ff] = tn(h_rows[...], d_up).astype(bf16)
    dw_ref[0, :, 2 * ff : 3 * ff] = tn(c_rows[...], act).astype(bf16)
    result = nn(act, down_w).astype(bf16)
    d_rows = (nt(d_gate, gate_w) + nt(d_up, up_w)).astype(bf16)
    for block in range(blocks):
        pick = picks[block]
        part = slice(block * room, (block + 1) * room)
        here = pl.ds(block * rows, rows)
        sum_out[here, :] += tn(pick, result[part])
        sum_dh[here, :] += tn(pick, d_rows[part])
        dgate_ref[block, pl.ds(at, 1), :] = jnp.sum(
            pick.astype(f32) * d_gates[part], axis=0, keepdims=True
        )

    @pl.when(expert == pl.num_programs(0) - 1)
    def _():
        out_ref[...] = sum_out[...].astype(bf16).reshape(out_ref.shape)
        dh_ref[...] = sum_dh[...].astype(bf16).reshape(dh_ref.shape)


def experts(room, hidden, h_all, c_all, meta, wg, wu, wd, sgu, sd):
    blocks, rows, width = h_all.shape
    n_experts, _, inner = wg.shape

    def once(shape):
        return pl.BlockSpec(shape, lambda e: (0,) * len(shape), pipeline_mode=pl.Buffered(1))

    def each(shape, **kind):
        return pl.BlockSpec((1,) + shape[1:], lambda e: (e, 0, 0), **kind)

    single = dict(pipeline_mode=pl.Buffered(1))
    return pl.pallas_call(
        functools.partial(experts_kernel, room, hidden),
        grid=(n_experts,),
        in_specs=[
            once(h_all.shape),
            once(c_all.shape),
            once(meta.shape),
            each(wg.shape),
            each(wu.shape),
            each(wd.shape),
            once(sgu.shape),
            once(sd.shape),
        ],
        out_specs=[
            once(h_all.shape),
            once(h_all.shape),
            once(meta.shape),
            pl.BlockSpec((1, width, 3 * inner), lambda e: (e, 0, 0), **single),
            once(sgu.shape),
            once(sd.shape),
        ],
        out_shape=[
            jax.ShapeDtypeStruct(h_all.shape, bf16),
            jax.ShapeDtypeStruct(h_all.shape, bf16),
            jax.ShapeDtypeStruct(meta.shape, f32),
            jax.ShapeDtypeStruct((n_experts, width, 3 * inner), bf16),
            jax.ShapeDtypeStruct(sgu.shape, bf16),
            jax.ShapeDtypeStruct(sd.shape, bf16),
        ],
        scratch_shapes=[
            pltpu.VMEM((blocks * rows, width), f32),
            pltpu.VMEM((blocks * rows, width), f32),
            pltpu.VMEM((blocks * room, width), bf16),
            pltpu.VMEM((blocks * room, width), bf16),
            pltpu.VMEM((blocks, room, rows), bf16),
            pltpu.VMEM((blocks * room, 128), f32),
        ],
        compiler_params=pltpu.CompilerParams(vmem_limit_bytes=VMEM_LIMIT),
        name="experts",
    )(h_all, c_all, meta, wg, wu, wd, sgu, sd)


def experts_line_kernel(room, hidden, shards, refs):
    n = shards // KEY_VALUE_HEADS
    h_ref, meta_ref = refs[:2]
    c_refs = refs[2 : 2 + n]
    (
        wg_ref,
        wu_ref,
        wd_ref,
        sgu_ref,
        sd_ref,
        dh_out,
        dgate_out,
        mix_out,
        e_mine,
        e_other,
        gu_mine,
        gu_other,
        dsd_ref,
        h_all,
        c_all,
        metas,
        wgu,
        wd,
        picks,
        kept_gu,
        kept_act,
        kept_shared,
        row_a,
        row_b,
        dh_stage,
        mix_stage,
        dg_stage,
        down_stage,
        gu_stage,
        send_sems,
        recv_sems,
        local_sems,
    ) = refs[2 + n :]
    wires = Wires(shards, send_sems, recv_sems, local_sems)
    core, chip, outer, inner = place()
    rows, width = h_ref.shape
    ff = wd.shape[1]
    experts_here = KEY_VALUE_HEADS

    def device(at):
        return core, at * KEY_VALUE_HEADS + inner

    own_h = wires.local(h_ref, h_all.at[outer], wires.take(1))
    own_meta = wires.local(meta_ref.at[outer], metas.at[outer], wires.take(1))
    own_h.start()
    own_meta.start()
    c_base = wires.take(n)

    def c_copy(d):
        return wires.local(
            c_refs[d], c_all.at[lax.rem(outer - d + n, n)], c_base + d
        )

    w_base = wires.take(3 * experts_here)

    def weights(e):
        return (
            wires.local(wg_ref.at[e], wgu.at[e, :, pl.ds(0, ff)], w_base + 3 * e),
            wires.local(wu_ref.at[e], wgu.at[e, :, pl.ds(ff, ff)], w_base + 3 * e + 1),
            wires.local(wd_ref.at[e], wd.at[e], w_base + 3 * e + 2),
        )

    c_copy(0).start()
    for e in range(experts_here):
        for copy in weights(e):
            copy.start()
    for d in range(1, n):
        c_copy(d).start()

    wires.greet(["outer", "core"])

    up_base, down_base = wires.take(n), wires.take(n)

    def hop(step, upward):
        sign = 1 if upward else -1
        to = outer + sign
        block = outer - sign * step
        come = block - sign
        inside = (to >= 0) & (to < n) & (block >= 0) & (block < n)
        arrives = (come >= 0) & (come < n)
        base = up_base if upward else down_base
        block, come = lax.rem(block + n, n), lax.rem(come + n, n)
        send = wires.remote(
            h_ref if step == 0 else h_all.at[block],
            h_all.at[block],
            base + step,
            device(lax.rem(to + n, n)),
        )
        receive = wires.remote(
            h_all.at[come], h_all.at[come], base + step, device(lax.rem(to + n, n))
        )
        return inside, arrives, send, receive

    def hop_start(step):
        for upward in (True, False):
            inside, _, send, _ = hop(step, upward)
            pl.when(inside)(send.start)

    def hop_arrive(step):
        for upward in (True, False):
            _, arrives, _, receive = hop(step, upward)
            pl.when(arrives)(receive.wait_recv)

    hop_start(0)
    meta_in = wires.exchange(
        "outer", lambda r, d: meta_ref.at[r], lambda r, d: metas.at[r], own=False
    )

    dh_send, dh_recv = wires.take(n), wires.take(n)
    dg_send, dg_recv = wires.take(n), wires.take(n)

    def give_back(stage, target, k, block, sends, receives):
        return pltpu.make_async_remote_copy(
            src_ref=stage,
            dst_ref=target.at[outer],
            send_sem=send_sems.at[sends + k],
            recv_sem=recv_sems.at[receives + outer],
            device_id=device(block),
            device_id_type=MESH,
        )

    def take_back(target, origin, receives):
        return pltpu.make_async_remote_copy(
            src_ref=target.at[origin],
            dst_ref=target.at[origin],
            send_sem=send_sems.at[receives],
            recv_sem=recv_sems.at[receives + origin],
            device_id=device(origin),
            device_id_type=MESH,
        )

    dh_own = wires.local(dh_stage.at[0], dh_out.at[outer], wires.take(1))
    dg_own = wires.local(dg_stage.at[0], dgate_out.at[outer], wires.take(1))
    mix_base = wires.take(n)

    def mix_copy(k, block):
        return wires.local(
            mix_stage.at[k % 2], mix_out.at[lax.rem(outer - block + n, n)], mix_base + k
        )

    slots = lax.broadcasted_iota(jnp.int32, (room, rows), 0).astype(f32)
    order = [
        lax.rem(jnp.where(outer < n // 2, outer + k, outer - k + n), n) for k in range(n)
    ]
    gate_w, up_w, down_w = sgu_ref[:, 0:hidden], sgu_ref[:, hidden : 2 * hidden], sd_ref[...]

    for k, block in enumerate(order):
        if k == 0:
            own_h.wait()
            own_meta.wait()
            c_copy(0).wait()
        else:
            hop_arrive(k - 1)
            if k < n - 1:
                hop_start(k)
            if k == 1:
                meta_in()
                for d in range(1, n):
                    c_copy(d).wait()
        hid, cot = h_all[block], c_all[block]
        for e in range(experts_here):
            at = lax.rem(inner - e + experts_here, experts_here)
            slot_row = metas[block, pl.ds(at + experts_here, 1), :]
            picks[block, pl.ds(e * room, room), :] = (slots == slot_row).astype(bf16)
        row_a[...] = nn(picks[block], hid).astype(bf16)
        row_b[...] = nn(picks[block], cot).astype(bf16)
        dg_stage[k] = jnp.zeros(dg_stage.shape[1:], f32)

        def one_expert(e, carry, k=k, block=block):
            if k == 0:
                for copy in weights(e):
                    copy.wait()
            at = lax.rem(inner - e + experts_here, experts_here)
            part = pl.ds(pl.multiple_of(e * room, 16), room)
            pick = picks[block, part, :].astype(f32)
            gate = jnp.sum(pick * metas[block, pl.ds(at, 1), :], axis=1, keepdims=True)
            first = nn(row_a[part, :], wgu[e])
            both, active, slope = swiglu_parts(first[:, 0:ff], first[:, ff : 2 * ff])
            act = both.astype(bf16)
            d_act = nt(row_b[part, :], wd[e])
            d_gates = jnp.sum(d_act * act.astype(f32), axis=1, keepdims=True)
            dg_stage[k, pl.ds(at, 1), :] = jnp.sum(pick * d_gates, axis=0, keepdims=True)
            d_act = d_act * gate
            act = (act.astype(f32) * gate).astype(bf16)
            here = pl.ds(pl.multiple_of(block * room, 16), room)
            kept_act[e, here, :] = act
            kept_gu[e, here, 0:ff] = (d_act * slope).astype(bf16)
            kept_gu[e, here, ff : 2 * ff] = (d_act * active).astype(bf16)
            row_a[part, :] = nn(act, wd[e]).astype(bf16)
            row_b[part, :] = nt(kept_gu[e, here, :], wgu[e]).astype(bf16)
            return carry

        lax.fori_loop(0, experts_here, one_expert, 0)
        both, active, slope = swiglu_parts(nn(hid, gate_w), nn(hid, up_w))
        act = both.astype(bf16)
        d_act = nt(cot, down_w)
        d_gate = (d_act * slope).astype(bf16)
        d_up = (d_act * active).astype(bf16)
        kept_shared[block, :, 0:hidden] = d_gate
        kept_shared[block, :, hidden : 2 * hidden] = d_up
        kept_shared[block, :, 2 * hidden : 3 * hidden] = act
        dh_stage[k] = (
            tn(picks[block], row_b[...]) + nt(d_gate, gate_w) + nt(d_up, up_w)
        ).astype(bf16)
        if k == 0:
            dh_own.start()
            dg_own.start()
        else:
            give_back(dh_stage.at[k], dh_out, k, block, dh_send, dh_recv).start()
            give_back(dg_stage.at[k], dgate_out, k, block, dg_send, dg_recv).start()
        if k >= 2:
            mix_copy(k - 2, order[k - 2]).wait()
        mix_stage[k % 2] = (tn(picks[block], row_a[...]) + nn(act, down_w)).astype(bf16)
        mix_copy(k, block).start()

    half = width // 2
    mine, other = pl.ds(core * half, half), pl.ds((1 - core) * half, half)
    sibling = (1 - core, chip)
    left, right = pl.ds(0, 2 * ff), pl.ds(2 * ff, ff)
    keep_base, give_base = wires.take(2 * experts_here + 1), wires.take(2 * experts_here + 1)

    def keep(e):
        return (
            wires.local(wgu.at[e, mine, :], e_mine.at[e, :, left], keep_base + 2 * e),
            wires.local(down_stage.at[e % 2, mine, :], e_mine.at[e, :, right], keep_base + 2 * e + 1),
        )

    def give(e):
        return (
            wires.remote(wgu.at[e, other, :], e_other.at[e, :, left], give_base + 2 * e, sibling),
            wires.remote(
                down_stage.at[e % 2, other, :],
                e_other.at[e, :, right],
                give_base + 2 * e + 1,
                sibling,
            ),
        )

    for e in range(experts_here):
        for block in range(n):
            part = pl.ds(block * room, room)
            pick = picks[block, pl.ds(e * room, room), :]
            row_a[part, :] = nn(pick, h_all[block]).astype(bf16)
            row_b[part, :] = nn(pick, c_all[block]).astype(bf16)
        wgu[e] = tn(row_a[...], kept_gu[e]).astype(bf16)
        if e >= 2:
            keep(e - 2)[1].wait()
            give(e - 2)[1].wait_send()
        down_stage[e % 2] = tn(row_b[...], kept_act[e]).astype(bf16)
        for copy in keep(e) + give(e):
            copy.start()
    hid_all = h_all[...].reshape(n * rows, width)
    shared = kept_shared[...].reshape(n * rows, 3 * hidden)
    gu_stage[...] = tn(hid_all, shared[:, 0 : 2 * hidden]).astype(bf16)
    gu_keep = wires.local(gu_stage.at[mine, :], gu_mine, keep_base + 2 * experts_here)
    gu_give = wires.remote(gu_stage.at[other, :], gu_other, give_base + 2 * experts_here, sibling)
    gu_keep.start()
    gu_give.start()
    dsd_ref[...] = tn(shared[:, 2 * hidden :], c_all[...].reshape(n * rows, width)).astype(bf16)

    for step in range(n - 1):
        for upward in (True, False):
            inside, _, send, _ = hop(step, upward)
            pl.when(inside)(send.wait_send)
    dh_own.wait()
    dg_own.wait()
    for k in range(max(0, n - 2), n):
        mix_copy(k, order[k]).wait()
    for k in range(1, n):
        give_back(dh_stage.at[k], dh_out, k, order[k], dh_send, dh_recv).wait_send()
        give_back(dg_stage.at[k], dgate_out, k, order[k], dg_send, dg_recv).wait_send()
    for d in range(1, n):
        origin = lax.rem(outer + d, n)
        take_back(dh_out, origin, dh_recv).wait_recv()
        take_back(dgate_out, origin, dg_recv).wait_recv()
    for e in range(experts_here):
        for which, (kept, given) in enumerate(zip(keep(e), give(e))):
            if which == 0 or e >= experts_here - 2:
                kept.wait()
                given.wait_send()
            given.wait_recv()
    gu_keep.wait()
    gu_give.wait()
    wires.finish()


def experts_line(room, hidden, shards, collective, h_own, meta, c_parts, wg, wu, wd, sgu, sd):
    n = shards // KEY_VALUE_HEADS
    rows, width = h_own.shape
    n_experts, _, ff = wg.shape
    half = width // 2
    any_spec = pl.BlockSpec(memory_space=pl.ANY)
    vmem = pl.BlockSpec(memory_space=pltpu.VMEM)
    e_shape = (n_experts, half, 3 * ff)
    sems = 64 + 24 * n

    def kernel(*refs):
        experts_line_kernel(room, hidden, shards, refs)

    return pl.pallas_call(
        kernel,
        in_specs=[any_spec] * (2 + n + 3) + [vmem] * 2,
        out_specs=[any_spec] * 7 + [vmem],
        out_shape=[
            jax.ShapeDtypeStruct((n, rows, width), bf16),
            jax.ShapeDtypeStruct(meta.shape, f32),
            jax.ShapeDtypeStruct((n, rows, width), bf16),
            jax.ShapeDtypeStruct(e_shape, bf16),
            jax.ShapeDtypeStruct(e_shape, bf16),
            jax.ShapeDtypeStruct((half, 2 * hidden), bf16),
            jax.ShapeDtypeStruct((half, 2 * hidden), bf16),
            jax.ShapeDtypeStruct(sd.shape, bf16),
        ],
        scratch_shapes=[
            pltpu.VMEM((n, rows, width), bf16),
            pltpu.VMEM((n, rows, width), bf16),
            pltpu.VMEM(meta.shape, f32),
            pltpu.VMEM((n_experts, width, 2 * ff), bf16),
            pltpu.VMEM((n_experts, ff, width), bf16),
            pltpu.VMEM((n, n_experts * room, rows), bf16),
            pltpu.VMEM((n_experts, n * room, 2 * ff), bf16),
            pltpu.VMEM((n_experts, n * room, ff), bf16),
            pltpu.VMEM((n, rows, 3 * hidden), bf16),
            pltpu.VMEM((n * room, width), bf16),
            pltpu.VMEM((n * room, width), bf16),
            pltpu.VMEM((n, rows, width), bf16),
            pltpu.VMEM((2, rows, width), bf16),
            pltpu.VMEM((n,) + meta.shape[1:], f32),
            pltpu.VMEM((2, width, ff), bf16),
            pltpu.VMEM((width, 2 * hidden), bf16),
        ]
        + [pltpu.SemaphoreType.DMA((sems,))] * 3,
        compiler_params=pltpu.CompilerParams(
            collective_id=collective, has_side_effects=True, vmem_limit_bytes=VMEM_LIMIT
        ),
        name="experts_line",
    )(h_own, meta, *c_parts, wg, wu, wd, sgu, sd)


def experts_split(room, hidden, shards, collectives, h_own, meta, c_parts, wg, wu, wd, sgu, sd):
    n_out, n_in = shards // KEY_VALUE_HEADS, KEY_VALUE_HEADS
    rows, width = h_own.shape
    core = lax.axis_index("seq")
    half = width // 2

    def spread_hidden(wires, ins, outs):
        waits = [
            wires.exchange("outer", lambda r, d: ins[0], lambda r, d: outs[0].at[d]),
            wires.exchange("outer", lambda r, d: ins[1].at[r], lambda r, d: outs[1].at[d]),
        ]
        for wait in waits:
            wait()

    h_all, meta_all = transfer(
        "spread_hidden",
        collectives[0],
        shards,
        ["outer"],
        2 * n_out,
        spread_hidden,
        [h_own, meta],
        [((n_out, rows, width), bf16), (meta.shape, f32)],
    )
    c_all = jnp.stack(c_parts)
    at_once = math.gcd(n_out, 4)
    parts = [
        experts(
            room,
            hidden,
            h_all[i : i + at_once],
            c_all[i : i + at_once],
            meta_all[i : i + at_once],
            wg,
            wu,
            wd,
            sgu,
            sd,
        )
        for i in range(0, n_out, at_once)
    ]
    mix_part, dh_part, dgate_part = (
        jnp.concatenate([part[k] for part in parts], axis=0) for k in range(3)
    )
    e_grad, sgu_grad, sd_grad = (
        sum(part[k].astype(f32) for part in parts).astype(bf16) for k in range(3, 6)
    )

    def sum_hidden(wires, ins, outs):
        core = lax.axis_index("seq")
        dh_ref, dg_ref, e_ref, gu_ref = ins
        dhs, dgs, es, gus = outs
        other = pl.ds((1 - core) * half, half)
        waits = [
            wires.exchange(
                "outer", lambda r, d: dh_ref.at[(n_out - d) % n_out], lambda r, d: dhs.at[r]
            ),
            wires.exchange(
                "outer", lambda r, d: dg_ref.at[(n_out - d) % n_out], lambda r, d: dgs.at[r]
            ),
            wires.sibling(e_ref.at[:, other], es, es),
            wires.sibling(gu_ref.at[other], gus, gus),
        ]
        for wait in waits:
            wait()

    dhs, dgs, es, gus = transfer(
        "sum_hidden",
        collectives[1],
        shards,
        ["outer", "core"],
        2 * n_out + 8,
        sum_hidden,
        [dh_part, dgate_part, e_grad, sgu_grad],
        [
            ((n_out, rows, width), bf16),
            (meta.shape, f32),
            ((n_in, half, e_grad.shape[2]), bf16),
            ((half, 2 * hidden), bf16),
        ],
    )
    e_mine = lax.dynamic_slice_in_dim(e_grad, core * half, half, 1)
    gu_mine = lax.dynamic_slice_in_dim(sgu_grad, core * half, half, 0)
    return dhs, dgs, mix_part, e_mine, es, gu_mine, gus, sd_grad


def norm_rows(values, gain_vector):
    inverse = lax.rsqrt(jnp.mean(values * values, axis=-1, keepdims=True) + epsilon)
    normed = values * inverse
    return (normed, inverse, normed * gain_vector)


def norm_back(grad_hidden, normed, inverse, gain_vector):
    grad_normed = grad_hidden * gain_vector
    gain_grad = jnp.sum(grad_hidden * normed, axis=(0, 1))
    inner_mean = jnp.mean(grad_normed * normed, axis=-1, keepdims=True)
    return (inverse * (grad_normed - normed * inner_mean), gain_grad)


def pad_rows(array, axis):
    size = array.shape[axis]
    widths = [(0, 0)] * array.ndim
    widths[axis] = (0, round_up(size, 16) - size)
    return jnp.pad(array, widths) if widths[axis][1] else array


def pad_to(array, axis, size):
    widths = [(0, 0)] * array.ndim
    widths[axis] = (0, size - array.shape[axis])
    return jnp.pad(array, widths) if widths[axis][1] else array


def body(
    tokens,
    routes,
    out_grad,
    attn_gain,
    ffn_gain,
    query_projection,
    key_projection,
    value_projection,
    w_out,
    w_router,
    shared_gate,
    shared_up,
    shared_down,
    expert_gate,
    expert_up,
    expert_down,
):
    shards = lax.axis_size("fsdp")
    n_in = KEY_VALUE_HEADS
    n_out = shards // n_in
    core, chip, outer, inner = place()
    seg, seqs, width = tokens.shape
    rows = seg * seqs
    topk = routes.shape[2]
    n_experts = w_router.shape[1]
    w_rows = query_projection.shape[0]
    w_pad = round_up(w_rows, 16)
    d_rows = shared_down.shape[0]
    d_pad = round_up(d_rows, 16)
    half_chips = shards // 2
    q_cols = GROUP_MEMBERS * HEAD_SIZE
    cols = q_cols + 2 * HEAD_SIZE
    ff = expert_gate.shape[2]
    hid_core = n_in * d_rows
    hid = 2 * hid_core
    hid_pad = round_up(hid, 128)
    small = round_up(n_experts + 2, 128)
    chunk = n_in * seg
    half_width, half_ff = width // 2, ff // 2
    room = round_up(max(2, (3 * rows * topk + 2 * n_experts - 1) // (2 * n_experts)), 16)

    small_piece = pad_to(
        jnp.concatenate([w_router, attn_gain[:, None], ffn_gain[:, None]], axis=1), 1, small
    )
    q_pieces = pad_rows(
        jnp.concatenate(
            [
                query_projection.reshape(w_rows, n_in, q_cols),
                key_projection.reshape(w_rows, n_in, HEAD_SIZE),
                value_projection.reshape(w_rows, n_in, HEAD_SIZE),
                jnp.broadcast_to(small_piece[:, None], (w_rows, n_in, small)),
            ],
            axis=2,
        ).transpose(1, 0, 2),
        1,
    )

    def hidden_piece(weight):
        piece = weight.reshape(w_rows, 2, n_out, hid_core).transpose(2, 0, 1, 3)
        return pad_to(piece.reshape(n_out, w_rows, hid), 2, hid_pad)

    gu_pieces = pad_rows(
        jnp.concatenate([hidden_piece(shared_gate), hidden_piece(shared_up)], axis=2), 1
    )
    out_piece = pad_rows(w_out, 0)
    down_piece = pad_rows(shared_down, 0)
    x_own = tokens.transpose(1, 0, 2)
    c_own = out_grad.transpose(1, 0, 2)
    cot = c_own.reshape(rows, width)

    def shift(block, step):
        axis, amount = step
        if axis == "outer":
            pairs = [(f, (f + amount * n_in) % shards) for f in range(shards)]
        else:
            pairs = [(f, f // n_in * n_in + (f + amount) % n_in) for f in range(shards)]
        return lax.ppermute(block, "fsdp", pairs)

    def gather_expert(wires, mine, every, size):
        core, chip, outer, inner = place()
        part, other = pl.ds(core * size, size), pl.ds((1 - core) * size, size)
        device = (1 - core, chip)
        arrive = wires.exchange(
            "inner", lambda r, d: mine.at[0, part], lambda r, d: every.at[d, part], own=False
        )
        own = wires.sibling(mine.at[0], every.at[0], every.at[0])
        base = wires.take(n_in)

        def hand_on(d):
            wires.remote(every.at[d, part], every.at[d, part], base + d, device).start()

        def settle():
            arrive(hand_on)
            own()
            for d in range(1, n_in):
                wires.remote(every.at[d, part], every.at[d, part], base + d, device).wait_send()
                wires.remote(every.at[d, other], every.at[d, other], base + d, device).wait_recv()

        return settle

    def out_rows(wires, o_ref, wo_ref):
        core, chip, outer, inner = place()
        to_inner = 2 * core + chip // half_chips
        slot = lax.rem(chip, half_chips)
        base = wires.take(half_chips)
        sends = wires.take(2 * n_out)

        def copy(k):
            to = (k // n_out, lax.rem(k, n_out) * n_in + to_inner)
            here = (to[0] == core) & (to[1] == chip)
            return here, pltpu.make_async_remote_copy(
                src_ref=o_ref,
                dst_ref=wo_ref.at[slot],
                send_sem=wires.send_sems.at[sends + k],
                recv_sem=wires.recv_sems.at[base + slot],
                device_id=to,
                device_id_type=MESH,
            )

        def start(k):
            here, send = copy(k)
            pl.when(jnp.logical_not(here))(send.start)
            pl.when(here)(lambda: wires.local(o_ref, wo_ref.at[slot], base).start())

        def leave(k):
            here, send = copy(k)
            pl.when(jnp.logical_not(here))(send.wait_send)

        def come(i):
            origin = (inner // 2, half_chips * lax.rem(inner, 2) + i)
            here = (origin[0] == core) & (origin[1] == chip)
            place_of = wo_ref.at[i]
            pl.when(jnp.logical_not(here))(
                wires.remote(place_of, place_of, base + i, origin).wait_recv
            )
            pl.when(here)(lambda: wires.local(o_ref, place_of, base).wait())

        repeat(0, 2 * n_out, start)
        wires.leaving.append(lambda: repeat(0, 2 * n_out, leave))
        return lambda: repeat(0, half_chips, come)

    own_rows = half_chips // 2

    def out_rows_back(wires, grad_ref, sums_ref):
        core, chip, outer, inner = place()
        from_inner = 2 * core + chip // half_chips
        from_core = lax.rem(chip, half_chips) // own_rows
        sends = wires.take(own_rows)
        base = wires.take(n_out)

        def copy(i):
            to = (inner // 2, half_chips * lax.rem(inner, 2) + core * own_rows + i)
            here = (to[0] == core) & (to[1] == chip)
            return here, pltpu.make_async_remote_copy(
                src_ref=grad_ref.at[i],
                dst_ref=sums_ref.at[outer],
                send_sem=wires.send_sems.at[sends + i],
                recv_sem=wires.recv_sems.at[base + outer],
                device_id=to,
                device_id_type=MESH,
            )

        def start(i):
            here, send = copy(i)
            pl.when(jnp.logical_not(here))(send.start)
            pl.when(here)(lambda: wires.local(grad_ref.at[i], sums_ref.at[outer], base).start())

        def leave(i):
            here, send = copy(i)
            pl.when(jnp.logical_not(here))(send.wait_send)

        def come(k):
            origin = (from_core, k * n_in + from_inner)
            here = (origin[0] == core) & (origin[1] == chip)
            place_of = sums_ref.at[k]
            pl.when(jnp.logical_not(here))(
                wires.remote(place_of, place_of, base + k, origin).wait_recv
            )
            pl.when(here)(lambda: wires.local(place_of, place_of, base).wait())

        repeat(0, own_rows, start)
        wires.leaving.append(lambda: repeat(0, own_rows, leave))
        return lambda: repeat(0, n_out, come)

    def fetch(wires, ins, outs):
        x_ref, q_ref, o_ref = ins
        xs_ref, wq_ref, wo_ref = outs
        core, chip, outer, inner = place()
        x_in = wires.exchange("plane", lambda r, d: x_ref.at[r // n_in], lambda r, d: xs_ref.at[r])
        q_in = wires.exchange(
            "chips", lambda r, d: q_ref.at[lax.rem(r, n_in)], lambda r, d: wq_ref.at[core, r]
        )
        o_in = out_rows(wires, o_ref, wo_ref)
        q_in()
        q_other = wires.sibling(wq_ref.at[core], wq_ref.at[core], wq_ref.at[1 - core])
        x_in()
        o_in()
        q_other()

    xs, wq, wo = transfer(
        "fetch",
        0,
        shards,
        ["all"],
        4 * shards + 16,
        fetch,
        [x_own, q_pieces, out_piece],
        [
            ((2 * n_in, seg, width), bf16),
            ((2, shards, w_pad, cols + small), bf16),
            ((half_chips, w_pad, width), bf16),
        ],
    )
    wq = wq[:, :, :w_rows].reshape(width, cols + small)
    wo = wo[:, :w_rows].reshape(q_cols, width)
    wq, small_w = wq[:, :cols], wq[:, cols:]
    router_w = small_w[:, :n_experts]
    gain_one = small_w[:, n_experts].astype(f32)
    gain_two = small_w[:, n_experts + 1].astype(f32)

    normed_all, _, h1 = norm_rows(xs.reshape(2 * chunk, width).astype(f32), gain_one)
    h1 = h1.astype(bf16)
    qkv = nn(h1, wq).astype(bf16)

    def spread_kv(wires, ins, outs):
        kv_in = wires.exchange("outer", lambda r, d: ins[0], lambda r, d: outs[0].at[r])
        g_in = gather_expert(wires, ins[1], outs[1], half_width)
        u_in = gather_expert(wires, ins[2], outs[2], half_width)
        kv_in()
        g_in()
        u_in()

    kv_all, e_gate, e_up = transfer(
        "spread_kv",
        1,
        shards,
        ["outer", "plane"],
        n_out + 8 * n_in,
        spread_kv,
        [qkv[:, q_cols:], expert_gate, expert_up],
        [
            ((n_out, 2 * chunk, 2 * HEAD_SIZE), bf16),
            ((n_in, width, ff), bf16),
            ((n_in, width, ff), bf16),
        ],
    )
    kv_all, cot_late = lax.optimization_barrier((kv_all, cot))
    c_parts = [cot] + [shift(cot_late, ("outer", d)) for d in range(1, n_out)]
    mixed, log_rows = attend(chunk, n_out, qkv, kv_all)
    mixed_low = mixed.astype(bf16)
    out_part = nn(mixed_low, wo).astype(bf16).reshape(2 * n_in, seg, width)

    def sum_out(wires, ins, outs):
        core, chip, outer, inner = place()
        part_ref, gu_ref, s_ref, ed_ref = ins
        parts_ref, wgu_ref, ws_ref, ad_ref = outs
        part_in = wires.exchange("plane", lambda r, d: part_ref.at[r], lambda r, d: parts_ref.at[r])
        gu_in = wires.exchange(
            "chips", lambda r, d: gu_ref.at[r // n_in], lambda r, d: wgu_ref.at[core, r]
        )
        s_in = wires.exchange("inner", lambda r, d: s_ref, lambda r, d: ws_ref.at[core, r])
        d_in = gather_expert(wires, ed_ref, ad_ref, half_ff)
        gu_in()
        gu_other = wires.sibling(wgu_ref.at[core], wgu_ref.at[core], wgu_ref.at[1 - core])
        s_in()
        s_other = wires.sibling(ws_ref.at[core], ws_ref.at[core], ws_ref.at[1 - core])
        part_in()
        d_in()
        gu_other()
        s_other()

    out_parts, sgu, ws, e_down = transfer(
        "sum_out",
        2,
        shards,
        ["all"],
        shards + 8 * n_in + 16,
        sum_out,
        [out_part, gu_pieces, down_piece, expert_down],
        [
            ((2 * n_in, seg, width), bf16),
            ((2, shards, w_pad, 2 * hid_pad), bf16),
            ((2, n_in, d_pad, width), bf16),
            ((n_in, ff, width), bf16),
        ],
    )
    sgu = sgu[:, :, :w_rows].reshape(width, 2 * hid_pad)
    ws = pad_to(ws[:, :, :d_rows].reshape(hid, width), 0, hid_pad)
    inputs = x_own.astype(f32)
    residual = inputs + jnp.sum(out_parts.astype(f32).reshape(2, n_in, seg, width), axis=1)

    normed_two, inverse_two, scaled_two = norm_rows(residual, gain_two)
    hidden_two = scaled_two.astype(bf16).reshape(rows, width)
    logits = nn(hidden_two, router_w)
    flat_routes = routes.transpose(1, 0, 2).reshape(rows, topk)
    chooser = (flat_routes[:, :, None] == jnp.arange(n_experts, dtype=jnp.int32)).astype(f32)
    taken = jnp.sum(chooser, axis=1)
    chosen = jnp.where(taken > 0, logits, masked_score)
    exponent = jnp.where(
        taken > 0, jnp.exp(chosen - jnp.max(chosen, axis=-1, keepdims=True)), 0.0
    )
    gates = exponent / jnp.sum(exponent, axis=-1, keepdims=True)
    before = (
        lax.broadcasted_iota(jnp.int32, (rows, rows), 0)
        < lax.broadcasted_iota(jnp.int32, (rows, rows), 1)
    ).astype(bf16)
    slots = jnp.where(taken.T > 0, nn(taken.T.astype(bf16), before), -1.0)
    meta = jnp.concatenate(
        [gates.T.reshape(n_out, n_in, rows), slots.reshape(n_out, n_in, rows)], axis=1
    )

    line = n_out == 4
    run = functools.partial(experts_line if line else experts_split, room, hid_pad, shards)
    dhs, dgs, mix_part, e_mine, es, gu_mine, gus, sd_grad = run(
        3 if line else (3, 4), hidden_two, meta, c_parts, e_gate, e_up, e_down, sgu, ws
    )
    dhs, mix_late = lax.optimization_barrier((dhs, mix_part))
    mixes = [mix_late[0]] + [
        shift(mix_late[n_out - d], ("outer", d)) for d in range(1, n_out)
    ]

    gu_half = (gu_mine.astype(f32) + gus.astype(f32)).astype(bf16)
    gu_half = pad_rows(gu_half.reshape(shards, w_rows, 2 * hid_pad), 1)
    sd_send = pad_rows(sd_grad[:hid].reshape(2 * n_in, d_rows, width), 1)

    grad_float = c_own.astype(f32)
    grad_gates = dgs[:, :n_in].reshape(n_experts, rows).T
    grad_logits = gates * (grad_gates - jnp.sum(gates * grad_gates, axis=-1, keepdims=True))
    router_grad = lax.dot_general(
        hidden_two.astype(f32),
        grad_logits,
        (((0,), (0,)), ((), ())),
        precision=lax.Precision.HIGHEST,
        preferred_element_type=f32,
    )
    grad_hidden_two = jnp.sum(dhs.astype(f32), axis=0) + lax.dot_general(
        grad_logits,
        router_w.astype(f32),
        (((1,), (1,)), ((), ())),
        precision=lax.Precision.HIGHEST,
        preferred_element_type=f32,
    )
    grad_norm_two, gain_two_grad = norm_back(
        grad_hidden_two.reshape(seqs, seg, width), normed_two, inverse_two, gain_two
    )
    grad_residual = grad_float + grad_norm_two
    grad_attn = grad_residual.astype(bf16)

    def spread_grad(wires, ins, outs):
        first = wires.exchange("plane", lambda r, d: ins[0].at[r // n_in], lambda r, d: outs[0].at[r])
        second = wires.exchange("chips", lambda r, d: ins[1].at[r], lambda r, d: outs[1].at[r])
        first()
        second()

    grad_all, gus = transfer(
        "spread_grad",
        5,
        shards,
        ["all"],
        shards + 2 * n_in,
        spread_grad,
        [grad_attn, gu_half],
        [((2 * n_in, seg, width), bf16), ((shards, w_pad, 2 * hid_pad), bf16)],
    )
    grad_all, es = lax.optimization_barrier((grad_all, es))

    e_halves = [(e_mine[d].astype(f32) + es[d].astype(f32)).astype(bf16) for d in range(n_in)]
    e_parts = [e_halves[0]] + [shift(e_halves[n_in - d], ("inner", d)) for d in range(1, n_in)]
    grad_all = grad_all.reshape(2 * chunk, width)
    grad_mixed = nt(grad_all, wo).astype(bf16)
    wo_grad = pad_rows(tn(mixed_low, grad_all).astype(bf16).reshape(half_chips, w_rows, width), 1)
    delta_rows = jnp.sum(
        (grad_mixed.astype(f32) * mixed).reshape(2, chunk, GROUP_MEMBERS, HEAD_SIZE), axis=-1
    ).transpose(2, 0, 1)

    dq, dkv_part = attend_back(chunk, n_out, qkv, kv_all, grad_mixed, log_rows, delta_rows)

    dkv_part, mixes = lax.optimization_barrier((dkv_part, mixes))
    total_out = residual + sum(mix.astype(f32) for mix in mixes).reshape(seqs, seg, width)

    def sum_kv(wires, ins, outs):
        core, chip, outer, inner = place()
        wo_part = ins[1].at[pl.ds((1 - core) * own_rows, own_rows)]
        waits = [
            wires.exchange("outer", lambda r, d: ins[0].at[r], lambda r, d: outs[0].at[r]),
            wires.sibling(wo_part, outs[1], outs[1]),
        ]
        for wait in waits:
            wait()

    kvs, wos = transfer(
        "sum_kv",
        6,
        shards,
        ["outer", "core"],
        n_out + 1,
        sum_kv,
        [dkv_part, wo_grad],
        [(kv_all.shape, bf16), ((own_rows, w_pad, width), bf16)],
    )
    wo_mine = lax.dynamic_slice_in_dim(wo_grad, core * own_rows, own_rows, 0)
    wo_half = (wo_mine.astype(f32) + wos.astype(f32)).astype(bf16)
    dkv = jnp.sum(kvs.astype(f32), axis=0)
    key_scale = jnp.concatenate(
        [jnp.full((HEAD_SIZE,), HEAD_SIZE**-0.5, f32), jnp.ones((HEAD_SIZE,), f32)]
    )
    dqkv = jnp.concatenate([dq, (dkv * key_scale).astype(bf16)], axis=1)
    dh1_part = nt(dqkv, wq).astype(bf16).reshape(2 * n_in, seg, width)
    wq_send = pad_rows(tn(h1, dqkv).astype(bf16).reshape(2 * shards, w_rows, cols), 1)
    e_sum = sum(part.astype(f32) for part in e_parts).astype(bf16)
    gain_one_grad = jnp.sum(
        dh1_part.reshape(2 * chunk, width).astype(f32) * normed_all, axis=0
    )
    small_grad = pad_to(
        jnp.concatenate([router_grad, gain_one_grad[:, None], gain_two_grad[:, None]], axis=1),
        1,
        small,
    )
    small_send = pad_rows(small_grad.astype(bf16).reshape(2 * shards, w_rows, small), 1)

    def sum_first(wires, ins, outs):
        dh_ref, wq_ref, small_ref, s_ref, o_ref, e_ref = ins
        dhs, wqs, smalls, sds, wos, es = outs
        waits = [
            wires.exchange("plane", lambda r, d: dh_ref.at[r], lambda r, d: dhs.at[r]),
            wires.exchange("all", lambda r, d: wq_ref.at[r], lambda r, d: wqs.at[r]),
            wires.exchange("all", lambda r, d: small_ref.at[r], lambda r, d: smalls.at[r]),
            wires.exchange("plane", lambda r, d: s_ref.at[r], lambda r, d: sds.at[r]),
            out_rows_back(wires, o_ref, wos),
            wires.sibling(e_ref, es, es),
        ]
        for wait in waits:
            wait()

    dh1s, wq_parts, small_parts, sds, wos, e_other = transfer(
        "sum_first",
        7,
        shards,
        ["all"],
        4 * n_in + 6 * shards + 16,
        sum_first,
        [dh1_part, wq_send, small_send, sd_send, wo_half, e_sum],
        [
            ((2 * n_in, seg, width), bf16),
            ((2 * shards, w_pad, cols), bf16),
            ((2 * shards, w_pad, small), bf16),
            ((2 * n_in, d_pad, width), bf16),
            ((n_out, w_pad, width), bf16),
            (e_sum.shape, bf16),
        ],
    )
    grad_hidden_one = jnp.sum(dh1s.astype(f32).reshape(2, n_in, seg, width), axis=1)
    normed_one, inverse_one, _ = norm_rows(inputs, gain_one)
    grad_norm_one = norm_back(grad_hidden_one, normed_one, inverse_one, gain_one)[0]
    tokens_grad = grad_residual + grad_norm_one

    wq_total = jnp.sum(
        wq_parts[:, :w_rows].astype(f32).reshape(2 * n_out, n_in, w_rows, cols), axis=0
    ).transpose(1, 0, 2)
    query_grad = wq_total[:, :, :q_cols].reshape(w_rows, n_in * q_cols)
    key_grad = wq_total[:, :, q_cols : q_cols + HEAD_SIZE].reshape(w_rows, n_in * HEAD_SIZE)
    value_grad = wq_total[:, :, q_cols + HEAD_SIZE :].reshape(w_rows, n_in * HEAD_SIZE)
    gu_total = jnp.sum(
        gus[:, :w_rows].astype(f32).reshape(n_out, n_in, w_rows, 2 * hid_pad), axis=1
    )

    def hidden_whole(piece):
        piece = piece[:, :, :hid].reshape(n_out, w_rows, 2, hid_core)
        return piece.transpose(1, 2, 0, 3).reshape(w_rows, n_out * hid)

    gate_w_grad = hidden_whole(gu_total[:, :, :hid_pad])
    up_w_grad = hidden_whole(gu_total[:, :, hid_pad:])
    down_w_grad = jnp.sum(sds[:, :d_rows].astype(f32), axis=0)
    out_w_grad = jnp.sum(wos[:, :w_rows].astype(f32), axis=0)
    small_total = jnp.sum(small_parts[:, :w_rows].astype(f32), axis=0)

    own, came = e_sum.astype(f32), e_other.astype(f32)
    e_total = jnp.concatenate(
        [jnp.where(core == 0, own, came), jnp.where(core == 0, came, own)], axis=0
    )

    return (
        total_out.astype(bf16).transpose(1, 0, 2),
        tokens_grad.transpose(1, 0, 2),
        small_total[:, n_experts],
        small_total[:, n_experts + 1],
        query_grad,
        key_grad,
        value_grad,
        out_w_grad,
        small_total[:, :n_experts],
        gate_w_grad,
        up_w_grad,
        down_w_grad,
        e_total[:, :ff][None],
        e_total[:, ff : 2 * ff][None],
        e_total[:, 2 * ff :].T[None],
    )


def solution(mesh):
    rows = P(("seq", "fsdp"), None, None)
    matrix = P(("seq", "fsdp"), None)
    vector = P(("seq", "fsdp"))
    expert = P("fsdp", None, None)
    return jax.shard_map(
        body,
        mesh=mesh,
        in_specs=(rows,) * 3 + (vector,) * 2 + (matrix,) * 8 + (expert,) * 3,
        out_specs=(rows,) * 2 + (vector,) * 2 + (matrix,) * 8 + (expert,) * 3,
        check_vma=False,
    )
```

```python
import functools
import math

import jax
import jax.numpy as jnp
from jax import lax
from jax.experimental import pallas as pl
from jax.experimental.pallas import tpu as pltpu
from jax.sharding import PartitionSpec as P

QUERY_HEADS = 12
KEY_VALUE_HEADS = 4
HEAD_SIZE = 128
GROUP_MEMBERS = QUERY_HEADS // KEY_VALUE_HEADS

epsilon = 1e-06
masked_score = -1e30
MESH = pl.DeviceIdType.MESH
VMEM_LIMIT = 63 * 1024 * 1024
f32 = jnp.float32
bf16 = jnp.bfloat16


def round_up(number, step):
    return -(-number // step) * step


def nn(left, right):
    return lax.dot_general(left, right, (((1,), (0,)), ((), ())), preferred_element_type=f32)


def nt(left, right):
    return lax.dot_general(left, right, (((1,), (1,)), ((), ())), preferred_element_type=f32)


def tn(left, right):
    return lax.dot_general(left, right, (((0,), (0,)), ((), ())), preferred_element_type=f32)


def across(inner, step):
    low = lax.rem(inner + step, 2)
    high = lax.rem(inner // 2 + step // 2, 2)
    return low + 2 * high


def place():
    core = lax.axis_index("seq")
    chip = lax.axis_index("fsdp")
    return core, chip, chip // KEY_VALUE_HEADS, lax.rem(chip, KEY_VALUE_HEADS)


def group(kind, shards):
    core, chip, outer, inner = place()
    if kind == "plane":
        size = 2 * KEY_VALUE_HEADS
        return (
            size,
            core * KEY_VALUE_HEADS + inner,
            lambda r: (r // KEY_VALUE_HEADS, outer * KEY_VALUE_HEADS + lax.rem(r, KEY_VALUE_HEADS)),
        )
    if kind == "inner":
        return KEY_VALUE_HEADS, inner, lambda r: (core, outer * KEY_VALUE_HEADS + r)
    if kind == "outer":
        return shards // KEY_VALUE_HEADS, outer, lambda r: (core, r * KEY_VALUE_HEADS + inner)
    if kind == "chips":
        return shards, chip, lambda r: (core, r)
    if kind == "all":
        return 2 * shards, core * shards + chip, lambda r: (r // shards, lax.rem(r, shards))
    return 2, core, lambda r: (r, chip)


def repeat(first, last, step):
    if last - first <= 16:
        for index in range(first, last):
            step(index)
    else:

        def one(index, carry):
            step(index)
            return carry

        lax.fori_loop(first, last, one, 0)


class Wires:
    def __init__(self, shards, send_sems, recv_sems, local_sems):
        self.shards = shards
        self.send_sems, self.recv_sems, self.local_sems = send_sems, recv_sems, local_sems
        self.used = 0
        self.leaving = []

    def greet(self, kinds):
        barrier = pltpu.get_barrier_semaphore()
        total = 0
        for kind in kinds:
            size, me, device = group(kind, self.shards)

            def signal(d, size=size, me=me, device=device):
                pl.semaphore_signal(
                    barrier, inc=1, device_id=device(lax.rem(me + d, size)), device_id_type=MESH
                )

            repeat(1, size, signal)
            total += size - 1
        pl.semaphore_wait(barrier, total)

    def take(self, count):
        base = self.used
        self.used += count
        return base

    def remote(self, source, target, index, device):
        return pltpu.make_async_remote_copy(
            src_ref=source,
            dst_ref=target,
            send_sem=self.send_sems.at[index],
            recv_sem=self.recv_sems.at[index],
            device_id=device,
            device_id_type=MESH,
        )

    def local(self, source, target, index):
        return pltpu.make_async_copy(source, target, self.local_sems.at[index])

    def exchange(self, kind, source_for, target_from, own=True):
        size, me, device = group(kind, self.shards)
        base = self.take(size)

        def copy(d):
            to = lax.rem(me + d, size)
            return self.remote(source_for(to, d), target_from(me, d), base + d, device(to))

        repeat(1, size, lambda d: copy(d).start())
        if own:
            self.local(source_for(me, 0), target_from(me, 0), base).start()
        self.leaving.append(lambda: repeat(1, size, lambda d: copy(d).wait_send()))

        def arrive(then=None):
            def one(d):
                came = lax.rem(me - d + size, size)
                place_of = target_from(came, d)
                self.remote(place_of, place_of, base + d, device(came)).wait_recv()
                if then is not None:
                    then(d)

            repeat(1, size, one)
            if own:
                self.local(source_for(me, 0), target_from(me, 0), base).wait()

        return arrive

    def sibling(self, source, target, comes):
        core, chip, _, _ = place()
        device = (1 - core, chip)
        index = self.take(1)
        copy = self.remote(source, target, index, device)
        copy.start()
        self.leaving.append(copy.wait_send)
        return self.remote(comes, comes, index, device).wait_recv

    def finish(self):
        for leave in self.leaving:
            leave()


def transfer(name, collective, shards, kinds, sems, body, operands, outs):
    count = len(operands)

    def kernel(*refs):
        ins, results = refs[:count], refs[count : count + len(outs)]
        wires = Wires(shards, *refs[count + len(outs) :])
        wires.greet(kinds)
        body(wires, ins, results)
        wires.finish()

    return pl.pallas_call(
        kernel,
        out_shape=[jax.ShapeDtypeStruct(shape, kind) for shape, kind in outs],
        in_specs=[pl.BlockSpec(memory_space=pl.ANY)] * count,
        out_specs=[pl.BlockSpec(memory_space=pl.ANY)] * len(outs),
        scratch_shapes=[pltpu.SemaphoreType.DMA((sems,))] * 3,
        compiler_params=pltpu.CompilerParams(collective_id=collective, has_side_effects=True),
        name=name,
    )(*operands)


def neighbours(wires, n, sources, targets, sends, comes):
    core, chip, outer, inner = place()
    base = wires.take(2)

    def copy(way):
        sign = (1, -1)[way]
        to = lax.rem(outer + sign + n, n)
        device = (core, to * KEY_VALUE_HEADS + inner)
        return wires.remote(sources[way], targets[way], base + way, device)

    def come(way):
        sign = (1, -1)[way]
        origin = lax.rem(outer - sign + n, n)
        device = (core, origin * KEY_VALUE_HEADS + inner)
        return wires.remote(targets[way], targets[way], base + way, device)

    def each(conditions, action):
        for way in range(2):
            pl.when(conditions[way])(lambda way=way: action(way))

    each(sends, lambda way: copy(way).start())
    wires.leaving.append(lambda: each(sends, lambda way: copy(way).wait_send()))
    return lambda: each(comes, lambda way: come(way).wait_recv())


def gather_step(wires, n, step, sources, targets):
    outer = place()[2]
    sends = ((outer >= step) & (outer < n - 1), (outer < n - step) & (outer > 0))
    comes = (outer > step, outer < n - 1 - step)
    return neighbours(wires, n, sources, targets, sends, comes)


def sum_step(wires, n, step, sources, targets):
    outer = place()[2]
    sends = (
        (outer <= step) & (outer < n - 1),
        (outer >= n - 1 - step) & (outer > 0),
    )
    comes = (
        (outer >= 1) & (outer <= step + 1),
        (outer <= n - 2) & (outer >= n - 2 - step),
    )
    return neighbours(wires, n, sources, targets, sends, comes)


def out_rows_back(wires, shards, grad_ref, sums_ref):
    core, chip, outer, inner = place()
    n_in, n_out, half_chips = KEY_VALUE_HEADS, shards // KEY_VALUE_HEADS, shards // 2
    own_rows = half_chips // 2
    rows = sums_ref.shape[1]
    from_inner = 2 * core + chip // half_chips
    from_core = lax.rem(chip, half_chips) // own_rows
    sends = wires.take(own_rows)
    base = wires.take(n_out)

    def copy(i):
        to = (inner // 2, half_chips * lax.rem(inner, 2) + core * own_rows + i)
        here = (to[0] == core) & (to[1] == chip)
        return here, pltpu.make_async_remote_copy(
            src_ref=grad_ref.at[pl.ds(i * rows, rows)],
            dst_ref=sums_ref.at[outer],
            send_sem=wires.send_sems.at[sends + i],
            recv_sem=wires.recv_sems.at[base + outer],
            device_id=to,
            device_id_type=MESH,
        )

    def start(i):
        here, send = copy(i)
        pl.when(jnp.logical_not(here))(send.start)
        pl.when(here)(lambda: wires.local(grad_ref.at[pl.ds(i * rows, rows)], sums_ref.at[outer], base).start())

    def leave(i):
        here, send = copy(i)
        pl.when(jnp.logical_not(here))(send.wait_send)

    def come(k):
        origin = (from_core, k * n_in + from_inner)
        here = (origin[0] == core) & (origin[1] == chip)
        place_of = sums_ref.at[k]
        pl.when(jnp.logical_not(here))(
            wires.remote(place_of, place_of, base + k, origin).wait_recv
        )
        pl.when(here)(lambda: wires.local(place_of, place_of, base).wait())

    repeat(0, own_rows, start)
    wires.leaving.append(lambda: repeat(0, own_rows, leave))
    return lambda: repeat(0, n_out, come)


class Line:
    def __init__(self, wires, source, every):
        self.wires, self.source, self.every = wires, source, every
        self.n = every.shape[0]
        self.core, _, self.outer, self.inner = place()
        self.bases = {1: wires.take(self.n), -1: wires.take(self.n)}

    def device(self, at):
        return self.core, at * KEY_VALUE_HEADS + self.inner

    def order(self):
        low = self.outer < self.n // 2
        return [
            lax.rem(jnp.where(low, self.outer + k, self.outer - k + self.n), self.n)
            for k in range(self.n)
        ]

    def hop(self, step, sign):
        to = lax.rem(self.outer + sign + self.n, self.n)
        block = lax.rem(self.outer - sign * step + 2 * self.n, self.n)
        source = self.source if step == 0 else self.every.at[block]
        index = self.bases[sign] + step
        return self.wires.remote(source, self.every.at[block], index, self.device(to))

    def sends(self, step, sign):
        to, block = self.outer + sign, self.outer - sign * step
        return (to >= 0) & (to < self.n) & (block >= 0) & (block < self.n)

    def start(self, step):
        for sign in (1, -1):
            pl.when(self.sends(step, sign))(lambda sign=sign: self.hop(step, sign).start())

    def arrive(self, step):
        for sign in (1, -1):
            come = self.outer - sign * (step + 1)

            def wait(sign=sign, come=come):
                block = self.every.at[lax.rem(come + self.n, self.n)]
                to = lax.rem(self.outer - sign + self.n, self.n)
                index = self.bases[sign] + step
                self.wires.remote(block, block, index, self.device(to)).wait_recv()

            pl.when((come >= 0) & (come < self.n))(wait)

    def leave(self):
        for step in range(self.n - 1):
            for sign in (1, -1):
                pl.when(self.sends(step, sign))(
                    lambda step=step, sign=sign: self.hop(step, sign).wait_send()
                )


def far_first(outer, n):
    low = outer < n // 2
    order = []
    for k in range(n - 1):
        down = n - 1 - k
        order.append(
            jnp.where(low, jnp.where(down <= outer, down - 1, down), jnp.where(k >= outer, k + 1, k))
        )
    return order


def causal(scores):
    key_at = lax.broadcasted_iota(jnp.int32, scores.shape, 0)
    query_at = lax.broadcasted_iota(jnp.int32, scores.shape, 1)
    return jnp.where(key_at <= query_at, scores, masked_score)


def each_pair(block, outer, own, pair):
    def some(head, carry):
        if own:
            pair(head, 0, block, 0, True)
            pair(head, 1, block, 0, False)
            pair(head, 1, block, 1, True)
        else:
            pair(head, 1, block, 0, False)

            @pl.when(block < outer)
            def _():
                pair(head, 0, block, 0, False)
                pair(head, 1, block, 1, False)

        return carry

    lax.fori_loop(0, GROUP_MEMBERS, some, 0)


def attend_kernel(shards, chunk, passing, *refs):
    q_ref, kv_ref, *refs = refs
    pass_from, refs = refs[:passing], refs[passing:]
    mixed_ref, log_ref, kv_out, *refs = refs
    pass_to, refs = refs[:passing], refs[passing:]
    kv_all, largest, total, summed, send_sems, recv_sems, local_sems = refs
    wires = Wires(shards, send_sems, recv_sems, local_sems)
    factor = HEAD_SIZE**-0.5 * math.log2(math.e)
    line = Line(wires, kv_ref, kv_all)
    outer = line.outer
    own = wires.local(kv_ref, kv_all.at[outer], wires.take(1))
    own.start()
    wires.greet(["outer"])
    line.start(0)
    passed = gather_step(wires, line.n, 1, pass_from, pass_to) if passing else None
    largest[...] = jnp.full_like(largest, masked_score)
    total[...] = jnp.zeros_like(total)
    summed[...] = jnp.zeros_like(summed)

    def pair(head, half, block, key_half, masked):
        cols = pl.ds(pl.multiple_of(head * HEAD_SIZE, HEAD_SIZE), HEAD_SIZE)
        rows = pl.ds(key_half * chunk, chunk)
        query = q_ref[pl.ds(half * chunk, chunk), cols]
        scores = nt(kv_all[block, rows, 0:HEAD_SIZE], query)
        if masked:
            scores = causal(scores)
        before = largest[head, half]
        new = jnp.maximum(before, jnp.max(scores, axis=0, keepdims=True))
        weights = jnp.exp2((scores - new) * factor)
        shrink = jnp.exp2((before - new) * factor)
        largest[head, half] = new
        total[head, half] = total[head, half] * shrink + jnp.sum(weights, axis=0, keepdims=True)
        summed[head, half] = summed[head, half] * shrink + tn(
            kv_all[block, rows, HEAD_SIZE : 2 * HEAD_SIZE], weights.astype(bf16)
        )

    for k, block in enumerate(line.order()):
        if k == 0:
            own.wait()
        else:
            line.arrive(k - 1)
            if k < line.n - 1:
                line.start(k)
        each_pair(block, outer, k == 0, pair)
    keep = wires.local(kv_all, kv_out, wires.take(1))
    keep.start()
    for head in range(GROUP_MEMBERS):
        for half in range(2):
            mixed_ref[
                half * chunk : (half + 1) * chunk, head * HEAD_SIZE : (head + 1) * HEAD_SIZE
            ] = (summed[head, half] / total[head, half]).T
            log_ref[head, half : half + 1, :] = largest[head, half] * factor + jnp.log2(
                total[head, half]
            )
    line.leave()
    if passing:
        passed()
    wires.finish()
    keep.wait()


def attend(collective, shards, chunk, q, kv, passing):
    n_out = shards // KEY_VALUE_HEADS
    rows = 2 * chunk
    kv_shape = (n_out,) + kv.shape
    vmem = pl.BlockSpec(memory_space=pltpu.VMEM)
    hbm = pl.BlockSpec(memory_space=pl.ANY)
    state = (GROUP_MEMBERS, 2, 1, chunk)
    return pl.pallas_call(
        functools.partial(attend_kernel, shards, chunk, len(passing)),
        in_specs=[vmem, hbm] + [hbm] * len(passing),
        out_specs=[vmem, vmem, hbm] + [hbm] * len(passing),
        out_shape=[
            jax.ShapeDtypeStruct((rows, GROUP_MEMBERS * HEAD_SIZE), f32),
            jax.ShapeDtypeStruct((GROUP_MEMBERS, 2, chunk), f32),
            jax.ShapeDtypeStruct(kv_shape, bf16),
        ]
        + [jax.ShapeDtypeStruct(block.shape, block.dtype) for block in passing],
        scratch_shapes=[
            pltpu.VMEM(kv_shape, bf16),
            pltpu.VMEM(state, f32),
            pltpu.VMEM(state, f32),
            pltpu.VMEM((GROUP_MEMBERS, 2, HEAD_SIZE, chunk), f32),
        ]
        + [pltpu.SemaphoreType.DMA((2 * n_out + 8,))] * 3,
        compiler_params=pltpu.CompilerParams(
            collective_id=collective, has_side_effects=True, vmem_limit_bytes=VMEM_LIMIT
        ),
        name="attend",
    )(q, kv, *passing)


def attend_back_kernel(shards, chunk, own_rows, *refs):
    q_ref, kv_ref, grad_ref, log_ref, delta_ref, wo_ref, *refs = refs
    dqkv_ref, wo_other, *refs = refs
    came, stage, sums, dq_sums, send_sems, recv_sems, local_sems = refs
    wires = Wires(shards, send_sems, recv_sems, local_sems)
    core, chip, outer, inner = place()
    n = kv_ref.shape[0]
    scale = HEAD_SIZE**-0.5
    factor = scale * math.log2(math.e)
    wires.greet(["outer", "core"])
    wo_in = wires.sibling(
        wo_ref.at[pl.ds((1 - core) * own_rows, own_rows)], wo_other, wo_other
    )
    send_base, recv_base = wires.take(n), wires.take(n)
    dq_sums[...] = jnp.zeros_like(dq_sums)

    def pair(head, half, block, key_half, masked):
        cols = pl.ds(pl.multiple_of(head * HEAD_SIZE, HEAD_SIZE), HEAD_SIZE)
        mine, rows = pl.ds(half * chunk, chunk), pl.ds(key_half * chunk, chunk)
        query, grad = q_ref[mine, cols], grad_ref[mine, cols]
        key = kv_ref[block, rows, 0:HEAD_SIZE]
        value = kv_ref[block, rows, HEAD_SIZE : 2 * HEAD_SIZE]
        scores = nt(key, query)
        if masked:
            scores = causal(scores)
        weights = jnp.exp2(scores * factor - log_ref[head, half : half + 1, :])
        grad_scores = (
            weights * (nt(value, grad) - delta_ref[head, half : half + 1, :])
        ).astype(bf16)
        sums[rows, 0:HEAD_SIZE] += nn(grad_scores, query)
        sums[rows, HEAD_SIZE : 2 * HEAD_SIZE] += nn(weights.astype(bf16), grad)
        dq_sums[mine, cols] += tn(grad_scores, key)

    def send(k, block):
        return pltpu.make_async_remote_copy(
            src_ref=stage.at[k],
            dst_ref=came.at[outer],
            send_sem=send_sems.at[send_base + k],
            recv_sem=recv_sems.at[recv_base + outer],
            device_id=(core, block * KEY_VALUE_HEADS + inner),
            device_id_type=MESH,
        )

    order = far_first(outer, n)
    for k, block in enumerate(order + [outer]):
        sums[...] = jnp.zeros_like(sums)
        each_pair(block, outer, k == n - 1, pair)
        if k < n - 1:
            stage[k] = sums[...].astype(bf16)
            send(k, block).start()
    width = GROUP_MEMBERS * HEAD_SIZE
    dqkv_ref[:, 0:width] = (dq_sums[...] * scale).astype(bf16)
    for d in range(1, n):
        origin = lax.rem(outer + d, n)
        pltpu.make_async_remote_copy(
            src_ref=came.at[origin],
            dst_ref=came.at[origin],
            send_sem=send_sems.at[send_base],
            recv_sem=recv_sems.at[recv_base + origin],
            device_id=(core, origin * KEY_VALUE_HEADS + inner),
            device_id_type=MESH,
        ).wait_recv()
        sums[...] += came[origin].astype(f32)
    dqkv_ref[:, width : width + HEAD_SIZE] = (sums[:, 0:HEAD_SIZE] * scale).astype(bf16)
    dqkv_ref[:, width + HEAD_SIZE :] = sums[:, HEAD_SIZE:].astype(bf16)
    for k, block in enumerate(order):
        send(k, block).wait_send()
    wo_in()
    wires.finish()


def attend_back(collective, shards, chunk, q, kv_all, grad_mixed, log_rows, delta_rows, wo_grad):
    n_out, rows, kv_cols = kv_all.shape
    own_rows = wo_grad.shape[0] // 2
    vmem = pl.BlockSpec(memory_space=pltpu.VMEM)
    hbm = pl.BlockSpec(memory_space=pl.ANY)
    width = GROUP_MEMBERS * HEAD_SIZE
    return pl.pallas_call(
        functools.partial(attend_back_kernel, shards, chunk, own_rows),
        in_specs=[vmem] * 5 + [hbm],
        out_specs=[vmem, hbm],
        out_shape=[
            jax.ShapeDtypeStruct((rows, width + kv_cols), bf16),
            jax.ShapeDtypeStruct((own_rows,) + wo_grad.shape[1:], bf16),
        ],
        scratch_shapes=[
            pltpu.VMEM(kv_all.shape, bf16),
            pltpu.VMEM(kv_all.shape, bf16),
            pltpu.VMEM((rows, kv_cols), f32),
            pltpu.VMEM((rows, width), f32),
        ]
        + [pltpu.SemaphoreType.DMA((2 * n_out + 8,))] * 3,
        compiler_params=pltpu.CompilerParams(
            collective_id=collective, has_side_effects=True, vmem_limit_bytes=VMEM_LIMIT
        ),
        name="attend_back",
    )(q, kv_all, grad_mixed, log_rows, delta_rows, wo_grad)


def finish_kernel(shards, chunk, gain_col, *refs):
    (
        q_ref,
        kv_ref,
        grad_ref,
        wo_ref,
        mixed_ref,
        log_ref,
        h1_ref,
        wq_ref,
        gain_ref,
        small_ref,
        sd_ref,
        mix_ref,
        mix_up,
        mix_down,
        dh1_out,
        wq_out,
        small_out,
        wo_out,
        sd_out,
        mix_up_out,
        mix_down_out,
        dmixed,
        delta,
        came,
        stage,
        sums,
        dq_sums,
        dqkv,
        dwo,
        wo_came,
        wo_half,
        wo_recv,
        dwq,
        wq_came,
        wq_half,
        wq_recv,
        small_all,
        small_came,
        small_half,
        small_recv,
        dh_stage,
        dh_recv,
        sd_recv,
        mix_came,
        mix_term,
        send_sems,
        recv_sems,
        local_sems,
    ) = refs
    wires = Wires(shards, send_sems, recv_sems, local_sems)
    core, chip, outer, inner = place()
    n = kv_ref.shape[0]
    scale = HEAD_SIZE**-0.5
    factor = scale * math.log2(math.e)
    width = GROUP_MEMBERS * HEAD_SIZE
    wide = h1_ref.shape[1]
    half_wide = wide // 2
    w_rows = wq_recv.shape[1]
    seg = dh_recv.shape[1]
    mine, other = pl.ds(core * half_wide, half_wide), pl.ds((1 - core) * half_wide, half_wide)
    wires.greet(["all"])
    mix_first = sum_step(
        wires, n, 1, [mix_up, mix_down], [mix_came.at[0], mix_came.at[1]]
    )
    mix_own = [
        wires.local(mix_ref.at[slot], mix_term.at[way], wires.take(1))
        for way, slot in enumerate((3 % n, (n - 3) % n))
    ]
    for copy in mix_own:
        copy.start()
    sd_in = wires.exchange("plane", lambda r, d: sd_ref.at[r], lambda r, d: sd_recv.at[r])

    for half in range(2):
        rows = pl.ds(half * chunk, chunk)
        part = nt(grad_ref[rows, :], wo_ref[...]).astype(bf16)
        dmixed[rows, :] = part
        weighted = part.astype(f32) * mixed_ref[rows, :]
        for head in range(GROUP_MEMBERS):
            cols = slice(head * HEAD_SIZE, (head + 1) * HEAD_SIZE)
            delta[head, half] = jnp.sum(weighted[:, cols].T, axis=0, keepdims=True)

    send_base, recv_base = wires.take(n), wires.take(n)
    dq_sums[...] = jnp.zeros_like(dq_sums)

    def pair(head, half, block, key_half, masked):
        cols = pl.ds(pl.multiple_of(head * HEAD_SIZE, HEAD_SIZE), HEAD_SIZE)
        here, rows = pl.ds(half * chunk, chunk), pl.ds(key_half * chunk, chunk)
        query, grad = q_ref[here, cols], dmixed[here, cols]
        key = kv_ref[block, rows, 0:HEAD_SIZE]
        value = kv_ref[block, rows, HEAD_SIZE : 2 * HEAD_SIZE]
        scores = nt(key, query)
        if masked:
            scores = causal(scores)
        weights = jnp.exp2(scores * factor - log_ref[head, half : half + 1, :])
        grad_scores = (weights * (nt(value, grad) - delta[head, half])).astype(bf16)
        sums[rows, 0:HEAD_SIZE] += nn(grad_scores, query)
        sums[rows, HEAD_SIZE : 2 * HEAD_SIZE] += nn(weights.astype(bf16), grad)
        dq_sums[here, cols] += tn(grad_scores, key)

    def send(k, block):
        return pltpu.make_async_remote_copy(
            src_ref=stage.at[k],
            dst_ref=came.at[outer],
            send_sem=send_sems.at[send_base + k],
            recv_sem=recv_sems.at[recv_base + outer],
            device_id=(core, block * KEY_VALUE_HEADS + inner),
            device_id_type=MESH,
        )

    order = far_first(outer, n)
    for k, block in enumerate(order + [outer]):
        sums[...] = jnp.zeros_like(sums)
        each_pair(block, outer, k == n - 1, pair)
        if k < n - 1:
            stage[k] = sums[...].astype(bf16)
            send(k, block).start()

    dqkv[:, 0:width] = (dq_sums[...] * scale).astype(bf16)
    dwo[...] = tn(mixed_ref[...].astype(bf16), grad_ref[...]).astype(bf16)
    wo_rows = wo_half.shape[0]
    wo_in = wires.sibling(dwo.at[pl.ds((1 - core) * wo_rows, wo_rows)], wo_came, wo_came)
    dwq[:, 0:width] = tn(h1_ref[...], dqkv[:, 0:width]).astype(bf16)
    q_cols = pl.ds(0, width)
    q_in = wires.sibling(dwq.at[other, q_cols], wq_came.at[:, q_cols], wq_came.at[:, q_cols])
    wo_in()
    wo_half[...] = (
        dwo[pl.ds(core * wo_rows, wo_rows), :].astype(f32) + wo_came[...].astype(f32)
    ).astype(bf16)
    wo_parts = out_rows_back(wires, shards, wo_half, wo_recv)
    q_in()
    wq_half[:, 0:width] = (
        dwq[mine, 0:width].astype(f32) + wq_came[:, 0:width].astype(f32)
    ).astype(bf16)

    def pieces(cols):
        return wires.exchange(
            "chips",
            lambda r, d: wq_half.at[pl.ds(r * w_rows, w_rows), cols],
            lambda r, d: wq_recv.at[r, :, cols],
        )

    q_parts = pieces(q_cols)

    for d in range(1, n):
        origin = lax.rem(outer + d, n)
        pltpu.make_async_remote_copy(
            src_ref=came.at[origin],
            dst_ref=came.at[origin],
            send_sem=send_sems.at[send_base],
            recv_sem=recv_sems.at[recv_base + origin],
            device_id=(core, origin * KEY_VALUE_HEADS + inner),
            device_id_type=MESH,
        ).wait_recv()
        sums[...] += came[origin].astype(f32)
    dqkv[:, width : width + HEAD_SIZE] = (sums[:, 0:HEAD_SIZE] * scale).astype(bf16)
    dqkv[:, width + HEAD_SIZE :] = sums[:, HEAD_SIZE:].astype(bf16)

    gain_sum = jnp.zeros((1, wide), f32)
    for half in range(2):
        rows = pl.ds(half * chunk, chunk)
        part = nt(dqkv[rows, :], wq_ref[...]).astype(bf16)
        dh_stage[rows, :] = part
        gain_sum = gain_sum + jnp.sum(
            part.astype(f32) * h1_ref[rows, :].astype(f32), axis=0, keepdims=True
        )
    dh_in = wires.exchange(
        "plane", lambda r, d: dh_stage.at[pl.ds(r * seg, seg)], lambda r, d: dh_recv.at[r]
    )
    dwq[:, width:] = tn(h1_ref[...], dqkv[:, width:]).astype(bf16)
    kv_cols = pl.ds(width, 2 * HEAD_SIZE)
    kv_in = wires.sibling(dwq.at[other, kv_cols], wq_came.at[:, kv_cols], wq_came.at[:, kv_cols])
    column = (gain_sum / gain_ref[...])
    columns = jnp.broadcast_to(column, (small_all.shape[1], wide)).T
    at_col = lax.broadcasted_iota(jnp.int32, columns.shape, 1)
    small_all[...] = jnp.where(at_col == gain_col, columns, small_ref[...].astype(f32)).astype(bf16)
    small_in = wires.sibling(small_all.at[other], small_came, small_came)
    kv_in()
    wq_half[:, width:] = (
        dwq[mine, width:].astype(f32) + wq_came[:, width:].astype(f32)
    ).astype(bf16)
    kv_parts = pieces(kv_cols)
    small_in()
    small_half[...] = (small_all[mine, :].astype(f32) + small_came[...].astype(f32)).astype(bf16)
    small_parts = wires.exchange(
        "chips",
        lambda r, d: small_half.at[pl.ds(r * w_rows, w_rows)],
        lambda r, d: small_recv.at[r],
    )
    mix_first()
    for way, copy in enumerate(mix_own):
        copy.wait()
        inside = (outer > 0, outer < n - 1)[way]
        mix_term[way] = (
            mix_term[way].astype(f32) + jnp.where(inside, mix_came[way].astype(f32), 0.0)
        ).astype(bf16)
    mix_last = sum_step(
        wires, n, 2, [mix_term.at[0], mix_term.at[1]], [mix_up_out, mix_down_out]
    )

    sd_in()
    sd_out[...] = jnp.sum(sd_recv[...].astype(f32), axis=0)
    wo_parts()
    wo_out[...] = jnp.sum(wo_recv[...].astype(f32), axis=0)
    q_parts()
    kv_parts()
    for j in range(KEY_VALUE_HEADS):
        total = wq_recv[j].astype(f32)
        for k in range(1, n):
            total = total + wq_recv[k * KEY_VALUE_HEADS + j].astype(f32)
        wq_out[j] = total
    small_parts()
    small_out[...] = jnp.sum(small_recv[...].astype(f32), axis=0)
    dh_in()
    for core_half in range(2):
        total = dh_recv[core_half * KEY_VALUE_HEADS].astype(f32)
        for j in range(1, KEY_VALUE_HEADS):
            total = total + dh_recv[core_half * KEY_VALUE_HEADS + j].astype(f32)
        dh1_out[core_half] = total
    mix_last()
    for k, block in enumerate(order):
        send(k, block).wait_send()
    wires.finish()


def finish(
    collective,
    shards,
    chunk,
    gain_col,
    q,
    kv_all,
    grad_all,
    wo,
    mixed,
    log_rows,
    h1,
    wq,
    gain_row,
    small_grad,
    sd_send,
    mix_part,
    mix_terms,
):
    n, rows, kv_cols = kv_all.shape
    width, wide = wo.shape
    cols = wq.shape[1]
    small = small_grad.shape[1]
    n_in = KEY_VALUE_HEADS
    seg = rows // (2 * n_in)
    w_rows = wide // (2 * shards)
    d_rows = sd_send.shape[1]
    block = mix_part.shape[1:]
    vmem = pl.BlockSpec(memory_space=pltpu.VMEM)
    hbm = pl.BlockSpec(memory_space=pl.ANY)

    def array(shape, kind=bf16):
        return jax.ShapeDtypeStruct(shape, kind)

    scratch = [
        ((rows, width), bf16),
        ((GROUP_MEMBERS, 2, 1, chunk), f32),
        (kv_all.shape, bf16),
        (kv_all.shape, bf16),
        ((rows, kv_cols), f32),
        ((rows, width), f32),
        ((rows, cols), bf16),
        ((width, wide), bf16),
        ((width // 2, wide), bf16),
        ((width // 2, wide), bf16),
        ((n, w_rows, wide), bf16),
        ((wide, cols), bf16),
        ((wide // 2, cols), bf16),
        ((wide // 2, cols), bf16),
        ((shards, w_rows, cols), bf16),
        ((wide, small), bf16),
        ((wide // 2, small), bf16),
        ((wide // 2, small), bf16),
        ((shards, w_rows, small), bf16),
        ((rows, wide), bf16),
        ((2 * n_in, seg, wide), bf16),
        ((2 * n_in, d_rows, wide), bf16),
        ((2,) + block, bf16),
        ((2,) + block, bf16),
    ]
    return pl.pallas_call(
        functools.partial(finish_kernel, shards, chunk, gain_col),
        in_specs=[vmem] * 10 + [hbm] * 4,
        out_specs=[vmem] * 5 + [hbm] * 2,
        out_shape=[
            array((2, seg, wide), f32),
            array((n_in, w_rows, cols), f32),
            array((w_rows, small), f32),
            array((w_rows, wide), f32),
            array((d_rows, wide), f32),
            array(block),
            array(block),
        ],
        scratch_shapes=[pltpu.VMEM(shape, kind) for shape, kind in scratch]
        + [pltpu.SemaphoreType.DMA((6 * shards + 64,))] * 3,
        compiler_params=pltpu.CompilerParams(
            collective_id=collective, has_side_effects=True, vmem_limit_bytes=VMEM_LIMIT
        ),
        name="finish",
    )(
        q,
        kv_all,
        grad_all,
        wo,
        mixed,
        log_rows,
        h1,
        wq,
        gain_row,
        small_grad,
        sd_send,
        mix_part,
        *mix_terms,
    )


def swiglu_parts(gate_part, up_part):
    sigmoid = jax.nn.sigmoid(gate_part)
    active = gate_part * sigmoid
    slope = up_part * sigmoid * (1.0 + gate_part * (1.0 - sigmoid))
    return active * up_part, active, slope


def experts_kernel(
    room,
    hidden,
    h_ref,
    c_ref,
    meta_ref,
    wg_ref,
    wu_ref,
    wd_ref,
    sgu_ref,
    sd_ref,
    out_ref,
    dh_ref,
    dgate_ref,
    dw_ref,
    dsgu_ref,
    dsd_ref,
    sum_out,
    sum_dh,
    h_rows,
    c_rows,
    picks,
    gate_col,
):
    expert = pl.program_id(0)
    inner = lax.rem(lax.axis_index("fsdp"), KEY_VALUE_HEADS)
    at = across(inner, expert)
    blocks, rows, width = h_ref.shape

    @pl.when(expert == 0)
    def _():
        dgate_ref[...] = jnp.zeros_like(dgate_ref)
        hid = h_ref[...].reshape(blocks * rows, width)
        cot = c_ref[...].reshape(blocks * rows, width)
        gate_w, up_w, down_w = sgu_ref[:, 0:hidden], sgu_ref[:, hidden : 2 * hidden], sd_ref[...]
        both, active, slope = swiglu_parts(nn(hid, gate_w), nn(hid, up_w))
        act = both.astype(bf16)
        d_act = nt(cot, down_w)
        d_gate = (d_act * slope).astype(bf16)
        d_up = (d_act * active).astype(bf16)
        sum_out[...] = nn(act, down_w)
        sum_dh[...] = nt(d_gate, gate_w) + nt(d_up, up_w)
        dsgu_ref[:, 0:hidden] = tn(hid, d_gate).astype(bf16)
        dsgu_ref[:, hidden : 2 * hidden] = tn(hid, d_up).astype(bf16)
        dsd_ref[...] = tn(act, cot).astype(bf16)

    slots = lax.broadcasted_iota(jnp.int32, (room, rows), 0).astype(f32)
    for block in range(blocks):
        part = pl.ds(block * room, room)
        gate_row = meta_ref[block, pl.ds(at, 1), :]
        slot_row = meta_ref[block, pl.ds(at + KEY_VALUE_HEADS, 1), :]
        pick = (slots == slot_row).astype(f32)
        gate_col[part, :] = jnp.broadcast_to(
            jnp.sum(pick * gate_row, axis=1, keepdims=True), (room, gate_col.shape[1])
        )
        pick = pick.astype(bf16)
        picks[block] = pick
        h_rows[part, :] = nn(pick, h_ref[block]).astype(bf16)
        c_rows[part, :] = nn(pick, c_ref[block]).astype(bf16)
    gate = gate_col[:, 0:1]
    gate_w, up_w, down_w = wg_ref[0], wu_ref[0], wd_ref[0]
    both, active, slope = swiglu_parts(nn(h_rows[...], gate_w), nn(h_rows[...], up_w))
    act = both.astype(bf16)
    d_act = nt(c_rows[...], down_w)
    d_gates = jnp.sum(d_act * act.astype(f32), axis=1, keepdims=True)
    d_act = d_act * gate
    act = (act.astype(f32) * gate).astype(bf16)
    d_gate = (d_act * slope).astype(bf16)
    d_up = (d_act * active).astype(bf16)
    ff = act.shape[1]
    dw_ref[0, :, 0:ff] = tn(h_rows[...], d_gate).astype(bf16)
    dw_ref[0, :, ff : 2 * ff] = tn(h_rows[...], d_up).astype(bf16)
    dw_ref[0, :, 2 * ff : 3 * ff] = tn(c_rows[...], act).astype(bf16)
    result = nn(act, down_w).astype(bf16)
    d_rows = (nt(d_gate, gate_w) + nt(d_up, up_w)).astype(bf16)
    for block in range(blocks):
        pick = picks[block]
        part = slice(block * room, (block + 1) * room)
        here = pl.ds(block * rows, rows)
        sum_out[here, :] += tn(pick, result[part])
        sum_dh[here, :] += tn(pick, d_rows[part])
        dgate_ref[block, pl.ds(at, 1), :] = jnp.sum(
            pick.astype(f32) * d_gates[part], axis=0, keepdims=True
        )

    @pl.when(expert == pl.num_programs(0) - 1)
    def _():
        out_ref[...] = sum_out[...].astype(bf16).reshape(out_ref.shape)
        dh_ref[...] = sum_dh[...].astype(bf16).reshape(dh_ref.shape)


def experts(room, hidden, h_all, c_all, meta, wg, wu, wd, sgu, sd):
    blocks, rows, width = h_all.shape
    n_experts, _, inner = wg.shape

    def once(shape):
        return pl.BlockSpec(shape, lambda e: (0,) * len(shape), pipeline_mode=pl.Buffered(1))

    def each(shape, **kind):
        return pl.BlockSpec((1,) + shape[1:], lambda e: (e, 0, 0), **kind)

    single = dict(pipeline_mode=pl.Buffered(1))
    return pl.pallas_call(
        functools.partial(experts_kernel, room, hidden),
        grid=(n_experts,),
        in_specs=[
            once(h_all.shape),
            once(c_all.shape),
            once(meta.shape),
            each(wg.shape),
            each(wu.shape),
            each(wd.shape),
            once(sgu.shape),
            once(sd.shape),
        ],
        out_specs=[
            once(h_all.shape),
            once(h_all.shape),
            once(meta.shape),
            pl.BlockSpec((1, width, 3 * inner), lambda e: (e, 0, 0), **single),
            once(sgu.shape),
            once(sd.shape),
        ],
        out_shape=[
            jax.ShapeDtypeStruct(h_all.shape, bf16),
            jax.ShapeDtypeStruct(h_all.shape, bf16),
            jax.ShapeDtypeStruct(meta.shape, f32),
            jax.ShapeDtypeStruct((n_experts, width, 3 * inner), bf16),
            jax.ShapeDtypeStruct(sgu.shape, bf16),
            jax.ShapeDtypeStruct(sd.shape, bf16),
        ],
        scratch_shapes=[
            pltpu.VMEM((blocks * rows, width), f32),
            pltpu.VMEM((blocks * rows, width), f32),
            pltpu.VMEM((blocks * room, width), bf16),
            pltpu.VMEM((blocks * room, width), bf16),
            pltpu.VMEM((blocks, room, rows), bf16),
            pltpu.VMEM((blocks * room, 128), f32),
        ],
        compiler_params=pltpu.CompilerParams(vmem_limit_bytes=VMEM_LIMIT),
        name="experts",
    )(h_all, c_all, meta, wg, wu, wd, sgu, sd)


def experts_line_kernel(room, hidden, shards, refs):
    n = shards // KEY_VALUE_HEADS
    h_ref, meta_ref = refs[:2]
    c_refs = refs[2 : 1 + 2 * n]
    (
        wg_ref,
        wu_ref,
        wd_ref,
        side_x,
        side_y,
        cross_a,
        cross_b,
        sgu_ref,
        sd_ref,
        dh_out,
        dgate_out,
        mix_out,
        e_mine,
        e_other,
        gu_mine,
        gu_other,
        dsd_ref,
        h_all,
        c_all,
        metas,
        wgu,
        wd,
        picks,
        kept_gu,
        kept_act,
        kept_shared,
        row_a,
        row_b,
        dh_stage,
        mix_stage,
        dg_stage,
        down_stage,
        gu_stage,
        send_sems,
        recv_sems,
        local_sems,
    ) = refs[1 + 2 * n :]
    wires = Wires(shards, send_sems, recv_sems, local_sems)
    core, chip, outer, inner = place()
    rows, width = h_ref.shape
    ff = wd.shape[1]
    experts_here = KEY_VALUE_HEADS

    own_h = wires.local(h_ref, h_all.at[outer], wires.take(1))
    own_meta = wires.local(meta_ref.at[outer], metas.at[outer], wires.take(1))
    own_h.start()
    own_meta.start()
    c_own = wires.local(c_refs[0], c_all.at[outer], wires.take(1))
    c_base = wires.take(2 * n - 2)

    def c_each(action):
        for k in range(2 * n - 2):
            block = outer - 1 - k if k < n - 1 else outer + 1 + k - (n - 1)

            def one(k=k, block=block):
                at = lax.rem(block + n, n)
                action(wires.local(c_refs[1 + k], c_all.at[at], c_base + k))

            pl.when((block >= 0) & (block < n))(one)

    deep, tall = ff // 2, width // 2
    own_weights = (
        wires.local(wg_ref.at[0], wgu.at[0, :, pl.ds(0, ff)], wires.take(1)),
        wires.local(wu_ref.at[0], wgu.at[0, :, pl.ds(ff, ff)], wires.take(1)),
        wires.local(wd_ref.at[0], wd.at[0], wires.take(1)),
    )

    def half_pieces(e, source, first_col, of_core):
        cols = source.shape[1]
        found = [
            (
                source.at[pl.ds(k * tall, tall)],
                wgu.at[e, pl.ds(of_core * tall, tall), pl.ds(k * ff + first_col, cols)],
            )
            for k in range(2)
        ]
        found += [
            (
                source.at[pl.ds(2 * tall + k * deep, deep)],
                wd.at[e, pl.ds(of_core * deep, deep), pl.ds(k * ff + first_col, cols)],
            )
            for k in range(width // ff)
        ]
        return found

    sides = ((1, side_x, 0), (2, side_y, 0), (3, cross_a, 0), (3, cross_b, ff // 2))
    half_sems = [wires.take(2 + width // ff) for _ in sides]

    def half_local(which):
        e, source, first_col = sides[which]
        return [
            wires.local(here, there, half_sems[which] + k)
            for k, (here, there) in enumerate(half_pieces(e, source, first_col, core))
        ]

    def half_remote(which, of_core):
        e, source, first_col = sides[which]
        return [
            wires.remote(here, there, half_sems[which] + k, (1 - core, chip))
            for k, (here, there) in enumerate(half_pieces(e, source, first_col, of_core))
        ]

    c_own.start()
    for copy in own_weights:
        copy.start()
    for which in range(len(sides)):
        for copy in half_local(which):
            copy.start()
    c_each(lambda copy: copy.start())

    wires.greet(["outer", "core"])

    line = Line(wires, h_ref, h_all)
    device = line.device
    line.start(0)
    for which in range(len(sides)):
        for copy in half_remote(which, core):
            copy.start()
    meta_in = wires.exchange(
        "outer", lambda r, d: meta_ref.at[r], lambda r, d: metas.at[r], own=False
    )

    dh_send, dh_recv = wires.take(n), wires.take(n)
    dg_send, dg_recv = wires.take(n), wires.take(n)

    def give_back(stage, target, k, block, sends, receives):
        return pltpu.make_async_remote_copy(
            src_ref=stage,
            dst_ref=target.at[outer],
            send_sem=send_sems.at[sends + k],
            recv_sem=recv_sems.at[receives + outer],
            device_id=device(block),
            device_id_type=MESH,
        )

    def take_back(target, origin, receives):
        return pltpu.make_async_remote_copy(
            src_ref=target.at[origin],
            dst_ref=target.at[origin],
            send_sem=send_sems.at[receives],
            recv_sem=recv_sems.at[receives + origin],
            device_id=device(origin),
            device_id_type=MESH,
        )

    dh_own = wires.local(dh_stage.at[0], dh_out.at[outer], wires.take(1))
    dg_own = wires.local(dg_stage.at[0], dgate_out.at[outer], wires.take(1))
    mix_base = wires.take(n)

    def mix_copy(k, block):
        return wires.local(
            mix_stage.at[k % 2], mix_out.at[lax.rem(outer - block + n, n)], mix_base + k
        )

    slots = lax.broadcasted_iota(jnp.int32, (room, rows), 0).astype(f32)
    order = line.order()
    gate_w, up_w, down_w = sgu_ref[:, 0:hidden], sgu_ref[:, hidden : 2 * hidden], sd_ref[...]

    for k, block in enumerate(order):
        if k == 0:
            own_h.wait()
            own_meta.wait()
            c_own.wait()
        else:
            line.arrive(k - 1)
            if k < n - 1:
                line.start(k)
            if k == 1:
                meta_in()
                c_each(lambda copy: copy.wait())
        hid, cot = h_all[block], c_all[block]
        for e in range(experts_here):
            at = across(inner, e)
            slot_row = metas[block, pl.ds(at + experts_here, 1), :]
            picks[block, pl.ds(e * room, room), :] = (slots == slot_row).astype(bf16)
        row_a[...] = nn(picks[block], hid).astype(bf16)
        row_b[...] = nn(picks[block], cot).astype(bf16)
        dg_stage[k] = jnp.zeros(dg_stage.shape[1:], f32)

        def one_expert(e, carry, k=k, block=block):
            at = across(inner, e)
            part = pl.ds(pl.multiple_of(e * room, 16), room)
            pick = picks[block, part, :].astype(f32)
            gate = jnp.sum(pick * metas[block, pl.ds(at, 1), :], axis=1, keepdims=True)
            first = nn(row_a[part, :], wgu[e])
            both, active, slope = swiglu_parts(first[:, 0:ff], first[:, ff : 2 * ff])
            act = both.astype(bf16)
            d_act = nt(row_b[part, :], wd[e])
            d_gates = jnp.sum(d_act * act.astype(f32), axis=1, keepdims=True)
            dg_stage[k, pl.ds(at, 1), :] = jnp.sum(pick * d_gates, axis=0, keepdims=True)
            d_act = d_act * gate
            act = (act.astype(f32) * gate).astype(bf16)
            here = pl.ds(pl.multiple_of(block * room, 16), room)
            kept_act[e, here, :] = act
            kept_gu[e, here, 0:ff] = (d_act * slope).astype(bf16)
            kept_gu[e, here, ff : 2 * ff] = (d_act * active).astype(bf16)
            row_a[part, :] = nn(act, wd[e]).astype(bf16)
            row_b[part, :] = nt(kept_gu[e, here, :], wgu[e]).astype(bf16)
            return carry

        if k == 0:
            for copy in own_weights:
                copy.wait()
            one_expert(0, 0)
            for which in range(len(sides)):
                for copy in half_local(which):
                    copy.wait()
                for copy in half_remote(which, 1 - core):
                    copy.wait_recv()
            lax.fori_loop(1, experts_here, one_expert, 0)
        else:
            lax.fori_loop(0, experts_here, one_expert, 0)
        both, active, slope = swiglu_parts(nn(hid, gate_w), nn(hid, up_w))
        act = both.astype(bf16)
        d_act = nt(cot, down_w)
        d_gate = (d_act * slope).astype(bf16)
        d_up = (d_act * active).astype(bf16)
        kept_shared[block, :, 0:hidden] = d_gate
        kept_shared[block, :, hidden : 2 * hidden] = d_up
        kept_shared[block, :, 2 * hidden : 3 * hidden] = act
        dh_stage[k] = (
            tn(picks[block], row_b[...]) + nt(d_gate, gate_w) + nt(d_up, up_w)
        ).astype(bf16)
        if k == 0:
            dh_own.start()
            dg_own.start()
        else:
            give_back(dh_stage.at[k], dh_out, k, block, dh_send, dh_recv).start()
            give_back(dg_stage.at[k], dgate_out, k, block, dg_send, dg_recv).start()
        if k >= 2:
            mix_copy(k - 2, order[k - 2]).wait()
        mix_stage[k % 2] = (tn(picks[block], row_a[...]) + nn(act, down_w)).astype(bf16)
        mix_copy(k, block).start()

    half = width // 2
    mine, other = pl.ds(core * half, half), pl.ds((1 - core) * half, half)
    sibling = (1 - core, chip)
    left, right = pl.ds(0, 2 * ff), pl.ds(2 * ff, ff)
    keep_base, give_base = wires.take(2 * experts_here + 1), wires.take(2 * experts_here + 1)

    def keep(e):
        return (
            wires.local(wgu.at[e, mine, :], e_mine.at[e, :, left], keep_base + 2 * e),
            wires.local(down_stage.at[e % 2, mine, :], e_mine.at[e, :, right], keep_base + 2 * e + 1),
        )

    def give(e):
        return (
            wires.remote(wgu.at[e, other, :], e_other.at[e, :, left], give_base + 2 * e, sibling),
            wires.remote(
                down_stage.at[e % 2, other, :],
                e_other.at[e, :, right],
                give_base + 2 * e + 1,
                sibling,
            ),
        )

    for e in range(experts_here):
        for block in range(n):
            part = pl.ds(block * room, room)
            pick = picks[block, pl.ds(e * room, room), :]
            row_a[part, :] = nn(pick, h_all[block]).astype(bf16)
            row_b[part, :] = nn(pick, c_all[block]).astype(bf16)
        wgu[e] = tn(row_a[...], kept_gu[e]).astype(bf16)
        if e >= 2:
            keep(e - 2)[1].wait()
            give(e - 2)[1].wait_send()
        down_stage[e % 2] = tn(row_b[...], kept_act[e]).astype(bf16)
        for copy in keep(e) + give(e):
            copy.start()
    hid_all = h_all[...].reshape(n * rows, width)
    shared = kept_shared[...].reshape(n * rows, 3 * hidden)
    gu_stage[...] = tn(hid_all, shared[:, 0 : 2 * hidden]).astype(bf16)
    gu_keep = wires.local(gu_stage.at[mine, :], gu_mine, keep_base + 2 * experts_here)
    gu_give = wires.remote(gu_stage.at[other, :], gu_other, give_base + 2 * experts_here, sibling)
    gu_keep.start()
    gu_give.start()
    dsd_ref[...] = tn(shared[:, 2 * hidden :], c_all[...].reshape(n * rows, width)).astype(bf16)

    line.leave()
    for which in range(len(sides)):
        for copy in half_remote(which, core):
            copy.wait_send()
    dh_own.wait()
    dg_own.wait()
    for k in range(max(0, n - 2), n):
        mix_copy(k, order[k]).wait()
    for k in range(1, n):
        give_back(dh_stage.at[k], dh_out, k, order[k], dh_send, dh_recv).wait_send()
        give_back(dg_stage.at[k], dgate_out, k, order[k], dg_send, dg_recv).wait_send()
    for d in range(1, n):
        origin = lax.rem(outer + d, n)
        take_back(dh_out, origin, dh_recv).wait_recv()
        take_back(dgate_out, origin, dg_recv).wait_recv()
    for e in range(experts_here):
        for which, (kept, given) in enumerate(zip(keep(e), give(e))):
            if which == 0 or e >= experts_here - 2:
                kept.wait()
                given.wait_send()
            given.wait_recv()
    gu_keep.wait()
    gu_give.wait()
    wires.finish()


def experts_line(room, hidden, shards, collective, h_own, meta, c_parts, weights, sides, sgu, sd):
    n = shards // KEY_VALUE_HEADS
    rows, width = h_own.shape
    n_experts, ff = KEY_VALUE_HEADS, weights[0].shape[2]
    half = width // 2
    any_spec = pl.BlockSpec(memory_space=pl.ANY)
    vmem = pl.BlockSpec(memory_space=pltpu.VMEM)
    e_shape = (n_experts, half, 3 * ff)
    sems = 96 + 24 * n

    def kernel(*refs):
        experts_line_kernel(room, hidden, shards, refs)

    return pl.pallas_call(
        kernel,
        in_specs=[any_spec] * (2 + len(c_parts) + 3 + len(sides)) + [vmem] * 2,
        out_specs=[any_spec] * 7 + [vmem],
        out_shape=[
            jax.ShapeDtypeStruct((n, rows, width), bf16),
            jax.ShapeDtypeStruct(meta.shape, f32),
            jax.ShapeDtypeStruct((n, rows, width), bf16),
            jax.ShapeDtypeStruct(e_shape, bf16),
            jax.ShapeDtypeStruct(e_shape, bf16),
            jax.ShapeDtypeStruct((half, 2 * hidden), bf16),
            jax.ShapeDtypeStruct((half, 2 * hidden), bf16),
            jax.ShapeDtypeStruct(sd.shape, bf16),
        ],
        scratch_shapes=[
            pltpu.VMEM((n, rows, width), bf16),
            pltpu.VMEM((n, rows, width), bf16),
            pltpu.VMEM(meta.shape, f32),
            pltpu.VMEM((n_experts, width, 2 * ff), bf16),
            pltpu.VMEM((n_experts, ff, width), bf16),
            pltpu.VMEM((n, n_experts * room, rows), bf16),
            pltpu.VMEM((n_experts, n * room, 2 * ff), bf16),
            pltpu.VMEM((n_experts, n * room, ff), bf16),
            pltpu.VMEM((n, rows, 3 * hidden), bf16),
            pltpu.VMEM((n * room, width), bf16),
            pltpu.VMEM((n * room, width), bf16),
            pltpu.VMEM((n, rows, width), bf16),
            pltpu.VMEM((2, rows, width), bf16),
            pltpu.VMEM((n,) + meta.shape[1:], f32),
            pltpu.VMEM((2, width, ff), bf16),
            pltpu.VMEM((width, 2 * hidden), bf16),
        ]
        + [pltpu.SemaphoreType.DMA((sems,))] * 3,
        compiler_params=pltpu.CompilerParams(
            collective_id=collective, has_side_effects=True, vmem_limit_bytes=VMEM_LIMIT
        ),
        name="experts_line",
    )(h_own, meta, *c_parts, *weights, *sides, sgu, sd)


def experts_split(room, hidden, shards, collectives, h_own, meta, c_parts, weights, sides, sgu, sd):
    n_out, n_in = shards // KEY_VALUE_HEADS, KEY_VALUE_HEADS
    rows, width = h_own.shape
    core = lax.axis_index("seq")
    half = width // 2

    def spread_hidden(wires, ins, outs):
        waits = [
            wires.exchange("outer", lambda r, d: ins[0], lambda r, d: outs[0].at[d]),
            wires.exchange("outer", lambda r, d: ins[1].at[r], lambda r, d: outs[1].at[d]),
        ]
        waits += [
            wires.exchange(
                "inner",
                lambda r, d, k=k: ins[k].at[0],
                lambda r, d, k=k: outs[k].at[across(r, lax.rem(r + d, n_in))],
            )
            for k in range(2, 5)
        ]
        for wait in waits:
            wait()

    h_all, meta_all, wg, wu, wd = transfer(
        "spread_hidden",
        collectives[0],
        shards,
        ["outer", "inner"],
        2 * n_out + 3 * n_in,
        spread_hidden,
        [h_own, meta, *weights],
        [((n_out, rows, width), bf16), (meta.shape, f32)]
        + [((n_in,) + weight.shape[1:], bf16) for weight in weights],
    )
    c_all = jnp.stack(c_parts)
    at_once = math.gcd(n_out, 4)
    parts = [
        experts(
            room,
            hidden,
            h_all[i : i + at_once],
            c_all[i : i + at_once],
            meta_all[i : i + at_once],
            wg,
            wu,
            wd,
            sgu,
            sd,
        )
        for i in range(0, n_out, at_once)
    ]
    mix_part, dh_part, dgate_part = (
        jnp.concatenate([part[k] for part in parts], axis=0) for k in range(3)
    )
    e_grad, sgu_grad, sd_grad = (
        sum(part[k].astype(f32) for part in parts).astype(bf16) for k in range(3, 6)
    )

    def sum_hidden(wires, ins, outs):
        core = lax.axis_index("seq")
        dh_ref, dg_ref, e_ref, gu_ref = ins
        dhs, dgs, es, gus = outs
        other = pl.ds((1 - core) * half, half)
        waits = [
            wires.exchange(
                "outer", lambda r, d: dh_ref.at[(n_out - d) % n_out], lambda r, d: dhs.at[r]
            ),
            wires.exchange(
                "outer", lambda r, d: dg_ref.at[(n_out - d) % n_out], lambda r, d: dgs.at[r]
            ),
            wires.sibling(e_ref.at[:, other], es, es),
            wires.sibling(gu_ref.at[other], gus, gus),
        ]
        for wait in waits:
            wait()

    dhs, dgs, es, gus = transfer(
        "sum_hidden",
        collectives[1],
        shards,
        ["outer", "core"],
        2 * n_out + 8,
        sum_hidden,
        [dh_part, dgate_part, e_grad, sgu_grad],
        [
            ((n_out, rows, width), bf16),
            (meta.shape, f32),
            ((n_in, half, e_grad.shape[2]), bf16),
            ((half, 2 * hidden), bf16),
        ],
    )
    e_mine = lax.dynamic_slice_in_dim(e_grad, core * half, half, 1)
    gu_mine = lax.dynamic_slice_in_dim(sgu_grad, core * half, half, 0)
    return dhs, dgs, mix_part, e_mine, es, gu_mine, gus, sd_grad


def norm_rows(values, gain_vector):
    inverse = lax.rsqrt(jnp.mean(values * values, axis=-1, keepdims=True) + epsilon)
    normed = values * inverse
    return (normed, inverse, normed * gain_vector)


def norm_back(grad_hidden, normed, inverse, gain_vector):
    grad_normed = grad_hidden * gain_vector
    gain_grad = jnp.sum(grad_hidden * normed, axis=(0, 1))
    inner_mean = jnp.mean(grad_normed * normed, axis=-1, keepdims=True)
    return (inverse * (grad_normed - normed * inner_mean), gain_grad)


def pad_rows(array, axis):
    size = array.shape[axis]
    widths = [(0, 0)] * array.ndim
    widths[axis] = (0, round_up(size, 16) - size)
    return jnp.pad(array, widths) if widths[axis][1] else array


def pad_to(array, axis, size):
    widths = [(0, 0)] * array.ndim
    widths[axis] = (0, size - array.shape[axis])
    return jnp.pad(array, widths) if widths[axis][1] else array


def body(
    tokens,
    routes,
    out_grad,
    attn_gain,
    ffn_gain,
    query_projection,
    key_projection,
    value_projection,
    w_out,
    w_router,
    shared_gate,
    shared_up,
    shared_down,
    expert_gate,
    expert_up,
    expert_down,
):
    shards = lax.axis_size("fsdp")
    n_in = KEY_VALUE_HEADS
    n_out = shards // n_in
    core, chip, outer, inner = place()
    seg, seqs, width = tokens.shape
    rows = seg * seqs
    topk = routes.shape[2]
    n_experts = w_router.shape[1]
    w_rows = query_projection.shape[0]
    w_pad = round_up(w_rows, 16)
    d_rows = shared_down.shape[0]
    d_pad = round_up(d_rows, 16)
    half_chips = shards // 2
    q_cols = GROUP_MEMBERS * HEAD_SIZE
    cols = q_cols + 2 * HEAD_SIZE
    ff = expert_gate.shape[2]
    hid_core = n_in * d_rows
    hid = 2 * hid_core
    hid_pad = round_up(hid, 128)
    small = round_up(n_experts + 2, 128)
    chunk = n_in * seg
    half_width, half_ff = width // 2, ff // 2
    room = round_up(max(2, (3 * rows * topk + 2 * n_experts - 1) // (2 * n_experts)), 16)

    small_piece = pad_to(
        jnp.concatenate([w_router, attn_gain[:, None], ffn_gain[:, None]], axis=1), 1, small
    )
    q_pieces = pad_rows(
        jnp.concatenate(
            [
                query_projection.reshape(w_rows, n_in, q_cols),
                key_projection.reshape(w_rows, n_in, HEAD_SIZE),
                value_projection.reshape(w_rows, n_in, HEAD_SIZE),
                jnp.broadcast_to(small_piece[:, None], (w_rows, n_in, small)),
            ],
            axis=2,
        ).transpose(1, 0, 2),
        1,
    )

    def hidden_piece(weight):
        piece = weight.reshape(w_rows, 2, n_out, hid_core).transpose(2, 0, 1, 3)
        return pad_to(piece.reshape(n_out, w_rows, hid), 2, hid_pad)

    gu_pieces = pad_rows(
        jnp.concatenate([hidden_piece(shared_gate), hidden_piece(shared_up)], axis=2), 1
    )
    out_piece = pad_rows(w_out, 0)
    down_piece = pad_rows(shared_down, 0)
    x_own = tokens.transpose(1, 0, 2)
    c_own = out_grad.transpose(1, 0, 2)
    cot = c_own.reshape(rows, width)

    def shift(block, amount):
        return lax.ppermute(
            block, "fsdp", [(f, (f + amount * n_in) % shards) for f in range(shards)]
        )

    def swap(block, step):
        return lax.ppermute(
            block, "fsdp", [(f, f // n_in * n_in + (f % n_in ^ step)) for f in range(shards)]
        )

    def out_rows(wires, o_ref, wo_ref):
        core, chip, outer, inner = place()
        to_inner = 2 * core + chip // half_chips
        slot = lax.rem(chip, half_chips)
        base = wires.take(half_chips)
        sends = wires.take(n_out)
        across_core = wires.take(1)
        first = inner // 2 == core

        def copy(k):
            to = (core, k * n_in + to_inner)
            return to[1] == chip, pltpu.make_async_remote_copy(
                src_ref=o_ref,
                dst_ref=wo_ref.at[slot],
                send_sem=wires.send_sems.at[sends + k],
                recv_sem=wires.recv_sems.at[base + slot],
                device_id=to,
                device_id_type=MESH,
            )

        def start(k):
            here, send = copy(k)
            pl.when(jnp.logical_not(here))(send.start)
            pl.when(here)(lambda: wires.local(o_ref, wo_ref.at[slot], base).start())

        def leave(k):
            here, send = copy(k)
            pl.when(jnp.logical_not(here))(send.wait_send)

        def come(i):
            origin = (core, half_chips * lax.rem(inner, 2) + i)
            here = origin[1] == chip
            place_of = wo_ref.at[i]
            pl.when(jnp.logical_not(here))(
                wires.remote(place_of, place_of, base + i, origin).wait_recv
            )
            pl.when(here)(lambda: wires.local(o_ref, place_of, base).wait())

        def hand_on():
            return wires.remote(wo_ref, wo_ref, across_core, (1 - core, chip))

        def arrive():
            @pl.when(first)
            def _():
                repeat(0, half_chips, come)
                hand_on().start()

        def settle():
            @pl.when(first)
            def _():
                hand_on().wait_send()

            @pl.when(jnp.logical_not(first))
            def _():
                hand_on().wait_recv()

        repeat(0, n_out, start)
        wires.leaving.append(lambda: repeat(0, n_out, leave))
        return arrive, settle

    own_rows = half_chips // 2
    line = n_out == 4

    def fetch(wires, ins, outs):
        x_ref, q_ref, o_ref, *c_refs = ins
        xs_ref, wq_ref, wo_ref, *passed = outs
        core, chip, outer, inner = place()
        q_in = wires.exchange(
            "chips", lambda r, d: q_ref.at[lax.rem(r, n_in)], lambda r, d: wq_ref.at[core, r]
        )
        x_in = wires.exchange("plane", lambda r, d: x_ref.at[r // n_in], lambda r, d: xs_ref.at[r])
        o_in, o_settle = out_rows(wires, o_ref, wo_ref)
        if line:
            c_in = gather_step(wires, n_out, 0, c_refs * 2, passed)
        q_in()
        q_other = wires.sibling(wq_ref.at[core], wq_ref.at[core], wq_ref.at[1 - core])
        o_in()
        x_in()
        q_other()
        o_settle()
        if line:
            c_in()

    xs, wq, wo, *c_first = transfer(
        "fetch",
        0,
        shards,
        ["all"],
        4 * shards + 16,
        fetch,
        [x_own, q_pieces, out_piece] + [cot] * line,
        [
            ((2 * n_in, seg, width), bf16),
            ((2, shards, w_pad, cols + small), bf16),
            ((half_chips, w_pad, width), bf16),
        ]
        + [(cot.shape, bf16)] * (2 * line),
    )
    down_half = lax.dynamic_slice_in_dim(expert_down[0], core * half_ff, half_ff, 0)
    expert_half = jnp.concatenate(
        [
            lax.dynamic_slice_in_dim(expert_gate[0], core * half_width, half_width, 0),
            lax.dynamic_slice_in_dim(expert_up[0], core * half_width, half_width, 0),
        ]
        + [down_half[:, k : k + ff] for k in range(0, width, ff)],
        axis=0,
    )
    wq, expert_half = lax.optimization_barrier((wq, expert_half))
    side_x, side_y = swap(expert_half, 1), swap(expert_half, 2)
    wq = wq[:, :, :w_rows].reshape(width, cols + small)
    wo = wo[:, :w_rows].reshape(q_cols, width)
    wq, small_w = wq[:, :cols], wq[:, cols:]
    router_w = small_w[:, :n_experts]
    gain_one = small_w[:, n_experts].astype(f32)
    gain_two = small_w[:, n_experts + 1].astype(f32)

    h1 = norm_rows(xs.reshape(2 * chunk, width).astype(f32), gain_one)[2].astype(bf16)
    qkv = nn(h1, wq).astype(bf16)

    mixed, log_rows, kv_all, *c_second = attend(
        1, shards, chunk, qkv[:, :q_cols], qkv[:, q_cols:], c_first
    )
    mixed, side_x, side_y = lax.optimization_barrier((mixed, side_x, side_y))
    cross_a, cross_b = swap(side_x[:, : ff // 2], 2), swap(side_y[:, ff // 2 :], 1)
    mixed_low = mixed.astype(bf16)
    out_part = nn(mixed_low, wo).astype(bf16).reshape(2 * n_in, seg, width)

    out_part, cross_a, cross_b = lax.optimization_barrier((out_part, cross_a, cross_b))

    def sum_out(wires, ins, outs):
        core, chip, outer, inner = place()
        part_ref, gu_ref, s_ref, *c_refs = ins
        parts_ref, wgu_ref, ws_ref, *passed = outs
        gu_in = wires.exchange(
            "chips", lambda r, d: gu_ref.at[r // n_in], lambda r, d: wgu_ref.at[core, r]
        )
        part_in = wires.exchange("plane", lambda r, d: part_ref.at[r], lambda r, d: parts_ref.at[r])
        s_in = wires.exchange("inner", lambda r, d: s_ref, lambda r, d: ws_ref.at[core, r])
        if line:
            c_in = gather_step(wires, n_out, 2, c_refs, passed)
        gu_in()
        gu_other = wires.sibling(wgu_ref.at[core], wgu_ref.at[core], wgu_ref.at[1 - core])
        s_in()
        s_other = wires.sibling(ws_ref.at[core], ws_ref.at[core], ws_ref.at[1 - core])
        part_in()
        gu_other()
        s_other()
        if line:
            c_in()

    out_parts, sgu, ws, *c_third = transfer(
        "sum_out",
        2,
        shards,
        ["all"],
        shards + 8 * n_in + 16,
        sum_out,
        [out_part, gu_pieces, down_piece, *c_second],
        [
            ((2 * n_in, seg, width), bf16),
            ((2, shards, w_pad, 2 * hid_pad), bf16),
            ((2, n_in, d_pad, width), bf16),
        ]
        + [(cot.shape, bf16)] * (2 * line),
    )
    if line:
        c_parts = [cot] + [came[way] for way in range(2) for came in (c_first, c_second, c_third)]
    else:
        c_parts = [cot] + [shift(cot, d) for d in range(1, n_out)]
    sgu = sgu[:, :, :w_rows].reshape(width, 2 * hid_pad)
    ws = pad_to(ws[:, :, :d_rows].reshape(hid, width), 0, hid_pad)
    inputs = x_own.astype(f32)
    residual = inputs + jnp.sum(out_parts.astype(f32).reshape(2, n_in, seg, width), axis=1)

    normed_two, inverse_two, scaled_two = norm_rows(residual, gain_two)
    hidden_two = scaled_two.astype(bf16).reshape(rows, width)
    logits = nn(hidden_two, router_w)
    flat_routes = routes.transpose(1, 0, 2).reshape(rows, topk)
    chooser = (flat_routes[:, :, None] == jnp.arange(n_experts, dtype=jnp.int32)).astype(f32)
    taken = jnp.sum(chooser, axis=1)
    chosen = jnp.where(taken > 0, logits, masked_score)
    exponent = jnp.where(
        taken > 0, jnp.exp(chosen - jnp.max(chosen, axis=-1, keepdims=True)), 0.0
    )
    gates = exponent / jnp.sum(exponent, axis=-1, keepdims=True)
    before = (
        lax.broadcasted_iota(jnp.int32, (rows, rows), 0)
        < lax.broadcasted_iota(jnp.int32, (rows, rows), 1)
    ).astype(bf16)
    slots = jnp.where(taken.T > 0, nn(taken.T.astype(bf16), before), -1.0)
    meta = jnp.concatenate(
        [gates.T.reshape(n_out, n_in, rows), slots.reshape(n_out, n_in, rows)], axis=1
    )

    run = functools.partial(experts_line if line else experts_split, room, hid_pad, shards)
    dhs, dgs, mix_part, e_mine, es, gu_mine, gus, sd_grad = run(
        3 if line else (3, 4),
        hidden_two,
        meta,
        c_parts,
        (expert_gate, expert_up, expert_down),
        (side_x, side_y, cross_a, cross_b),
        sgu,
        ws,
    )

    def mix_terms(step, came):
        if not line:
            return []
        terms = []
        for way, slot in enumerate(((step + 1) % n_out, (n_out - 1 - step) % n_out)):
            term = mix_part[slot].astype(f32)
            if came:
                inside = (outer > 0, outer < n_out - 1)[way]
                term = term + jnp.where(inside, came[way].astype(f32), 0.0)
            terms.append(term.astype(bf16))
        return terms

    gu_half = (gu_mine.astype(f32) + gus.astype(f32)).astype(bf16)
    gu_half = pad_rows(gu_half.reshape(shards, w_rows, 2 * hid_pad), 1)
    sd_send = pad_rows(sd_grad[:hid].reshape(2 * n_in, d_rows, width), 1)

    grad_float = c_own.astype(f32)
    grad_gates = dgs[:, :n_in].reshape(n_experts, rows).T
    grad_logits = gates * (grad_gates - jnp.sum(gates * grad_gates, axis=-1, keepdims=True))
    router_grad = lax.dot_general(
        hidden_two.astype(f32),
        grad_logits,
        (((0,), (0,)), ((), ())),
        precision=lax.Precision.HIGHEST,
        preferred_element_type=f32,
    )
    grad_hidden_two = jnp.sum(dhs.astype(f32), axis=0) + lax.dot_general(
        grad_logits,
        router_w.astype(f32),
        (((1,), (1,)), ((), ())),
        precision=lax.Precision.HIGHEST,
        preferred_element_type=f32,
    )
    grad_norm_two, gain_two_grad = norm_back(
        grad_hidden_two.reshape(seqs, seg, width), normed_two, inverse_two, gain_two
    )
    grad_residual = grad_float + grad_norm_two
    grad_attn = grad_residual.astype(bf16)

    def spread_grad(wires, ins, outs):
        second = wires.exchange("chips", lambda r, d: ins[1].at[r], lambda r, d: outs[1].at[r])
        first = wires.exchange("plane", lambda r, d: ins[0].at[r // n_in], lambda r, d: outs[0].at[r])
        if line:
            mix_in = sum_step(wires, n_out, 0, ins[2:], outs[2:])
        first()
        second()
        if line:
            mix_in()

    grad_all, gus, *mix_first = transfer(
        "spread_grad",
        5,
        shards,
        ["all"],
        shards + 2 * n_in + 4,
        spread_grad,
        [grad_attn, gu_half] + mix_terms(0, []),
        [((2 * n_in, seg, width), bf16), ((shards, w_pad, 2 * hid_pad), bf16)]
        + [(cot.shape, bf16)] * (2 * line),
    )
    grad_all, es = lax.optimization_barrier((grad_all, es))

    def e_term(e):
        return e_mine[e].astype(f32) + es[e].astype(f32)

    e_parts = [swap(e_term(e).astype(bf16), e) for e in range(1, n_in)]
    grad_all = grad_all.reshape(2 * chunk, width)
    small_grad = pad_to(
        jnp.concatenate(
            [router_grad, jnp.zeros((width, 1), f32), gain_two_grad[:, None]], axis=1
        ),
        1,
        small,
    )
    if line:
        grad_hidden_one, wq_total, small_total, out_w_grad, down_w_grad, *mix_third = finish(
            6,
            shards,
            chunk,
            n_experts,
            qkv[:, :q_cols],
            kv_all,
            grad_all,
            wo,
            mixed,
            log_rows,
            h1,
            wq,
            gain_one[None],
            small_grad.astype(bf16),
            sd_send,
            mix_part,
            mix_terms(1, mix_first),
        )
        mixes = [mix_part[0].astype(f32)] + [
            jnp.where(inside, came.astype(f32), 0.0)
            for inside, came in zip((outer > 0, outer < n_out - 1), mix_third)
        ]
    else:
        mixes = [mix_part[0].astype(f32)] + [
            shift(mix_part[n_out - d], d).astype(f32) for d in range(1, n_out)
        ]
        grad_mixed = nt(grad_all, wo).astype(bf16)
        wo_grad = tn(mixed_low, grad_all).astype(bf16).reshape(half_chips, w_rows, width)
        wo_grad = pad_rows(wo_grad, 1)
        delta_rows = jnp.sum(
            (grad_mixed.astype(f32) * mixed).reshape(2, chunk, GROUP_MEMBERS, HEAD_SIZE), axis=-1
        ).transpose(2, 0, 1)
        dqkv, wos = attend_back(
            6,
            shards,
            chunk,
            qkv[:, :q_cols],
            kv_all,
            grad_mixed,
            log_rows,
            delta_rows,
            wo_grad,
        )
        wo_mine = lax.dynamic_slice_in_dim(wo_grad, core * own_rows, own_rows, 0)
        wo_half = (wo_mine.astype(f32) + wos.astype(f32)).astype(bf16)
        dh1_part = nt(dqkv, wq).astype(bf16).reshape(2 * n_in, seg, width)
        wq_send = pad_rows(tn(h1, dqkv).astype(bf16).reshape(2 * shards, w_rows, cols), 1)
        gain_one_grad = (
            jnp.sum(
                dh1_part.reshape(2 * chunk, width).astype(f32) * h1.astype(f32), axis=0
            )
            / gain_one
        )
        small_grad = small_grad.at[:, n_experts].set(gain_one_grad)
        small_send = pad_rows(small_grad.astype(bf16).reshape(2 * shards, w_rows, small), 1)

        def sum_first(wires, ins, outs):
            dh_ref, wq_ref, small_ref, s_ref, o_ref = ins
            dhs, wqs, smalls, sds, wos = outs
            waits = [
                out_rows_back(wires, shards, o_ref, wos),
                wires.exchange("all", lambda r, d: wq_ref.at[r], lambda r, d: wqs.at[r]),
                wires.exchange("plane", lambda r, d: dh_ref.at[r], lambda r, d: dhs.at[r]),
                wires.exchange("all", lambda r, d: small_ref.at[r], lambda r, d: smalls.at[r]),
                wires.exchange("plane", lambda r, d: s_ref.at[r], lambda r, d: sds.at[r]),
            ]
            for wait in waits:
                wait()

        dh1s, wq_parts, small_parts, sds, wos = transfer(
            "sum_first",
            7,
            shards,
            ["all"],
            4 * n_in + 6 * shards + 16,
            sum_first,
            [dh1_part, wq_send, small_send, sd_send, wo_half.reshape(own_rows * w_pad, width)],
            [
                ((2 * n_in, seg, width), bf16),
                ((2 * shards, w_pad, cols), bf16),
                ((2 * shards, w_pad, small), bf16),
                ((2 * n_in, d_pad, width), bf16),
                ((n_out, w_pad, width), bf16),
            ],
        )
        grad_hidden_one = jnp.sum(dh1s.astype(f32).reshape(2, n_in, seg, width), axis=1)
        wq_total = jnp.sum(
            wq_parts[:, :w_rows].astype(f32).reshape(2 * n_out, n_in, w_rows, cols), axis=0
        )
        down_w_grad = jnp.sum(sds[:, :d_rows].astype(f32), axis=0)
        out_w_grad = jnp.sum(wos[:, :w_rows].astype(f32), axis=0)
        small_total = jnp.sum(small_parts[:, :w_rows].astype(f32), axis=0)
    total_out = residual + sum(mixes).reshape(seqs, seg, width)
    e_sum = (e_term(0) + sum(part.astype(f32) for part in e_parts)).astype(bf16)
    e_other = lax.ppermute(e_sum, "seq", [(0, 1), (1, 0)])
    normed_one, inverse_one, _ = norm_rows(inputs, gain_one)
    grad_norm_one = norm_back(grad_hidden_one, normed_one, inverse_one, gain_one)[0]
    tokens_grad = grad_residual + grad_norm_one

    wq_total = wq_total.transpose(1, 0, 2)
    query_grad = wq_total[:, :, :q_cols].reshape(w_rows, n_in * q_cols)
    key_grad = wq_total[:, :, q_cols : q_cols + HEAD_SIZE].reshape(w_rows, n_in * HEAD_SIZE)
    value_grad = wq_total[:, :, q_cols + HEAD_SIZE :].reshape(w_rows, n_in * HEAD_SIZE)
    gu_total = jnp.sum(
        gus[:, :w_rows].astype(f32).reshape(n_out, n_in, w_rows, 2 * hid_pad), axis=1
    )

    def hidden_whole(piece):
        piece = piece[:, :, :hid].reshape(n_out, w_rows, 2, hid_core)
        return piece.transpose(1, 2, 0, 3).reshape(w_rows, n_out * hid)

    gate_w_grad = hidden_whole(gu_total[:, :, :hid_pad])
    up_w_grad = hidden_whole(gu_total[:, :, hid_pad:])
    own, came = e_sum.astype(f32), e_other.astype(f32)
    e_total = jnp.concatenate(
        [jnp.where(core == 0, own, came), jnp.where(core == 0, came, own)], axis=0
    )

    return (
        total_out.astype(bf16).transpose(1, 0, 2),
        tokens_grad.transpose(1, 0, 2),
        small_total[:, n_experts],
        small_total[:, n_experts + 1],
        query_grad,
        key_grad,
        value_grad,
        out_w_grad,
        small_total[:, :n_experts],
        gate_w_grad,
        up_w_grad,
        down_w_grad,
        e_total[:, :ff][None],
        e_total[:, ff : 2 * ff][None],
        e_total[:, 2 * ff :].T[None],
    )


def solution(mesh):
    rows = P(("seq", "fsdp"), None, None)
    matrix = P(("seq", "fsdp"), None)
    vector = P(("seq", "fsdp"))
    expert = P("fsdp", None, None)
    return jax.shard_map(
        body,
        mesh=mesh,
        in_specs=(rows,) * 3 + (vector,) * 2 + (matrix,) * 8 + (expert,) * 3,
        out_specs=(rows,) * 2 + (vector,) * 2 + (matrix,) * 8 + (expert,) * 3,
        check_vma=False,
    )
```

```python
import functools
import math

import jax
import jax.numpy as jnp
from jax import lax
from jax.experimental import pallas as pl
from jax.experimental.pallas import tpu as pltpu
from jax.sharding import PartitionSpec as P

QUERY_HEADS = 12
KEY_VALUE_HEADS = 4
HEAD_SIZE = 128
GROUP_MEMBERS = QUERY_HEADS // KEY_VALUE_HEADS

epsilon = 1e-06
masked_score = -1e30
MESH = pl.DeviceIdType.MESH
VMEM_LIMIT = 63 * 1024 * 1024
f32 = jnp.float32
bf16 = jnp.bfloat16


def round_up(number, step):
    return -(-number // step) * step


def nn(left, right):
    return lax.dot_general(left, right, (((1,), (0,)), ((), ())), preferred_element_type=f32)


def nt(left, right):
    return lax.dot_general(left, right, (((1,), (1,)), ((), ())), preferred_element_type=f32)


def tn(left, right):
    return lax.dot_general(left, right, (((0,), (0,)), ((), ())), preferred_element_type=f32)


def across(inner, step):
    low = lax.rem(inner + step, 2)
    high = lax.rem(inner // 2 + step // 2, 2)
    return low + 2 * high


def place():
    core = lax.axis_index("seq")
    chip = lax.axis_index("fsdp")
    return core, chip, chip // KEY_VALUE_HEADS, lax.rem(chip, KEY_VALUE_HEADS)


def group(kind, shards):
    core, chip, outer, inner = place()
    if kind == "plane":
        size = 2 * KEY_VALUE_HEADS
        return (
            size,
            core * KEY_VALUE_HEADS + inner,
            lambda r: (r // KEY_VALUE_HEADS, outer * KEY_VALUE_HEADS + lax.rem(r, KEY_VALUE_HEADS)),
        )
    if kind == "inner":
        return KEY_VALUE_HEADS, inner, lambda r: (core, outer * KEY_VALUE_HEADS + r)
    if kind == "outer":
        return shards // KEY_VALUE_HEADS, outer, lambda r: (core, r * KEY_VALUE_HEADS + inner)
    if kind == "chips":
        return shards, chip, lambda r: (core, r)
    if kind == "all":
        return 2 * shards, core * shards + chip, lambda r: (r // shards, lax.rem(r, shards))
    return 2, core, lambda r: (r, chip)


def repeat(first, last, step):
    if last - first <= 16:
        for index in range(first, last):
            step(index)
    else:

        def one(index, carry):
            step(index)
            return carry

        lax.fori_loop(first, last, one, 0)


class Wires:
    def __init__(self, shards, send_sems, recv_sems, local_sems):
        self.shards = shards
        self.send_sems, self.recv_sems, self.local_sems = send_sems, recv_sems, local_sems
        self.used = 0
        self.leaving = []

    def greet(self, kinds):
        barrier = pltpu.get_barrier_semaphore()
        total = 0
        for kind in kinds:
            size, me, device = group(kind, self.shards)

            def signal(d, size=size, me=me, device=device):
                pl.semaphore_signal(
                    barrier, inc=1, device_id=device(lax.rem(me + d, size)), device_id_type=MESH
                )

            repeat(1, size, signal)
            total += size - 1
        pl.semaphore_wait(barrier, total)

    def take(self, count):
        base = self.used
        self.used += count
        return base

    def remote(self, source, target, index, device):
        return pltpu.make_async_remote_copy(
            src_ref=source,
            dst_ref=target,
            send_sem=self.send_sems.at[index],
            recv_sem=self.recv_sems.at[index],
            device_id=device,
            device_id_type=MESH,
        )

    def local(self, source, target, index):
        return pltpu.make_async_copy(source, target, self.local_sems.at[index])

    def exchange(self, kind, source_for, target_from, own=True):
        size, me, device = group(kind, self.shards)
        base = self.take(size)

        def copy(d):
            to = lax.rem(me + d, size)
            return self.remote(source_for(to, d), target_from(me, d), base + d, device(to))

        repeat(1, size, lambda d: copy(d).start())
        if own:
            self.local(source_for(me, 0), target_from(me, 0), base).start()
        self.leaving.append(lambda: repeat(1, size, lambda d: copy(d).wait_send()))

        def arrive(then=None):
            def one(d):
                came = lax.rem(me - d + size, size)
                place_of = target_from(came, d)
                self.remote(place_of, place_of, base + d, device(came)).wait_recv()
                if then is not None:
                    then(d)

            repeat(1, size, one)
            if own:
                self.local(source_for(me, 0), target_from(me, 0), base).wait()

        return arrive

    def sibling(self, source, target, comes):
        core, chip, _, _ = place()
        device = (1 - core, chip)
        index = self.take(1)
        copy = self.remote(source, target, index, device)
        copy.start()
        self.leaving.append(copy.wait_send)
        return self.remote(comes, comes, index, device).wait_recv

    def finish(self):
        for leave in self.leaving:
            leave()


def transfer(name, collective, shards, kinds, sems, body, operands, outs, scratch=()):
    count = len(operands)

    def kernel(*refs):
        ins, results = refs[:count], refs[count : count + len(outs)]
        room, sem_refs = refs[count + len(outs) : -3], refs[-3:]
        wires = Wires(shards, *sem_refs)
        wires.greet(kinds)
        body(wires, ins, results, *room)
        wires.finish()

    return pl.pallas_call(
        kernel,
        out_shape=[jax.ShapeDtypeStruct(shape, kind) for shape, kind in outs],
        in_specs=[pl.BlockSpec(memory_space=pl.ANY)] * count,
        out_specs=[pl.BlockSpec(memory_space=pl.ANY)] * len(outs),
        scratch_shapes=[pltpu.VMEM(shape, kind) for shape, kind in scratch]
        + [pltpu.SemaphoreType.DMA((sems,))] * 3,
        compiler_params=pltpu.CompilerParams(
            collective_id=collective, has_side_effects=True, vmem_limit_bytes=VMEM_LIMIT
        ),
        name=name,
    )(*operands)


def add_pieces(wires, first, second, result, left, right, total):
    items, rows, _ = first.shape
    size = left.shape[1]
    per_item = rows // size
    count = items * per_item
    load_base, store_base = wires.take(4), wires.take(2)

    def cut(i):
        return i // per_item, pl.ds(i % per_item * size, size)

    def loads(i):
        slot = i % 2
        return (
            wires.local(first.at[cut(i)], left.at[slot], load_base + 2 * slot),
            wires.local(second.at[cut(i)], right.at[slot], load_base + 2 * slot + 1),
        )

    def store(i):
        return wires.local(total.at[i % 2], result.at[cut(i)], store_base + i % 2)

    for copy in loads(0):
        copy.start()
    for i in range(count):
        if i + 1 < count:
            for copy in loads(i + 1):
                copy.start()
        for copy in loads(i):
            copy.wait()
        if i >= 2:
            store(i - 2).wait()
        total[i % 2] = (left[i % 2].astype(f32) + right[i % 2].astype(f32)).astype(bf16)
        store(i).start()
    for i in range(max(0, count - 2), count):
        store(i).wait()


def neighbours(wires, n, sources, targets, sends, comes):
    core, chip, outer, inner = place()
    base = wires.take(2)

    def copy(way):
        sign = (1, -1)[way]
        to = lax.rem(outer + sign + n, n)
        device = (core, to * KEY_VALUE_HEADS + inner)
        return wires.remote(sources[way], targets[way], base + way, device)

    def come(way):
        sign = (1, -1)[way]
        origin = lax.rem(outer - sign + n, n)
        device = (core, origin * KEY_VALUE_HEADS + inner)
        return wires.remote(targets[way], targets[way], base + way, device)

    def each(conditions, action):
        for way in range(2):
            pl.when(conditions[way])(lambda way=way: action(way))

    each(sends, lambda way: copy(way).start())
    wires.leaving.append(lambda: each(sends, lambda way: copy(way).wait_send()))
    return lambda: each(comes, lambda way: come(way).wait_recv())


def gather_step(wires, n, step, sources, targets):
    outer = place()[2]
    sends = ((outer >= step) & (outer < n - 1), (outer < n - step) & (outer > 0))
    comes = (outer > step, outer < n - 1 - step)
    return neighbours(wires, n, sources, targets, sends, comes)


def sum_step(wires, n, step, sources, targets):
    outer = place()[2]
    sends = (
        (outer <= step) & (outer < n - 1),
        (outer >= n - 1 - step) & (outer > 0),
    )
    comes = (
        (outer >= 1) & (outer <= step + 1),
        (outer <= n - 2) & (outer >= n - 2 - step),
    )
    return neighbours(wires, n, sources, targets, sends, comes)


def out_rows_back(wires, shards, grad_ref, sums_ref):
    core, chip, outer, inner = place()
    n_in, n_out, half_chips = KEY_VALUE_HEADS, shards // KEY_VALUE_HEADS, shards // 2
    own_rows = half_chips // 2
    rows = sums_ref.shape[1]
    from_inner = 2 * core + chip // half_chips
    from_core = lax.rem(chip, half_chips) // own_rows
    sends = wires.take(own_rows)
    base = wires.take(n_out)

    def copy(i):
        to = (inner // 2, half_chips * lax.rem(inner, 2) + core * own_rows + i)
        here = (to[0] == core) & (to[1] == chip)
        return here, pltpu.make_async_remote_copy(
            src_ref=grad_ref.at[pl.ds(i * rows, rows)],
            dst_ref=sums_ref.at[outer],
            send_sem=wires.send_sems.at[sends + i],
            recv_sem=wires.recv_sems.at[base + outer],
            device_id=to,
            device_id_type=MESH,
        )

    def start(i):
        here, send = copy(i)
        pl.when(jnp.logical_not(here))(send.start)
        pl.when(here)(lambda: wires.local(grad_ref.at[pl.ds(i * rows, rows)], sums_ref.at[outer], base).start())

    def leave(i):
        here, send = copy(i)
        pl.when(jnp.logical_not(here))(send.wait_send)

    def come(k):
        origin = (from_core, k * n_in + from_inner)
        here = (origin[0] == core) & (origin[1] == chip)
        place_of = sums_ref.at[k]
        pl.when(jnp.logical_not(here))(
            wires.remote(place_of, place_of, base + k, origin).wait_recv
        )
        pl.when(here)(lambda: wires.local(place_of, place_of, base).wait())

    repeat(0, own_rows, start)
    wires.leaving.append(lambda: repeat(0, own_rows, leave))
    return lambda: repeat(0, n_out, come)


class Line:
    def __init__(self, wires, source, every):
        self.wires, self.source, self.every = wires, source, every
        self.n = every.shape[0]
        self.core, _, self.outer, self.inner = place()
        self.bases = {1: wires.take(self.n), -1: wires.take(self.n)}

    def device(self, at):
        return self.core, at * KEY_VALUE_HEADS + self.inner

    def order(self):
        low = self.outer < self.n // 2
        return [
            lax.rem(jnp.where(low, self.outer + k, self.outer - k + self.n), self.n)
            for k in range(self.n)
        ]

    def hop(self, step, sign):
        to = lax.rem(self.outer + sign + self.n, self.n)
        block = lax.rem(self.outer - sign * step + 2 * self.n, self.n)
        source = self.source if step == 0 else self.every.at[block]
        index = self.bases[sign] + step
        return self.wires.remote(source, self.every.at[block], index, self.device(to))

    def sends(self, step, sign):
        to, block = self.outer + sign, self.outer - sign * step
        return (to >= 0) & (to < self.n) & (block >= 0) & (block < self.n)

    def start(self, step):
        for sign in (1, -1):
            pl.when(self.sends(step, sign))(lambda sign=sign: self.hop(step, sign).start())

    def arrive(self, step):
        for sign in (1, -1):
            come = self.outer - sign * (step + 1)

            def wait(sign=sign, come=come):
                block = self.every.at[lax.rem(come + self.n, self.n)]
                to = lax.rem(self.outer - sign + self.n, self.n)
                index = self.bases[sign] + step
                self.wires.remote(block, block, index, self.device(to)).wait_recv()

            pl.when((come >= 0) & (come < self.n))(wait)

    def leave(self):
        for step in range(self.n - 1):
            for sign in (1, -1):
                pl.when(self.sends(step, sign))(
                    lambda step=step, sign=sign: self.hop(step, sign).wait_send()
                )


def far_first(outer, n):
    low = outer < n // 2
    order = []
    for k in range(n - 1):
        down = n - 1 - k
        order.append(
            jnp.where(low, jnp.where(down <= outer, down - 1, down), jnp.where(k >= outer, k + 1, k))
        )
    return order


def causal(scores):
    key_at = lax.broadcasted_iota(jnp.int32, scores.shape, 0)
    query_at = lax.broadcasted_iota(jnp.int32, scores.shape, 1)
    return jnp.where(key_at <= query_at, scores, masked_score)


def each_pair(block, outer, own, pair):
    def some(head, carry):
        if own:
            pair(head, 0, block, 0, True)
            pair(head, 1, block, 0, False)
            pair(head, 1, block, 1, True)
        else:
            pair(head, 1, block, 0, False)

            @pl.when(block < outer)
            def _():
                pair(head, 0, block, 0, False)
                pair(head, 1, block, 1, False)

        return carry

    lax.fori_loop(0, GROUP_MEMBERS, some, 0)


def attend_kernel(shards, chunk, joined, *refs):
    q_ref, kv_ref, *refs = refs
    if joined:
        wo_ref, gu_ref, s_ref, *refs = refs
        pass_from, refs = refs[:2], refs[2:]
    mixed_ref, log_ref, kv_out, *refs = refs
    if joined:
        out_ref, wgu_ref, ws_ref, *refs = refs
        pass_once, pass_twice, refs = refs[:2], refs[2:4], refs[4:]
        out_stage, out_recv, *refs = refs
    kv_all, largest, total, summed, send_sems, recv_sems, local_sems = refs
    core, chip, _, inner = place()
    wires = Wires(shards, send_sems, recv_sems, local_sems)
    factor = HEAD_SIZE**-0.5 * math.log2(math.e)
    line = Line(wires, kv_ref, kv_all)
    outer = line.outer
    own = wires.local(kv_ref, kv_all.at[outer], wires.take(1))
    own.start()
    wires.greet(["all"] if joined else ["outer"])
    line.start(0)
    largest[...] = jnp.full_like(largest, masked_score)
    total[...] = jnp.zeros_like(total)
    summed[...] = jnp.zeros_like(summed)

    def pair(head, half, block, key_half, masked):
        cols = pl.ds(pl.multiple_of(head * HEAD_SIZE, HEAD_SIZE), HEAD_SIZE)
        rows = pl.ds(key_half * chunk, chunk)
        query = q_ref[pl.ds(half * chunk, chunk), cols]
        scores = nt(kv_all[block, rows, 0:HEAD_SIZE], query)
        if masked:
            scores = causal(scores)
        before = largest[head, half]
        new = jnp.maximum(before, jnp.max(scores, axis=0, keepdims=True))
        weights = jnp.exp2((scores - new) * factor)
        shrink = jnp.exp2((before - new) * factor)
        largest[head, half] = new
        total[head, half] = total[head, half] * shrink + jnp.sum(weights, axis=0, keepdims=True)
        summed[head, half] = summed[head, half] * shrink + tn(
            kv_all[block, rows, HEAD_SIZE : 2 * HEAD_SIZE], weights.astype(bf16)
        )

    for k, block in enumerate(line.order()):
        if k == 0:
            own.wait()
        else:
            line.arrive(k - 1)
            if k < line.n - 1:
                line.start(k)
        if joined and k == line.n - 2:
            passed = gather_step(wires, line.n, 1, pass_from, pass_once)
            gu_in, gu_settle, s_in, s_settle = spread_shared(wires, gu_ref, s_ref, wgu_ref, ws_ref)
        each_pair(block, outer, k == 0, pair)
    keep = wires.local(kv_all, kv_out, wires.take(1))
    keep.start()
    for head in range(GROUP_MEMBERS):
        for half in range(2):
            mixed_ref[
                half * chunk : (half + 1) * chunk, head * HEAD_SIZE : (head + 1) * HEAD_SIZE
            ] = (summed[head, half] / total[head, half]).T
            log_ref[head, half : half + 1, :] = largest[head, half] * factor + jnp.log2(
                total[head, half]
            )
    if joined:
        seg = out_ref.shape[1]
        for half in range(2):
            rows = pl.ds(half * chunk, chunk)
            out_stage[rows, :] = nn(mixed_ref[rows, :].astype(bf16), wo_ref[...]).astype(bf16)
        out_in = wires.exchange(
            "plane", lambda r, d: out_stage.at[pl.ds(r * seg, seg)], lambda r, d: out_recv.at[r]
        )
        passed()
        passed = gather_step(wires, line.n, 2, pass_once, pass_twice)
        gu_in()
        gu_settle.start()
        s_in()
        s_settle.start()
        out_in()
        for half in range(2):
            parts = out_recv[half * KEY_VALUE_HEADS].astype(f32)
            for j in range(1, KEY_VALUE_HEADS):
                parts = parts + out_recv[half * KEY_VALUE_HEADS + j].astype(f32)
            out_ref[half] = parts
        gu_settle.wait()
        s_settle.wait()
        passed()
    line.leave()
    wires.finish()
    keep.wait()


def spread_shared(wires, gu_ref, s_ref, wgu_ref, ws_ref):
    core, chip, _, _ = place()
    sibling = (1 - core, chip)
    gu_in = wires.exchange(
        "chips",
        lambda r, d: gu_ref.at[r // KEY_VALUE_HEADS],
        lambda r, d: wgu_ref.at[core, r],
    )
    s_in = wires.exchange("inner", lambda r, d: s_ref, lambda r, d: ws_ref.at[core, r])
    gu_settle = wires.remote(wgu_ref.at[core], wgu_ref.at[core], wires.take(1), sibling)
    s_settle = wires.remote(ws_ref.at[core], ws_ref.at[core], wires.take(1), sibling)
    return gu_in, gu_settle, s_in, s_settle


def attend(collective, shards, chunk, q, kv, wo=None, gu=None, down=None, passing=()):
    joined = wo is not None
    n_out = shards // KEY_VALUE_HEADS
    rows = 2 * chunk
    seg = chunk // KEY_VALUE_HEADS
    more_outs, more_scratch = [], []
    if joined:
        wide = wo.shape[1]
        block = jax.ShapeDtypeStruct(passing[0].shape, bf16)
        more_outs = [
            jax.ShapeDtypeStruct((2, seg, wide), f32),
            jax.ShapeDtypeStruct((2, shards) + gu.shape[1:], bf16),
            jax.ShapeDtypeStruct((2, KEY_VALUE_HEADS) + down.shape, bf16),
        ] + [block] * 4
        more_scratch = [
            pltpu.VMEM((rows, wide), bf16),
            pltpu.VMEM((2 * KEY_VALUE_HEADS, seg, wide), bf16),
        ]
    kv_shape = (n_out,) + kv.shape
    vmem = pl.BlockSpec(memory_space=pltpu.VMEM)
    hbm = pl.BlockSpec(memory_space=pl.ANY)
    state = (GROUP_MEMBERS, 2, 1, chunk)
    return pl.pallas_call(
        functools.partial(attend_kernel, shards, chunk, joined),
        in_specs=[vmem, hbm] + [vmem, hbm, hbm, hbm, hbm] * joined,
        out_specs=[vmem, vmem, hbm] + ([vmem] + [hbm] * 6) * joined,
        out_shape=[
            jax.ShapeDtypeStruct((rows, GROUP_MEMBERS * HEAD_SIZE), f32),
            jax.ShapeDtypeStruct((GROUP_MEMBERS, 2, chunk), f32),
            jax.ShapeDtypeStruct(kv_shape, bf16),
        ]
        + more_outs,
        scratch_shapes=more_scratch
        + [
            pltpu.VMEM(kv_shape, bf16),
            pltpu.VMEM(state, f32),
            pltpu.VMEM(state, f32),
            pltpu.VMEM((GROUP_MEMBERS, 2, HEAD_SIZE, chunk), f32),
        ]
        + [pltpu.SemaphoreType.DMA((2 * n_out + shards + 32,))] * 3,
        compiler_params=pltpu.CompilerParams(
            collective_id=collective, has_side_effects=True, vmem_limit_bytes=VMEM_LIMIT
        ),
        name="attend",
    )(q, kv, *((wo, gu, down, *passing) if joined else ()))


def attend_back_kernel(shards, chunk, own_rows, *refs):
    q_ref, kv_ref, grad_ref, log_ref, delta_ref, wo_ref, *refs = refs
    dqkv_ref, wo_other, *refs = refs
    came, stage, sums, dq_sums, send_sems, recv_sems, local_sems = refs
    wires = Wires(shards, send_sems, recv_sems, local_sems)
    core, chip, outer, inner = place()
    n = kv_ref.shape[0]
    scale = HEAD_SIZE**-0.5
    factor = scale * math.log2(math.e)
    wires.greet(["outer", "core"])
    wo_in = wires.sibling(
        wo_ref.at[pl.ds((1 - core) * own_rows, own_rows)], wo_other, wo_other
    )
    send_base, recv_base = wires.take(n), wires.take(n)
    dq_sums[...] = jnp.zeros_like(dq_sums)

    def pair(head, half, block, key_half, masked):
        cols = pl.ds(pl.multiple_of(head * HEAD_SIZE, HEAD_SIZE), HEAD_SIZE)
        mine, rows = pl.ds(half * chunk, chunk), pl.ds(key_half * chunk, chunk)
        query, grad = q_ref[mine, cols], grad_ref[mine, cols]
        key = kv_ref[block, rows, 0:HEAD_SIZE]
        value = kv_ref[block, rows, HEAD_SIZE : 2 * HEAD_SIZE]
        scores = nt(key, query)
        if masked:
            scores = causal(scores)
        weights = jnp.exp2(scores * factor - log_ref[head, half : half + 1, :])
        grad_scores = (
            weights * (nt(value, grad) - delta_ref[head, half : half + 1, :])
        ).astype(bf16)
        sums[rows, 0:HEAD_SIZE] += nn(grad_scores, query)
        sums[rows, HEAD_SIZE : 2 * HEAD_SIZE] += nn(weights.astype(bf16), grad)
        dq_sums[mine, cols] += tn(grad_scores, key)

    def send(k, block):
        return pltpu.make_async_remote_copy(
            src_ref=stage.at[k],
            dst_ref=came.at[outer],
            send_sem=send_sems.at[send_base + k],
            recv_sem=recv_sems.at[recv_base + outer],
            device_id=(core, block * KEY_VALUE_HEADS + inner),
            device_id_type=MESH,
        )

    order = far_first(outer, n)
    for k, block in enumerate(order + [outer]):
        sums[...] = jnp.zeros_like(sums)
        each_pair(block, outer, k == n - 1, pair)
        if k < n - 1:
            stage[k] = sums[...].astype(bf16)
            send(k, block).start()
    width = GROUP_MEMBERS * HEAD_SIZE
    dqkv_ref[:, 0:width] = (dq_sums[...] * scale).astype(bf16)
    for d in range(1, n):
        origin = lax.rem(outer + d, n)
        pltpu.make_async_remote_copy(
            src_ref=came.at[origin],
            dst_ref=came.at[origin],
            send_sem=send_sems.at[send_base],
            recv_sem=recv_sems.at[recv_base + origin],
            device_id=(core, origin * KEY_VALUE_HEADS + inner),
            device_id_type=MESH,
        ).wait_recv()
        sums[...] += came[origin].astype(f32)
    dqkv_ref[:, width : width + HEAD_SIZE] = (sums[:, 0:HEAD_SIZE] * scale).astype(bf16)
    dqkv_ref[:, width + HEAD_SIZE :] = sums[:, HEAD_SIZE:].astype(bf16)
    for k, block in enumerate(order):
        send(k, block).wait_send()
    wo_in()
    wires.finish()


def attend_back(collective, shards, chunk, q, kv_all, grad_mixed, log_rows, delta_rows, wo_grad):
    n_out, rows, kv_cols = kv_all.shape
    own_rows = wo_grad.shape[0] // 2
    vmem = pl.BlockSpec(memory_space=pltpu.VMEM)
    hbm = pl.BlockSpec(memory_space=pl.ANY)
    width = GROUP_MEMBERS * HEAD_SIZE
    return pl.pallas_call(
        functools.partial(attend_back_kernel, shards, chunk, own_rows),
        in_specs=[vmem] * 5 + [hbm],
        out_specs=[vmem, hbm],
        out_shape=[
            jax.ShapeDtypeStruct((rows, width + kv_cols), bf16),
            jax.ShapeDtypeStruct((own_rows,) + wo_grad.shape[1:], bf16),
        ],
        scratch_shapes=[
            pltpu.VMEM(kv_all.shape, bf16),
            pltpu.VMEM(kv_all.shape, bf16),
            pltpu.VMEM((rows, kv_cols), f32),
            pltpu.VMEM((rows, width), f32),
        ]
        + [pltpu.SemaphoreType.DMA((2 * n_out + 8,))] * 3,
        compiler_params=pltpu.CompilerParams(
            collective_id=collective, has_side_effects=True, vmem_limit_bytes=VMEM_LIMIT
        ),
        name="attend_back",
    )(q, kv_all, grad_mixed, log_rows, delta_rows, wo_grad)


def finish_kernel(shards, chunk, gain_col, *refs):
    (
        q_ref,
        kv_ref,
        grad_ref,
        wo_ref,
        mixed_ref,
        log_ref,
        h1_ref,
        wq_ref,
        gain_ref,
        small_ref,
        sd_ref,
        mix_ref,
        mix_up,
        mix_down,
        e_ref,
        dh1_out,
        wq_out,
        small_out,
        wo_out,
        sd_out,
        mix_up_out,
        mix_down_out,
        e_mine,
        e_other,
        dmixed,
        delta,
        came,
        stage,
        sums,
        dq_sums,
        dqkv,
        dwo,
        wo_came,
        wo_half,
        wo_recv,
        dwq,
        wq_came,
        wq_half,
        wq_recv,
        small_all,
        small_came,
        small_half,
        small_recv,
        dh_stage,
        dh_recv,
        sd_recv,
        mix_came,
        mix_term,
        e_came,
        e_term,
        e_last,
        e_own,
        send_sems,
        recv_sems,
        local_sems,
    ) = refs
    wires = Wires(shards, send_sems, recv_sems, local_sems)
    core, chip, outer, inner = place()
    n = kv_ref.shape[0]
    scale = HEAD_SIZE**-0.5
    factor = scale * math.log2(math.e)
    width = GROUP_MEMBERS * HEAD_SIZE
    wide = h1_ref.shape[1]
    half_wide = wide // 2
    w_rows = wq_recv.shape[1]
    seg = dh_recv.shape[1]
    mine, other = pl.ds(core * half_wide, half_wide), pl.ds((1 - core) * half_wide, half_wide)
    wires.greet(["all"])
    mix_first = sum_step(
        wires, n, 1, [mix_up, mix_down], [mix_came.at[0], mix_came.at[1]]
    )
    mix_own = [
        wires.local(mix_ref.at[slot], mix_term.at[way], wires.take(1))
        for way, slot in enumerate((3 % n, (n - 3) % n))
    ]
    for copy in mix_own:
        copy.start()
    sd_in = wires.exchange("plane", lambda r, d: sd_ref.at[r], lambda r, d: sd_recv.at[r])

    e_cols = e_ref.shape[2] // 2
    e_cuts = (pl.ds(0, e_cols), pl.ds(e_cols, e_cols))
    e_sides = ((1, 2), (2, 1))

    def plane_device(step):
        return core, outer * KEY_VALUE_HEADS + across(inner, step)

    e_local, e_first, e_second = wires.take(3), wires.take(4), wires.take(2)
    e_loads = [wires.local(e_ref.at[0], e_own, e_local)]
    e_sends = []
    for way, (near, far) in enumerate(e_sides):
        e_loads.append(wires.local(e_ref.at[far, :, e_cuts[way]], e_term.at[way], e_local + 1 + way))
        for k, e in enumerate((near, 3)):
            e_sends.append(
                wires.remote(
                    e_ref.at[e, :, e_cuts[way]],
                    e_came.at[way, k],
                    e_first + 2 * way + k,
                    plane_device(near),
                )
            )
    for copy in e_sends + e_loads:
        copy.start()

    for half in range(2):
        rows = pl.ds(half * chunk, chunk)
        part = nt(grad_ref[rows, :], wo_ref[...]).astype(bf16)
        dmixed[rows, :] = part
        weighted = part.astype(f32) * mixed_ref[rows, :]
        for head in range(GROUP_MEMBERS):
            cols = slice(head * HEAD_SIZE, (head + 1) * HEAD_SIZE)
            delta[head, half] = jnp.sum(weighted[:, cols].T, axis=0, keepdims=True)

    send_base, recv_base = wires.take(n), wires.take(n)
    dq_sums[...] = jnp.zeros_like(dq_sums)

    def pair(head, half, block, key_half, masked):
        cols = pl.ds(pl.multiple_of(head * HEAD_SIZE, HEAD_SIZE), HEAD_SIZE)
        here, rows = pl.ds(half * chunk, chunk), pl.ds(key_half * chunk, chunk)
        query, grad = q_ref[here, cols], dmixed[here, cols]
        key = kv_ref[block, rows, 0:HEAD_SIZE]
        value = kv_ref[block, rows, HEAD_SIZE : 2 * HEAD_SIZE]
        scores = nt(key, query)
        if masked:
            scores = causal(scores)
        weights = jnp.exp2(scores * factor - log_ref[head, half : half + 1, :])
        grad_scores = (weights * (nt(value, grad) - delta[head, half])).astype(bf16)
        sums[rows, 0:HEAD_SIZE] += nn(grad_scores, query)
        sums[rows, HEAD_SIZE : 2 * HEAD_SIZE] += nn(weights.astype(bf16), grad)
        dq_sums[here, cols] += tn(grad_scores, key)

    def send(k, block):
        return pltpu.make_async_remote_copy(
            src_ref=stage.at[k],
            dst_ref=came.at[outer],
            send_sem=send_sems.at[send_base + k],
            recv_sem=recv_sems.at[recv_base + outer],
            device_id=(core, block * KEY_VALUE_HEADS + inner),
            device_id_type=MESH,
        )

    order = far_first(outer, n)
    for k, block in enumerate(order + [outer]):
        sums[...] = jnp.zeros_like(sums)
        each_pair(block, outer, k == n - 1, pair)
        if k < n - 1:
            stage[k] = sums[...].astype(bf16)
            send(k, block).start()

    dqkv[:, 0:width] = (dq_sums[...] * scale).astype(bf16)
    dwo[...] = tn(mixed_ref[...].astype(bf16), grad_ref[...]).astype(bf16)
    wo_rows = wo_half.shape[0]
    wo_in = wires.sibling(dwo.at[pl.ds((1 - core) * wo_rows, wo_rows)], wo_came, wo_came)
    dwq[:, 0:width] = tn(h1_ref[...], dqkv[:, 0:width]).astype(bf16)
    q_cols = pl.ds(0, width)
    q_in = wires.sibling(dwq.at[other, q_cols], wq_came.at[:, q_cols], wq_came.at[:, q_cols])
    wo_in()
    wo_half[...] = (
        dwo[pl.ds(core * wo_rows, wo_rows), :].astype(f32) + wo_came[...].astype(f32)
    ).astype(bf16)
    wo_parts = out_rows_back(wires, shards, wo_half, wo_recv)
    q_in()
    wq_half[:, 0:width] = (
        dwq[mine, 0:width].astype(f32) + wq_came[:, 0:width].astype(f32)
    ).astype(bf16)

    def pieces(cols):
        return wires.exchange(
            "chips",
            lambda r, d: wq_half.at[pl.ds(r * w_rows, w_rows), cols],
            lambda r, d: wq_recv.at[r, :, cols],
        )

    q_parts = pieces(q_cols)

    for copy in e_sends:
        copy.wait()
    for copy in e_loads:
        copy.wait()
    e_passed = []
    for way, (near, far) in enumerate(e_sides):
        e_term[way] = (e_term[way].astype(f32) + e_came[way, 1].astype(f32)).astype(bf16)
        e_passed.append(
            wires.remote(e_term.at[way], e_last.at[way], e_second + way, plane_device(far))
        )
    for copy in e_passed:
        copy.start()

    for d in range(1, n):
        origin = lax.rem(outer + d, n)
        pltpu.make_async_remote_copy(
            src_ref=came.at[origin],
            dst_ref=came.at[origin],
            send_sem=send_sems.at[send_base],
            recv_sem=recv_sems.at[recv_base + origin],
            device_id=(core, origin * KEY_VALUE_HEADS + inner),
            device_id_type=MESH,
        ).wait_recv()
        sums[...] += came[origin].astype(f32)
    dqkv[:, width : width + HEAD_SIZE] = (sums[:, 0:HEAD_SIZE] * scale).astype(bf16)
    dqkv[:, width + HEAD_SIZE :] = sums[:, HEAD_SIZE:].astype(bf16)

    gain_sum = jnp.zeros((1, wide), f32)
    for half in range(2):
        rows = pl.ds(half * chunk, chunk)
        part = nt(dqkv[rows, :], wq_ref[...]).astype(bf16)
        dh_stage[rows, :] = part
        gain_sum = gain_sum + jnp.sum(
            part.astype(f32) * h1_ref[rows, :].astype(f32), axis=0, keepdims=True
        )
    dh_in = wires.exchange(
        "plane", lambda r, d: dh_stage.at[pl.ds(r * seg, seg)], lambda r, d: dh_recv.at[r]
    )
    dwq[:, width:] = tn(h1_ref[...], dqkv[:, width:]).astype(bf16)
    kv_cols = pl.ds(width, 2 * HEAD_SIZE)
    kv_in = wires.sibling(dwq.at[other, kv_cols], wq_came.at[:, kv_cols], wq_came.at[:, kv_cols])
    column = (gain_sum / gain_ref[...])
    columns = jnp.broadcast_to(column, (small_all.shape[1], wide)).T
    at_col = lax.broadcasted_iota(jnp.int32, columns.shape, 1)
    small_all[...] = jnp.where(at_col == gain_col, columns, small_ref[...].astype(f32)).astype(bf16)
    small_in = wires.sibling(small_all.at[other], small_came, small_came)
    kv_in()
    wq_half[:, width:] = (
        dwq[mine, width:].astype(f32) + wq_came[:, width:].astype(f32)
    ).astype(bf16)
    kv_parts = pieces(kv_cols)
    small_in()
    small_half[...] = (small_all[mine, :].astype(f32) + small_came[...].astype(f32)).astype(bf16)
    small_parts = wires.exchange(
        "chips",
        lambda r, d: small_half.at[pl.ds(r * w_rows, w_rows)],
        lambda r, d: small_recv.at[r],
    )
    mix_first()
    for way, copy in enumerate(mix_own):
        copy.wait()
        inside = (outer > 0, outer < n - 1)[way]
        mix_term[way] = (
            mix_term[way].astype(f32) + jnp.where(inside, mix_came[way].astype(f32), 0.0)
        ).astype(bf16)
    mix_last = sum_step(
        wires, n, 2, [mix_term.at[0], mix_term.at[1]], [mix_up_out, mix_down_out]
    )

    for way, copy in enumerate(e_passed):
        copy.wait()
        e_own[:, e_cuts[way]] = (
            e_own[:, e_cuts[way]].astype(f32)
            + e_came[way, 0].astype(f32)
            + e_last[way].astype(f32)
        ).astype(bf16)
    e_keep = wires.local(e_own, e_mine, e_local)
    e_keep.start()
    e_in = wires.sibling(e_own, e_other, e_other)
    sd_in()
    sd_out[...] = jnp.sum(sd_recv[...].astype(f32), axis=0)
    wo_parts()
    wo_out[...] = jnp.sum(wo_recv[...].astype(f32), axis=0)
    q_parts()
    kv_parts()
    for j in range(KEY_VALUE_HEADS):
        total = wq_recv[j].astype(f32)
        for k in range(1, n):
            total = total + wq_recv[k * KEY_VALUE_HEADS + j].astype(f32)
        wq_out[j] = total
    small_parts()
    small_out[...] = jnp.sum(small_recv[...].astype(f32), axis=0)
    dh_in()
    for core_half in range(2):
        total = dh_recv[core_half * KEY_VALUE_HEADS].astype(f32)
        for j in range(1, KEY_VALUE_HEADS):
            total = total + dh_recv[core_half * KEY_VALUE_HEADS + j].astype(f32)
        dh1_out[core_half] = total
    mix_last()
    e_in()
    e_keep.wait()
    for k, block in enumerate(order):
        send(k, block).wait_send()
    wires.finish()


def finish(
    collective,
    shards,
    chunk,
    gain_col,
    q,
    kv_all,
    grad_all,
    wo,
    mixed,
    log_rows,
    h1,
    wq,
    gain_row,
    small_grad,
    sd_send,
    mix_part,
    mix_terms,
    e_sum,
):
    n, rows, kv_cols = kv_all.shape
    width, wide = wo.shape
    cols = wq.shape[1]
    small = small_grad.shape[1]
    n_in = KEY_VALUE_HEADS
    seg = rows // (2 * n_in)
    w_rows = wide // (2 * shards)
    d_rows = sd_send.shape[1]
    block = mix_part.shape[1:]
    vmem = pl.BlockSpec(memory_space=pltpu.VMEM)
    hbm = pl.BlockSpec(memory_space=pl.ANY)

    def array(shape, kind=bf16):
        return jax.ShapeDtypeStruct(shape, kind)

    scratch = [
        ((rows, width), bf16),
        ((GROUP_MEMBERS, 2, 1, chunk), f32),
        (kv_all.shape, bf16),
        (kv_all.shape, bf16),
        ((rows, kv_cols), f32),
        ((rows, width), f32),
        ((rows, cols), bf16),
        ((width, wide), bf16),
        ((width // 2, wide), bf16),
        ((width // 2, wide), bf16),
        ((n, w_rows, wide), bf16),
        ((wide, cols), bf16),
        ((wide // 2, cols), bf16),
        ((wide // 2, cols), bf16),
        ((shards, w_rows, cols), bf16),
        ((wide, small), bf16),
        ((wide // 2, small), bf16),
        ((wide // 2, small), bf16),
        ((shards, w_rows, small), bf16),
        ((rows, wide), bf16),
        ((2 * n_in, seg, wide), bf16),
        ((2 * n_in, d_rows, wide), bf16),
        ((2,) + block, bf16),
        ((2,) + block, bf16),
        ((2, 2, e_sum.shape[1], e_sum.shape[2] // 2), bf16),
        ((2, e_sum.shape[1], e_sum.shape[2] // 2), bf16),
        ((2, e_sum.shape[1], e_sum.shape[2] // 2), bf16),
        (e_sum.shape[1:], bf16),
    ]
    return pl.pallas_call(
        functools.partial(finish_kernel, shards, chunk, gain_col),
        in_specs=[vmem] * 10 + [hbm] * 5,
        out_specs=[vmem] * 5 + [hbm] * 4,
        out_shape=[
            array((2, seg, wide), f32),
            array((n_in, w_rows, cols), f32),
            array((w_rows, small), f32),
            array((w_rows, wide), f32),
            array((d_rows, wide), f32),
            array(block),
            array(block),
            array(e_sum.shape[1:]),
            array(e_sum.shape[1:]),
        ],
        scratch_shapes=[pltpu.VMEM(shape, kind) for shape, kind in scratch]
        + [pltpu.SemaphoreType.DMA((6 * shards + 64,))] * 3,
        compiler_params=pltpu.CompilerParams(
            collective_id=collective, has_side_effects=True, vmem_limit_bytes=VMEM_LIMIT
        ),
        name="finish",
    )(
        q,
        kv_all,
        grad_all,
        wo,
        mixed,
        log_rows,
        h1,
        wq,
        gain_row,
        small_grad,
        sd_send,
        mix_part,
        *mix_terms,
        e_sum,
    )


def swiglu_parts(gate_part, up_part):
    sigmoid = jax.nn.sigmoid(gate_part)
    active = gate_part * sigmoid
    slope = up_part * sigmoid * (1.0 + gate_part * (1.0 - sigmoid))
    return active * up_part, active, slope


def experts_kernel(
    room,
    hidden,
    h_ref,
    c_ref,
    meta_ref,
    wg_ref,
    wu_ref,
    wd_ref,
    sgu_ref,
    sd_ref,
    out_ref,
    dh_ref,
    dgate_ref,
    dw_ref,
    dsgu_ref,
    dsd_ref,
    sum_out,
    sum_dh,
    h_rows,
    c_rows,
    picks,
    gate_col,
):
    expert = pl.program_id(0)
    inner = lax.rem(lax.axis_index("fsdp"), KEY_VALUE_HEADS)
    at = across(inner, expert)
    blocks, rows, width = h_ref.shape

    @pl.when(expert == 0)
    def _():
        dgate_ref[...] = jnp.zeros_like(dgate_ref)
        hid = h_ref[...].reshape(blocks * rows, width)
        cot = c_ref[...].reshape(blocks * rows, width)
        gate_w, up_w, down_w = sgu_ref[:, 0:hidden], sgu_ref[:, hidden : 2 * hidden], sd_ref[...]
        both, active, slope = swiglu_parts(nn(hid, gate_w), nn(hid, up_w))
        act = both.astype(bf16)
        d_act = nt(cot, down_w)
        d_gate = (d_act * slope).astype(bf16)
        d_up = (d_act * active).astype(bf16)
        sum_out[...] = nn(act, down_w)
        sum_dh[...] = nt(d_gate, gate_w) + nt(d_up, up_w)
        dsgu_ref[:, 0:hidden] = tn(hid, d_gate).astype(bf16)
        dsgu_ref[:, hidden : 2 * hidden] = tn(hid, d_up).astype(bf16)
        dsd_ref[...] = tn(act, cot).astype(bf16)

    slots = lax.broadcasted_iota(jnp.int32, (room, rows), 0).astype(f32)
    for block in range(blocks):
        part = pl.ds(block * room, room)
        gate_row = meta_ref[block, pl.ds(at, 1), :]
        slot_row = meta_ref[block, pl.ds(at + KEY_VALUE_HEADS, 1), :]
        pick = (slots == slot_row).astype(f32)
        gate_col[part, :] = jnp.broadcast_to(
            jnp.sum(pick * gate_row, axis=1, keepdims=True), (room, gate_col.shape[1])
        )
        pick = pick.astype(bf16)
        picks[block] = pick
        h_rows[part, :] = nn(pick, h_ref[block]).astype(bf16)
        c_rows[part, :] = nn(pick, c_ref[block]).astype(bf16)
    gate = gate_col[:, 0:1]
    gate_w, up_w, down_w = wg_ref[0], wu_ref[0], wd_ref[0]
    both, active, slope = swiglu_parts(nn(h_rows[...], gate_w), nn(h_rows[...], up_w))
    act = both.astype(bf16)
    d_act = nt(c_rows[...], down_w)
    d_gates = jnp.sum(d_act * act.astype(f32), axis=1, keepdims=True)
    d_act = d_act * gate
    act = (act.astype(f32) * gate).astype(bf16)
    d_gate = (d_act * slope).astype(bf16)
    d_up = (d_act * active).astype(bf16)
    ff = act.shape[1]
    dw_ref[0, :, 0:ff] = tn(h_rows[...], d_gate).astype(bf16)
    dw_ref[0, :, ff : 2 * ff] = tn(h_rows[...], d_up).astype(bf16)
    dw_ref[0, :, 2 * ff : 3 * ff] = tn(c_rows[...], act).astype(bf16)
    result = nn(act, down_w).astype(bf16)
    d_rows = (nt(d_gate, gate_w) + nt(d_up, up_w)).astype(bf16)
    for block in range(blocks):
        pick = picks[block]
        part = slice(block * room, (block + 1) * room)
        here = pl.ds(block * rows, rows)
        sum_out[here, :] += tn(pick, result[part])
        sum_dh[here, :] += tn(pick, d_rows[part])
        dgate_ref[block, pl.ds(at, 1), :] = jnp.sum(
            pick.astype(f32) * d_gates[part], axis=0, keepdims=True
        )

    @pl.when(expert == pl.num_programs(0) - 1)
    def _():
        out_ref[...] = sum_out[...].astype(bf16).reshape(out_ref.shape)
        dh_ref[...] = sum_dh[...].astype(bf16).reshape(dh_ref.shape)


def experts(room, hidden, h_all, c_all, meta, wg, wu, wd, sgu, sd):
    blocks, rows, width = h_all.shape
    n_experts, _, inner = wg.shape

    def once(shape):
        return pl.BlockSpec(shape, lambda e: (0,) * len(shape), pipeline_mode=pl.Buffered(1))

    def each(shape, **kind):
        return pl.BlockSpec((1,) + shape[1:], lambda e: (e, 0, 0), **kind)

    single = dict(pipeline_mode=pl.Buffered(1))
    return pl.pallas_call(
        functools.partial(experts_kernel, room, hidden),
        grid=(n_experts,),
        in_specs=[
            once(h_all.shape),
            once(c_all.shape),
            once(meta.shape),
            each(wg.shape),
            each(wu.shape),
            each(wd.shape),
            once(sgu.shape),
            once(sd.shape),
        ],
        out_specs=[
            once(h_all.shape),
            once(h_all.shape),
            once(meta.shape),
            pl.BlockSpec((1, width, 3 * inner), lambda e: (e, 0, 0), **single),
            once(sgu.shape),
            once(sd.shape),
        ],
        out_shape=[
            jax.ShapeDtypeStruct(h_all.shape, bf16),
            jax.ShapeDtypeStruct(h_all.shape, bf16),
            jax.ShapeDtypeStruct(meta.shape, f32),
            jax.ShapeDtypeStruct((n_experts, width, 3 * inner), bf16),
            jax.ShapeDtypeStruct(sgu.shape, bf16),
            jax.ShapeDtypeStruct(sd.shape, bf16),
        ],
        scratch_shapes=[
            pltpu.VMEM((blocks * rows, width), f32),
            pltpu.VMEM((blocks * rows, width), f32),
            pltpu.VMEM((blocks * room, width), bf16),
            pltpu.VMEM((blocks * room, width), bf16),
            pltpu.VMEM((blocks, room, rows), bf16),
            pltpu.VMEM((blocks * room, 128), f32),
        ],
        compiler_params=pltpu.CompilerParams(vmem_limit_bytes=VMEM_LIMIT),
        name="experts",
    )(h_all, c_all, meta, wg, wu, wd, sgu, sd)


def experts_line_kernel(room, hidden, shards, refs):
    n = shards // KEY_VALUE_HEADS
    h_ref, meta_ref = refs[:2]
    c_refs = refs[2 : 1 + 2 * n]
    (
        wg_ref,
        wu_ref,
        wd_ref,
        side_x,
        side_y,
        sgu_ref,
        sd_ref,
        dh_out,
        dgate_out,
        mix_out,
        e_mine,
        e_other,
        gu_mine,
        gu_other,
        dsd_ref,
        h_all,
        c_all,
        metas,
        wgu,
        wd,
        picks,
        kept_gu,
        kept_act,
        kept_shared,
        row_a,
        row_b,
        own_a,
        own_b,
        dh_stage,
        mix_stage,
        dg_stage,
        down_stage,
        gu_stage,
        send_sems,
        recv_sems,
        local_sems,
    ) = refs[1 + 2 * n :]
    wires = Wires(shards, send_sems, recv_sems, local_sems)
    core, chip, outer, inner = place()
    rows, width = h_ref.shape
    ff = wd.shape[1]
    experts_here = KEY_VALUE_HEADS

    own_h = wires.local(h_ref, h_all.at[outer], wires.take(1))
    own_meta = wires.local(meta_ref.at[outer], metas.at[outer], wires.take(1))
    own_h.start()
    own_meta.start()
    c_own = wires.local(c_refs[0], c_all.at[outer], wires.take(1))
    c_base = wires.take(2 * n - 2)

    def c_each(action):
        for k in range(2 * n - 2):
            block = outer - 1 - k if k < n - 1 else outer + 1 + k - (n - 1)

            def one(k=k, block=block):
                at = lax.rem(block + n, n)
                action(wires.local(c_refs[1 + k], c_all.at[at], c_base + k))

            pl.when((block >= 0) & (block < n))(one)

    deep, tall = ff // 2, width // 2
    own_weights = (
        wires.local(wg_ref.at[0], wgu.at[0, :, pl.ds(0, ff)], wires.take(1)),
        wires.local(wu_ref.at[0], wgu.at[0, :, pl.ds(ff, ff)], wires.take(1)),
        wires.local(wd_ref.at[0], wd.at[0], wires.take(1)),
    )

    def half_places(e, first_col, cols, of_core):
        found = [
            wgu.at[e, pl.ds(of_core * tall, tall), pl.ds(k * ff + first_col, cols)]
            for k in range(2)
        ]
        found += [
            wd.at[e, pl.ds(of_core * deep, deep), pl.ds(k * ff + first_col, cols)]
            for k in range(width // ff)
        ]
        return found

    def half_sources(source, first_col, cols):
        starts = [(k * tall, tall) for k in range(2)]
        starts += [(2 * tall + k * deep, deep) for k in range(width // ff)]
        return [source.at[pl.ds(at, size), pl.ds(first_col, cols)] for at, size in starts]

    per_half = 2 + width // ff
    sides = ((1, side_x, 0, ff), (2, side_y, 0, ff), (3, side_x, 0, ff // 2), (3, side_y, ff // 2, ff // 2))
    half_sems = [wires.take(per_half) for _ in sides]
    cross_sems = [wires.take(per_half) for _ in range(2)]

    def half_local(which):
        e, source, first_col, cols = sides[which]
        return [
            wires.local(here, there, half_sems[which] + k)
            for k, (here, there) in enumerate(
                zip(half_sources(source, first_col, cols), half_places(e, first_col, cols, core))
            )
        ]

    def half_remote(which, of_core):
        e, source, first_col, cols = sides[which]
        places = half_places(e, first_col, cols, of_core)
        here = half_sources(source, first_col, cols) if which < 2 else places
        return [
            wires.remote(here[k], places[k], half_sems[which] + k, (1 - core, chip))
            for k in range(per_half)
        ]

    def cross_remote(which):
        _, source, first_col, cols = sides[2 + which]
        return [
            wires.remote(
                here,
                there,
                cross_sems[which] + k,
                (core, outer * KEY_VALUE_HEADS + across(inner, 2 - which)),
            )
            for k, (here, there) in enumerate(
                zip(half_sources(source, first_col, cols), half_places(3, first_col, cols, core))
            )
        ]

    c_own.start()
    for copy in own_weights:
        copy.start()
    for which in range(2):
        for copy in half_local(which):
            copy.start()
    c_each(lambda copy: copy.start())

    wires.greet(["outer", "plane"])

    line = Line(wires, h_ref, h_all)
    device = line.device
    line.start(0)
    for which in range(2):
        for copy in cross_remote(which):
            copy.start()
    for which in range(2):
        for copy in half_remote(which, core):
            copy.start()
    meta_in = wires.exchange(
        "outer", lambda r, d: meta_ref.at[r], lambda r, d: metas.at[r], own=False
    )

    dh_send, dh_recv = wires.take(n), wires.take(n)
    dg_send, dg_recv = wires.take(n), wires.take(n)

    def give_back(stage, target, k, block, sends, receives):
        return pltpu.make_async_remote_copy(
            src_ref=stage,
            dst_ref=target.at[outer],
            send_sem=send_sems.at[sends + k],
            recv_sem=recv_sems.at[receives + outer],
            device_id=device(block),
            device_id_type=MESH,
        )

    def take_back(target, origin, receives):
        return pltpu.make_async_remote_copy(
            src_ref=target.at[origin],
            dst_ref=target.at[origin],
            send_sem=send_sems.at[receives],
            recv_sem=recv_sems.at[receives + origin],
            device_id=device(origin),
            device_id_type=MESH,
        )

    dh_own = wires.local(dh_stage.at[n - 1], dh_out.at[outer], wires.take(1))
    dg_own = wires.local(dg_stage.at[n - 1], dgate_out.at[outer], wires.take(1))
    mix_base = wires.take(n)

    def mix_copy(k, block):
        return wires.local(
            mix_stage.at[k % 2], mix_out.at[lax.rem(outer - block + n, n)], mix_base + k
        )

    slots = lax.broadcasted_iota(jnp.int32, (room, rows), 0).astype(f32)
    order = line.order()
    gate_w, up_w, down_w = sgu_ref[:, 0:hidden], sgu_ref[:, hidden : 2 * hidden], sd_ref[...]

    def choose(k, block, left, right):
        for e in range(experts_here):
            at = across(inner, e)
            slot_row = metas[block, pl.ds(at + experts_here, 1), :]
            picks[block, pl.ds(e * room, room), :] = (slots == slot_row).astype(bf16)
        left[...] = nn(picks[block], h_all[block]).astype(bf16)
        right[...] = nn(picks[block], c_all[block]).astype(bf16)
        dg_stage[k] = jnp.zeros(dg_stage.shape[1:], f32)

    def one_expert(e, k, block, left, right):
        at = across(inner, e)
        part = pl.ds(pl.multiple_of(e * room, 16), room)
        pick = picks[block, part, :].astype(f32)
        gate = jnp.sum(pick * metas[block, pl.ds(at, 1), :], axis=1, keepdims=True)
        first = nn(left[part, :], wgu[e])
        both, active, slope = swiglu_parts(first[:, 0:ff], first[:, ff : 2 * ff])
        act = both.astype(bf16)
        d_act = nt(right[part, :], wd[e])
        d_gates = jnp.sum(d_act * act.astype(f32), axis=1, keepdims=True)
        dg_stage[k, pl.ds(at, 1), :] = jnp.sum(pick * d_gates, axis=0, keepdims=True)
        d_act = d_act * gate
        act = (act.astype(f32) * gate).astype(bf16)
        here = pl.ds(pl.multiple_of(block * room, 16), room)
        kept_act[e, here, :] = act
        kept_gu[e, here, 0:ff] = (d_act * slope).astype(bf16)
        kept_gu[e, here, ff : 2 * ff] = (d_act * active).astype(bf16)
        left[part, :] = nn(act, wd[e]).astype(bf16)
        right[part, :] = nt(kept_gu[e, here, :], wgu[e]).astype(bf16)

    def some_experts(begin, end, k, block, left, right):
        def one(e, carry):
            one_expert(e, k, block, left, right)
            return carry

        lax.fori_loop(begin, end, one, 0)

    order = order[1:] + order[:1]
    last = n - 1
    own_h.wait()
    own_meta.wait()
    c_own.wait()
    choose(last, outer, own_a, own_b)
    for copy in own_weights:
        copy.wait()
    one_expert(0, last, outer, own_a, own_b)
    for which in range(2):
        for copy in half_local(which):
            copy.wait()
        for copy in half_remote(which, 1 - core):
            copy.wait_recv()
    some_experts(1, experts_here - 1, last, outer, own_a, own_b)

    for k, block in enumerate(order):
        if k < last:
            line.arrive(k)
            if k < last - 1:
                line.start(k + 1)
        if k == 0:
            meta_in()
            c_each(lambda copy: copy.wait())
        left, right = (row_a, row_b) if k < last else (own_a, own_b)
        hid, cot = h_all[block], c_all[block]
        if k < last:
            choose(k, block, left, right)
        if k == 0:
            some_experts(0, experts_here - 1, k, block, left, right)
            for which in range(2):
                for copy in cross_remote(which):
                    copy.wait_recv()
                for copy in half_remote(2 + which, core):
                    copy.start()
            for which in range(2):
                for copy in half_remote(2 + which, 1 - core):
                    copy.wait_recv()
            some_experts(experts_here - 1, experts_here, k, block, left, right)
        elif k < last:
            some_experts(0, experts_here, k, block, left, right)
        else:
            some_experts(experts_here - 1, experts_here, k, block, left, right)
        both, active, slope = swiglu_parts(nn(hid, gate_w), nn(hid, up_w))
        act = both.astype(bf16)
        d_act = nt(cot, down_w)
        d_gate = (d_act * slope).astype(bf16)
        d_up = (d_act * active).astype(bf16)
        kept_shared[block, :, 0:hidden] = d_gate
        kept_shared[block, :, hidden : 2 * hidden] = d_up
        kept_shared[block, :, 2 * hidden : 3 * hidden] = act
        dh_stage[k] = (
            tn(picks[block], right[...]) + nt(d_gate, gate_w) + nt(d_up, up_w)
        ).astype(bf16)
        if k == n - 1:
            dh_own.start()
            dg_own.start()
        else:
            give_back(dh_stage.at[k], dh_out, k, block, dh_send, dh_recv).start()
            give_back(dg_stage.at[k], dgate_out, k, block, dg_send, dg_recv).start()
        if k >= 2:
            mix_copy(k - 2, order[k - 2]).wait()
        mix_stage[k % 2] = (tn(picks[block], left[...]) + nn(act, down_w)).astype(bf16)
        mix_copy(k, block).start()

    half = width // 2
    mine, other = pl.ds(core * half, half), pl.ds((1 - core) * half, half)
    sibling = (1 - core, chip)
    left, right = pl.ds(0, 2 * ff), pl.ds(2 * ff, ff)
    keep_base, give_base = wires.take(2 * experts_here + 1), wires.take(2 * experts_here + 1)

    def keep(e):
        return (
            wires.local(wgu.at[e, mine, :], e_mine.at[e, :, left], keep_base + 2 * e),
            wires.local(down_stage.at[e % 2, mine, :], e_mine.at[e, :, right], keep_base + 2 * e + 1),
        )

    def give(e):
        return (
            wires.remote(wgu.at[e, other, :], e_other.at[e, :, left], give_base + 2 * e, sibling),
            wires.remote(
                down_stage.at[e % 2, other, :],
                e_other.at[e, :, right],
                give_base + 2 * e + 1,
                sibling,
            ),
        )

    for which in (2, 3):
        for copy in half_remote(which, core):
            copy.wait_send()
    for e in range(experts_here):
        for block in range(n):
            part = pl.ds(block * room, room)
            pick = picks[block, pl.ds(e * room, room), :]
            row_a[part, :] = nn(pick, h_all[block]).astype(bf16)
            row_b[part, :] = nn(pick, c_all[block]).astype(bf16)
        wgu[e] = tn(row_a[...], kept_gu[e]).astype(bf16)
        if e >= 2:
            keep(e - 2)[1].wait()
            give(e - 2)[1].wait_send()
        down_stage[e % 2] = tn(row_b[...], kept_act[e]).astype(bf16)
        for copy in keep(e) + give(e):
            copy.start()
    hid_all = h_all[...].reshape(n * rows, width)
    shared = kept_shared[...].reshape(n * rows, 3 * hidden)
    gu_stage[...] = tn(hid_all, shared[:, 0 : 2 * hidden]).astype(bf16)
    gu_keep = wires.local(gu_stage.at[mine, :], gu_mine, keep_base + 2 * experts_here)
    gu_give = wires.remote(gu_stage.at[other, :], gu_other, give_base + 2 * experts_here, sibling)
    gu_keep.start()
    gu_give.start()
    dsd_ref[...] = tn(shared[:, 2 * hidden :], c_all[...].reshape(n * rows, width)).astype(bf16)

    def settle(e):
        for which, (kept, given) in enumerate(zip(keep(e), give(e))):
            if which == 0 or e >= experts_here - 2:
                kept.wait()
                given.wait_send()
            given.wait_recv()

    line.leave()
    for e in range(experts_here):
        settle(e)

    for which in range(2):
        for copy in half_remote(which, core):
            copy.wait_send()
    for which in range(2):
        for copy in cross_remote(which):
            copy.wait_send()
    dh_own.wait()
    dg_own.wait()
    for k in range(max(0, n - 2), n):
        mix_copy(k, order[k]).wait()
    for k in range(n - 1):
        give_back(dh_stage.at[k], dh_out, k, order[k], dh_send, dh_recv).wait_send()
        give_back(dg_stage.at[k], dgate_out, k, order[k], dg_send, dg_recv).wait_send()
    for d in range(1, n):
        origin = lax.rem(outer + d, n)
        take_back(dh_out, origin, dh_recv).wait_recv()
        take_back(dgate_out, origin, dg_recv).wait_recv()
    gu_keep.wait()
    gu_give.wait()
    wires.finish()


def experts_line(room, hidden, shards, collective, h_own, meta, c_parts, weights, sides, sgu, sd):
    n = shards // KEY_VALUE_HEADS
    rows, width = h_own.shape
    n_experts, ff = KEY_VALUE_HEADS, weights[0].shape[2]
    half = width // 2
    any_spec = pl.BlockSpec(memory_space=pl.ANY)
    vmem = pl.BlockSpec(memory_space=pltpu.VMEM)
    e_shape = (n_experts, half, 3 * ff)
    sems = 112 + 24 * n

    def kernel(*refs):
        experts_line_kernel(room, hidden, shards, refs)

    return pl.pallas_call(
        kernel,
        in_specs=[any_spec] * (2 + len(c_parts) + 3 + len(sides)) + [vmem] * 2,
        out_specs=[any_spec] * 7 + [vmem],
        out_shape=[
            jax.ShapeDtypeStruct((n, rows, width), bf16),
            jax.ShapeDtypeStruct(meta.shape, f32),
            jax.ShapeDtypeStruct((n, rows, width), bf16),
            jax.ShapeDtypeStruct(e_shape, bf16),
            jax.ShapeDtypeStruct(e_shape, bf16),
            jax.ShapeDtypeStruct((half, 2 * hidden), bf16),
            jax.ShapeDtypeStruct((half, 2 * hidden), bf16),
            jax.ShapeDtypeStruct(sd.shape, bf16),
        ],
        scratch_shapes=[
            pltpu.VMEM((n, rows, width), bf16),
            pltpu.VMEM((n, rows, width), bf16),
            pltpu.VMEM(meta.shape, f32),
            pltpu.VMEM((n_experts, width, 2 * ff), bf16),
            pltpu.VMEM((n_experts, ff, width), bf16),
            pltpu.VMEM((n, n_experts * room, rows), bf16),
            pltpu.VMEM((n_experts, n * room, 2 * ff), bf16),
            pltpu.VMEM((n_experts, n * room, ff), bf16),
            pltpu.VMEM((n, rows, 3 * hidden), bf16),
            pltpu.VMEM((n * room, width), bf16),
            pltpu.VMEM((n * room, width), bf16),
            pltpu.VMEM((n * room, width), bf16),
            pltpu.VMEM((n * room, width), bf16),
            pltpu.VMEM((n, rows, width), bf16),
            pltpu.VMEM((2, rows, width), bf16),
            pltpu.VMEM((n,) + meta.shape[1:], f32),
            pltpu.VMEM((2, width, ff), bf16),
            pltpu.VMEM((width, 2 * hidden), bf16),
        ]
        + [pltpu.SemaphoreType.DMA((sems,))] * 3,
        compiler_params=pltpu.CompilerParams(
            collective_id=collective, has_side_effects=True, vmem_limit_bytes=VMEM_LIMIT
        ),
        name="experts_line",
    )(h_own, meta, *c_parts, *weights, *sides, sgu, sd)


def experts_split(room, hidden, shards, collectives, h_own, meta, c_parts, weights, sides, sgu, sd):
    n_out, n_in = shards // KEY_VALUE_HEADS, KEY_VALUE_HEADS
    rows, width = h_own.shape
    core = lax.axis_index("seq")
    half = width // 2

    def spread_hidden(wires, ins, outs):
        waits = [
            wires.exchange("outer", lambda r, d: ins[0], lambda r, d: outs[0].at[d]),
            wires.exchange("outer", lambda r, d: ins[1].at[r], lambda r, d: outs[1].at[d]),
        ]
        waits += [
            wires.exchange(
                "inner",
                lambda r, d, k=k: ins[k].at[0],
                lambda r, d, k=k: outs[k].at[across(r, lax.rem(r + d, n_in))],
            )
            for k in range(2, 5)
        ]
        for wait in waits:
            wait()

    h_all, meta_all, wg, wu, wd = transfer(
        "spread_hidden",
        collectives[0],
        shards,
        ["outer", "inner"],
        2 * n_out + 3 * n_in,
        spread_hidden,
        [h_own, meta, *weights],
        [((n_out, rows, width), bf16), (meta.shape, f32)]
        + [((n_in,) + weight.shape[1:], bf16) for weight in weights],
    )
    c_all = jnp.stack(c_parts)
    at_once = math.gcd(n_out, 4)
    parts = [
        experts(
            room,
            hidden,
            h_all[i : i + at_once],
            c_all[i : i + at_once],
            meta_all[i : i + at_once],
            wg,
            wu,
            wd,
            sgu,
            sd,
        )
        for i in range(0, n_out, at_once)
    ]
    mix_part, dh_part, dgate_part = (
        jnp.concatenate([part[k] for part in parts], axis=0) for k in range(3)
    )
    e_grad, sgu_grad, sd_grad = (
        sum(part[k].astype(f32) for part in parts).astype(bf16) for k in range(3, 6)
    )

    def sum_hidden(wires, ins, outs):
        core = lax.axis_index("seq")
        dh_ref, dg_ref, e_ref, gu_ref = ins
        dhs, dgs, es, gus = outs
        other = pl.ds((1 - core) * half, half)
        waits = [
            wires.exchange(
                "outer", lambda r, d: dh_ref.at[(n_out - d) % n_out], lambda r, d: dhs.at[r]
            ),
            wires.exchange(
                "outer", lambda r, d: dg_ref.at[(n_out - d) % n_out], lambda r, d: dgs.at[r]
            ),
            wires.sibling(e_ref.at[:, other], es, es),
            wires.sibling(gu_ref.at[other], gus, gus),
        ]
        for wait in waits:
            wait()

    dhs, dgs, es, gus = transfer(
        "sum_hidden",
        collectives[1],
        shards,
        ["outer", "core"],
        2 * n_out + 8,
        sum_hidden,
        [dh_part, dgate_part, e_grad, sgu_grad],
        [
            ((n_out, rows, width), bf16),
            (meta.shape, f32),
            ((n_in, half, e_grad.shape[2]), bf16),
            ((half, 2 * hidden), bf16),
        ],
    )
    e_mine = lax.dynamic_slice_in_dim(e_grad, core * half, half, 1)
    gu_mine = lax.dynamic_slice_in_dim(sgu_grad, core * half, half, 0)
    return dhs, dgs, mix_part, e_mine, es, gu_mine, gus, sd_grad


def norm_rows(values, gain_vector):
    inverse = lax.rsqrt(jnp.mean(values * values, axis=-1, keepdims=True) + epsilon)
    normed = values * inverse
    return (normed, inverse, normed * gain_vector)


def norm_back(grad_hidden, normed, inverse, gain_vector):
    grad_normed = grad_hidden * gain_vector
    gain_grad = jnp.sum(grad_hidden * normed, axis=(0, 1))
    inner_mean = jnp.mean(grad_normed * normed, axis=-1, keepdims=True)
    return (inverse * (grad_normed - normed * inner_mean), gain_grad)


def pad_rows(array, axis):
    size = array.shape[axis]
    widths = [(0, 0)] * array.ndim
    widths[axis] = (0, round_up(size, 16) - size)
    return jnp.pad(array, widths) if widths[axis][1] else array


def pad_to(array, axis, size):
    widths = [(0, 0)] * array.ndim
    widths[axis] = (0, size - array.shape[axis])
    return jnp.pad(array, widths) if widths[axis][1] else array


def body(
    tokens,
    routes,
    out_grad,
    attn_gain,
    ffn_gain,
    query_projection,
    key_projection,
    value_projection,
    w_out,
    w_router,
    shared_gate,
    shared_up,
    shared_down,
    expert_gate,
    expert_up,
    expert_down,
):
    shards = lax.axis_size("fsdp")
    n_in = KEY_VALUE_HEADS
    n_out = shards // n_in
    core, chip, outer, inner = place()
    seg, seqs, width = tokens.shape
    rows = seg * seqs
    topk = routes.shape[2]
    n_experts = w_router.shape[1]
    w_rows = query_projection.shape[0]
    w_pad = round_up(w_rows, 16)
    d_rows = shared_down.shape[0]
    d_pad = round_up(d_rows, 16)
    half_chips = shards // 2
    q_cols = GROUP_MEMBERS * HEAD_SIZE
    cols = q_cols + 2 * HEAD_SIZE
    ff = expert_gate.shape[2]
    hid_core = n_in * d_rows
    hid = 2 * hid_core
    hid_pad = round_up(hid, 128)
    small = round_up(n_experts + 2, 128)
    chunk = n_in * seg
    half_width, half_ff = width // 2, ff // 2
    room = round_up(max(2, (3 * rows * topk + 2 * n_experts - 1) // (2 * n_experts)), 16)

    small_piece = pad_to(
        jnp.concatenate([w_router, attn_gain[:, None], ffn_gain[:, None]], axis=1), 1, small
    )
    q_pieces = pad_rows(
        jnp.concatenate(
            [
                query_projection.reshape(w_rows, n_in, q_cols),
                key_projection.reshape(w_rows, n_in, HEAD_SIZE),
                value_projection.reshape(w_rows, n_in, HEAD_SIZE),
                jnp.broadcast_to(small_piece[:, None], (w_rows, n_in, small)),
            ],
            axis=2,
        ).transpose(1, 0, 2),
        1,
    )

    def hidden_piece(weight):
        piece = weight.reshape(w_rows, 2, n_out, hid_core).transpose(2, 0, 1, 3)
        return pad_to(piece.reshape(n_out, w_rows, hid), 2, hid_pad)

    gu_pieces = pad_rows(
        jnp.concatenate([hidden_piece(shared_gate), hidden_piece(shared_up)], axis=2), 1
    )
    out_piece = pad_rows(w_out, 0)
    down_piece = pad_rows(shared_down, 0)
    x_own = tokens.transpose(1, 0, 2)
    c_own = out_grad.transpose(1, 0, 2)
    cot = c_own.reshape(rows, width)

    def shift(block, amount):
        return lax.ppermute(
            block, "fsdp", [(f, (f + amount * n_in) % shards) for f in range(shards)]
        )

    def swap(block, step):
        return lax.ppermute(
            block, "fsdp", [(f, f // n_in * n_in + (f % n_in ^ step)) for f in range(shards)]
        )

    def out_rows(wires, o_ref, wo_ref):
        core, chip, outer, inner = place()
        to_inner = 2 * core + chip // half_chips
        slot = lax.rem(chip, half_chips)
        base = wires.take(half_chips)
        sends = wires.take(n_out)
        across_core = wires.take(1)
        first = inner // 2 == core

        def copy(k):
            to = (core, k * n_in + to_inner)
            return to[1] == chip, pltpu.make_async_remote_copy(
                src_ref=o_ref,
                dst_ref=wo_ref.at[slot],
                send_sem=wires.send_sems.at[sends + k],
                recv_sem=wires.recv_sems.at[base + slot],
                device_id=to,
                device_id_type=MESH,
            )

        def start(k):
            here, send = copy(k)
            pl.when(jnp.logical_not(here))(send.start)
            pl.when(here)(lambda: wires.local(o_ref, wo_ref.at[slot], base).start())

        def leave(k):
            here, send = copy(k)
            pl.when(jnp.logical_not(here))(send.wait_send)

        def come(i):
            origin = (core, half_chips * lax.rem(inner, 2) + i)
            here = origin[1] == chip
            place_of = wo_ref.at[i]
            pl.when(jnp.logical_not(here))(
                wires.remote(place_of, place_of, base + i, origin).wait_recv
            )
            pl.when(here)(lambda: wires.local(o_ref, place_of, base).wait())

        def hand_on():
            return wires.remote(wo_ref, wo_ref, across_core, (1 - core, chip))

        def arrive():
            @pl.when(first)
            def _():
                repeat(0, half_chips, come)
                hand_on().start()

        def settle():
            @pl.when(first)
            def _():
                hand_on().wait_send()

            @pl.when(jnp.logical_not(first))
            def _():
                hand_on().wait_recv()

        repeat(0, n_out, start)
        wires.leaving.append(lambda: repeat(0, n_out, leave))
        return arrive, settle

    own_rows = half_chips // 2
    line = n_out == 4

    def fetch(wires, ins, outs):
        x_ref, q_ref, o_ref, *c_refs = ins
        xs_ref, wq_ref, wo_ref, *passed = outs
        core, chip, outer, inner = place()
        q_in = wires.exchange(
            "chips", lambda r, d: q_ref.at[lax.rem(r, n_in)], lambda r, d: wq_ref.at[core, r]
        )
        x_in = wires.exchange("plane", lambda r, d: x_ref.at[r // n_in], lambda r, d: xs_ref.at[r])
        o_in, o_settle = out_rows(wires, o_ref, wo_ref)
        if line:
            c_in = gather_step(wires, n_out, 0, c_refs * 2, passed)
        q_in()
        q_other = wires.sibling(wq_ref.at[core], wq_ref.at[core], wq_ref.at[1 - core])
        o_in()
        x_in()
        q_other()
        o_settle()
        if line:
            c_in()

    xs, wq, wo, *c_first = transfer(
        "fetch",
        0,
        shards,
        ["all"],
        4 * shards + 16,
        fetch,
        [x_own, q_pieces, out_piece] + [cot] * line,
        [
            ((2 * n_in, seg, width), bf16),
            ((2, shards, w_pad, cols + small), bf16),
            ((half_chips, w_pad, width), bf16),
        ]
        + [(cot.shape, bf16)] * (2 * line),
    )
    down_half = lax.dynamic_slice_in_dim(expert_down[0], core * half_ff, half_ff, 0)
    expert_half = jnp.concatenate(
        [
            lax.dynamic_slice_in_dim(expert_gate[0], core * half_width, half_width, 0),
            lax.dynamic_slice_in_dim(expert_up[0], core * half_width, half_width, 0),
        ]
        + [down_half[:, k : k + ff] for k in range(0, width, ff)],
        axis=0,
    )
    wq, expert_half = lax.optimization_barrier((wq, expert_half))
    side_x, side_y = swap(expert_half, 1), swap(expert_half, 2)
    wq = wq[:, :, :w_rows].reshape(width, cols + small)
    wo = wo[:, :w_rows].reshape(q_cols, width)
    wq, small_w = wq[:, :cols], wq[:, cols:]
    router_w = small_w[:, :n_experts]
    gain_one = small_w[:, n_experts].astype(f32)
    gain_two = small_w[:, n_experts + 1].astype(f32)

    h1 = norm_rows(xs.reshape(2 * chunk, width).astype(f32), gain_one)[2].astype(bf16)
    qkv = nn(h1, wq).astype(bf16)

    q_part, kv_part = qkv[:, :q_cols], qkv[:, q_cols:]
    inputs = x_own.astype(f32)
    if line:
        mixed, log_rows, kv_all, out_sum, sgu, ws, *c_later = attend(
            1, shards, chunk, q_part, kv_part, wo, gu_pieces, down_piece, c_first
        )
        c_parts = [cot] + [came[way] for way in range(2) for came in (c_first, c_later[:2], c_later[2:])]
        residual = inputs + out_sum
    else:
        mixed, log_rows, kv_all = attend(1, shards, chunk, q_part, kv_part)
        mixed_low = mixed.astype(bf16)
        out_part = nn(mixed_low, wo).astype(bf16).reshape(2 * n_in, seg, width)

        def sum_out(wires, ins, outs):
            part_ref, gu_ref, s_ref = ins
            parts_ref, wgu_ref, ws_ref = outs
            gu_in, gu_settle, s_in, s_settle = spread_shared(wires, gu_ref, s_ref, wgu_ref, ws_ref)
            part_in = wires.exchange(
                "plane", lambda r, d: part_ref.at[r], lambda r, d: parts_ref.at[r]
            )
            gu_in()
            gu_settle.start()
            s_in()
            s_settle.start()
            part_in()
            gu_settle.wait()
            s_settle.wait()

        out_parts, sgu, ws = transfer(
            "sum_out",
            2,
            shards,
            ["all"],
            shards + 8 * n_in + 16,
            sum_out,
            [out_part, gu_pieces, down_piece],
            [
                ((2 * n_in, seg, width), bf16),
                ((2, shards, w_pad, 2 * hid_pad), bf16),
                ((2, n_in, d_pad, width), bf16),
            ],
        )
        c_parts = [cot] + [shift(cot, d) for d in range(1, n_out)]
        residual = inputs + jnp.sum(out_parts.astype(f32).reshape(2, n_in, seg, width), axis=1)
    sgu = sgu[:, :, :w_rows].reshape(width, 2 * hid_pad)
    ws = pad_to(ws[:, :, :d_rows].reshape(hid, width), 0, hid_pad)

    normed_two, inverse_two, scaled_two = norm_rows(residual, gain_two)
    hidden_two = scaled_two.astype(bf16).reshape(rows, width)
    logits = nn(hidden_two, router_w)
    flat_routes = routes.transpose(1, 0, 2).reshape(rows, topk)
    chooser = (flat_routes[:, :, None] == jnp.arange(n_experts, dtype=jnp.int32)).astype(f32)
    taken = jnp.sum(chooser, axis=1)
    chosen = jnp.where(taken > 0, logits, masked_score)
    exponent = jnp.where(
        taken > 0, jnp.exp(chosen - jnp.max(chosen, axis=-1, keepdims=True)), 0.0
    )
    gates = exponent / jnp.sum(exponent, axis=-1, keepdims=True)
    before = (
        lax.broadcasted_iota(jnp.int32, (rows, rows), 0)
        < lax.broadcasted_iota(jnp.int32, (rows, rows), 1)
    ).astype(bf16)
    slots = jnp.where(taken.T > 0, nn(taken.T.astype(bf16), before), -1.0)
    meta = jnp.concatenate(
        [gates.T.reshape(n_out, n_in, rows), slots.reshape(n_out, n_in, rows)], axis=1
    )

    run = functools.partial(experts_line if line else experts_split, room, hid_pad, shards)
    dhs, dgs, mix_part, e_mine, e_other, gu_mine, gus, sd_grad = run(
        3 if line else (3, 4),
        hidden_two,
        meta,
        c_parts,
        (expert_gate, expert_up, expert_down),
        (side_x, side_y),
        sgu,
        ws,
    )

    def mix_terms(step, came):
        if not line:
            return []
        terms = []
        for way, slot in enumerate(((step + 1) % n_out, (n_out - 1 - step) % n_out)):
            term = mix_part[slot].astype(f32)
            if came:
                inside = (outer > 0, outer < n_out - 1)[way]
                term = term + jnp.where(inside, came[way].astype(f32), 0.0)
            terms.append(term.astype(bf16))
        return terms

    gu_half = (gu_mine.astype(f32) + gus.astype(f32)).astype(bf16)
    gu_half = pad_rows(gu_half.reshape(shards, w_rows, 2 * hid_pad), 1)
    sd_send = pad_rows(sd_grad[:hid].reshape(2 * n_in, d_rows, width), 1)

    grad_float = c_own.astype(f32)
    grad_gates = dgs[:, :n_in].reshape(n_experts, rows).T
    grad_logits = gates * (grad_gates - jnp.sum(gates * grad_gates, axis=-1, keepdims=True))
    router_grad = lax.dot_general(
        hidden_two.astype(f32),
        grad_logits,
        (((0,), (0,)), ((), ())),
        precision=lax.Precision.HIGHEST,
        preferred_element_type=f32,
    )
    grad_hidden_two = jnp.sum(dhs.astype(f32), axis=0) + lax.dot_general(
        grad_logits,
        router_w.astype(f32),
        (((1,), (1,)), ((), ())),
        precision=lax.Precision.HIGHEST,
        preferred_element_type=f32,
    )
    grad_norm_two, gain_two_grad = norm_back(
        grad_hidden_two.reshape(seqs, seg, width), normed_two, inverse_two, gain_two
    )
    grad_residual = grad_float + grad_norm_two
    grad_attn = grad_residual.astype(bf16)

    def spread_grad(wires, ins, outs, *room):
        second = wires.exchange("chips", lambda r, d: ins[1].at[r], lambda r, d: outs[1].at[r])
        first = wires.exchange("plane", lambda r, d: ins[0].at[r // n_in], lambda r, d: outs[0].at[r])
        if line:
            mix_in = sum_step(wires, n_out, 0, ins[2:4], outs[2:4])
            add_pieces(wires, ins[4], ins[5], outs[4], *room)
        first()
        second()
        if line:
            mix_in()

    e_piece = (2, half_width // 3, 3 * ff)
    grad_all, gus, *rest = transfer(
        "spread_grad",
        5,
        shards,
        ["all"],
        shards + 2 * n_in + 16,
        spread_grad,
        [grad_attn, gu_half] + mix_terms(0, []) + [e_mine, e_other] * line,
        [((2 * n_in, seg, width), bf16), ((shards, w_pad, 2 * hid_pad), bf16)]
        + [(cot.shape, bf16)] * (2 * line)
        + [(e_mine.shape, bf16)] * line,
        [(e_piece, bf16)] * (3 * line),
    )
    if line:
        *mix_first, e_sum = rest
    else:
        e_sum = (e_mine.astype(f32) + e_other.astype(f32)).astype(bf16)

    grad_all = grad_all.reshape(2 * chunk, width)
    small_grad = pad_to(
        jnp.concatenate(
            [router_grad, jnp.zeros((width, 1), f32), gain_two_grad[:, None]], axis=1
        ),
        1,
        small,
    )
    if line:
        grad_hidden_one, wq_total, small_total, out_w_grad, down_w_grad, *rest = finish(
            6,
            shards,
            chunk,
            n_experts,
            q_part,
            kv_all,
            grad_all,
            wo,
            mixed,
            log_rows,
            h1,
            wq,
            gain_one[None],
            small_grad.astype(bf16),
            sd_send,
            mix_part,
            mix_terms(1, mix_first),
            e_sum,
        )
        *mix_third, e_total, e_other = rest
        mixes = [mix_part[0].astype(f32)] + [
            jnp.where(inside, came.astype(f32), 0.0)
            for inside, came in zip((outer > 0, outer < n_out - 1), mix_third)
        ]
    else:
        mixes = [mix_part[0].astype(f32)] + [
            shift(mix_part[n_out - d], d).astype(f32) for d in range(1, n_out)
        ]
        grad_mixed = nt(grad_all, wo).astype(bf16)
        wo_grad = tn(mixed_low, grad_all).astype(bf16).reshape(half_chips, w_rows, width)
        wo_grad = pad_rows(wo_grad, 1)
        delta_rows = jnp.sum(
            (grad_mixed.astype(f32) * mixed).reshape(2, chunk, GROUP_MEMBERS, HEAD_SIZE), axis=-1
        ).transpose(2, 0, 1)
        dqkv, wos = attend_back(
            6,
            shards,
            chunk,
            qkv[:, :q_cols],
            kv_all,
            grad_mixed,
            log_rows,
            delta_rows,
            wo_grad,
        )
        wo_mine = lax.dynamic_slice_in_dim(wo_grad, core * own_rows, own_rows, 0)
        wo_half = (wo_mine.astype(f32) + wos.astype(f32)).astype(bf16)
        dh1_part = nt(dqkv, wq).astype(bf16).reshape(2 * n_in, seg, width)
        wq_send = pad_rows(tn(h1, dqkv).astype(bf16).reshape(2 * shards, w_rows, cols), 1)
        gain_one_grad = (
            jnp.sum(
                dh1_part.reshape(2 * chunk, width).astype(f32) * h1.astype(f32), axis=0
            )
            / gain_one
        )
        small_grad = small_grad.at[:, n_experts].set(gain_one_grad)
        small_send = pad_rows(small_grad.astype(bf16).reshape(2 * shards, w_rows, small), 1)

        def sum_first(wires, ins, outs):
            dh_ref, wq_ref, small_ref, s_ref, o_ref = ins
            dhs, wqs, smalls, sds, wos = outs
            waits = [
                out_rows_back(wires, shards, o_ref, wos),
                wires.exchange("all", lambda r, d: wq_ref.at[r], lambda r, d: wqs.at[r]),
                wires.exchange("plane", lambda r, d: dh_ref.at[r], lambda r, d: dhs.at[r]),
                wires.exchange("all", lambda r, d: small_ref.at[r], lambda r, d: smalls.at[r]),
                wires.exchange("plane", lambda r, d: s_ref.at[r], lambda r, d: sds.at[r]),
            ]
            for wait in waits:
                wait()

        dh1s, wq_parts, small_parts, sds, wos = transfer(
            "sum_first",
            7,
            shards,
            ["all"],
            4 * n_in + 6 * shards + 16,
            sum_first,
            [dh1_part, wq_send, small_send, sd_send, wo_half.reshape(own_rows * w_pad, width)],
            [
                ((2 * n_in, seg, width), bf16),
                ((2 * shards, w_pad, cols), bf16),
                ((2 * shards, w_pad, small), bf16),
                ((2 * n_in, d_pad, width), bf16),
                ((n_out, w_pad, width), bf16),
            ],
        )
        grad_hidden_one = jnp.sum(dh1s.astype(f32).reshape(2, n_in, seg, width), axis=1)
        wq_total = jnp.sum(
            wq_parts[:, :w_rows].astype(f32).reshape(2 * n_out, n_in, w_rows, cols), axis=0
        )
        down_w_grad = jnp.sum(sds[:, :d_rows].astype(f32), axis=0)
        out_w_grad = jnp.sum(wos[:, :w_rows].astype(f32), axis=0)
        small_total = jnp.sum(small_parts[:, :w_rows].astype(f32), axis=0)
        e_parts = [swap(e_sum[e], e) for e in range(1, n_in)]
        e_total = sum([part.astype(f32) for part in e_parts], e_sum[0].astype(f32)).astype(bf16)
        e_other = lax.ppermute(e_total, "seq", [(0, 1), (1, 0)])
    total_out = residual + sum(mixes).reshape(seqs, seg, width)
    normed_one, inverse_one, _ = norm_rows(inputs, gain_one)
    grad_norm_one = norm_back(grad_hidden_one, normed_one, inverse_one, gain_one)[0]
    tokens_grad = grad_residual + grad_norm_one

    wq_total = wq_total.transpose(1, 0, 2)
    query_grad = wq_total[:, :, :q_cols].reshape(w_rows, n_in * q_cols)
    key_grad = wq_total[:, :, q_cols : q_cols + HEAD_SIZE].reshape(w_rows, n_in * HEAD_SIZE)
    value_grad = wq_total[:, :, q_cols + HEAD_SIZE :].reshape(w_rows, n_in * HEAD_SIZE)
    gu_total = jnp.sum(
        gus[:, :w_rows].astype(f32).reshape(n_out, n_in, w_rows, 2 * hid_pad), axis=1
    )

    def hidden_whole(piece):
        piece = piece[:, :, :hid].reshape(n_out, w_rows, 2, hid_core)
        return piece.transpose(1, 2, 0, 3).reshape(w_rows, n_out * hid)

    gate_w_grad = hidden_whole(gu_total[:, :, :hid_pad])
    up_w_grad = hidden_whole(gu_total[:, :, hid_pad:])
    own, came = e_total.astype(f32), e_other.astype(f32)
    e_total = jnp.concatenate(
        [jnp.where(core == 0, own, came), jnp.where(core == 0, came, own)], axis=0
    )

    return (
        total_out.astype(bf16).transpose(1, 0, 2),
        tokens_grad.transpose(1, 0, 2),
        small_total[:, n_experts],
        small_total[:, n_experts + 1],
        query_grad,
        key_grad,
        value_grad,
        out_w_grad,
        small_total[:, :n_experts],
        gate_w_grad,
        up_w_grad,
        down_w_grad,
        e_total[:, :ff][None],
        e_total[:, ff : 2 * ff][None],
        e_total[:, 2 * ff :].T[None],
    )


def solution(mesh):
    rows = P(("seq", "fsdp"), None, None)
    matrix = P(("seq", "fsdp"), None)
    vector = P(("seq", "fsdp"))
    expert = P("fsdp", None, None)
    return jax.shard_map(
        body,
        mesh=mesh,
        in_specs=(rows,) * 3 + (vector,) * 2 + (matrix,) * 8 + (expert,) * 3,
        out_specs=(rows,) * 2 + (vector,) * 2 + (matrix,) * 8 + (expert,) * 3,
        check_vma=False,
    )
```

```python
import functools
import math

import jax
import jax.numpy as jnp
from jax import lax
from jax.experimental import pallas as pl
from jax.experimental.pallas import tpu as pltpu
from jax.sharding import PartitionSpec as P

QUERY_HEADS = 12
KEY_VALUE_HEADS = 4
HEAD_SIZE = 128
GROUP_MEMBERS = QUERY_HEADS // KEY_VALUE_HEADS

epsilon = 1e-06
masked_score = -1e30
MESH = pl.DeviceIdType.MESH
VMEM_LIMIT = 63 * 1024 * 1024
f32 = jnp.float32
bf16 = jnp.bfloat16


def round_up(number, step):
    return -(-number // step) * step


def nn(left, right):
    return lax.dot_general(left, right, (((1,), (0,)), ((), ())), preferred_element_type=f32)


def nt(left, right):
    return lax.dot_general(left, right, (((1,), (1,)), ((), ())), preferred_element_type=f32)


def tn(left, right):
    return lax.dot_general(left, right, (((0,), (0,)), ((), ())), preferred_element_type=f32)


def across(inner, step):
    low = lax.rem(inner + step, 2)
    high = lax.rem(inner // 2 + step // 2, 2)
    return low + 2 * high


def place():
    core = lax.axis_index("seq")
    chip = lax.axis_index("fsdp")
    return core, chip, chip // KEY_VALUE_HEADS, lax.rem(chip, KEY_VALUE_HEADS)


def group(kind, shards):
    core, chip, outer, inner = place()
    if kind == "plane":
        size = 2 * KEY_VALUE_HEADS
        return (
            size,
            core * KEY_VALUE_HEADS + inner,
            lambda r: (r // KEY_VALUE_HEADS, outer * KEY_VALUE_HEADS + lax.rem(r, KEY_VALUE_HEADS)),
        )
    if kind == "inner":
        return KEY_VALUE_HEADS, inner, lambda r: (core, outer * KEY_VALUE_HEADS + r)
    if kind == "outer":
        return shards // KEY_VALUE_HEADS, outer, lambda r: (core, r * KEY_VALUE_HEADS + inner)
    if kind == "chips":
        return shards, chip, lambda r: (core, r)
    if kind == "all":
        return 2 * shards, core * shards + chip, lambda r: (r // shards, lax.rem(r, shards))
    return 2, core, lambda r: (r, chip)


def repeat(first, last, step):
    if last - first <= 16:
        for index in range(first, last):
            step(index)
    else:

        def one(index, carry):
            step(index)
            return carry

        lax.fori_loop(first, last, one, 0)


class Wires:
    def __init__(self, shards, send_sems, recv_sems, local_sems):
        self.shards = shards
        self.send_sems, self.recv_sems, self.local_sems = send_sems, recv_sems, local_sems
        self.used = 0
        self.leaving = []

    def greet(self, kinds):
        barrier = pltpu.get_barrier_semaphore()
        total = 0
        for kind in kinds:
            size, me, device = group(kind, self.shards)

            def signal(d, size=size, me=me, device=device):
                pl.semaphore_signal(
                    barrier, inc=1, device_id=device(lax.rem(me + d, size)), device_id_type=MESH
                )

            repeat(1, size, signal)
            total += size - 1
        pl.semaphore_wait(barrier, total)

    def take(self, count):
        base = self.used
        self.used += count
        return base

    def remote(self, source, target, index, device):
        return pltpu.make_async_remote_copy(
            src_ref=source,
            dst_ref=target,
            send_sem=self.send_sems.at[index],
            recv_sem=self.recv_sems.at[index],
            device_id=device,
            device_id_type=MESH,
        )

    def local(self, source, target, index):
        return pltpu.make_async_copy(source, target, self.local_sems.at[index])

    def exchange(self, kind, source_for, target_from, own=True):
        size, me, device = group(kind, self.shards)
        base = self.take(size)

        def copy(d):
            to = lax.rem(me + d, size)
            return self.remote(source_for(to, d), target_from(me, d), base + d, device(to))

        repeat(1, size, lambda d: copy(d).start())
        if own:
            self.local(source_for(me, 0), target_from(me, 0), base).start()
        self.leaving.append(lambda: repeat(1, size, lambda d: copy(d).wait_send()))

        def arrive(then=None):
            def one(d):
                came = lax.rem(me - d + size, size)
                place_of = target_from(came, d)
                self.remote(place_of, place_of, base + d, device(came)).wait_recv()
                if then is not None:
                    then(d)

            repeat(1, size, one)
            if own:
                self.local(source_for(me, 0), target_from(me, 0), base).wait()

        return arrive

    def sibling(self, source, target, comes):
        core, chip, _, _ = place()
        device = (1 - core, chip)
        index = self.take(1)
        copy = self.remote(source, target, index, device)
        copy.start()
        self.leaving.append(copy.wait_send)
        return self.remote(comes, comes, index, device).wait_recv

    def finish(self):
        for leave in self.leaving:
            leave()


def transfer(name, collective, shards, kinds, sems, body, operands, outs, scratch=()):
    count = len(operands)

    def kernel(*refs):
        ins, results = refs[:count], refs[count : count + len(outs)]
        room, sem_refs = refs[count + len(outs) : -3], refs[-3:]
        wires = Wires(shards, *sem_refs)
        wires.greet(kinds)
        body(wires, ins, results, *room)
        wires.finish()

    return pl.pallas_call(
        kernel,
        out_shape=[jax.ShapeDtypeStruct(shape, kind) for shape, kind in outs],
        in_specs=[pl.BlockSpec(memory_space=pl.ANY)] * count,
        out_specs=[pl.BlockSpec(memory_space=pl.ANY)] * len(outs),
        scratch_shapes=[pltpu.VMEM(shape, kind) for shape, kind in scratch]
        + [pltpu.SemaphoreType.DMA((sems,))] * 3,
        compiler_params=pltpu.CompilerParams(
            collective_id=collective, has_side_effects=True, vmem_limit_bytes=VMEM_LIMIT
        ),
        name=name,
    )(*operands)


def add_pieces(wires, first, second, result, size, left, right, total):
    items, rows, _ = first.shape
    per_item = rows // size
    count = items * per_item
    load_base, store_base = wires.take(4), wires.take(2)

    def cut(i):
        return i // per_item, pl.ds(i % per_item * size, size)

    def loads(i):
        slot = i % 2
        return (
            wires.local(first.at[cut(i)], left(slot), load_base + 2 * slot),
            wires.local(second.at[cut(i)], right(slot), load_base + 2 * slot + 1),
        )

    def store(i):
        return wires.local(total(i % 2), result.at[cut(i)], store_base + i % 2)

    for copy in loads(0):
        copy.start()
    for i in range(count):
        if i + 1 < count:
            for copy in loads(i + 1):
                copy.start()
        for copy in loads(i):
            copy.wait()
        if i >= 2:
            store(i - 2).wait()
        slot = i % 2
        total(slot)[...] = (left(slot)[...].astype(f32) + right(slot)[...].astype(f32)).astype(bf16)
        store(i).start()
    for i in range(max(0, count - 2), count):
        store(i).wait()


def neighbours(wires, n, sources, targets, sends, comes):
    core, chip, outer, inner = place()
    base = wires.take(2)

    def copy(way):
        sign = (1, -1)[way]
        to = lax.rem(outer + sign + n, n)
        device = (core, to * KEY_VALUE_HEADS + inner)
        return wires.remote(sources[way], targets[way], base + way, device)

    def come(way):
        sign = (1, -1)[way]
        origin = lax.rem(outer - sign + n, n)
        device = (core, origin * KEY_VALUE_HEADS + inner)
        return wires.remote(targets[way], targets[way], base + way, device)

    def each(conditions, action):
        for way in range(2):
            pl.when(conditions[way])(lambda way=way: action(way))

    each(sends, lambda way: copy(way).start())
    wires.leaving.append(lambda: each(sends, lambda way: copy(way).wait_send()))
    return lambda: each(comes, lambda way: come(way).wait_recv())


def gather_step(wires, n, step, sources, targets):
    outer = place()[2]
    sends = ((outer >= step) & (outer < n - 1), (outer < n - step) & (outer > 0))
    comes = (outer > step, outer < n - 1 - step)
    return neighbours(wires, n, sources, targets, sends, comes)


def sum_step(wires, n, step, sources, targets):
    outer = place()[2]
    sends = (
        (outer <= step) & (outer < n - 1),
        (outer >= n - 1 - step) & (outer > 0),
    )
    comes = (
        (outer >= 1) & (outer <= step + 1),
        (outer <= n - 2) & (outer >= n - 2 - step),
    )
    return neighbours(wires, n, sources, targets, sends, comes)


def out_rows_back(wires, shards, grad_ref, sums_ref):
    core, chip, outer, inner = place()
    n_in, n_out, half_chips = KEY_VALUE_HEADS, shards // KEY_VALUE_HEADS, shards // 2
    own_rows = half_chips // 2
    rows = sums_ref.shape[1]
    from_inner = 2 * core + chip // half_chips
    from_core = lax.rem(chip, half_chips) // own_rows
    sends = wires.take(own_rows)
    base = wires.take(n_out)

    def copy(i):
        to = (inner // 2, half_chips * lax.rem(inner, 2) + core * own_rows + i)
        here = (to[0] == core) & (to[1] == chip)
        return here, pltpu.make_async_remote_copy(
            src_ref=grad_ref.at[pl.ds(i * rows, rows)],
            dst_ref=sums_ref.at[outer],
            send_sem=wires.send_sems.at[sends + i],
            recv_sem=wires.recv_sems.at[base + outer],
            device_id=to,
            device_id_type=MESH,
        )

    def start(i):
        here, send = copy(i)
        pl.when(jnp.logical_not(here))(send.start)
        pl.when(here)(lambda: wires.local(grad_ref.at[pl.ds(i * rows, rows)], sums_ref.at[outer], base).start())

    def leave(i):
        here, send = copy(i)
        pl.when(jnp.logical_not(here))(send.wait_send)

    def come(k):
        origin = (from_core, k * n_in + from_inner)
        here = (origin[0] == core) & (origin[1] == chip)
        place_of = sums_ref.at[k]
        pl.when(jnp.logical_not(here))(
            wires.remote(place_of, place_of, base + k, origin).wait_recv
        )
        pl.when(here)(lambda: wires.local(place_of, place_of, base).wait())

    repeat(0, own_rows, start)
    wires.leaving.append(lambda: repeat(0, own_rows, leave))
    return lambda: repeat(0, n_out, come)


class Line:
    def __init__(self, wires, source, every):
        self.wires, self.source, self.every = wires, source, every
        self.n = every.shape[0]
        self.core, _, self.outer, self.inner = place()
        self.bases = {1: wires.take(self.n), -1: wires.take(self.n)}

    def device(self, at):
        return self.core, at * KEY_VALUE_HEADS + self.inner

    def order(self):
        low = self.outer < self.n // 2
        return [
            lax.rem(jnp.where(low, self.outer + k, self.outer - k + self.n), self.n)
            for k in range(self.n)
        ]

    def hop(self, step, sign):
        to = lax.rem(self.outer + sign + self.n, self.n)
        block = lax.rem(self.outer - sign * step + 2 * self.n, self.n)
        source = self.source if step == 0 else self.every.at[block]
        index = self.bases[sign] + step
        return self.wires.remote(source, self.every.at[block], index, self.device(to))

    def sends(self, step, sign):
        to, block = self.outer + sign, self.outer - sign * step
        return (to >= 0) & (to < self.n) & (block >= 0) & (block < self.n)

    def start(self, step):
        for sign in (1, -1):
            pl.when(self.sends(step, sign))(lambda sign=sign: self.hop(step, sign).start())

    def arrive(self, step):
        for sign in (1, -1):
            come = self.outer - sign * (step + 1)

            def wait(sign=sign, come=come):
                block = self.every.at[lax.rem(come + self.n, self.n)]
                to = lax.rem(self.outer - sign + self.n, self.n)
                index = self.bases[sign] + step
                self.wires.remote(block, block, index, self.device(to)).wait_recv()

            pl.when((come >= 0) & (come < self.n))(wait)

    def leave(self):
        for step in range(self.n - 1):
            for sign in (1, -1):
                pl.when(self.sends(step, sign))(
                    lambda step=step, sign=sign: self.hop(step, sign).wait_send()
                )


def far_first(outer, n):
    low = outer < n // 2
    order = []
    for k in range(n - 1):
        down = n - 1 - k
        order.append(
            jnp.where(low, jnp.where(down <= outer, down - 1, down), jnp.where(k >= outer, k + 1, k))
        )
    return order


def causal(scores):
    key_at = lax.broadcasted_iota(jnp.int32, scores.shape, 0)
    query_at = lax.broadcasted_iota(jnp.int32, scores.shape, 1)
    return jnp.where(key_at <= query_at, scores, masked_score)


def each_pair(block, outer, own, pair):
    def some(head, carry):
        if own:
            pair(head, 0, block, 0, True)
            pair(head, 1, block, 0, False)
            pair(head, 1, block, 1, True)
        else:
            pair(head, 1, block, 0, False)

            @pl.when(block < outer)
            def _():
                pair(head, 0, block, 0, False)
                pair(head, 1, block, 1, False)

        return carry

    lax.fori_loop(0, GROUP_MEMBERS, some, 0)


def attend_kernel(shards, chunk, joined, *refs):
    qkv_ref, *refs = refs
    if joined:
        wo_ref, gu_ref, s_ref, *refs = refs
        pass_from, refs = refs[:2], refs[2:]
    mixed_ref, log_ref, kv_out, *refs = refs
    if joined:
        out_ref, wgu_ref, ws_ref, *refs = refs
        pass_once, pass_twice, refs = refs[:2], refs[2:4], refs[4:]
        out_stage, out_recv, *refs = refs
    q_ref, kv_all, largest, total, summed, send_sems, recv_sems, local_sems = refs
    core, chip, _, inner = place()
    q_width = GROUP_MEMBERS * HEAD_SIZE
    kv_ref = qkv_ref.at[:, pl.ds(q_width, 2 * HEAD_SIZE)]
    wires = Wires(shards, send_sems, recv_sems, local_sems)
    factor = HEAD_SIZE**-0.5 * math.log2(math.e)
    line = Line(wires, kv_ref, kv_all)
    outer = line.outer
    own = wires.local(kv_ref, kv_all.at[outer], wires.take(1))
    own.start()
    own_q = wires.local(qkv_ref.at[:, pl.ds(0, q_width)], q_ref, wires.take(1))
    own_q.start()
    wires.greet(["all"] if joined else ["outer"])
    line.start(0)
    largest[...] = jnp.full_like(largest, masked_score)
    total[...] = jnp.zeros_like(total)
    summed[...] = jnp.zeros_like(summed)

    def pair(head, half, block, key_half, masked):
        cols = pl.ds(pl.multiple_of(head * HEAD_SIZE, HEAD_SIZE), HEAD_SIZE)
        rows = pl.ds(key_half * chunk, chunk)
        query = q_ref[pl.ds(half * chunk, chunk), cols]
        scores = nt(kv_all[block, rows, 0:HEAD_SIZE], query)
        if masked:
            scores = causal(scores)
        before = largest[head, half]
        new = jnp.maximum(before, jnp.max(scores, axis=0, keepdims=True))
        weights = jnp.exp2((scores - new) * factor)
        shrink = jnp.exp2((before - new) * factor)
        largest[head, half] = new
        total[head, half] = total[head, half] * shrink + jnp.sum(weights, axis=0, keepdims=True)
        summed[head, half] = summed[head, half] * shrink + tn(
            kv_all[block, rows, HEAD_SIZE : 2 * HEAD_SIZE], weights.astype(bf16)
        )

    for k, block in enumerate(line.order()):
        if k == 0:
            own.wait()
            own_q.wait()
        else:
            line.arrive(k - 1)
            if k < line.n - 1:
                line.start(k)
        if joined and k == line.n - 2:
            passed = gather_step(wires, line.n, 1, pass_from, pass_once)
            gu_in, gu_settle, s_in, s_settle = spread_shared(wires, gu_ref, s_ref, wgu_ref, ws_ref)
        each_pair(block, outer, k == 0, pair)
    keep = wires.local(kv_all, kv_out, wires.take(1))
    keep.start()
    for head in range(GROUP_MEMBERS):
        for half in range(2):
            mixed_ref[
                half * chunk : (half + 1) * chunk, head * HEAD_SIZE : (head + 1) * HEAD_SIZE
            ] = (summed[head, half] / total[head, half]).T
            log_ref[head, half : half + 1, :] = largest[head, half] * factor + jnp.log2(
                total[head, half]
            )
    if joined:
        seg = out_ref.shape[1]
        for half in range(2):
            rows = pl.ds(half * chunk, chunk)
            out_stage[rows, :] = nn(mixed_ref[rows, :].astype(bf16), wo_ref[...]).astype(bf16)
        out_in = wires.exchange(
            "plane", lambda r, d: out_stage.at[pl.ds(r * seg, seg)], lambda r, d: out_recv.at[r]
        )
        passed()
        passed = gather_step(wires, line.n, 2, pass_once, pass_twice)
        gu_in()
        gu_settle.start()
        s_in()
        s_settle.start()
        out_in()
        for half in range(2):
            parts = out_recv[half * KEY_VALUE_HEADS].astype(f32)
            for j in range(1, KEY_VALUE_HEADS):
                parts = parts + out_recv[half * KEY_VALUE_HEADS + j].astype(f32)
            out_ref[half] = parts
        gu_settle.wait()
        s_settle.wait()
        passed()
    line.leave()
    wires.finish()
    keep.wait()


def spread_shared(wires, gu_ref, s_ref, wgu_ref, ws_ref):
    core, chip, _, _ = place()
    sibling = (1 - core, chip)
    gu_in = wires.exchange(
        "chips",
        lambda r, d: gu_ref.at[r // KEY_VALUE_HEADS],
        lambda r, d: wgu_ref.at[core, r],
    )
    s_in = wires.exchange("inner", lambda r, d: s_ref, lambda r, d: ws_ref.at[core, r])
    gu_settle = wires.remote(wgu_ref.at[core], wgu_ref.at[core], wires.take(1), sibling)
    s_settle = wires.remote(ws_ref.at[core], ws_ref.at[core], wires.take(1), sibling)
    return gu_in, gu_settle, s_in, s_settle


def attend(collective, shards, chunk, qkv, wo=None, gu=None, down=None, passing=()):
    joined = wo is not None
    n_out = shards // KEY_VALUE_HEADS
    rows = 2 * chunk
    seg = chunk // KEY_VALUE_HEADS
    more_outs, more_scratch = [], []
    if joined:
        wide = wo.shape[1]
        block = jax.ShapeDtypeStruct(passing[0].shape, bf16)
        more_outs = [
            jax.ShapeDtypeStruct((2, seg, wide), f32),
            jax.ShapeDtypeStruct((2, shards) + gu.shape[1:], bf16),
            jax.ShapeDtypeStruct((2, KEY_VALUE_HEADS) + down.shape, bf16),
        ] + [block] * 4
        more_scratch = [
            pltpu.VMEM((rows, wide), bf16),
            pltpu.VMEM((2 * KEY_VALUE_HEADS, seg, wide), bf16),
        ]
    kv_shape = (n_out, rows, 2 * HEAD_SIZE)
    vmem = pl.BlockSpec(memory_space=pltpu.VMEM)
    hbm = pl.BlockSpec(memory_space=pl.ANY)
    state = (GROUP_MEMBERS, 2, 1, chunk)
    return pl.pallas_call(
        functools.partial(attend_kernel, shards, chunk, joined),
        in_specs=[hbm] + [vmem, hbm, hbm, hbm, hbm] * joined,
        out_specs=[vmem, vmem, hbm] + ([vmem] + [hbm] * 6) * joined,
        out_shape=[
            jax.ShapeDtypeStruct((rows, GROUP_MEMBERS * HEAD_SIZE), f32),
            jax.ShapeDtypeStruct((GROUP_MEMBERS, 2, chunk), f32),
            jax.ShapeDtypeStruct(kv_shape, bf16),
        ]
        + more_outs,
        scratch_shapes=more_scratch
        + [
            pltpu.VMEM((rows, GROUP_MEMBERS * HEAD_SIZE), bf16),
            pltpu.VMEM(kv_shape, bf16),
            pltpu.VMEM(state, f32),
            pltpu.VMEM(state, f32),
            pltpu.VMEM((GROUP_MEMBERS, 2, HEAD_SIZE, chunk), f32),
        ]
        + [pltpu.SemaphoreType.DMA((2 * n_out + shards + 32,))] * 3,
        compiler_params=pltpu.CompilerParams(
            collective_id=collective, has_side_effects=True, vmem_limit_bytes=VMEM_LIMIT
        ),
        name="attend",
    )(qkv, *((wo, gu, down, *passing) if joined else ()))


def attend_back_kernel(shards, chunk, own_rows, *refs):
    q_ref, kv_ref, grad_ref, log_ref, delta_ref, wo_ref, *refs = refs
    dqkv_ref, wo_other, *refs = refs
    came, stage, sums, dq_sums, send_sems, recv_sems, local_sems = refs
    wires = Wires(shards, send_sems, recv_sems, local_sems)
    core, chip, outer, inner = place()
    n = kv_ref.shape[0]
    scale = HEAD_SIZE**-0.5
    factor = scale * math.log2(math.e)
    wires.greet(["outer", "core"])
    wo_in = wires.sibling(
        wo_ref.at[pl.ds((1 - core) * own_rows, own_rows)], wo_other, wo_other
    )
    send_base, recv_base = wires.take(n), wires.take(n)
    dq_sums[...] = jnp.zeros_like(dq_sums)

    def pair(head, half, block, key_half, masked):
        cols = pl.ds(pl.multiple_of(head * HEAD_SIZE, HEAD_SIZE), HEAD_SIZE)
        mine, rows = pl.ds(half * chunk, chunk), pl.ds(key_half * chunk, chunk)
        query, grad = q_ref[mine, cols], grad_ref[mine, cols]
        key = kv_ref[block, rows, 0:HEAD_SIZE]
        value = kv_ref[block, rows, HEAD_SIZE : 2 * HEAD_SIZE]
        scores = nt(key, query)
        if masked:
            scores = causal(scores)
        weights = jnp.exp2(scores * factor - log_ref[head, half : half + 1, :])
        grad_scores = (
            weights * (nt(value, grad) - delta_ref[head, half : half + 1, :])
        ).astype(bf16)
        sums[rows, 0:HEAD_SIZE] += nn(grad_scores, query)
        sums[rows, HEAD_SIZE : 2 * HEAD_SIZE] += nn(weights.astype(bf16), grad)
        dq_sums[mine, cols] += tn(grad_scores, key)

    def send(k, block):
        return pltpu.make_async_remote_copy(
            src_ref=stage.at[k],
            dst_ref=came.at[outer],
            send_sem=send_sems.at[send_base + k],
            recv_sem=recv_sems.at[recv_base + outer],
            device_id=(core, block * KEY_VALUE_HEADS + inner),
            device_id_type=MESH,
        )

    order = far_first(outer, n)
    for k, block in enumerate(order + [outer]):
        sums[...] = jnp.zeros_like(sums)
        each_pair(block, outer, k == n - 1, pair)
        if k < n - 1:
            stage[k] = sums[...].astype(bf16)
            send(k, block).start()
    width = GROUP_MEMBERS * HEAD_SIZE
    dqkv_ref[:, 0:width] = (dq_sums[...] * scale).astype(bf16)
    for d in range(1, n):
        origin = lax.rem(outer + d, n)
        pltpu.make_async_remote_copy(
            src_ref=came.at[origin],
            dst_ref=came.at[origin],
            send_sem=send_sems.at[send_base],
            recv_sem=recv_sems.at[recv_base + origin],
            device_id=(core, origin * KEY_VALUE_HEADS + inner),
            device_id_type=MESH,
        ).wait_recv()
        sums[...] += came[origin].astype(f32)
    dqkv_ref[:, width : width + HEAD_SIZE] = (sums[:, 0:HEAD_SIZE] * scale).astype(bf16)
    dqkv_ref[:, width + HEAD_SIZE :] = sums[:, HEAD_SIZE:].astype(bf16)
    for k, block in enumerate(order):
        send(k, block).wait_send()
    wo_in()
    wires.finish()


def attend_back(collective, shards, chunk, q, kv_all, grad_mixed, log_rows, delta_rows, wo_grad):
    n_out, rows, kv_cols = kv_all.shape
    own_rows = wo_grad.shape[0] // 2
    vmem = pl.BlockSpec(memory_space=pltpu.VMEM)
    hbm = pl.BlockSpec(memory_space=pl.ANY)
    width = GROUP_MEMBERS * HEAD_SIZE
    return pl.pallas_call(
        functools.partial(attend_back_kernel, shards, chunk, own_rows),
        in_specs=[vmem] * 5 + [hbm],
        out_specs=[vmem, hbm],
        out_shape=[
            jax.ShapeDtypeStruct((rows, width + kv_cols), bf16),
            jax.ShapeDtypeStruct((own_rows,) + wo_grad.shape[1:], bf16),
        ],
        scratch_shapes=[
            pltpu.VMEM(kv_all.shape, bf16),
            pltpu.VMEM(kv_all.shape, bf16),
            pltpu.VMEM((rows, kv_cols), f32),
            pltpu.VMEM((rows, width), f32),
        ]
        + [pltpu.SemaphoreType.DMA((2 * n_out + 8,))] * 3,
        compiler_params=pltpu.CompilerParams(
            collective_id=collective, has_side_effects=True, vmem_limit_bytes=VMEM_LIMIT
        ),
        name="attend_back",
    )(q, kv_all, grad_mixed, log_rows, delta_rows, wo_grad)


def finish_kernel(shards, chunk, gain_col, *refs):
    (
        kv_ref,
        wo_ref,
        mixed_ref,
        log_ref,
        h1_ref,
        wq_ref,
        gain_ref,
        small_ref,
        qkv_ref,
        grad_own,
        gu_ref,
        sd_ref,
        mix_ref,
        mix_up,
        mix_down,
        e_first_ref,
        e_second_ref,
        dh1_out,
        wq_out,
        small_out,
        wo_out,
        sd_out,
        gu_out,
        mix_up_out,
        mix_down_out,
        e_both,
        e_ref,
        q_ref,
        grad_all,
        dmixed,
        delta,
        came,
        stage,
        sums,
        dq_sums,
        dqkv,
        dwo,
        wo_came,
        wo_recv,
        dwq,
        wq_came,
        wq_recv,
        small_all,
        small_came,
        small_recv,
        dh_stage,
        dh_recv,
        sd_recv,
        mix_came,
        mix_term,
        mix_came_last,
        mix_term_last,
        e_came,
        e_term,
        e_last,
        e_own,
        send_sems,
        recv_sems,
        local_sems,
    ) = refs
    wires = Wires(shards, send_sems, recv_sems, local_sems)
    core, chip, outer, inner = place()
    n = kv_ref.shape[0]
    scale = HEAD_SIZE**-0.5
    factor = scale * math.log2(math.e)
    width = GROUP_MEMBERS * HEAD_SIZE
    wide = h1_ref.shape[1]
    half_wide = wide // 2
    w_rows = wq_recv.shape[1]
    seg = dh_recv.shape[1]
    mine, other = pl.ds(core * half_wide, half_wide), pl.ds((1 - core) * half_wide, half_wide)
    wires.greet(["all"])
    q_load = wires.local(qkv_ref.at[:, pl.ds(0, width)], q_ref, wires.take(1))
    q_load.start()
    grad_in = wires.exchange(
        "plane", lambda r, d: grad_own.at[r // KEY_VALUE_HEADS], lambda r, d: grad_all.at[r]
    )
    gu_in = wires.exchange("chips", lambda r, d: gu_ref.at[r], lambda r, d: gu_out.at[r])
    sd_in = wires.exchange("plane", lambda r, d: sd_ref.at[r], lambda r, d: sd_recv.at[r])

    mix_steps = [sum_step(wires, n, 0, [mix_up, mix_down], [mix_came.at[0], mix_came.at[1]])]
    mix_loads = [
        wires.local(mix_ref.at[slot], target.at[way], wires.take(1))
        for target, slots in ((mix_term, (2 % n, (n - 2) % n)), (mix_term_last, (3 % n, (n - 3) % n)))
        for way, slot in enumerate(slots)
    ]
    for copy in mix_loads:
        copy.start()

    def mix_on(step, came, term, targets):
        mix_steps[-1]()
        for way in range(2):
            mix_loads[2 * (step - 1) + way].wait()
            inside = (outer > 0, outer < n - 1)[way]
            term[way] = (
                term[way].astype(f32) + jnp.where(inside, came[way].astype(f32), 0.0)
            ).astype(bf16)
        mix_steps.append(sum_step(wires, n, step, [term.at[0], term.at[1]], targets))

    add_pieces(
        wires,
        e_first_ref,
        e_second_ref,
        e_ref,
        half_wide // 3,
        lambda slot: dh_stage.at[pl.ds(slot * (half_wide // 3), half_wide // 3)],
        lambda slot: dh_stage.at[pl.ds((2 + slot) * (half_wide // 3), half_wide // 3)],
        lambda slot: e_own.at[pl.ds(slot * (half_wide // 3), half_wide // 3)],
    )

    e_cols = e_ref.shape[2] // 2
    e_cuts = (pl.ds(0, e_cols), pl.ds(e_cols, e_cols))
    e_sides = ((1, 2), (2, 1))

    def plane_device(step):
        return core, outer * KEY_VALUE_HEADS + across(inner, step)

    e_local, e_first, e_second = wires.take(3), wires.take(4), wires.take(2)
    e_loads = [wires.local(e_ref.at[0], e_own, e_local)]
    e_sends = []
    for way, (near, far) in enumerate(e_sides):
        e_loads.append(wires.local(e_ref.at[far, :, e_cuts[way]], e_term.at[way], e_local + 1 + way))
        for k, e in enumerate((near, 3)):
            e_sends.append(
                wires.remote(
                    e_ref.at[e, :, e_cuts[way]],
                    e_came.at[way, k],
                    e_first + 2 * way + k,
                    plane_device(near),
                )
            )
    for copy in e_sends + e_loads:
        copy.start()

    grad_in()
    q_load.wait()
    mix_on(1, mix_came, mix_term, [mix_came_last.at[0], mix_came_last.at[1]])
    per_half = grad_all.shape[0] // 2
    for half in range(2):
        rows = pl.ds(half * chunk, chunk)
        grad = grad_all[pl.ds(half * per_half, per_half)].reshape(chunk, wide)
        part = nt(grad, wo_ref[...]).astype(bf16)
        dmixed[rows, :] = part
        weighted = part.astype(f32) * mixed_ref[rows, :]
        for head in range(GROUP_MEMBERS):
            cols = slice(head * HEAD_SIZE, (head + 1) * HEAD_SIZE)
            delta[head, half] = jnp.sum(weighted[:, cols].T, axis=0, keepdims=True)

    send_base, recv_base = wires.take(n), wires.take(n)
    dq_sums[...] = jnp.zeros_like(dq_sums)

    def pair(head, half, block, key_half, masked):
        cols = pl.ds(pl.multiple_of(head * HEAD_SIZE, HEAD_SIZE), HEAD_SIZE)
        here, rows = pl.ds(half * chunk, chunk), pl.ds(key_half * chunk, chunk)
        query, grad = q_ref[here, cols], dmixed[here, cols]
        key = kv_ref[block, rows, 0:HEAD_SIZE]
        value = kv_ref[block, rows, HEAD_SIZE : 2 * HEAD_SIZE]
        scores = nt(key, query)
        if masked:
            scores = causal(scores)
        weights = jnp.exp2(scores * factor - log_ref[head, half : half + 1, :])
        grad_scores = (weights * (nt(value, grad) - delta[head, half])).astype(bf16)
        sums[rows, 0:HEAD_SIZE] += nn(grad_scores, query)
        sums[rows, HEAD_SIZE : 2 * HEAD_SIZE] += nn(weights.astype(bf16), grad)
        dq_sums[here, cols] += tn(grad_scores, key)

    def send(k, block):
        return pltpu.make_async_remote_copy(
            src_ref=stage.at[k],
            dst_ref=came.at[outer],
            send_sem=send_sems.at[send_base + k],
            recv_sem=recv_sems.at[recv_base + outer],
            device_id=(core, block * KEY_VALUE_HEADS + inner),
            device_id_type=MESH,
        )

    order = far_first(outer, n)
    for k, block in enumerate(order + [outer]):
        sums[...] = jnp.zeros_like(sums)
        each_pair(block, outer, k == n - 1, pair)
        if k < n - 1:
            stage[k] = sums[...].astype(bf16)
            send(k, block).start()

    dqkv[:, 0:width] = (dq_sums[...] * scale).astype(bf16)
    dwo[...] = tn(
        mixed_ref[...].astype(bf16), grad_all[...].reshape(2 * chunk, wide)
    ).astype(bf16)
    wo_rows = wo_came.shape[0]
    wo_in = wires.sibling(dwo.at[pl.ds((1 - core) * wo_rows, wo_rows)], wo_came, wo_came)
    dwq[:, 0:width] = tn(h1_ref[...], dqkv[:, 0:width]).astype(bf16)
    q_cols = pl.ds(0, width)
    q_in = wires.sibling(dwq.at[other, q_cols], wq_came.at[:, q_cols], wq_came.at[:, q_cols])
    wo_in()
    wo_came[...] = (
        dwo[pl.ds(core * wo_rows, wo_rows), :].astype(f32) + wo_came[...].astype(f32)
    ).astype(bf16)
    wo_parts = out_rows_back(wires, shards, wo_came, wo_recv)
    q_in()
    wq_came[:, 0:width] = (
        dwq[mine, 0:width].astype(f32) + wq_came[:, 0:width].astype(f32)
    ).astype(bf16)

    def pieces(cols):
        return wires.exchange(
            "chips",
            lambda r, d: wq_came.at[pl.ds(r * w_rows, w_rows), cols],
            lambda r, d: wq_recv.at[r, :, cols],
        )

    q_parts = pieces(q_cols)

    for copy in e_sends:
        copy.wait()
    for copy in e_loads:
        copy.wait()
    e_passed = []
    for way, (near, far) in enumerate(e_sides):
        e_term[way] = (e_term[way].astype(f32) + e_came[way, 1].astype(f32)).astype(bf16)
        e_passed.append(
            wires.remote(e_term.at[way], e_last.at[way], e_second + way, plane_device(far))
        )
    for copy in e_passed:
        copy.start()

    for d in range(1, n):
        origin = lax.rem(outer + d, n)
        pltpu.make_async_remote_copy(
            src_ref=came.at[origin],
            dst_ref=came.at[origin],
            send_sem=send_sems.at[send_base],
            recv_sem=recv_sems.at[recv_base + origin],
            device_id=(core, origin * KEY_VALUE_HEADS + inner),
            device_id_type=MESH,
        ).wait_recv()
        sums[...] += came[origin].astype(f32)
    dqkv[:, width : width + HEAD_SIZE] = (sums[:, 0:HEAD_SIZE] * scale).astype(bf16)
    dqkv[:, width + HEAD_SIZE :] = sums[:, HEAD_SIZE:].astype(bf16)

    gain_sum = jnp.zeros((1, wide), f32)
    for half in range(2):
        rows = pl.ds(half * chunk, chunk)
        part = nt(dqkv[rows, :], wq_ref[...]).astype(bf16)
        dh_stage[rows, :] = part
        gain_sum = gain_sum + jnp.sum(
            part.astype(f32) * h1_ref[rows, :].astype(f32), axis=0, keepdims=True
        )
    dh_in = wires.exchange(
        "plane", lambda r, d: dh_stage.at[pl.ds(r * seg, seg)], lambda r, d: dh_recv.at[r]
    )
    dwq[:, width:] = tn(h1_ref[...], dqkv[:, width:]).astype(bf16)
    kv_cols = pl.ds(width, 2 * HEAD_SIZE)
    kv_in = wires.sibling(dwq.at[other, kv_cols], wq_came.at[:, kv_cols], wq_came.at[:, kv_cols])
    column = (gain_sum / gain_ref[...])
    columns = jnp.broadcast_to(column, (small_all.shape[1], wide)).T
    at_col = lax.broadcasted_iota(jnp.int32, columns.shape, 1)
    small_all[...] = jnp.where(at_col == gain_col, columns, small_ref[...].astype(f32)).astype(bf16)
    small_in = wires.sibling(small_all.at[other], small_came, small_came)
    kv_in()
    wq_came[:, width:] = (
        dwq[mine, width:].astype(f32) + wq_came[:, width:].astype(f32)
    ).astype(bf16)
    kv_parts = pieces(kv_cols)
    small_in()
    small_came[...] = (small_all[mine, :].astype(f32) + small_came[...].astype(f32)).astype(bf16)
    small_parts = wires.exchange(
        "chips",
        lambda r, d: small_came.at[pl.ds(r * w_rows, w_rows)],
        lambda r, d: small_recv.at[r],
    )
    mix_on(2, mix_came_last, mix_term_last, [mix_up_out, mix_down_out])

    for way, copy in enumerate(e_passed):
        copy.wait()
        e_own[:, e_cuts[way]] = (
            e_own[:, e_cuts[way]].astype(f32)
            + e_came[way, 0].astype(f32)
            + e_last[way].astype(f32)
        ).astype(bf16)
    e_keep = wires.local(e_own, e_both.at[mine], e_local)
    e_keep.start()
    e_in = wires.sibling(e_own, e_both.at[mine], e_both.at[other])
    sd_in()
    sd_out[...] = jnp.sum(sd_recv[...].astype(f32), axis=0)
    wo_parts()
    wo_out[...] = jnp.sum(wo_recv[...].astype(f32), axis=0)
    q_parts()
    kv_parts()
    for j in range(KEY_VALUE_HEADS):
        total = wq_recv[j].astype(f32)
        for k in range(1, n):
            total = total + wq_recv[k * KEY_VALUE_HEADS + j].astype(f32)
        wq_out[j] = total
    small_parts()
    small_out[...] = jnp.sum(small_recv[...].astype(f32), axis=0)
    dh_in()
    for core_half in range(2):
        total = dh_recv[core_half * KEY_VALUE_HEADS].astype(f32)
        for j in range(1, KEY_VALUE_HEADS):
            total = total + dh_recv[core_half * KEY_VALUE_HEADS + j].astype(f32)
        dh1_out[core_half] = total
    mix_steps[-1]()
    gu_in()
    e_in()
    e_keep.wait()
    for k, block in enumerate(order):
        send(k, block).wait_send()
    wires.finish()


def finish(
    collective,
    shards,
    chunk,
    gain_col,
    kv_all,
    wo,
    mixed,
    log_rows,
    h1,
    wq,
    gain_row,
    small_grad,
    qkv,
    grad_own,
    gu_half,
    sd_send,
    mix_part,
    mix_terms,
    e_mine,
    e_other,
):
    n, rows, kv_cols = kv_all.shape
    width, wide = wo.shape
    cols = wq.shape[1]
    small = small_grad.shape[1]
    n_in = KEY_VALUE_HEADS
    seg = rows // (2 * n_in)
    w_rows = wide // (2 * shards)
    d_rows = sd_send.shape[1]
    block = mix_part.shape[1:]
    vmem = pl.BlockSpec(memory_space=pltpu.VMEM)
    hbm = pl.BlockSpec(memory_space=pl.ANY)

    def array(shape, kind=bf16):
        return jax.ShapeDtypeStruct(shape, kind)

    e_rows, e_cols = e_mine.shape[1:]
    scratch = [
        ((rows, width), bf16),
        ((2 * n_in, seg, wide), bf16),
        ((rows, width), bf16),
        ((GROUP_MEMBERS, 2, 1, chunk), f32),
        (kv_all.shape, bf16),
        (kv_all.shape, bf16),
        ((rows, kv_cols), f32),
        ((rows, width), f32),
        ((rows, cols), bf16),
        ((width, wide), bf16),
        ((width // 2, wide), bf16),
        ((n, w_rows, wide), bf16),
        ((wide, cols), bf16),
        ((wide // 2, cols), bf16),
        ((shards, w_rows, cols), bf16),
        ((wide, small), bf16),
        ((wide // 2, small), bf16),
        ((shards, w_rows, small), bf16),
        ((rows, wide), bf16),
        ((2 * n_in, seg, wide), bf16),
        ((2 * n_in, d_rows, wide), bf16),
        ((2,) + block, bf16),
        ((2,) + block, bf16),
        ((2,) + block, bf16),
        ((2,) + block, bf16),
        ((2, 2, e_rows, e_cols // 2), bf16),
        ((2, e_rows, e_cols // 2), bf16),
        ((2, e_rows, e_cols // 2), bf16),
        ((e_rows, e_cols), bf16),
    ]
    return pl.pallas_call(
        functools.partial(finish_kernel, shards, chunk, gain_col),
        in_specs=[vmem] * 8 + [hbm] * 9,
        out_specs=[vmem] * 5 + [hbm] * 5,
        out_shape=[
            array((2, seg, wide), f32),
            array((n_in, w_rows, cols), f32),
            array((w_rows, small), f32),
            array((w_rows, wide), f32),
            array((d_rows, wide), f32),
            array(gu_half.shape),
            array(block),
            array(block),
            array((2 * e_rows, e_cols)),
            array(e_mine.shape),
        ],
        scratch_shapes=[pltpu.VMEM(shape, kind) for shape, kind in scratch]
        + [pltpu.SemaphoreType.DMA((6 * shards + 96,))] * 3,
        compiler_params=pltpu.CompilerParams(
            collective_id=collective, has_side_effects=True, vmem_limit_bytes=VMEM_LIMIT
        ),
        name="finish",
    )(
        kv_all,
        wo,
        mixed,
        log_rows,
        h1,
        wq,
        gain_row,
        small_grad,
        qkv,
        grad_own,
        gu_half,
        sd_send,
        mix_part,
        *mix_terms,
        e_mine,
        e_other,
    )


def swiglu_parts(gate_part, up_part):
    sigmoid = jax.nn.sigmoid(gate_part)
    active = gate_part * sigmoid
    slope = up_part * sigmoid * (1.0 + gate_part * (1.0 - sigmoid))
    return active * up_part, active, slope


def experts_kernel(
    room,
    hidden,
    h_ref,
    c_ref,
    meta_ref,
    wg_ref,
    wu_ref,
    wd_ref,
    sgu_ref,
    sd_ref,
    out_ref,
    dh_ref,
    dgate_ref,
    dw_ref,
    dsgu_ref,
    dsd_ref,
    sum_out,
    sum_dh,
    h_rows,
    c_rows,
    picks,
    gate_col,
):
    expert = pl.program_id(0)
    inner = lax.rem(lax.axis_index("fsdp"), KEY_VALUE_HEADS)
    at = across(inner, expert)
    blocks, rows, width = h_ref.shape

    @pl.when(expert == 0)
    def _():
        dgate_ref[...] = jnp.zeros_like(dgate_ref)
        hid = h_ref[...].reshape(blocks * rows, width)
        cot = c_ref[...].reshape(blocks * rows, width)
        gate_w, up_w, down_w = sgu_ref[:, 0:hidden], sgu_ref[:, hidden : 2 * hidden], sd_ref[...]
        both, active, slope = swiglu_parts(nn(hid, gate_w), nn(hid, up_w))
        act = both.astype(bf16)
        d_act = nt(cot, down_w)
        d_gate = (d_act * slope).astype(bf16)
        d_up = (d_act * active).astype(bf16)
        sum_out[...] = nn(act, down_w)
        sum_dh[...] = nt(d_gate, gate_w) + nt(d_up, up_w)
        dsgu_ref[:, 0:hidden] = tn(hid, d_gate).astype(bf16)
        dsgu_ref[:, hidden : 2 * hidden] = tn(hid, d_up).astype(bf16)
        dsd_ref[...] = tn(act, cot).astype(bf16)

    slots = lax.broadcasted_iota(jnp.int32, (room, rows), 0).astype(f32)
    for block in range(blocks):
        part = pl.ds(block * room, room)
        gate_row = meta_ref[block, pl.ds(at, 1), :]
        slot_row = meta_ref[block, pl.ds(at + KEY_VALUE_HEADS, 1), :]
        pick = (slots == slot_row).astype(f32)
        gate_col[part, :] = jnp.broadcast_to(
            jnp.sum(pick * gate_row, axis=1, keepdims=True), (room, gate_col.shape[1])
        )
        pick = pick.astype(bf16)
        picks[block] = pick
        h_rows[part, :] = nn(pick, h_ref[block]).astype(bf16)
        c_rows[part, :] = nn(pick, c_ref[block]).astype(bf16)
    gate = gate_col[:, 0:1]
    gate_w, up_w, down_w = wg_ref[0], wu_ref[0], wd_ref[0]
    both, active, slope = swiglu_parts(nn(h_rows[...], gate_w), nn(h_rows[...], up_w))
    act = both.astype(bf16)
    d_act = nt(c_rows[...], down_w)
    d_gates = jnp.sum(d_act * act.astype(f32), axis=1, keepdims=True)
    d_act = d_act * gate
    act = (act.astype(f32) * gate).astype(bf16)
    d_gate = (d_act * slope).astype(bf16)
    d_up = (d_act * active).astype(bf16)
    ff = act.shape[1]
    dw_ref[0, :, 0:ff] = tn(h_rows[...], d_gate).astype(bf16)
    dw_ref[0, :, ff : 2 * ff] = tn(h_rows[...], d_up).astype(bf16)
    dw_ref[0, :, 2 * ff : 3 * ff] = tn(c_rows[...], act).astype(bf16)
    result = nn(act, down_w).astype(bf16)
    d_rows = (nt(d_gate, gate_w) + nt(d_up, up_w)).astype(bf16)
    for block in range(blocks):
        pick = picks[block]
        part = slice(block * room, (block + 1) * room)
        here = pl.ds(block * rows, rows)
        sum_out[here, :] += tn(pick, result[part])
        sum_dh[here, :] += tn(pick, d_rows[part])
        dgate_ref[block, pl.ds(at, 1), :] = jnp.sum(
            pick.astype(f32) * d_gates[part], axis=0, keepdims=True
        )

    @pl.when(expert == pl.num_programs(0) - 1)
    def _():
        out_ref[...] = sum_out[...].astype(bf16).reshape(out_ref.shape)
        dh_ref[...] = sum_dh[...].astype(bf16).reshape(dh_ref.shape)


def experts(room, hidden, h_all, c_all, meta, wg, wu, wd, sgu, sd):
    blocks, rows, width = h_all.shape
    n_experts, _, inner = wg.shape

    def once(shape):
        return pl.BlockSpec(shape, lambda e: (0,) * len(shape), pipeline_mode=pl.Buffered(1))

    def each(shape, **kind):
        return pl.BlockSpec((1,) + shape[1:], lambda e: (e, 0, 0), **kind)

    single = dict(pipeline_mode=pl.Buffered(1))
    return pl.pallas_call(
        functools.partial(experts_kernel, room, hidden),
        grid=(n_experts,),
        in_specs=[
            once(h_all.shape),
            once(c_all.shape),
            once(meta.shape),
            each(wg.shape),
            each(wu.shape),
            each(wd.shape),
            once(sgu.shape),
            once(sd.shape),
        ],
        out_specs=[
            once(h_all.shape),
            once(h_all.shape),
            once(meta.shape),
            pl.BlockSpec((1, width, 3 * inner), lambda e: (e, 0, 0), **single),
            once(sgu.shape),
            once(sd.shape),
        ],
        out_shape=[
            jax.ShapeDtypeStruct(h_all.shape, bf16),
            jax.ShapeDtypeStruct(h_all.shape, bf16),
            jax.ShapeDtypeStruct(meta.shape, f32),
            jax.ShapeDtypeStruct((n_experts, width, 3 * inner), bf16),
            jax.ShapeDtypeStruct(sgu.shape, bf16),
            jax.ShapeDtypeStruct(sd.shape, bf16),
        ],
        scratch_shapes=[
            pltpu.VMEM((blocks * rows, width), f32),
            pltpu.VMEM((blocks * rows, width), f32),
            pltpu.VMEM((blocks * room, width), bf16),
            pltpu.VMEM((blocks * room, width), bf16),
            pltpu.VMEM((blocks, room, rows), bf16),
            pltpu.VMEM((blocks * room, 128), f32),
        ],
        compiler_params=pltpu.CompilerParams(vmem_limit_bytes=VMEM_LIMIT),
        name="experts",
    )(h_all, c_all, meta, wg, wu, wd, sgu, sd)


def experts_line_kernel(room, hidden, shards, refs):
    n = shards // KEY_VALUE_HEADS
    h_ref, meta_ref = refs[:2]
    c_refs = refs[2 : 1 + 2 * n]
    (
        wg_ref,
        wu_ref,
        wd_ref,
        side_x,
        side_y,
        sgu_ref,
        sd_ref,
        dh_out,
        dgate_out,
        mix_out,
        e_mine,
        e_other,
        gu_mine,
        gu_other,
        dsd_ref,
        h_all,
        c_all,
        metas,
        wgu,
        wd,
        picks,
        kept_gu,
        kept_act,
        kept_shared,
        row_a,
        row_b,
        own_a,
        own_b,
        dh_stage,
        mix_stage,
        dg_stage,
        down_stage,
        gu_stage,
        send_sems,
        recv_sems,
        local_sems,
    ) = refs[1 + 2 * n :]
    wires = Wires(shards, send_sems, recv_sems, local_sems)
    core, chip, outer, inner = place()
    rows, width = h_ref.shape
    ff = wd.shape[1]
    experts_here = KEY_VALUE_HEADS

    own_h = wires.local(h_ref, h_all.at[outer], wires.take(1))
    own_meta = wires.local(meta_ref.at[outer], metas.at[outer], wires.take(1))
    own_h.start()
    own_meta.start()
    c_own = wires.local(c_refs[0], c_all.at[outer], wires.take(1))
    c_base = wires.take(2 * n - 2)

    def c_each(action):
        for k in range(2 * n - 2):
            block = outer - 1 - k if k < n - 1 else outer + 1 + k - (n - 1)

            def one(k=k, block=block):
                at = lax.rem(block + n, n)
                action(wires.local(c_refs[1 + k], c_all.at[at], c_base + k))

            pl.when((block >= 0) & (block < n))(one)

    deep, tall = ff // 2, width // 2
    own_weights = (
        wires.local(wg_ref.at[0], wgu.at[0, :, pl.ds(0, ff)], wires.take(1)),
        wires.local(wu_ref.at[0], wgu.at[0, :, pl.ds(ff, ff)], wires.take(1)),
        wires.local(wd_ref.at[0], wd.at[0], wires.take(1)),
    )

    def half_places(e, first_col, cols, of_core):
        found = [
            wgu.at[e, pl.ds(of_core * tall, tall), pl.ds(k * ff + first_col, cols)]
            for k in range(2)
        ]
        found += [
            wd.at[e, pl.ds(of_core * deep, deep), pl.ds(k * ff + first_col, cols)]
            for k in range(width // ff)
        ]
        return found

    def half_sources(source, first_col, cols):
        starts = [(k * tall, tall) for k in range(2)]
        starts += [(2 * tall + k * deep, deep) for k in range(width // ff)]
        return [source.at[pl.ds(at, size), pl.ds(first_col, cols)] for at, size in starts]

    per_half = 2 + width // ff
    sides = ((1, side_x, 0, ff), (2, side_y, 0, ff), (3, side_x, 0, ff // 2), (3, side_y, ff // 2, ff // 2))
    half_sems = [wires.take(per_half) for _ in sides]
    cross_sems = [wires.take(per_half) for _ in range(2)]

    def half_local(which):
        e, source, first_col, cols = sides[which]
        return [
            wires.local(here, there, half_sems[which] + k)
            for k, (here, there) in enumerate(
                zip(half_sources(source, first_col, cols), half_places(e, first_col, cols, core))
            )
        ]

    def half_remote(which, of_core):
        e, source, first_col, cols = sides[which]
        places = half_places(e, first_col, cols, of_core)
        here = half_sources(source, first_col, cols) if which < 2 else places
        return [
            wires.remote(here[k], places[k], half_sems[which] + k, (1 - core, chip))
            for k in range(per_half)
        ]

    def cross_remote(which):
        _, source, first_col, cols = sides[2 + which]
        return [
            wires.remote(
                here,
                there,
                cross_sems[which] + k,
                (core, outer * KEY_VALUE_HEADS + across(inner, 2 - which)),
            )
            for k, (here, there) in enumerate(
                zip(half_sources(source, first_col, cols), half_places(3, first_col, cols, core))
            )
        ]

    c_own.start()
    for copy in own_weights:
        copy.start()
    for which in range(2):
        for copy in half_local(which):
            copy.start()
    c_each(lambda copy: copy.start())

    wires.greet(["outer", "plane"])

    line = Line(wires, h_ref, h_all)
    device = line.device
    line.start(0)
    for which in range(2):
        for copy in cross_remote(which):
            copy.start()
    for which in range(2):
        for copy in half_remote(which, core):
            copy.start()
    meta_in = wires.exchange(
        "outer", lambda r, d: meta_ref.at[r], lambda r, d: metas.at[r], own=False
    )

    dh_send, dh_recv = wires.take(n), wires.take(n)
    dg_send, dg_recv = wires.take(n), wires.take(n)

    def give_back(stage, target, k, block, sends, receives):
        return pltpu.make_async_remote_copy(
            src_ref=stage,
            dst_ref=target.at[outer],
            send_sem=send_sems.at[sends + k],
            recv_sem=recv_sems.at[receives + outer],
            device_id=device(block),
            device_id_type=MESH,
        )

    def take_back(target, origin, receives):
        return pltpu.make_async_remote_copy(
            src_ref=target.at[origin],
            dst_ref=target.at[origin],
            send_sem=send_sems.at[receives],
            recv_sem=recv_sems.at[receives + origin],
            device_id=device(origin),
            device_id_type=MESH,
        )

    dh_own = wires.local(dh_stage.at[n - 1], dh_out.at[outer], wires.take(1))
    dg_own = wires.local(dg_stage.at[n - 1], dgate_out.at[outer], wires.take(1))
    mix_base = wires.take(n)

    def mix_copy(k, block):
        return wires.local(
            mix_stage.at[k % 2], mix_out.at[lax.rem(outer - block + n, n)], mix_base + k
        )

    slots = lax.broadcasted_iota(jnp.int32, (room, rows), 0).astype(f32)
    order = line.order()
    gate_w, up_w, down_w = sgu_ref[:, 0:hidden], sgu_ref[:, hidden : 2 * hidden], sd_ref[...]

    def choose(k, block, left, right):
        for e in range(experts_here):
            at = across(inner, e)
            slot_row = metas[block, pl.ds(at + experts_here, 1), :]
            picks[block, pl.ds(e * room, room), :] = (slots == slot_row).astype(bf16)
        left[...] = nn(picks[block], h_all[block]).astype(bf16)
        right[...] = nn(picks[block], c_all[block]).astype(bf16)
        dg_stage[k] = jnp.zeros(dg_stage.shape[1:], f32)

    def one_expert(e, k, block, left, right):
        at = across(inner, e)
        part = pl.ds(pl.multiple_of(e * room, 16), room)
        pick = picks[block, part, :].astype(f32)
        gate = jnp.sum(pick * metas[block, pl.ds(at, 1), :], axis=1, keepdims=True)
        first = nn(left[part, :], wgu[e])
        both, active, slope = swiglu_parts(first[:, 0:ff], first[:, ff : 2 * ff])
        act = both.astype(bf16)
        d_act = nt(right[part, :], wd[e])
        d_gates = jnp.sum(d_act * act.astype(f32), axis=1, keepdims=True)
        dg_stage[k, pl.ds(at, 1), :] = jnp.sum(pick * d_gates, axis=0, keepdims=True)
        d_act = d_act * gate
        act = (act.astype(f32) * gate).astype(bf16)
        here = pl.ds(pl.multiple_of(block * room, 16), room)
        kept_act[e, here, :] = act
        kept_gu[e, here, 0:ff] = (d_act * slope).astype(bf16)
        kept_gu[e, here, ff : 2 * ff] = (d_act * active).astype(bf16)
        left[part, :] = nn(act, wd[e]).astype(bf16)
        right[part, :] = nt(kept_gu[e, here, :], wgu[e]).astype(bf16)

    def some_experts(begin, end, k, block, left, right):
        def one(e, carry):
            one_expert(e, k, block, left, right)
            return carry

        lax.fori_loop(begin, end, one, 0)

    order = order[1:] + order[:1]
    last = n - 1
    own_h.wait()
    own_meta.wait()
    c_own.wait()
    choose(last, outer, own_a, own_b)
    for copy in own_weights:
        copy.wait()
    one_expert(0, last, outer, own_a, own_b)
    for which in range(2):
        for copy in half_local(which):
            copy.wait()
        for copy in half_remote(which, 1 - core):
            copy.wait_recv()
    some_experts(1, experts_here - 1, last, outer, own_a, own_b)

    for k, block in enumerate(order):
        if k < last:
            line.arrive(k)
            if k < last - 1:
                line.start(k + 1)
        if k == 0:
            meta_in()
            c_each(lambda copy: copy.wait())
        left, right = (row_a, row_b) if k < last else (own_a, own_b)
        hid, cot = h_all[block], c_all[block]
        if k < last:
            choose(k, block, left, right)
        if k == 0:
            some_experts(0, experts_here - 1, k, block, left, right)
            for which in range(2):
                for copy in cross_remote(which):
                    copy.wait_recv()
                for copy in half_remote(2 + which, core):
                    copy.start()
            for which in range(2):
                for copy in half_remote(2 + which, 1 - core):
                    copy.wait_recv()
            some_experts(experts_here - 1, experts_here, k, block, left, right)
        elif k < last:
            some_experts(0, experts_here, k, block, left, right)
        else:
            some_experts(experts_here - 1, experts_here, k, block, left, right)
        both, active, slope = swiglu_parts(nn(hid, gate_w), nn(hid, up_w))
        act = both.astype(bf16)
        d_act = nt(cot, down_w)
        d_gate = (d_act * slope).astype(bf16)
        d_up = (d_act * active).astype(bf16)
        kept_shared[block, :, 0:hidden] = d_gate
        kept_shared[block, :, hidden : 2 * hidden] = d_up
        kept_shared[block, :, 2 * hidden : 3 * hidden] = act
        dh_stage[k] = (
            tn(picks[block], right[...]) + nt(d_gate, gate_w) + nt(d_up, up_w)
        ).astype(bf16)
        if k == n - 1:
            dh_own.start()
            dg_own.start()
        else:
            give_back(dh_stage.at[k], dh_out, k, block, dh_send, dh_recv).start()
            give_back(dg_stage.at[k], dgate_out, k, block, dg_send, dg_recv).start()
        if k >= 2:
            mix_copy(k - 2, order[k - 2]).wait()
        mix_stage[k % 2] = (tn(picks[block], left[...]) + nn(act, down_w)).astype(bf16)
        mix_copy(k, block).start()

    half = width // 2
    mine, other = pl.ds(core * half, half), pl.ds((1 - core) * half, half)
    sibling = (1 - core, chip)
    left, right = pl.ds(0, 2 * ff), pl.ds(2 * ff, ff)
    keep_base, give_base = wires.take(2 * experts_here + 1), wires.take(2 * experts_here + 1)

    def keep(e):
        return (
            wires.local(wgu.at[e, mine, :], e_mine.at[e, :, left], keep_base + 2 * e),
            wires.local(down_stage.at[e % 2, mine, :], e_mine.at[e, :, right], keep_base + 2 * e + 1),
        )

    def give(e):
        return (
            wires.remote(wgu.at[e, other, :], e_other.at[e, :, left], give_base + 2 * e, sibling),
            wires.remote(
                down_stage.at[e % 2, other, :],
                e_other.at[e, :, right],
                give_base + 2 * e + 1,
                sibling,
            ),
        )

    for which in (2, 3):
        for copy in half_remote(which, core):
            copy.wait_send()
    for e in range(experts_here):
        for block in range(n):
            part = pl.ds(block * room, room)
            pick = picks[block, pl.ds(e * room, room), :]
            row_a[part, :] = nn(pick, h_all[block]).astype(bf16)
            row_b[part, :] = nn(pick, c_all[block]).astype(bf16)
        wgu[e] = tn(row_a[...], kept_gu[e]).astype(bf16)
        if e >= 2:
            keep(e - 2)[1].wait()
            give(e - 2)[1].wait_send()
        down_stage[e % 2] = tn(row_b[...], kept_act[e]).astype(bf16)
        for copy in keep(e) + give(e):
            copy.start()
    hid_all = h_all[...].reshape(n * rows, width)
    shared = kept_shared[...].reshape(n * rows, 3 * hidden)
    gu_stage[...] = tn(hid_all, shared[:, 0 : 2 * hidden]).astype(bf16)
    gu_keep = wires.local(gu_stage.at[mine, :], gu_mine, keep_base + 2 * experts_here)
    gu_give = wires.remote(gu_stage.at[other, :], gu_other, give_base + 2 * experts_here, sibling)
    gu_keep.start()
    gu_give.start()
    dsd_ref[...] = tn(shared[:, 2 * hidden :], c_all[...].reshape(n * rows, width)).astype(bf16)

    def settle(e):
        for which, (kept, given) in enumerate(zip(keep(e), give(e))):
            if which == 0 or e >= experts_here - 2:
                kept.wait()
                given.wait_send()
            given.wait_recv()

    line.leave()
    for e in range(experts_here):
        settle(e)

    for which in range(2):
        for copy in half_remote(which, core):
            copy.wait_send()
    for which in range(2):
        for copy in cross_remote(which):
            copy.wait_send()
    dh_own.wait()
    dg_own.wait()
    for k in range(max(0, n - 2), n):
        mix_copy(k, order[k]).wait()
    for k in range(n - 1):
        give_back(dh_stage.at[k], dh_out, k, order[k], dh_send, dh_recv).wait_send()
        give_back(dg_stage.at[k], dgate_out, k, order[k], dg_send, dg_recv).wait_send()
    for d in range(1, n):
        origin = lax.rem(outer + d, n)
        take_back(dh_out, origin, dh_recv).wait_recv()
        take_back(dgate_out, origin, dg_recv).wait_recv()
    gu_keep.wait()
    gu_give.wait()
    wires.finish()


def experts_line(room, hidden, shards, collective, h_own, meta, c_parts, weights, sides, sgu, sd):
    n = shards // KEY_VALUE_HEADS
    rows, width = h_own.shape
    n_experts, ff = KEY_VALUE_HEADS, weights[0].shape[2]
    half = width // 2
    any_spec = pl.BlockSpec(memory_space=pl.ANY)
    vmem = pl.BlockSpec(memory_space=pltpu.VMEM)
    e_shape = (n_experts, half, 3 * ff)
    sems = 112 + 24 * n

    def kernel(*refs):
        experts_line_kernel(room, hidden, shards, refs)

    return pl.pallas_call(
        kernel,
        in_specs=[any_spec] * (2 + len(c_parts) + 3 + len(sides)) + [vmem] * 2,
        out_specs=[any_spec] * 7 + [vmem],
        out_shape=[
            jax.ShapeDtypeStruct((n, rows, width), bf16),
            jax.ShapeDtypeStruct(meta.shape, f32),
            jax.ShapeDtypeStruct((n, rows, width), bf16),
            jax.ShapeDtypeStruct(e_shape, bf16),
            jax.ShapeDtypeStruct(e_shape, bf16),
            jax.ShapeDtypeStruct((half, 2 * hidden), bf16),
            jax.ShapeDtypeStruct((half, 2 * hidden), bf16),
            jax.ShapeDtypeStruct(sd.shape, bf16),
        ],
        scratch_shapes=[
            pltpu.VMEM((n, rows, width), bf16),
            pltpu.VMEM((n, rows, width), bf16),
            pltpu.VMEM(meta.shape, f32),
            pltpu.VMEM((n_experts, width, 2 * ff), bf16),
            pltpu.VMEM((n_experts, ff, width), bf16),
            pltpu.VMEM((n, n_experts * room, rows), bf16),
            pltpu.VMEM((n_experts, n * room, 2 * ff), bf16),
            pltpu.VMEM((n_experts, n * room, ff), bf16),
            pltpu.VMEM((n, rows, 3 * hidden), bf16),
            pltpu.VMEM((n * room, width), bf16),
            pltpu.VMEM((n * room, width), bf16),
            pltpu.VMEM((n * room, width), bf16),
            pltpu.VMEM((n * room, width), bf16),
            pltpu.VMEM((n, rows, width), bf16),
            pltpu.VMEM((2, rows, width), bf16),
            pltpu.VMEM((n,) + meta.shape[1:], f32),
            pltpu.VMEM((2, width, ff), bf16),
            pltpu.VMEM((width, 2 * hidden), bf16),
        ]
        + [pltpu.SemaphoreType.DMA((sems,))] * 3,
        compiler_params=pltpu.CompilerParams(
            collective_id=collective, has_side_effects=True, vmem_limit_bytes=VMEM_LIMIT
        ),
        name="experts_line",
    )(h_own, meta, *c_parts, *weights, *sides, sgu, sd)


def experts_split(room, hidden, shards, collectives, h_own, meta, c_parts, weights, sides, sgu, sd):
    n_out, n_in = shards // KEY_VALUE_HEADS, KEY_VALUE_HEADS
    rows, width = h_own.shape
    core = lax.axis_index("seq")
    half = width // 2

    def spread_hidden(wires, ins, outs):
        waits = [
            wires.exchange("outer", lambda r, d: ins[0], lambda r, d: outs[0].at[d]),
            wires.exchange("outer", lambda r, d: ins[1].at[r], lambda r, d: outs[1].at[d]),
        ]
        waits += [
            wires.exchange(
                "inner",
                lambda r, d, k=k: ins[k].at[0],
                lambda r, d, k=k: outs[k].at[across(r, lax.rem(r + d, n_in))],
            )
            for k in range(2, 5)
        ]
        for wait in waits:
            wait()

    h_all, meta_all, wg, wu, wd = transfer(
        "spread_hidden",
        collectives[0],
        shards,
        ["outer", "inner"],
        2 * n_out + 3 * n_in,
        spread_hidden,
        [h_own, meta, *weights],
        [((n_out, rows, width), bf16), (meta.shape, f32)]
        + [((n_in,) + weight.shape[1:], bf16) for weight in weights],
    )
    c_all = jnp.stack(c_parts)
    at_once = math.gcd(n_out, 4)
    parts = [
        experts(
            room,
            hidden,
            h_all[i : i + at_once],
            c_all[i : i + at_once],
            meta_all[i : i + at_once],
            wg,
            wu,
            wd,
            sgu,
            sd,
        )
        for i in range(0, n_out, at_once)
    ]
    mix_part, dh_part, dgate_part = (
        jnp.concatenate([part[k] for part in parts], axis=0) for k in range(3)
    )
    e_grad, sgu_grad, sd_grad = (
        sum(part[k].astype(f32) for part in parts).astype(bf16) for k in range(3, 6)
    )

    def sum_hidden(wires, ins, outs):
        core = lax.axis_index("seq")
        dh_ref, dg_ref, e_ref, gu_ref = ins
        dhs, dgs, es, gus = outs
        other = pl.ds((1 - core) * half, half)
        waits = [
            wires.exchange(
                "outer", lambda r, d: dh_ref.at[(n_out - d) % n_out], lambda r, d: dhs.at[r]
            ),
            wires.exchange(
                "outer", lambda r, d: dg_ref.at[(n_out - d) % n_out], lambda r, d: dgs.at[r]
            ),
            wires.sibling(e_ref.at[:, other], es, es),
            wires.sibling(gu_ref.at[other], gus, gus),
        ]
        for wait in waits:
            wait()

    dhs, dgs, es, gus = transfer(
        "sum_hidden",
        collectives[1],
        shards,
        ["outer", "core"],
        2 * n_out + 8,
        sum_hidden,
        [dh_part, dgate_part, e_grad, sgu_grad],
        [
            ((n_out, rows, width), bf16),
            (meta.shape, f32),
            ((n_in, half, e_grad.shape[2]), bf16),
            ((half, 2 * hidden), bf16),
        ],
    )
    e_mine = lax.dynamic_slice_in_dim(e_grad, core * half, half, 1)
    gu_mine = lax.dynamic_slice_in_dim(sgu_grad, core * half, half, 0)
    return dhs, dgs, mix_part, e_mine, es, gu_mine, gus, sd_grad


def norm_rows(values, gain_vector):
    inverse = lax.rsqrt(jnp.mean(values * values, axis=-1, keepdims=True) + epsilon)
    normed = values * inverse
    return (normed, inverse, normed * gain_vector)


def norm_back(grad_hidden, normed, inverse, gain_vector):
    grad_normed = grad_hidden * gain_vector
    gain_grad = jnp.sum(grad_hidden * normed, axis=(0, 1))
    inner_mean = jnp.mean(grad_normed * normed, axis=-1, keepdims=True)
    return (inverse * (grad_normed - normed * inner_mean), gain_grad)


def pad_rows(array, axis):
    size = array.shape[axis]
    widths = [(0, 0)] * array.ndim
    widths[axis] = (0, round_up(size, 16) - size)
    return jnp.pad(array, widths) if widths[axis][1] else array


def pad_to(array, axis, size):
    widths = [(0, 0)] * array.ndim
    widths[axis] = (0, size - array.shape[axis])
    return jnp.pad(array, widths) if widths[axis][1] else array


def body(
    tokens,
    routes,
    out_grad,
    attn_gain,
    ffn_gain,
    query_projection,
    key_projection,
    value_projection,
    w_out,
    w_router,
    shared_gate,
    shared_up,
    shared_down,
    expert_gate,
    expert_up,
    expert_down,
):
    shards = lax.axis_size("fsdp")
    n_in = KEY_VALUE_HEADS
    n_out = shards // n_in
    core, chip, outer, inner = place()
    seg, seqs, width = tokens.shape
    rows = seg * seqs
    topk = routes.shape[2]
    n_experts = w_router.shape[1]
    w_rows = query_projection.shape[0]
    w_pad = round_up(w_rows, 16)
    d_rows = shared_down.shape[0]
    d_pad = round_up(d_rows, 16)
    half_chips = shards // 2
    q_cols = GROUP_MEMBERS * HEAD_SIZE
    cols = q_cols + 2 * HEAD_SIZE
    ff = expert_gate.shape[2]
    hid_core = n_in * d_rows
    hid = 2 * hid_core
    hid_pad = round_up(hid, 128)
    small = round_up(n_experts + 2, 128)
    chunk = n_in * seg
    half_width, half_ff = width // 2, ff // 2
    room = round_up(max(2, (3 * rows * topk + 2 * n_experts - 1) // (2 * n_experts)), 16)

    small_piece = pad_to(
        jnp.concatenate([w_router, attn_gain[:, None], ffn_gain[:, None]], axis=1), 1, small
    )
    q_pieces = pad_rows(
        jnp.concatenate(
            [
                query_projection.reshape(w_rows, n_in, q_cols),
                key_projection.reshape(w_rows, n_in, HEAD_SIZE),
                value_projection.reshape(w_rows, n_in, HEAD_SIZE),
                jnp.broadcast_to(small_piece[:, None], (w_rows, n_in, small)),
            ],
            axis=2,
        ).transpose(1, 0, 2),
        1,
    )

    def hidden_piece(weight):
        piece = weight.reshape(w_rows, 2, n_out, hid_core).transpose(2, 0, 1, 3)
        return pad_to(piece.reshape(n_out, w_rows, hid), 2, hid_pad)

    gu_pieces = pad_rows(
        jnp.concatenate([hidden_piece(shared_gate), hidden_piece(shared_up)], axis=2), 1
    )
    out_piece = pad_rows(w_out, 0)
    down_piece = pad_rows(shared_down, 0)
    x_own = tokens.transpose(1, 0, 2)
    c_own = out_grad.transpose(1, 0, 2)
    cot = c_own.reshape(rows, width)

    def shift(block, amount):
        return lax.ppermute(
            block, "fsdp", [(f, (f + amount * n_in) % shards) for f in range(shards)]
        )

    def swap(block, step):
        return lax.ppermute(
            block, "fsdp", [(f, f // n_in * n_in + (f % n_in ^ step)) for f in range(shards)]
        )

    def out_rows(wires, o_ref, wo_ref):
        core, chip, outer, inner = place()
        to_inner = 2 * core + chip // half_chips
        slot = lax.rem(chip, half_chips)
        base = wires.take(half_chips)
        sends = wires.take(n_out)
        across_core = wires.take(1)
        first = inner // 2 == core

        def copy(k):
            to = (core, k * n_in + to_inner)
            return to[1] == chip, pltpu.make_async_remote_copy(
                src_ref=o_ref,
                dst_ref=wo_ref.at[slot],
                send_sem=wires.send_sems.at[sends + k],
                recv_sem=wires.recv_sems.at[base + slot],
                device_id=to,
                device_id_type=MESH,
            )

        def start(k):
            here, send = copy(k)
            pl.when(jnp.logical_not(here))(send.start)
            pl.when(here)(lambda: wires.local(o_ref, wo_ref.at[slot], base).start())

        def leave(k):
            here, send = copy(k)
            pl.when(jnp.logical_not(here))(send.wait_send)

        def come(i):
            origin = (core, half_chips * lax.rem(inner, 2) + i)
            here = origin[1] == chip
            place_of = wo_ref.at[i]
            pl.when(jnp.logical_not(here))(
                wires.remote(place_of, place_of, base + i, origin).wait_recv
            )
            pl.when(here)(lambda: wires.local(o_ref, place_of, base).wait())

        def hand_on():
            return wires.remote(wo_ref, wo_ref, across_core, (1 - core, chip))

        def arrive():
            @pl.when(first)
            def _():
                repeat(0, half_chips, come)
                hand_on().start()

        def settle():
            @pl.when(first)
            def _():
                hand_on().wait_send()

            @pl.when(jnp.logical_not(first))
            def _():
                hand_on().wait_recv()

        repeat(0, n_out, start)
        wires.leaving.append(lambda: repeat(0, n_out, leave))
        return arrive, settle

    own_rows = half_chips // 2
    line = n_out == 4

    def fetch(wires, ins, outs):
        x_ref, q_ref, o_ref, *c_refs = ins
        xs_ref, wq_ref, wo_ref, *passed = outs
        core, chip, outer, inner = place()
        q_in = wires.exchange(
            "chips", lambda r, d: q_ref.at[lax.rem(r, n_in)], lambda r, d: wq_ref.at[core, r]
        )
        x_in = wires.exchange("plane", lambda r, d: x_ref.at[r // n_in], lambda r, d: xs_ref.at[r])
        o_in, o_settle = out_rows(wires, o_ref, wo_ref)
        if line:
            c_in = gather_step(wires, n_out, 0, c_refs * 2, passed)
        q_in()
        q_other = wires.sibling(wq_ref.at[core], wq_ref.at[core], wq_ref.at[1 - core])
        o_in()
        x_in()
        q_other()
        o_settle()
        if line:
            c_in()

    xs, wq, wo, *c_first = transfer(
        "fetch",
        0,
        shards,
        ["all"],
        4 * shards + 16,
        fetch,
        [x_own, q_pieces, out_piece] + [cot] * line,
        [
            ((2 * n_in, seg, width), bf16),
            ((2, shards, w_pad, cols + small), bf16),
            ((half_chips, w_pad, width), bf16),
        ]
        + [(cot.shape, bf16)] * (2 * line),
    )
    down_half = lax.dynamic_slice_in_dim(expert_down[0], core * half_ff, half_ff, 0)
    expert_half = jnp.concatenate(
        [
            lax.dynamic_slice_in_dim(expert_gate[0], core * half_width, half_width, 0),
            lax.dynamic_slice_in_dim(expert_up[0], core * half_width, half_width, 0),
        ]
        + [down_half[:, k : k + ff] for k in range(0, width, ff)],
        axis=0,
    )
    wq, expert_half = lax.optimization_barrier((wq, expert_half))
    side_x, side_y = swap(expert_half, 1), swap(expert_half, 2)
    wq = wq[:, :, :w_rows].reshape(width, cols + small)
    wo = wo[:, :w_rows].reshape(q_cols, width)
    wq, small_w = wq[:, :cols], wq[:, cols:]
    router_w = small_w[:, :n_experts]
    gain_one = small_w[:, n_experts].astype(f32)
    gain_two = small_w[:, n_experts + 1].astype(f32)

    h1 = norm_rows(xs.reshape(2 * chunk, width).astype(f32), gain_one)[2].astype(bf16)
    qkv = nn(h1, wq).astype(bf16)

    inputs = x_own.astype(f32)
    if line:
        mixed, log_rows, kv_all, out_sum, sgu, ws, *c_later = attend(
            1, shards, chunk, qkv, wo, gu_pieces, down_piece, c_first
        )
        c_parts = [cot] + [came[way] for way in range(2) for came in (c_first, c_later[:2], c_later[2:])]
        residual = inputs + out_sum
    else:
        mixed, log_rows, kv_all = attend(1, shards, chunk, qkv)
        mixed_low = mixed.astype(bf16)
        out_part = nn(mixed_low, wo).astype(bf16).reshape(2 * n_in, seg, width)

        def sum_out(wires, ins, outs):
            part_ref, gu_ref, s_ref = ins
            parts_ref, wgu_ref, ws_ref = outs
            gu_in, gu_settle, s_in, s_settle = spread_shared(wires, gu_ref, s_ref, wgu_ref, ws_ref)
            part_in = wires.exchange(
                "plane", lambda r, d: part_ref.at[r], lambda r, d: parts_ref.at[r]
            )
            gu_in()
            gu_settle.start()
            s_in()
            s_settle.start()
            part_in()
            gu_settle.wait()
            s_settle.wait()

        out_parts, sgu, ws = transfer(
            "sum_out",
            2,
            shards,
            ["all"],
            shards + 8 * n_in + 16,
            sum_out,
            [out_part, gu_pieces, down_piece],
            [
                ((2 * n_in, seg, width), bf16),
                ((2, shards, w_pad, 2 * hid_pad), bf16),
                ((2, n_in, d_pad, width), bf16),
            ],
        )
        c_parts = [cot] + [shift(cot, d) for d in range(1, n_out)]
        residual = inputs + jnp.sum(out_parts.astype(f32).reshape(2, n_in, seg, width), axis=1)
    sgu = sgu[:, :, :w_rows].reshape(width, 2 * hid_pad)
    ws = pad_to(ws[:, :, :d_rows].reshape(hid, width), 0, hid_pad)

    normed_two, inverse_two, scaled_two = norm_rows(residual, gain_two)
    hidden_two = scaled_two.astype(bf16).reshape(rows, width)
    logits = nn(hidden_two, router_w)
    flat_routes = routes.transpose(1, 0, 2).reshape(rows, topk)
    chooser = (flat_routes[:, :, None] == jnp.arange(n_experts, dtype=jnp.int32)).astype(f32)
    taken = jnp.sum(chooser, axis=1)
    chosen = jnp.where(taken > 0, logits, masked_score)
    exponent = jnp.where(
        taken > 0, jnp.exp(chosen - jnp.max(chosen, axis=-1, keepdims=True)), 0.0
    )
    gates = exponent / jnp.sum(exponent, axis=-1, keepdims=True)
    before = (
        lax.broadcasted_iota(jnp.int32, (rows, rows), 0)
        < lax.broadcasted_iota(jnp.int32, (rows, rows), 1)
    ).astype(bf16)
    slots = jnp.where(taken.T > 0, nn(taken.T.astype(bf16), before), -1.0)
    meta = jnp.concatenate(
        [gates.T.reshape(n_out, n_in, rows), slots.reshape(n_out, n_in, rows)], axis=1
    )

    run = functools.partial(experts_line if line else experts_split, room, hid_pad, shards)
    dhs, dgs, mix_part, e_mine, e_other, gu_mine, gus, sd_grad = run(
        3 if line else (3, 4),
        hidden_two,
        meta,
        c_parts,
        (expert_gate, expert_up, expert_down),
        (side_x, side_y),
        sgu,
        ws,
    )

    gu_half = (gu_mine.astype(f32) + gus.astype(f32)).astype(bf16)
    gu_half = pad_rows(gu_half.reshape(shards, w_rows, 2 * hid_pad), 1)
    sd_send = pad_rows(sd_grad[:hid].reshape(2 * n_in, d_rows, width), 1)

    grad_float = c_own.astype(f32)
    grad_gates = dgs[:, :n_in].reshape(n_experts, rows).T
    grad_logits = gates * (grad_gates - jnp.sum(gates * grad_gates, axis=-1, keepdims=True))
    router_grad = lax.dot_general(
        hidden_two.astype(f32),
        grad_logits,
        (((0,), (0,)), ((), ())),
        precision=lax.Precision.HIGHEST,
        preferred_element_type=f32,
    )
    grad_hidden_two = jnp.sum(dhs.astype(f32), axis=0) + lax.dot_general(
        grad_logits,
        router_w.astype(f32),
        (((1,), (1,)), ((), ())),
        precision=lax.Precision.HIGHEST,
        preferred_element_type=f32,
    )
    grad_norm_two, gain_two_grad = norm_back(
        grad_hidden_two.reshape(seqs, seg, width), normed_two, inverse_two, gain_two
    )
    grad_residual = grad_float + grad_norm_two
    grad_attn = grad_residual.astype(bf16)

    small_grad = pad_to(
        jnp.concatenate(
            [router_grad, jnp.zeros((width, 1), f32), gain_two_grad[:, None]], axis=1
        ),
        1,
        small,
    )
    if line:
        grad_hidden_one, wq_total, small_total, out_w_grad, down_w_grad, gus, *rest = finish(
            6,
            shards,
            chunk,
            n_experts,
            kv_all,
            wo,
            mixed,
            log_rows,
            h1,
            wq,
            gain_one[None],
            small_grad.astype(bf16),
            qkv,
            grad_attn,
            gu_half,
            sd_send,
            mix_part,
            (mix_part[1 % n_out], mix_part[(n_out - 1) % n_out]),
            e_mine,
            e_other,
        )
        *mix_third, e_total, _ = rest
        mixes = [mix_part[0].astype(f32)] + [
            jnp.where(inside, came.astype(f32), 0.0)
            for inside, came in zip((outer > 0, outer < n_out - 1), mix_third)
        ]
    else:
        mixes = [mix_part[0].astype(f32)] + [
            shift(mix_part[n_out - d], d).astype(f32) for d in range(1, n_out)
        ]

        def spread_grad(wires, ins, outs):
            second = wires.exchange("chips", lambda r, d: ins[1].at[r], lambda r, d: outs[1].at[r])
            first = wires.exchange(
                "plane", lambda r, d: ins[0].at[r // n_in], lambda r, d: outs[0].at[r]
            )
            first()
            second()

        grad_all, gus = transfer(
            "spread_grad",
            5,
            shards,
            ["all"],
            shards + 2 * n_in + 16,
            spread_grad,
            [grad_attn, gu_half],
            [((2 * n_in, seg, width), bf16), ((shards, w_pad, 2 * hid_pad), bf16)],
        )
        grad_all = grad_all.reshape(2 * chunk, width)
        e_sum = (e_mine.astype(f32) + e_other.astype(f32)).astype(bf16)
        grad_mixed = nt(grad_all, wo).astype(bf16)
        wo_grad = tn(mixed_low, grad_all).astype(bf16).reshape(half_chips, w_rows, width)
        wo_grad = pad_rows(wo_grad, 1)
        delta_rows = jnp.sum(
            (grad_mixed.astype(f32) * mixed).reshape(2, chunk, GROUP_MEMBERS, HEAD_SIZE), axis=-1
        ).transpose(2, 0, 1)
        dqkv, wos = attend_back(
            6,
            shards,
            chunk,
            qkv[:, :q_cols],
            kv_all,
            grad_mixed,
            log_rows,
            delta_rows,
            wo_grad,
        )
        wo_mine = lax.dynamic_slice_in_dim(wo_grad, core * own_rows, own_rows, 0)
        wo_half = (wo_mine.astype(f32) + wos.astype(f32)).astype(bf16)
        dh1_part = nt(dqkv, wq).astype(bf16).reshape(2 * n_in, seg, width)
        wq_send = pad_rows(tn(h1, dqkv).astype(bf16).reshape(2 * shards, w_rows, cols), 1)
        gain_one_grad = (
            jnp.sum(
                dh1_part.reshape(2 * chunk, width).astype(f32) * h1.astype(f32), axis=0
            )
            / gain_one
        )
        small_grad = small_grad.at[:, n_experts].set(gain_one_grad)
        small_send = pad_rows(small_grad.astype(bf16).reshape(2 * shards, w_rows, small), 1)

        def sum_first(wires, ins, outs):
            dh_ref, wq_ref, small_ref, s_ref, o_ref = ins
            dhs, wqs, smalls, sds, wos = outs
            waits = [
                out_rows_back(wires, shards, o_ref, wos),
                wires.exchange("all", lambda r, d: wq_ref.at[r], lambda r, d: wqs.at[r]),
                wires.exchange("plane", lambda r, d: dh_ref.at[r], lambda r, d: dhs.at[r]),
                wires.exchange("all", lambda r, d: small_ref.at[r], lambda r, d: smalls.at[r]),
                wires.exchange("plane", lambda r, d: s_ref.at[r], lambda r, d: sds.at[r]),
            ]
            for wait in waits:
                wait()

        dh1s, wq_parts, small_parts, sds, wos = transfer(
            "sum_first",
            7,
            shards,
            ["all"],
            4 * n_in + 6 * shards + 16,
            sum_first,
            [dh1_part, wq_send, small_send, sd_send, wo_half.reshape(own_rows * w_pad, width)],
            [
                ((2 * n_in, seg, width), bf16),
                ((2 * shards, w_pad, cols), bf16),
                ((2 * shards, w_pad, small), bf16),
                ((2 * n_in, d_pad, width), bf16),
                ((n_out, w_pad, width), bf16),
            ],
        )
        grad_hidden_one = jnp.sum(dh1s.astype(f32).reshape(2, n_in, seg, width), axis=1)
        wq_total = jnp.sum(
            wq_parts[:, :w_rows].astype(f32).reshape(2 * n_out, n_in, w_rows, cols), axis=0
        )
        down_w_grad = jnp.sum(sds[:, :d_rows].astype(f32), axis=0)
        out_w_grad = jnp.sum(wos[:, :w_rows].astype(f32), axis=0)
        small_total = jnp.sum(small_parts[:, :w_rows].astype(f32), axis=0)
        e_parts = [swap(e_sum[e], e) for e in range(1, n_in)]
        e_total = sum([part.astype(f32) for part in e_parts], e_sum[0].astype(f32)).astype(bf16)
        e_came = lax.ppermute(e_total, "seq", [(0, 1), (1, 0)])
        e_total = jnp.where(
            core == 0,
            jnp.concatenate([e_total, e_came], axis=0),
            jnp.concatenate([e_came, e_total], axis=0),
        )
    total_out = residual + sum(mixes).reshape(seqs, seg, width)
    normed_one, inverse_one, _ = norm_rows(inputs, gain_one)
    grad_norm_one = norm_back(grad_hidden_one, normed_one, inverse_one, gain_one)[0]
    tokens_grad = grad_residual + grad_norm_one

    wq_total = wq_total.transpose(1, 0, 2)
    query_grad = wq_total[:, :, :q_cols].reshape(w_rows, n_in * q_cols)
    key_grad = wq_total[:, :, q_cols : q_cols + HEAD_SIZE].reshape(w_rows, n_in * HEAD_SIZE)
    value_grad = wq_total[:, :, q_cols + HEAD_SIZE :].reshape(w_rows, n_in * HEAD_SIZE)
    gu_total = jnp.sum(
        gus[:, :w_rows].astype(f32).reshape(n_out, n_in, w_rows, 2 * hid_pad), axis=1
    )

    def hidden_whole(piece):
        piece = piece[:, :, :hid].reshape(n_out, w_rows, 2, hid_core)
        return piece.transpose(1, 2, 0, 3).reshape(w_rows, n_out * hid)

    gate_w_grad = hidden_whole(gu_total[:, :, :hid_pad])
    up_w_grad = hidden_whole(gu_total[:, :, hid_pad:])
    e_total = e_total.astype(f32)

    return (
        total_out.astype(bf16).transpose(1, 0, 2),
        tokens_grad.transpose(1, 0, 2),
        small_total[:, n_experts],
        small_total[:, n_experts + 1],
        query_grad,
        key_grad,
        value_grad,
        out_w_grad,
        small_total[:, :n_experts],
        gate_w_grad,
        up_w_grad,
        down_w_grad,
        e_total[:, :ff][None],
        e_total[:, ff : 2 * ff][None],
        e_total[:, 2 * ff :].T[None],
    )


def solution(mesh):
    rows = P(("seq", "fsdp"), None, None)
    matrix = P(("seq", "fsdp"), None)
    vector = P(("seq", "fsdp"))
    expert = P("fsdp", None, None)
    return jax.shard_map(
        body,
        mesh=mesh,
        in_specs=(rows,) * 3 + (vector,) * 2 + (matrix,) * 8 + (expert,) * 3,
        out_specs=(rows,) * 2 + (vector,) * 2 + (matrix,) * 8 + (expert,) * 3,
        check_vma=False,
    )
```

```python
import functools
import math

import jax
import jax.numpy as jnp
from jax import lax
from jax.experimental import pallas as pl
from jax.experimental.pallas import tpu as pltpu
from jax.sharding import PartitionSpec as P

QUERY_HEADS = 12
KEY_VALUE_HEADS = 4
HEAD_SIZE = 128
GROUP_MEMBERS = QUERY_HEADS // KEY_VALUE_HEADS

epsilon = 1e-06
masked_score = -1e30
MESH = pl.DeviceIdType.MESH
VMEM_LIMIT = 63 * 1024 * 1024
f32 = jnp.float32
bf16 = jnp.bfloat16


def round_up(number, step):
    return -(-number // step) * step


def nn(left, right):
    return lax.dot_general(left, right, (((1,), (0,)), ((), ())), preferred_element_type=f32)


def nt(left, right):
    return lax.dot_general(left, right, (((1,), (1,)), ((), ())), preferred_element_type=f32)


def tn(left, right):
    return lax.dot_general(left, right, (((0,), (0,)), ((), ())), preferred_element_type=f32)


def across(inner, step):
    low = lax.rem(inner + step, 2)
    high = lax.rem(inner // 2 + step // 2, 2)
    return low + 2 * high


def place():
    core = lax.axis_index("seq")
    chip = lax.axis_index("fsdp")
    return core, chip, chip // KEY_VALUE_HEADS, lax.rem(chip, KEY_VALUE_HEADS)


def group(kind, shards):
    core, chip, outer, inner = place()
    if kind == "plane":
        size = 2 * KEY_VALUE_HEADS
        return (
            size,
            core * KEY_VALUE_HEADS + inner,
            lambda r: (r // KEY_VALUE_HEADS, outer * KEY_VALUE_HEADS + lax.rem(r, KEY_VALUE_HEADS)),
        )
    if kind == "inner":
        return KEY_VALUE_HEADS, inner, lambda r: (core, outer * KEY_VALUE_HEADS + r)
    if kind == "outer":
        return shards // KEY_VALUE_HEADS, outer, lambda r: (core, r * KEY_VALUE_HEADS + inner)
    if kind == "chips":
        return shards, chip, lambda r: (core, r)
    if kind == "all":
        return 2 * shards, core * shards + chip, lambda r: (r // shards, lax.rem(r, shards))
    return 2, core, lambda r: (r, chip)


def repeat(first, last, step):
    if last - first <= 16:
        for index in range(first, last):
            step(index)
    else:

        def one(index, carry):
            step(index)
            return carry

        lax.fori_loop(first, last, one, 0)


class Wires:
    def __init__(self, shards, send_sems, recv_sems, local_sems):
        self.shards = shards
        self.send_sems, self.recv_sems, self.local_sems = send_sems, recv_sems, local_sems
        self.used = 0
        self.leaving = []

    def greet(self, kinds):
        barrier = pltpu.get_barrier_semaphore()
        total = 0
        for kind in kinds:
            size, me, device = group(kind, self.shards)

            def signal(d, size=size, me=me, device=device):
                pl.semaphore_signal(
                    barrier, inc=1, device_id=device(lax.rem(me + d, size)), device_id_type=MESH
                )

            repeat(1, size, signal)
            total += size - 1
        pl.semaphore_wait(barrier, total)

    def take(self, count):
        base = self.used
        self.used += count
        return base

    def remote(self, source, target, index, device):
        return pltpu.make_async_remote_copy(
            src_ref=source,
            dst_ref=target,
            send_sem=self.send_sems.at[index],
            recv_sem=self.recv_sems.at[index],
            device_id=device,
            device_id_type=MESH,
        )

    def local(self, source, target, index):
        return pltpu.make_async_copy(source, target, self.local_sems.at[index])

    def exchange(self, kind, source_for, target_from, own=True):
        size, me, device = group(kind, self.shards)
        base = self.take(size)

        def copy(d):
            to = lax.rem(me + d, size)
            return self.remote(source_for(to, d), target_from(me, d), base + d, device(to))

        repeat(1, size, lambda d: copy(d).start())
        if own:
            self.local(source_for(me, 0), target_from(me, 0), base).start()
        self.leaving.append(lambda: repeat(1, size, lambda d: copy(d).wait_send()))

        def arrive(then=None):
            def one(d):
                came = lax.rem(me - d + size, size)
                place_of = target_from(came, d)
                self.remote(place_of, place_of, base + d, device(came)).wait_recv()
                if then is not None:
                    then(d)

            repeat(1, size, one)
            if own:
                self.local(source_for(me, 0), target_from(me, 0), base).wait()

        return arrive

    def sibling(self, source, target, comes):
        core, chip, _, _ = place()
        device = (1 - core, chip)
        index = self.take(1)
        copy = self.remote(source, target, index, device)
        copy.start()
        self.leaving.append(copy.wait_send)
        return self.remote(comes, comes, index, device).wait_recv

    def finish(self):
        for leave in self.leaving:
            leave()


def transfer(name, collective, shards, kinds, sems, body, operands, outs, scratch=()):
    count = len(operands)

    def kernel(*refs):
        ins, results = refs[:count], refs[count : count + len(outs)]
        room, sem_refs = refs[count + len(outs) : -3], refs[-3:]
        wires = Wires(shards, *sem_refs)
        wires.greet(kinds)
        body(wires, ins, results, *room)
        wires.finish()

    return pl.pallas_call(
        kernel,
        out_shape=[jax.ShapeDtypeStruct(shape, kind) for shape, kind in outs],
        in_specs=[pl.BlockSpec(memory_space=pl.ANY)] * count,
        out_specs=[pl.BlockSpec(memory_space=pl.ANY)] * len(outs),
        scratch_shapes=[pltpu.VMEM(shape, kind) for shape, kind in scratch]
        + [pltpu.SemaphoreType.DMA((sems,))] * 3,
        compiler_params=pltpu.CompilerParams(
            collective_id=collective, has_side_effects=True, vmem_limit_bytes=VMEM_LIMIT
        ),
        name=name,
    )(*operands)


def add_pieces(wires, first, second, result, size, left, right, total):
    items, rows, _ = first.shape
    per_item = rows // size
    count = items * per_item
    load_base, store_base = wires.take(4), wires.take(2)

    def cut(i):
        return i // per_item, pl.ds(i % per_item * size, size)

    def loads(i):
        slot = i % 2
        return (
            wires.local(first.at[cut(i)], left(slot), load_base + 2 * slot),
            wires.local(second.at[cut(i)], right(slot), load_base + 2 * slot + 1),
        )

    def store(i):
        return wires.local(total(i % 2), result.at[cut(i)], store_base + i % 2)

    for copy in loads(0):
        copy.start()
    for i in range(count):
        if i + 1 < count:
            for copy in loads(i + 1):
                copy.start()
        for copy in loads(i):
            copy.wait()
        if i >= 2:
            store(i - 2).wait()
        slot = i % 2
        total(slot)[...] = (left(slot)[...].astype(f32) + right(slot)[...].astype(f32)).astype(bf16)
        store(i).start()
    for i in range(max(0, count - 2), count):
        store(i).wait()


def neighbours(wires, n, sources, targets, sends, comes):
    core, chip, outer, inner = place()
    base = wires.take(2)

    def copy(way):
        sign = (1, -1)[way]
        to = lax.rem(outer + sign + n, n)
        device = (core, to * KEY_VALUE_HEADS + inner)
        return wires.remote(sources[way], targets[way], base + way, device)

    def come(way):
        sign = (1, -1)[way]
        origin = lax.rem(outer - sign + n, n)
        device = (core, origin * KEY_VALUE_HEADS + inner)
        return wires.remote(targets[way], targets[way], base + way, device)

    def each(conditions, action):
        for way in range(2):
            pl.when(conditions[way])(lambda way=way: action(way))

    each(sends, lambda way: copy(way).start())
    wires.leaving.append(lambda: each(sends, lambda way: copy(way).wait_send()))
    return lambda: each(comes, lambda way: come(way).wait_recv())


def gather_step(wires, n, step, sources, targets):
    outer = place()[2]
    sends = ((outer >= step) & (outer < n - 1), (outer < n - step) & (outer > 0))
    comes = (outer > step, outer < n - 1 - step)
    return neighbours(wires, n, sources, targets, sends, comes)


def sum_step(wires, n, step, sources, targets):
    outer = place()[2]
    sends = (
        (outer <= step) & (outer < n - 1),
        (outer >= n - 1 - step) & (outer > 0),
    )
    comes = (
        (outer >= 1) & (outer <= step + 1),
        (outer <= n - 2) & (outer >= n - 2 - step),
    )
    return neighbours(wires, n, sources, targets, sends, comes)


def out_rows_back(wires, shards, grad_ref, sums_ref):
    core, chip, outer, inner = place()
    n_in, n_out, half_chips = KEY_VALUE_HEADS, shards // KEY_VALUE_HEADS, shards // 2
    own_rows = half_chips // 2
    rows = sums_ref.shape[1]
    from_inner = 2 * core + chip // half_chips
    from_core = lax.rem(chip, half_chips) // own_rows
    sends = wires.take(own_rows)
    base = wires.take(n_out)

    def copy(i):
        to = (inner // 2, half_chips * lax.rem(inner, 2) + core * own_rows + i)
        here = (to[0] == core) & (to[1] == chip)
        return here, pltpu.make_async_remote_copy(
            src_ref=grad_ref.at[pl.ds(i * rows, rows)],
            dst_ref=sums_ref.at[outer],
            send_sem=wires.send_sems.at[sends + i],
            recv_sem=wires.recv_sems.at[base + outer],
            device_id=to,
            device_id_type=MESH,
        )

    def start(i):
        here, send = copy(i)
        pl.when(jnp.logical_not(here))(send.start)
        pl.when(here)(lambda: wires.local(grad_ref.at[pl.ds(i * rows, rows)], sums_ref.at[outer], base).start())

    def leave(i):
        here, send = copy(i)
        pl.when(jnp.logical_not(here))(send.wait_send)

    def come(k):
        origin = (from_core, k * n_in + from_inner)
        here = (origin[0] == core) & (origin[1] == chip)
        place_of = sums_ref.at[k]
        pl.when(jnp.logical_not(here))(
            wires.remote(place_of, place_of, base + k, origin).wait_recv
        )
        pl.when(here)(lambda: wires.local(place_of, place_of, base).wait())

    repeat(0, own_rows, start)
    wires.leaving.append(lambda: repeat(0, own_rows, leave))
    return lambda: repeat(0, n_out, come)


class Line:
    def __init__(self, wires, source, every):
        self.wires, self.source, self.every = wires, source, every
        self.n = every.shape[0]
        self.core, _, self.outer, self.inner = place()
        self.bases = {1: wires.take(self.n), -1: wires.take(self.n)}

    def device(self, at):
        return self.core, at * KEY_VALUE_HEADS + self.inner

    def order(self):
        low = self.outer < self.n // 2
        return [
            lax.rem(jnp.where(low, self.outer + k, self.outer - k + self.n), self.n)
            for k in range(self.n)
        ]

    def hop(self, step, sign):
        to = lax.rem(self.outer + sign + self.n, self.n)
        block = lax.rem(self.outer - sign * step + 2 * self.n, self.n)
        source = self.source if step == 0 else self.every.at[block]
        index = self.bases[sign] + step
        return self.wires.remote(source, self.every.at[block], index, self.device(to))

    def sends(self, step, sign):
        to, block = self.outer + sign, self.outer - sign * step
        return (to >= 0) & (to < self.n) & (block >= 0) & (block < self.n)

    def start(self, step):
        for sign in (1, -1):
            pl.when(self.sends(step, sign))(lambda sign=sign: self.hop(step, sign).start())

    def arrive(self, step):
        for sign in (1, -1):
            come = self.outer - sign * (step + 1)

            def wait(sign=sign, come=come):
                block = self.every.at[lax.rem(come + self.n, self.n)]
                to = lax.rem(self.outer - sign + self.n, self.n)
                index = self.bases[sign] + step
                self.wires.remote(block, block, index, self.device(to)).wait_recv()

            pl.when((come >= 0) & (come < self.n))(wait)

    def leave(self):
        for step in range(self.n - 1):
            for sign in (1, -1):
                pl.when(self.sends(step, sign))(
                    lambda step=step, sign=sign: self.hop(step, sign).wait_send()
                )


def far_first(outer, n):
    low = outer < n // 2
    order = []
    for k in range(n - 1):
        down = n - 1 - k
        order.append(
            jnp.where(low, jnp.where(down <= outer, down - 1, down), jnp.where(k >= outer, k + 1, k))
        )
    return order


def causal(scores):
    key_at = lax.broadcasted_iota(jnp.int32, scores.shape, 0)
    query_at = lax.broadcasted_iota(jnp.int32, scores.shape, 1)
    return jnp.where(key_at <= query_at, scores, masked_score)


def each_pair(block, outer, own, pair):
    def some(head, carry):
        if own:
            pair(head, 0, block, 0, True)
            pair(head, 1, block, 0, False)
            pair(head, 1, block, 1, True)
        else:
            pair(head, 1, block, 0, False)

            @pl.when(block < outer)
            def _():
                pair(head, 0, block, 0, False)
                pair(head, 1, block, 1, False)

        return carry

    lax.fori_loop(0, GROUP_MEMBERS, some, 0)


def attend_kernel(shards, chunk, joined, gain_col, out_rows, *refs):
    if joined:
        x_ref, q_pieces, o_ref, cot_ref, expert_ref, gu_ref, s_ref, *refs = refs
    else:
        qkv_in, *refs = refs
    mixed_ref, log_ref, kv_out, *refs = refs
    if joined:
        out_ref, h1_ref, qkv_ref, wgu_ref, ws_ref, wq_out, wo_out, side_x, side_y, *refs = refs
        passes, refs = (refs[:2], refs[2:4], refs[4:6]), refs[6:]
        out_stage, out_recv, xs, wq, wo, *refs = refs
    else:
        qkv_ref, *refs = refs
    kv_all, largest, total, summed, send_sems, recv_sems, local_sems = refs
    core, chip, outer, inner = place()
    q_width = GROUP_MEMBERS * HEAD_SIZE
    cols = q_width + 2 * HEAD_SIZE
    wires = Wires(shards, send_sems, recv_sems, local_sems)
    factor = HEAD_SIZE**-0.5 * math.log2(math.e)
    if joined:
        wires.greet(["all"])
        q_in = wires.exchange(
            "chips",
            lambda r, d: q_pieces.at[lax.rem(r, KEY_VALUE_HEADS)],
            lambda r, d: wq.at[core, r],
        )
        x_in = wires.exchange(
            "plane", lambda r, d: x_ref.at[r // KEY_VALUE_HEADS], lambda r, d: xs.at[r]
        )
        o_in, o_settle = out_rows(wires, o_ref, wo)
        passed = gather_step(wires, kv_all.shape[0], 0, [cot_ref, cot_ref], passes[0])
        q_in()
        wires.sibling(wq.at[core], wq.at[core], wq.at[1 - core])()
        x_in()
        sides = [
            wires.remote(
                expert_ref,
                side,
                wires.take(1),
                (core, outer * KEY_VALUE_HEADS + across(inner, step)),
            )
            for step, side in ((1, side_x), (2, side_y))
        ]
        for side in sides:
            side.start()
        wide = xs.shape[2]
        small = wq[:, :, :, cols:].reshape(wide, wq.shape[3] - cols).astype(f32)
        gain = small.T[gain_col : gain_col + 1, :]
        seg = xs.shape[1]
        for r in range(xs.shape[0]):
            values = xs[r].astype(f32)
            inverse = lax.rsqrt(jnp.mean(values * values, axis=-1, keepdims=True) + epsilon)
            h1_ref[r * seg : (r + 1) * seg, :] = (values * inverse * gain).astype(bf16)
        projection = wq[:, :, :, 0:cols].reshape(wide, cols)
        for half in range(2):
            rows = pl.ds(half * chunk, chunk)
            part = nn(h1_ref[rows, :], projection).astype(bf16)
            qkv_ref[rows, :] = part
            kv_all[outer, rows, :] = part[:, q_width:]
    else:
        load = wires.local(qkv_in, qkv_ref, wires.take(1))
        load.start()
        load.wait()
        kv_all[outer] = qkv_ref[:, q_width:]
        wires.greet(["outer"])
    line = Line(wires, kv_all.at[outer], kv_all)
    line.start(0)
    largest[...] = jnp.full_like(largest, masked_score)
    total[...] = jnp.zeros_like(total)
    summed[...] = jnp.zeros_like(summed)

    def pair(head, half, block, key_half, masked):
        cols = pl.ds(pl.multiple_of(head * HEAD_SIZE, HEAD_SIZE), HEAD_SIZE)
        rows = pl.ds(key_half * chunk, chunk)
        query = qkv_ref[pl.ds(half * chunk, chunk), cols]
        scores = nt(kv_all[block, rows, 0:HEAD_SIZE], query)
        if masked:
            scores = causal(scores)
        before = largest[head, half]
        new = jnp.maximum(before, jnp.max(scores, axis=0, keepdims=True))
        weights = jnp.exp2((scores - new) * factor)
        shrink = jnp.exp2((before - new) * factor)
        largest[head, half] = new
        total[head, half] = total[head, half] * shrink + jnp.sum(weights, axis=0, keepdims=True)
        summed[head, half] = summed[head, half] * shrink + tn(
            kv_all[block, rows, HEAD_SIZE : 2 * HEAD_SIZE], weights.astype(bf16)
        )

    for k, block in enumerate(line.order()):
        if k > 0:
            line.arrive(k - 1)
            if k < line.n - 1:
                line.start(k)
        if joined and k == line.n - 2:
            passed()
            passed = gather_step(wires, line.n, 1, passes[0], passes[1])
            o_in()
            gu_in, gu_settle, s_in, s_settle = spread_shared(wires, gu_ref, s_ref, wgu_ref, ws_ref)
        each_pair(block, outer, k == 0, pair)
    keep = wires.local(kv_all, kv_out, wires.take(1))
    keep.start()
    for head in range(GROUP_MEMBERS):
        for half in range(2):
            mixed_ref[
                half * chunk : (half + 1) * chunk, head * HEAD_SIZE : (head + 1) * HEAD_SIZE
            ] = (summed[head, half] / total[head, half]).T
            log_ref[head, half : half + 1, :] = largest[head, half] * factor + jnp.log2(
                total[head, half]
            )
    if joined:
        o_settle()
        w_out = wo[...].reshape(q_width, wide)
        for half in range(2):
            rows = pl.ds(half * chunk, chunk)
            out_stage[rows, :] = nn(mixed_ref[rows, :].astype(bf16), w_out).astype(bf16)
        out_in = wires.exchange(
            "plane", lambda r, d: out_stage.at[pl.ds(r * seg, seg)], lambda r, d: out_recv.at[r]
        )
        passed()
        passed = gather_step(wires, line.n, 2, passes[1], passes[2])
        kept = [wires.local(wq, wq_out, wires.take(1)), wires.local(wo, wo_out, wires.take(1))]
        for copy in kept:
            copy.start()
        gu_in()
        gu_settle.start()
        s_in()
        s_settle.start()
        out_in()
        for half in range(2):
            parts = out_recv[half * KEY_VALUE_HEADS].astype(f32)
            for j in range(1, KEY_VALUE_HEADS):
                parts = parts + out_recv[half * KEY_VALUE_HEADS + j].astype(f32)
            out_ref[half] = parts
        gu_settle.wait()
        s_settle.wait()
        passed()
        for copy in sides + kept:
            copy.wait()
    line.leave()
    wires.finish()
    keep.wait()


def spread_shared(wires, gu_ref, s_ref, wgu_ref, ws_ref):
    core, chip, _, _ = place()
    sibling = (1 - core, chip)
    gu_in = wires.exchange(
        "chips",
        lambda r, d: gu_ref.at[r // KEY_VALUE_HEADS],
        lambda r, d: wgu_ref.at[core, r],
    )
    s_in = wires.exchange("inner", lambda r, d: s_ref, lambda r, d: ws_ref.at[core, r])
    gu_settle = wires.remote(wgu_ref.at[core], wgu_ref.at[core], wires.take(1), sibling)
    s_settle = wires.remote(ws_ref.at[core], ws_ref.at[core], wires.take(1), sibling)
    return gu_in, gu_settle, s_in, s_settle


def attend(collective, shards, chunk, operands, gain_col=None, out_rows=None):
    joined = out_rows is not None
    n_out = shards // KEY_VALUE_HEADS
    rows = 2 * chunk
    seg = chunk // KEY_VALUE_HEADS
    cols = (GROUP_MEMBERS + 2) * HEAD_SIZE
    more_outs, more_scratch = [], [pltpu.VMEM((rows, cols), bf16)]
    if joined:
        _, q_pieces, out_piece, cot, expert_half, gu, down = operands
        wide = out_piece.shape[1]
        wq_shape = (2, shards) + q_pieces.shape[1:]
        wo_shape = (shards // 2,) + out_piece.shape

        def array(shape, kind=bf16):
            return jax.ShapeDtypeStruct(shape, kind)

        more_outs = [
            array((2, seg, wide), f32),
            array((rows, wide)),
            array((rows, cols)),
            array((2, shards) + gu.shape[1:]),
            array((2, KEY_VALUE_HEADS) + down.shape),
            array(wq_shape),
            array(wo_shape),
            array(expert_half.shape),
            array(expert_half.shape),
        ] + [array(cot.shape)] * 6
        more_scratch = [
            pltpu.VMEM((rows, wide), bf16),
            pltpu.VMEM((2 * KEY_VALUE_HEADS, seg, wide), bf16),
            pltpu.VMEM((2 * KEY_VALUE_HEADS, seg, wide), bf16),
            pltpu.VMEM(wq_shape, bf16),
            pltpu.VMEM(wo_shape, bf16),
        ]
    kv_shape = (n_out, rows, 2 * HEAD_SIZE)
    vmem = pl.BlockSpec(memory_space=pltpu.VMEM)
    hbm = pl.BlockSpec(memory_space=pl.ANY)
    state = (GROUP_MEMBERS, 2, 1, chunk)
    return pl.pallas_call(
        functools.partial(attend_kernel, shards, chunk, joined, gain_col, out_rows),
        in_specs=[hbm] * len(operands),
        out_specs=[vmem, vmem, hbm] + ([vmem] * 3 + [hbm] * 12) * joined,
        out_shape=[
            jax.ShapeDtypeStruct((rows, GROUP_MEMBERS * HEAD_SIZE), f32),
            jax.ShapeDtypeStruct((GROUP_MEMBERS, 2, chunk), f32),
            jax.ShapeDtypeStruct(kv_shape, bf16),
        ]
        + more_outs,
        scratch_shapes=more_scratch
        + [
            pltpu.VMEM(kv_shape, bf16),
            pltpu.VMEM(state, f32),
            pltpu.VMEM(state, f32),
            pltpu.VMEM((GROUP_MEMBERS, 2, HEAD_SIZE, chunk), f32),
        ]
        + [pltpu.SemaphoreType.DMA((2 * n_out + 4 * shards + 64,))] * 3,
        compiler_params=pltpu.CompilerParams(
            collective_id=collective, has_side_effects=True, vmem_limit_bytes=VMEM_LIMIT
        ),
        name="attend",
    )(*operands)


def attend_back_kernel(shards, chunk, own_rows, *refs):
    q_ref, kv_ref, grad_ref, log_ref, delta_ref, wo_ref, *refs = refs
    dqkv_ref, wo_other, *refs = refs
    came, stage, sums, dq_sums, send_sems, recv_sems, local_sems = refs
    wires = Wires(shards, send_sems, recv_sems, local_sems)
    core, chip, outer, inner = place()
    n = kv_ref.shape[0]
    scale = HEAD_SIZE**-0.5
    factor = scale * math.log2(math.e)
    wires.greet(["outer", "core"])
    wo_in = wires.sibling(
        wo_ref.at[pl.ds((1 - core) * own_rows, own_rows)], wo_other, wo_other
    )
    send_base, recv_base = wires.take(n), wires.take(n)
    dq_sums[...] = jnp.zeros_like(dq_sums)

    def pair(head, half, block, key_half, masked):
        cols = pl.ds(pl.multiple_of(head * HEAD_SIZE, HEAD_SIZE), HEAD_SIZE)
        mine, rows = pl.ds(half * chunk, chunk), pl.ds(key_half * chunk, chunk)
        query, grad = q_ref[mine, cols], grad_ref[mine, cols]
        key = kv_ref[block, rows, 0:HEAD_SIZE]
        value = kv_ref[block, rows, HEAD_SIZE : 2 * HEAD_SIZE]
        scores = nt(key, query)
        if masked:
            scores = causal(scores)
        weights = jnp.exp2(scores * factor - log_ref[head, half : half + 1, :])
        grad_scores = (
            weights * (nt(value, grad) - delta_ref[head, half : half + 1, :])
        ).astype(bf16)
        sums[rows, 0:HEAD_SIZE] += nn(grad_scores, query)
        sums[rows, HEAD_SIZE : 2 * HEAD_SIZE] += nn(weights.astype(bf16), grad)
        dq_sums[mine, cols] += tn(grad_scores, key)

    def send(k, block):
        return pltpu.make_async_remote_copy(
            src_ref=stage.at[k],
            dst_ref=came.at[outer],
            send_sem=send_sems.at[send_base + k],
            recv_sem=recv_sems.at[recv_base + outer],
            device_id=(core, block * KEY_VALUE_HEADS + inner),
            device_id_type=MESH,
        )

    order = far_first(outer, n)
    for k, block in enumerate(order + [outer]):
        sums[...] = jnp.zeros_like(sums)
        each_pair(block, outer, k == n - 1, pair)
        if k < n - 1:
            stage[k] = sums[...].astype(bf16)
            send(k, block).start()
    width = GROUP_MEMBERS * HEAD_SIZE
    dqkv_ref[:, 0:width] = (dq_sums[...] * scale).astype(bf16)
    for d in range(1, n):
        origin = lax.rem(outer + d, n)
        pltpu.make_async_remote_copy(
            src_ref=came.at[origin],
            dst_ref=came.at[origin],
            send_sem=send_sems.at[send_base],
            recv_sem=recv_sems.at[recv_base + origin],
            device_id=(core, origin * KEY_VALUE_HEADS + inner),
            device_id_type=MESH,
        ).wait_recv()
        sums[...] += came[origin].astype(f32)
    dqkv_ref[:, width : width + HEAD_SIZE] = (sums[:, 0:HEAD_SIZE] * scale).astype(bf16)
    dqkv_ref[:, width + HEAD_SIZE :] = sums[:, HEAD_SIZE:].astype(bf16)
    for k, block in enumerate(order):
        send(k, block).wait_send()
    wo_in()
    wires.finish()


def attend_back(collective, shards, chunk, q, kv_all, grad_mixed, log_rows, delta_rows, wo_grad):
    n_out, rows, kv_cols = kv_all.shape
    own_rows = wo_grad.shape[0] // 2
    vmem = pl.BlockSpec(memory_space=pltpu.VMEM)
    hbm = pl.BlockSpec(memory_space=pl.ANY)
    width = GROUP_MEMBERS * HEAD_SIZE
    return pl.pallas_call(
        functools.partial(attend_back_kernel, shards, chunk, own_rows),
        in_specs=[vmem] * 5 + [hbm],
        out_specs=[vmem, hbm],
        out_shape=[
            jax.ShapeDtypeStruct((rows, width + kv_cols), bf16),
            jax.ShapeDtypeStruct((own_rows,) + wo_grad.shape[1:], bf16),
        ],
        scratch_shapes=[
            pltpu.VMEM(kv_all.shape, bf16),
            pltpu.VMEM(kv_all.shape, bf16),
            pltpu.VMEM((rows, kv_cols), f32),
            pltpu.VMEM((rows, width), f32),
        ]
        + [pltpu.SemaphoreType.DMA((2 * n_out + 8,))] * 3,
        compiler_params=pltpu.CompilerParams(
            collective_id=collective, has_side_effects=True, vmem_limit_bytes=VMEM_LIMIT
        ),
        name="attend_back",
    )(q, kv_all, grad_mixed, log_rows, delta_rows, wo_grad)


def finish_kernel(shards, chunk, gain_col, *refs):
    (
        kv_ref,
        wo_ref,
        mixed_ref,
        log_ref,
        h1_ref,
        wq_ref,
        gain_ref,
        small_ref,
        qkv_ref,
        grad_own,
        gu_ref,
        sd_ref,
        mix_ref,
        mix_up,
        mix_down,
        e_first_ref,
        e_second_ref,
        dh1_out,
        wq_out,
        small_out,
        wo_out,
        sd_out,
        gu_out,
        mix_up_out,
        mix_down_out,
        e_both,
        e_ref,
        q_ref,
        grad_all,
        dmixed,
        delta,
        came,
        stage,
        sums,
        dq_sums,
        dqkv,
        dwo,
        wo_came,
        wo_recv,
        dwq,
        wq_came,
        wq_recv,
        small_all,
        small_came,
        small_recv,
        dh_stage,
        dh_recv,
        sd_recv,
        mix_came,
        mix_term,
        mix_came_last,
        mix_term_last,
        e_came,
        e_term,
        e_last,
        e_own,
        send_sems,
        recv_sems,
        local_sems,
    ) = refs
    wires = Wires(shards, send_sems, recv_sems, local_sems)
    core, chip, outer, inner = place()
    n = kv_ref.shape[0]
    scale = HEAD_SIZE**-0.5
    factor = scale * math.log2(math.e)
    width = GROUP_MEMBERS * HEAD_SIZE
    wide = h1_ref.shape[1]
    half_wide = wide // 2
    w_rows = wq_recv.shape[1]
    seg = dh_recv.shape[1]
    mine, other = pl.ds(core * half_wide, half_wide), pl.ds((1 - core) * half_wide, half_wide)
    wires.greet(["all"])
    q_load = wires.local(qkv_ref.at[:, pl.ds(0, width)], q_ref, wires.take(1))
    q_load.start()
    grad_in = wires.exchange(
        "plane", lambda r, d: grad_own.at[r // KEY_VALUE_HEADS], lambda r, d: grad_all.at[r]
    )
    gu_in = wires.exchange("chips", lambda r, d: gu_ref.at[r], lambda r, d: gu_out.at[r])
    sd_in = wires.exchange("plane", lambda r, d: sd_ref.at[r], lambda r, d: sd_recv.at[r])

    mix_steps = [sum_step(wires, n, 0, [mix_up, mix_down], [mix_came.at[0], mix_came.at[1]])]
    mix_loads = [
        wires.local(mix_ref.at[slot], target.at[way], wires.take(1))
        for target, slots in ((mix_term, (2 % n, (n - 2) % n)), (mix_term_last, (3 % n, (n - 3) % n)))
        for way, slot in enumerate(slots)
    ]
    for copy in mix_loads:
        copy.start()

    def mix_on(step, came, term, targets):
        mix_steps[-1]()
        for way in range(2):
            mix_loads[2 * (step - 1) + way].wait()
            inside = (outer > 0, outer < n - 1)[way]
            term[way] = (
                term[way].astype(f32) + jnp.where(inside, came[way].astype(f32), 0.0)
            ).astype(bf16)
        mix_steps.append(sum_step(wires, n, step, [term.at[0], term.at[1]], targets))

    add_pieces(
        wires,
        e_first_ref,
        e_second_ref,
        e_ref,
        half_wide // 3,
        lambda slot: dh_stage.at[pl.ds(slot * (half_wide // 3), half_wide // 3)],
        lambda slot: dh_stage.at[pl.ds((2 + slot) * (half_wide // 3), half_wide // 3)],
        lambda slot: e_own.at[pl.ds(slot * (half_wide // 3), half_wide // 3)],
    )

    e_cols = e_ref.shape[2] // 2
    e_cuts = (pl.ds(0, e_cols), pl.ds(e_cols, e_cols))
    e_sides = ((1, 2), (2, 1))

    def plane_device(step):
        return core, outer * KEY_VALUE_HEADS + across(inner, step)

    e_local, e_first, e_second = wires.take(3), wires.take(4), wires.take(2)
    e_loads = [wires.local(e_ref.at[0], e_own, e_local)]
    e_sends = []
    for way, (near, far) in enumerate(e_sides):
        e_loads.append(wires.local(e_ref.at[far, :, e_cuts[way]], e_term.at[way], e_local + 1 + way))
        for k, e in enumerate((near, 3)):
            e_sends.append(
                wires.remote(
                    e_ref.at[e, :, e_cuts[way]],
                    e_came.at[way, k],
                    e_first + 2 * way + k,
                    plane_device(near),
                )
            )
    for copy in e_sends + e_loads:
        copy.start()

    grad_in()
    q_load.wait()
    mix_on(1, mix_came, mix_term, [mix_came_last.at[0], mix_came_last.at[1]])
    per_half = grad_all.shape[0] // 2
    for half in range(2):
        rows = pl.ds(half * chunk, chunk)
        grad = grad_all[pl.ds(half * per_half, per_half)].reshape(chunk, wide)
        part = nt(grad, wo_ref[...]).astype(bf16)
        dmixed[rows, :] = part
        weighted = part.astype(f32) * mixed_ref[rows, :]
        for head in range(GROUP_MEMBERS):
            cols = slice(head * HEAD_SIZE, (head + 1) * HEAD_SIZE)
            delta[head, half] = jnp.sum(weighted[:, cols].T, axis=0, keepdims=True)

    send_base, recv_base = wires.take(n), wires.take(n)
    dq_sums[...] = jnp.zeros_like(dq_sums)

    def pair(head, half, block, key_half, masked):
        cols = pl.ds(pl.multiple_of(head * HEAD_SIZE, HEAD_SIZE), HEAD_SIZE)
        here, rows = pl.ds(half * chunk, chunk), pl.ds(key_half * chunk, chunk)
        query, grad = q_ref[here, cols], dmixed[here, cols]
        key = kv_ref[block, rows, 0:HEAD_SIZE]
        value = kv_ref[block, rows, HEAD_SIZE : 2 * HEAD_SIZE]
        scores = nt(key, query)
        if masked:
            scores = causal(scores)
        weights = jnp.exp2(scores * factor - log_ref[head, half : half + 1, :])
        grad_scores = (weights * (nt(value, grad) - delta[head, half])).astype(bf16)
        sums[rows, 0:HEAD_SIZE] += nn(grad_scores, query)
        sums[rows, HEAD_SIZE : 2 * HEAD_SIZE] += nn(weights.astype(bf16), grad)
        dq_sums[here, cols] += tn(grad_scores, key)

    def send(k, block):
        return pltpu.make_async_remote_copy(
            src_ref=stage.at[k],
            dst_ref=came.at[outer],
            send_sem=send_sems.at[send_base + k],
            recv_sem=recv_sems.at[recv_base + outer],
            device_id=(core, block * KEY_VALUE_HEADS + inner),
            device_id_type=MESH,
        )

    order = far_first(outer, n)
    for k, block in enumerate(order + [outer]):
        sums[...] = jnp.zeros_like(sums)
        each_pair(block, outer, k == n - 1, pair)
        if k < n - 1:
            stage[k] = sums[...].astype(bf16)
            send(k, block).start()

    dqkv[:, 0:width] = (dq_sums[...] * scale).astype(bf16)
    dwo[...] = tn(
        mixed_ref[...].astype(bf16), grad_all[...].reshape(2 * chunk, wide)
    ).astype(bf16)
    wo_rows = wo_came.shape[0]
    wo_in = wires.sibling(dwo.at[pl.ds((1 - core) * wo_rows, wo_rows)], wo_came, wo_came)
    dwq[:, 0:width] = tn(h1_ref[...], dqkv[:, 0:width]).astype(bf16)
    q_cols = pl.ds(0, width)
    q_in = wires.sibling(dwq.at[other, q_cols], wq_came.at[:, q_cols], wq_came.at[:, q_cols])
    wo_in()
    wo_came[...] = (
        dwo[pl.ds(core * wo_rows, wo_rows), :].astype(f32) + wo_came[...].astype(f32)
    ).astype(bf16)
    wo_parts = out_rows_back(wires, shards, wo_came, wo_recv)
    q_in()
    wq_came[:, 0:width] = (
        dwq[mine, 0:width].astype(f32) + wq_came[:, 0:width].astype(f32)
    ).astype(bf16)

    def pieces(cols):
        return wires.exchange(
            "chips",
            lambda r, d: wq_came.at[pl.ds(r * w_rows, w_rows), cols],
            lambda r, d: wq_recv.at[r, :, cols],
        )

    q_parts = pieces(q_cols)

    for copy in e_sends:
        copy.wait()
    for copy in e_loads:
        copy.wait()
    e_passed = []
    for way, (near, far) in enumerate(e_sides):
        e_term[way] = (e_term[way].astype(f32) + e_came[way, 1].astype(f32)).astype(bf16)
        e_passed.append(
            wires.remote(e_term.at[way], e_last.at[way], e_second + way, plane_device(far))
        )
    for copy in e_passed:
        copy.start()

    for d in range(1, n):
        origin = lax.rem(outer + d, n)
        pltpu.make_async_remote_copy(
            src_ref=came.at[origin],
            dst_ref=came.at[origin],
            send_sem=send_sems.at[send_base],
            recv_sem=recv_sems.at[recv_base + origin],
            device_id=(core, origin * KEY_VALUE_HEADS + inner),
            device_id_type=MESH,
        ).wait_recv()
        sums[...] += came[origin].astype(f32)
    dqkv[:, width : width + HEAD_SIZE] = (sums[:, 0:HEAD_SIZE] * scale).astype(bf16)
    dqkv[:, width + HEAD_SIZE :] = sums[:, HEAD_SIZE:].astype(bf16)

    gain_sum = jnp.zeros((1, wide), f32)
    for half in range(2):
        rows = pl.ds(half * chunk, chunk)
        part = nt(dqkv[rows, :], wq_ref[...]).astype(bf16)
        dh_stage[rows, :] = part
        gain_sum = gain_sum + jnp.sum(
            part.astype(f32) * h1_ref[rows, :].astype(f32), axis=0, keepdims=True
        )
    dh_in = wires.exchange(
        "plane", lambda r, d: dh_stage.at[pl.ds(r * seg, seg)], lambda r, d: dh_recv.at[r]
    )
    dwq[:, width:] = tn(h1_ref[...], dqkv[:, width:]).astype(bf16)
    kv_cols = pl.ds(width, 2 * HEAD_SIZE)
    kv_in = wires.sibling(dwq.at[other, kv_cols], wq_came.at[:, kv_cols], wq_came.at[:, kv_cols])
    column = (gain_sum / gain_ref[...])
    columns = jnp.broadcast_to(column, (small_all.shape[1], wide)).T
    at_col = lax.broadcasted_iota(jnp.int32, columns.shape, 1)
    small_all[...] = jnp.where(at_col == gain_col, columns, small_ref[...].astype(f32)).astype(bf16)
    small_in = wires.sibling(small_all.at[other], small_came, small_came)
    kv_in()
    wq_came[:, width:] = (
        dwq[mine, width:].astype(f32) + wq_came[:, width:].astype(f32)
    ).astype(bf16)
    kv_parts = pieces(kv_cols)
    small_in()
    small_came[...] = (small_all[mine, :].astype(f32) + small_came[...].astype(f32)).astype(bf16)
    small_parts = wires.exchange(
        "chips",
        lambda r, d: small_came.at[pl.ds(r * w_rows, w_rows)],
        lambda r, d: small_recv.at[r],
    )
    mix_on(2, mix_came_last, mix_term_last, [mix_up_out, mix_down_out])

    for way, copy in enumerate(e_passed):
        copy.wait()
        e_own[:, e_cuts[way]] = (
            e_own[:, e_cuts[way]].astype(f32)
            + e_came[way, 0].astype(f32)
            + e_last[way].astype(f32)
        ).astype(bf16)
    e_keep = wires.local(e_own, e_both.at[mine], e_local)
    e_keep.start()
    e_in = wires.sibling(e_own, e_both.at[mine], e_both.at[other])
    sd_in()
    sd_out[...] = jnp.sum(sd_recv[...].astype(f32), axis=0)
    wo_parts()
    wo_out[...] = jnp.sum(wo_recv[...].astype(f32), axis=0)
    q_parts()
    kv_parts()
    for j in range(KEY_VALUE_HEADS):
        total = wq_recv[j].astype(f32)
        for k in range(1, n):
            total = total + wq_recv[k * KEY_VALUE_HEADS + j].astype(f32)
        wq_out[j] = total
    small_parts()
    small_out[...] = jnp.sum(small_recv[...].astype(f32), axis=0)
    dh_in()
    for core_half in range(2):
        total = dh_recv[core_half * KEY_VALUE_HEADS].astype(f32)
        for j in range(1, KEY_VALUE_HEADS):
            total = total + dh_recv[core_half * KEY_VALUE_HEADS + j].astype(f32)
        dh1_out[core_half] = total
    mix_steps[-1]()
    gu_in()
    e_in()
    e_keep.wait()
    for k, block in enumerate(order):
        send(k, block).wait_send()
    wires.finish()


def finish(
    collective,
    shards,
    chunk,
    gain_col,
    kv_all,
    wo,
    mixed,
    log_rows,
    h1,
    wq,
    gain_row,
    small_grad,
    qkv,
    grad_own,
    gu_half,
    sd_send,
    mix_part,
    mix_terms,
    e_mine,
    e_other,
):
    n, rows, kv_cols = kv_all.shape
    width, wide = wo.shape
    cols = wq.shape[1]
    small = small_grad.shape[1]
    n_in = KEY_VALUE_HEADS
    seg = rows // (2 * n_in)
    w_rows = wide // (2 * shards)
    d_rows = sd_send.shape[1]
    block = mix_part.shape[1:]
    vmem = pl.BlockSpec(memory_space=pltpu.VMEM)
    hbm = pl.BlockSpec(memory_space=pl.ANY)

    def array(shape, kind=bf16):
        return jax.ShapeDtypeStruct(shape, kind)

    e_rows, e_cols = e_mine.shape[1:]
    scratch = [
        ((rows, width), bf16),
        ((2 * n_in, seg, wide), bf16),
        ((rows, width), bf16),
        ((GROUP_MEMBERS, 2, 1, chunk), f32),
        (kv_all.shape, bf16),
        (kv_all.shape, bf16),
        ((rows, kv_cols), f32),
        ((rows, width), f32),
        ((rows, cols), bf16),
        ((width, wide), bf16),
        ((width // 2, wide), bf16),
        ((n, w_rows, wide), bf16),
        ((wide, cols), bf16),
        ((wide // 2, cols), bf16),
        ((shards, w_rows, cols), bf16),
        ((wide, small), bf16),
        ((wide // 2, small), bf16),
        ((shards, w_rows, small), bf16),
        ((rows, wide), bf16),
        ((2 * n_in, seg, wide), bf16),
        ((2 * n_in, d_rows, wide), bf16),
        ((2,) + block, bf16),
        ((2,) + block, bf16),
        ((2,) + block, bf16),
        ((2,) + block, bf16),
        ((2, 2, e_rows, e_cols // 2), bf16),
        ((2, e_rows, e_cols // 2), bf16),
        ((2, e_rows, e_cols // 2), bf16),
        ((e_rows, e_cols), bf16),
    ]
    return pl.pallas_call(
        functools.partial(finish_kernel, shards, chunk, gain_col),
        in_specs=[vmem] * 8 + [hbm] * 9,
        out_specs=[vmem] * 5 + [hbm] * 5,
        out_shape=[
            array((2, seg, wide), f32),
            array((n_in, w_rows, cols), f32),
            array((w_rows, small), f32),
            array((w_rows, wide), f32),
            array((d_rows, wide), f32),
            array(gu_half.shape),
            array(block),
            array(block),
            array((2 * e_rows, e_cols)),
            array(e_mine.shape),
        ],
        scratch_shapes=[pltpu.VMEM(shape, kind) for shape, kind in scratch]
        + [pltpu.SemaphoreType.DMA((6 * shards + 96,))] * 3,
        compiler_params=pltpu.CompilerParams(
            collective_id=collective, has_side_effects=True, vmem_limit_bytes=VMEM_LIMIT
        ),
        name="finish",
    )(
        kv_all,
        wo,
        mixed,
        log_rows,
        h1,
        wq,
        gain_row,
        small_grad,
        qkv,
        grad_own,
        gu_half,
        sd_send,
        mix_part,
        *mix_terms,
        e_mine,
        e_other,
    )


def swiglu_parts(gate_part, up_part):
    sigmoid = jax.nn.sigmoid(gate_part)
    active = gate_part * sigmoid
    slope = up_part * sigmoid * (1.0 + gate_part * (1.0 - sigmoid))
    return active * up_part, active, slope


def experts_kernel(
    room,
    hidden,
    h_ref,
    c_ref,
    meta_ref,
    wg_ref,
    wu_ref,
    wd_ref,
    sgu_ref,
    sd_ref,
    out_ref,
    dh_ref,
    dgate_ref,
    dw_ref,
    dsgu_ref,
    dsd_ref,
    sum_out,
    sum_dh,
    h_rows,
    c_rows,
    picks,
    gate_col,
):
    expert = pl.program_id(0)
    inner = lax.rem(lax.axis_index("fsdp"), KEY_VALUE_HEADS)
    at = across(inner, expert)
    blocks, rows, width = h_ref.shape

    @pl.when(expert == 0)
    def _():
        dgate_ref[...] = jnp.zeros_like(dgate_ref)
        hid = h_ref[...].reshape(blocks * rows, width)
        cot = c_ref[...].reshape(blocks * rows, width)
        gate_w, up_w, down_w = sgu_ref[:, 0:hidden], sgu_ref[:, hidden : 2 * hidden], sd_ref[...]
        both, active, slope = swiglu_parts(nn(hid, gate_w), nn(hid, up_w))
        act = both.astype(bf16)
        d_act = nt(cot, down_w)
        d_gate = (d_act * slope).astype(bf16)
        d_up = (d_act * active).astype(bf16)
        sum_out[...] = nn(act, down_w)
        sum_dh[...] = nt(d_gate, gate_w) + nt(d_up, up_w)
        dsgu_ref[:, 0:hidden] = tn(hid, d_gate).astype(bf16)
        dsgu_ref[:, hidden : 2 * hidden] = tn(hid, d_up).astype(bf16)
        dsd_ref[...] = tn(act, cot).astype(bf16)

    slots = lax.broadcasted_iota(jnp.int32, (room, rows), 0).astype(f32)
    for block in range(blocks):
        part = pl.ds(block * room, room)
        gate_row = meta_ref[block, pl.ds(at, 1), :]
        slot_row = meta_ref[block, pl.ds(at + KEY_VALUE_HEADS, 1), :]
        pick = (slots == slot_row).astype(f32)
        gate_col[part, :] = jnp.broadcast_to(
            jnp.sum(pick * gate_row, axis=1, keepdims=True), (room, gate_col.shape[1])
        )
        pick = pick.astype(bf16)
        picks[block] = pick
        h_rows[part, :] = nn(pick, h_ref[block]).astype(bf16)
        c_rows[part, :] = nn(pick, c_ref[block]).astype(bf16)
    gate = gate_col[:, 0:1]
    gate_w, up_w, down_w = wg_ref[0], wu_ref[0], wd_ref[0]
    both, active, slope = swiglu_parts(nn(h_rows[...], gate_w), nn(h_rows[...], up_w))
    act = both.astype(bf16)
    d_act = nt(c_rows[...], down_w)
    d_gates = jnp.sum(d_act * act.astype(f32), axis=1, keepdims=True)
    d_act = d_act * gate
    act = (act.astype(f32) * gate).astype(bf16)
    d_gate = (d_act * slope).astype(bf16)
    d_up = (d_act * active).astype(bf16)
    ff = act.shape[1]
    dw_ref[0, :, 0:ff] = tn(h_rows[...], d_gate).astype(bf16)
    dw_ref[0, :, ff : 2 * ff] = tn(h_rows[...], d_up).astype(bf16)
    dw_ref[0, :, 2 * ff : 3 * ff] = tn(c_rows[...], act).astype(bf16)
    result = nn(act, down_w).astype(bf16)
    d_rows = (nt(d_gate, gate_w) + nt(d_up, up_w)).astype(bf16)
    for block in range(blocks):
        pick = picks[block]
        part = slice(block * room, (block + 1) * room)
        here = pl.ds(block * rows, rows)
        sum_out[here, :] += tn(pick, result[part])
        sum_dh[here, :] += tn(pick, d_rows[part])
        dgate_ref[block, pl.ds(at, 1), :] = jnp.sum(
            pick.astype(f32) * d_gates[part], axis=0, keepdims=True
        )

    @pl.when(expert == pl.num_programs(0) - 1)
    def _():
        out_ref[...] = sum_out[...].astype(bf16).reshape(out_ref.shape)
        dh_ref[...] = sum_dh[...].astype(bf16).reshape(dh_ref.shape)


def experts(room, hidden, h_all, c_all, meta, wg, wu, wd, sgu, sd):
    blocks, rows, width = h_all.shape
    n_experts, _, inner = wg.shape

    def once(shape):
        return pl.BlockSpec(shape, lambda e: (0,) * len(shape), pipeline_mode=pl.Buffered(1))

    def each(shape, **kind):
        return pl.BlockSpec((1,) + shape[1:], lambda e: (e, 0, 0), **kind)

    single = dict(pipeline_mode=pl.Buffered(1))
    return pl.pallas_call(
        functools.partial(experts_kernel, room, hidden),
        grid=(n_experts,),
        in_specs=[
            once(h_all.shape),
            once(c_all.shape),
            once(meta.shape),
            each(wg.shape),
            each(wu.shape),
            each(wd.shape),
            once(sgu.shape),
            once(sd.shape),
        ],
        out_specs=[
            once(h_all.shape),
            once(h_all.shape),
            once(meta.shape),
            pl.BlockSpec((1, width, 3 * inner), lambda e: (e, 0, 0), **single),
            once(sgu.shape),
            once(sd.shape),
        ],
        out_shape=[
            jax.ShapeDtypeStruct(h_all.shape, bf16),
            jax.ShapeDtypeStruct(h_all.shape, bf16),
            jax.ShapeDtypeStruct(meta.shape, f32),
            jax.ShapeDtypeStruct((n_experts, width, 3 * inner), bf16),
            jax.ShapeDtypeStruct(sgu.shape, bf16),
            jax.ShapeDtypeStruct(sd.shape, bf16),
        ],
        scratch_shapes=[
            pltpu.VMEM((blocks * rows, width), f32),
            pltpu.VMEM((blocks * rows, width), f32),
            pltpu.VMEM((blocks * room, width), bf16),
            pltpu.VMEM((blocks * room, width), bf16),
            pltpu.VMEM((blocks, room, rows), bf16),
            pltpu.VMEM((blocks * room, 128), f32),
        ],
        compiler_params=pltpu.CompilerParams(vmem_limit_bytes=VMEM_LIMIT),
        name="experts",
    )(h_all, c_all, meta, wg, wu, wd, sgu, sd)


def experts_line_kernel(room, hidden, shards, refs):
    n = shards // KEY_VALUE_HEADS
    h_ref, meta_ref = refs[:2]
    c_refs = refs[2 : 1 + 2 * n]
    (
        wg_ref,
        wu_ref,
        wd_ref,
        side_x,
        side_y,
        sgu_ref,
        sd_ref,
        dh_out,
        dgate_out,
        mix_out,
        e_mine,
        e_other,
        gu_mine,
        gu_other,
        dsd_ref,
        h_all,
        c_all,
        metas,
        wgu,
        wd,
        picks,
        kept_gu,
        kept_act,
        kept_shared,
        row_a,
        row_b,
        own_a,
        own_b,
        dh_stage,
        mix_stage,
        dg_stage,
        down_stage,
        gu_stage,
        send_sems,
        recv_sems,
        local_sems,
    ) = refs[1 + 2 * n :]
    wires = Wires(shards, send_sems, recv_sems, local_sems)
    core, chip, outer, inner = place()
    rows, width = h_ref.shape
    ff = wd.shape[1]
    experts_here = KEY_VALUE_HEADS

    own_h = wires.local(h_ref, h_all.at[outer], wires.take(1))
    own_meta = wires.local(meta_ref.at[outer], metas.at[outer], wires.take(1))
    own_h.start()
    own_meta.start()
    c_own = wires.local(c_refs[0], c_all.at[outer], wires.take(1))
    c_base = wires.take(2 * n - 2)

    def c_each(action):
        for k in range(2 * n - 2):
            block = outer - 1 - k if k < n - 1 else outer + 1 + k - (n - 1)

            def one(k=k, block=block):
                at = lax.rem(block + n, n)
                action(wires.local(c_refs[1 + k], c_all.at[at], c_base + k))

            pl.when((block >= 0) & (block < n))(one)

    deep, tall = ff // 2, width // 2
    own_weights = (
        wires.local(wg_ref.at[0], wgu.at[0, :, pl.ds(0, ff)], wires.take(1)),
        wires.local(wu_ref.at[0], wgu.at[0, :, pl.ds(ff, ff)], wires.take(1)),
        wires.local(wd_ref.at[0], wd.at[0], wires.take(1)),
    )

    def half_places(e, first_col, cols, of_core):
        found = [
            wgu.at[e, pl.ds(of_core * tall, tall), pl.ds(k * ff + first_col, cols)]
            for k in range(2)
        ]
        found += [
            wd.at[e, pl.ds(of_core * deep, deep), pl.ds(k * ff + first_col, cols)]
            for k in range(width // ff)
        ]
        return found

    def half_sources(source, first_col, cols):
        starts = [(k * tall, tall) for k in range(2)]
        starts += [(2 * tall + k * deep, deep) for k in range(width // ff)]
        return [source.at[pl.ds(at, size), pl.ds(first_col, cols)] for at, size in starts]

    per_half = 2 + width // ff
    sides = ((1, side_x, 0, ff), (2, side_y, 0, ff), (3, side_x, 0, ff // 2), (3, side_y, ff // 2, ff // 2))
    half_sems = [wires.take(per_half) for _ in sides]
    cross_sems = [wires.take(per_half) for _ in range(2)]

    def half_local(which):
        e, source, first_col, cols = sides[which]
        return [
            wires.local(here, there, half_sems[which] + k)
            for k, (here, there) in enumerate(
                zip(half_sources(source, first_col, cols), half_places(e, first_col, cols, core))
            )
        ]

    def half_remote(which, of_core):
        e, source, first_col, cols = sides[which]
        places = half_places(e, first_col, cols, of_core)
        here = half_sources(source, first_col, cols) if which < 2 else places
        return [
            wires.remote(here[k], places[k], half_sems[which] + k, (1 - core, chip))
            for k in range(per_half)
        ]

    def cross_remote(which):
        _, source, first_col, cols = sides[2 + which]
        return [
            wires.remote(
                here,
                there,
                cross_sems[which] + k,
                (core, outer * KEY_VALUE_HEADS + across(inner, 2 - which)),
            )
            for k, (here, there) in enumerate(
                zip(half_sources(source, first_col, cols), half_places(3, first_col, cols, core))
            )
        ]

    c_own.start()
    for copy in own_weights:
        copy.start()
    for which in range(2):
        for copy in half_local(which):
            copy.start()
    c_each(lambda copy: copy.start())

    wires.greet(["outer", "plane"])

    line = Line(wires, h_ref, h_all)
    device = line.device
    line.start(0)
    for which in range(2):
        for copy in cross_remote(which):
            copy.start()
    for which in range(2):
        for copy in half_remote(which, core):
            copy.start()
    meta_in = wires.exchange(
        "outer", lambda r, d: meta_ref.at[r], lambda r, d: metas.at[r], own=False
    )

    dh_send, dh_recv = wires.take(n), wires.take(n)
    dg_send, dg_recv = wires.take(n), wires.take(n)

    def give_back(stage, target, k, block, sends, receives):
        return pltpu.make_async_remote_copy(
            src_ref=stage,
            dst_ref=target.at[outer],
            send_sem=send_sems.at[sends + k],
            recv_sem=recv_sems.at[receives + outer],
            device_id=device(block),
            device_id_type=MESH,
        )

    def take_back(target, origin, receives):
        return pltpu.make_async_remote_copy(
            src_ref=target.at[origin],
            dst_ref=target.at[origin],
            send_sem=send_sems.at[receives],
            recv_sem=recv_sems.at[receives + origin],
            device_id=device(origin),
            device_id_type=MESH,
        )

    dh_own = wires.local(dh_stage.at[n - 1], dh_out.at[outer], wires.take(1))
    dg_own = wires.local(dg_stage.at[n - 1], dgate_out.at[outer], wires.take(1))
    mix_base = wires.take(n)

    def mix_copy(k, block):
        return wires.local(
            mix_stage.at[k % 2], mix_out.at[lax.rem(outer - block + n, n)], mix_base + k
        )

    slots = lax.broadcasted_iota(jnp.int32, (room, rows), 0).astype(f32)
    order = line.order()
    gate_w, up_w, down_w = sgu_ref[:, 0:hidden], sgu_ref[:, hidden : 2 * hidden], sd_ref[...]

    def choose(k, block, left, right):
        for e in range(experts_here):
            at = across(inner, e)
            slot_row = metas[block, pl.ds(at + experts_here, 1), :]
            picks[block, pl.ds(e * room, room), :] = (slots == slot_row).astype(bf16)
        left[...] = nn(picks[block], h_all[block]).astype(bf16)
        right[...] = nn(picks[block], c_all[block]).astype(bf16)
        dg_stage[k] = jnp.zeros(dg_stage.shape[1:], f32)

    def one_expert(e, k, block, left, right):
        at = across(inner, e)
        part = pl.ds(pl.multiple_of(e * room, 16), room)
        pick = picks[block, part, :].astype(f32)
        gate = jnp.sum(pick * metas[block, pl.ds(at, 1), :], axis=1, keepdims=True)
        first = nn(left[part, :], wgu[e])
        both, active, slope = swiglu_parts(first[:, 0:ff], first[:, ff : 2 * ff])
        act = both.astype(bf16)
        d_act = nt(right[part, :], wd[e])
        d_gates = jnp.sum(d_act * act.astype(f32), axis=1, keepdims=True)
        dg_stage[k, pl.ds(at, 1), :] = jnp.sum(pick * d_gates, axis=0, keepdims=True)
        d_act = d_act * gate
        act = (act.astype(f32) * gate).astype(bf16)
        here = pl.ds(pl.multiple_of(block * room, 16), room)
        kept_act[e, here, :] = act
        kept_gu[e, here, 0:ff] = (d_act * slope).astype(bf16)
        kept_gu[e, here, ff : 2 * ff] = (d_act * active).astype(bf16)
        left[part, :] = nn(act, wd[e]).astype(bf16)
        right[part, :] = nt(kept_gu[e, here, :], wgu[e]).astype(bf16)

    def some_experts(begin, end, k, block, left, right):
        def one(e, carry):
            one_expert(e, k, block, left, right)
            return carry

        lax.fori_loop(begin, end, one, 0)

    order = order[1:] + order[:1]
    last = n - 1
    own_h.wait()
    own_meta.wait()
    c_own.wait()
    choose(last, outer, own_a, own_b)
    for copy in own_weights:
        copy.wait()
    one_expert(0, last, outer, own_a, own_b)
    for which in range(2):
        for copy in half_local(which):
            copy.wait()
        for copy in half_remote(which, 1 - core):
            copy.wait_recv()
    some_experts(1, experts_here - 1, last, outer, own_a, own_b)

    for k, block in enumerate(order):
        if k < last:
            line.arrive(k)
            if k < last - 1:
                line.start(k + 1)
        if k == 0:
            meta_in()
            c_each(lambda copy: copy.wait())
        left, right = (row_a, row_b) if k < last else (own_a, own_b)
        hid, cot = h_all[block], c_all[block]
        if k < last:
            choose(k, block, left, right)
        if k == 0:
            some_experts(0, experts_here - 1, k, block, left, right)
            for which in range(2):
                for copy in cross_remote(which):
                    copy.wait_recv()
                for copy in half_remote(2 + which, core):
                    copy.start()
            for which in range(2):
                for copy in half_remote(2 + which, 1 - core):
                    copy.wait_recv()
            some_experts(experts_here - 1, experts_here, k, block, left, right)
        elif k < last:
            some_experts(0, experts_here, k, block, left, right)
        else:
            some_experts(experts_here - 1, experts_here, k, block, left, right)
        both, active, slope = swiglu_parts(nn(hid, gate_w), nn(hid, up_w))
        act = both.astype(bf16)
        d_act = nt(cot, down_w)
        d_gate = (d_act * slope).astype(bf16)
        d_up = (d_act * active).astype(bf16)
        kept_shared[block, :, 0:hidden] = d_gate
        kept_shared[block, :, hidden : 2 * hidden] = d_up
        kept_shared[block, :, 2 * hidden : 3 * hidden] = act
        dh_stage[k] = (
            tn(picks[block], right[...]) + nt(d_gate, gate_w) + nt(d_up, up_w)
        ).astype(bf16)
        if k == n - 1:
            dh_own.start()
            dg_own.start()
        else:
            give_back(dh_stage.at[k], dh_out, k, block, dh_send, dh_recv).start()
            give_back(dg_stage.at[k], dgate_out, k, block, dg_send, dg_recv).start()
        if k >= 2:
            mix_copy(k - 2, order[k - 2]).wait()
        mix_stage[k % 2] = (tn(picks[block], left[...]) + nn(act, down_w)).astype(bf16)
        mix_copy(k, block).start()

    half = width // 2
    mine, other = pl.ds(core * half, half), pl.ds((1 - core) * half, half)
    sibling = (1 - core, chip)
    left, right = pl.ds(0, 2 * ff), pl.ds(2 * ff, ff)
    keep_base, give_base = wires.take(2 * experts_here + 1), wires.take(2 * experts_here + 1)

    def keep(e):
        return (
            wires.local(wgu.at[e, mine, :], e_mine.at[e, :, left], keep_base + 2 * e),
            wires.local(down_stage.at[e % 2, mine, :], e_mine.at[e, :, right], keep_base + 2 * e + 1),
        )

    def give(e):
        return (
            wires.remote(wgu.at[e, other, :], e_other.at[e, :, left], give_base + 2 * e, sibling),
            wires.remote(
                down_stage.at[e % 2, other, :],
                e_other.at[e, :, right],
                give_base + 2 * e + 1,
                sibling,
            ),
        )

    for which in (2, 3):
        for copy in half_remote(which, core):
            copy.wait_send()
    for e in range(experts_here):
        for block in range(n):
            part = pl.ds(block * room, room)
            pick = picks[block, pl.ds(e * room, room), :]
            row_a[part, :] = nn(pick, h_all[block]).astype(bf16)
            row_b[part, :] = nn(pick, c_all[block]).astype(bf16)
        wgu[e] = tn(row_a[...], kept_gu[e]).astype(bf16)
        if e >= 2:
            keep(e - 2)[1].wait()
            give(e - 2)[1].wait_send()
        down_stage[e % 2] = tn(row_b[...], kept_act[e]).astype(bf16)
        for copy in keep(e) + give(e):
            copy.start()
    hid_all = h_all[...].reshape(n * rows, width)
    shared = kept_shared[...].reshape(n * rows, 3 * hidden)
    gu_stage[...] = tn(hid_all, shared[:, 0 : 2 * hidden]).astype(bf16)
    gu_keep = wires.local(gu_stage.at[mine, :], gu_mine, keep_base + 2 * experts_here)
    gu_give = wires.remote(gu_stage.at[other, :], gu_other, give_base + 2 * experts_here, sibling)
    gu_keep.start()
    gu_give.start()
    dsd_ref[...] = tn(shared[:, 2 * hidden :], c_all[...].reshape(n * rows, width)).astype(bf16)

    def settle(e):
        for which, (kept, given) in enumerate(zip(keep(e), give(e))):
            if which == 0 or e >= experts_here - 2:
                kept.wait()
                given.wait_send()
            given.wait_recv()

    line.leave()
    for e in range(experts_here):
        settle(e)

    for which in range(2):
        for copy in half_remote(which, core):
            copy.wait_send()
    for which in range(2):
        for copy in cross_remote(which):
            copy.wait_send()
    dh_own.wait()
    dg_own.wait()
    for k in range(max(0, n - 2), n):
        mix_copy(k, order[k]).wait()
    for k in range(n - 1):
        give_back(dh_stage.at[k], dh_out, k, order[k], dh_send, dh_recv).wait_send()
        give_back(dg_stage.at[k], dgate_out, k, order[k], dg_send, dg_recv).wait_send()
    for d in range(1, n):
        origin = lax.rem(outer + d, n)
        take_back(dh_out, origin, dh_recv).wait_recv()
        take_back(dgate_out, origin, dg_recv).wait_recv()
    gu_keep.wait()
    gu_give.wait()
    wires.finish()


def experts_line(room, hidden, shards, collective, h_own, meta, c_parts, weights, sides, sgu, sd):
    n = shards // KEY_VALUE_HEADS
    rows, width = h_own.shape
    n_experts, ff = KEY_VALUE_HEADS, weights[0].shape[2]
    half = width // 2
    any_spec = pl.BlockSpec(memory_space=pl.ANY)
    vmem = pl.BlockSpec(memory_space=pltpu.VMEM)
    e_shape = (n_experts, half, 3 * ff)
    sems = 112 + 24 * n

    def kernel(*refs):
        experts_line_kernel(room, hidden, shards, refs)

    return pl.pallas_call(
        kernel,
        in_specs=[any_spec] * (2 + len(c_parts) + 3 + len(sides)) + [vmem] * 2,
        out_specs=[any_spec] * 7 + [vmem],
        out_shape=[
            jax.ShapeDtypeStruct((n, rows, width), bf16),
            jax.ShapeDtypeStruct(meta.shape, f32),
            jax.ShapeDtypeStruct((n, rows, width), bf16),
            jax.ShapeDtypeStruct(e_shape, bf16),
            jax.ShapeDtypeStruct(e_shape, bf16),
            jax.ShapeDtypeStruct((half, 2 * hidden), bf16),
            jax.ShapeDtypeStruct((half, 2 * hidden), bf16),
            jax.ShapeDtypeStruct(sd.shape, bf16),
        ],
        scratch_shapes=[
            pltpu.VMEM((n, rows, width), bf16),
            pltpu.VMEM((n, rows, width), bf16),
            pltpu.VMEM(meta.shape, f32),
            pltpu.VMEM((n_experts, width, 2 * ff), bf16),
            pltpu.VMEM((n_experts, ff, width), bf16),
            pltpu.VMEM((n, n_experts * room, rows), bf16),
            pltpu.VMEM((n_experts, n * room, 2 * ff), bf16),
            pltpu.VMEM((n_experts, n * room, ff), bf16),
            pltpu.VMEM((n, rows, 3 * hidden), bf16),
            pltpu.VMEM((n * room, width), bf16),
            pltpu.VMEM((n * room, width), bf16),
            pltpu.VMEM((n * room, width), bf16),
            pltpu.VMEM((n * room, width), bf16),
            pltpu.VMEM((n, rows, width), bf16),
            pltpu.VMEM((2, rows, width), bf16),
            pltpu.VMEM((n,) + meta.shape[1:], f32),
            pltpu.VMEM((2, width, ff), bf16),
            pltpu.VMEM((width, 2 * hidden), bf16),
        ]
        + [pltpu.SemaphoreType.DMA((sems,))] * 3,
        compiler_params=pltpu.CompilerParams(
            collective_id=collective, has_side_effects=True, vmem_limit_bytes=VMEM_LIMIT
        ),
        name="experts_line",
    )(h_own, meta, *c_parts, *weights, *sides, sgu, sd)


def experts_split(room, hidden, shards, collectives, h_own, meta, c_parts, weights, sides, sgu, sd):
    n_out, n_in = shards // KEY_VALUE_HEADS, KEY_VALUE_HEADS
    rows, width = h_own.shape
    core = lax.axis_index("seq")
    half = width // 2

    def spread_hidden(wires, ins, outs):
        waits = [
            wires.exchange("outer", lambda r, d: ins[0], lambda r, d: outs[0].at[d]),
            wires.exchange("outer", lambda r, d: ins[1].at[r], lambda r, d: outs[1].at[d]),
        ]
        waits += [
            wires.exchange(
                "inner",
                lambda r, d, k=k: ins[k].at[0],
                lambda r, d, k=k: outs[k].at[across(r, lax.rem(r + d, n_in))],
            )
            for k in range(2, 5)
        ]
        for wait in waits:
            wait()

    h_all, meta_all, wg, wu, wd = transfer(
        "spread_hidden",
        collectives[0],
        shards,
        ["outer", "inner"],
        2 * n_out + 3 * n_in,
        spread_hidden,
        [h_own, meta, *weights],
        [((n_out, rows, width), bf16), (meta.shape, f32)]
        + [((n_in,) + weight.shape[1:], bf16) for weight in weights],
    )
    c_all = jnp.stack(c_parts)
    at_once = math.gcd(n_out, 4)
    parts = [
        experts(
            room,
            hidden,
            h_all[i : i + at_once],
            c_all[i : i + at_once],
            meta_all[i : i + at_once],
            wg,
            wu,
            wd,
            sgu,
            sd,
        )
        for i in range(0, n_out, at_once)
    ]
    mix_part, dh_part, dgate_part = (
        jnp.concatenate([part[k] for part in parts], axis=0) for k in range(3)
    )
    e_grad, sgu_grad, sd_grad = (
        sum(part[k].astype(f32) for part in parts).astype(bf16) for k in range(3, 6)
    )

    def sum_hidden(wires, ins, outs):
        core = lax.axis_index("seq")
        dh_ref, dg_ref, e_ref, gu_ref = ins
        dhs, dgs, es, gus = outs
        other = pl.ds((1 - core) * half, half)
        waits = [
            wires.exchange(
                "outer", lambda r, d: dh_ref.at[(n_out - d) % n_out], lambda r, d: dhs.at[r]
            ),
            wires.exchange(
                "outer", lambda r, d: dg_ref.at[(n_out - d) % n_out], lambda r, d: dgs.at[r]
            ),
            wires.sibling(e_ref.at[:, other], es, es),
            wires.sibling(gu_ref.at[other], gus, gus),
        ]
        for wait in waits:
            wait()

    dhs, dgs, es, gus = transfer(
        "sum_hidden",
        collectives[1],
        shards,
        ["outer", "core"],
        2 * n_out + 8,
        sum_hidden,
        [dh_part, dgate_part, e_grad, sgu_grad],
        [
            ((n_out, rows, width), bf16),
            (meta.shape, f32),
            ((n_in, half, e_grad.shape[2]), bf16),
            ((half, 2 * hidden), bf16),
        ],
    )
    e_mine = lax.dynamic_slice_in_dim(e_grad, core * half, half, 1)
    gu_mine = lax.dynamic_slice_in_dim(sgu_grad, core * half, half, 0)
    return dhs, dgs, mix_part, e_mine, es, gu_mine, gus, sd_grad


def norm_rows(values, gain_vector):
    inverse = lax.rsqrt(jnp.mean(values * values, axis=-1, keepdims=True) + epsilon)
    normed = values * inverse
    return (normed, inverse, normed * gain_vector)


def norm_back(grad_hidden, normed, inverse, gain_vector):
    grad_normed = grad_hidden * gain_vector
    gain_grad = jnp.sum(grad_hidden * normed, axis=(0, 1))
    inner_mean = jnp.mean(grad_normed * normed, axis=-1, keepdims=True)
    return (inverse * (grad_normed - normed * inner_mean), gain_grad)


def pad_rows(array, axis):
    size = array.shape[axis]
    widths = [(0, 0)] * array.ndim
    widths[axis] = (0, round_up(size, 16) - size)
    return jnp.pad(array, widths) if widths[axis][1] else array


def pad_to(array, axis, size):
    widths = [(0, 0)] * array.ndim
    widths[axis] = (0, size - array.shape[axis])
    return jnp.pad(array, widths) if widths[axis][1] else array


def body(
    tokens,
    routes,
    out_grad,
    attn_gain,
    ffn_gain,
    query_projection,
    key_projection,
    value_projection,
    w_out,
    w_router,
    shared_gate,
    shared_up,
    shared_down,
    expert_gate,
    expert_up,
    expert_down,
):
    shards = lax.axis_size("fsdp")
    n_in = KEY_VALUE_HEADS
    n_out = shards // n_in
    core, chip, outer, inner = place()
    seg, seqs, width = tokens.shape
    rows = seg * seqs
    topk = routes.shape[2]
    n_experts = w_router.shape[1]
    w_rows = query_projection.shape[0]
    w_pad = round_up(w_rows, 16)
    d_rows = shared_down.shape[0]
    d_pad = round_up(d_rows, 16)
    half_chips = shards // 2
    q_cols = GROUP_MEMBERS * HEAD_SIZE
    cols = q_cols + 2 * HEAD_SIZE
    ff = expert_gate.shape[2]
    hid_core = n_in * d_rows
    hid = 2 * hid_core
    hid_pad = round_up(hid, 128)
    small = round_up(n_experts + 2, 128)
    chunk = n_in * seg
    half_width, half_ff = width // 2, ff // 2
    room = round_up(max(2, (3 * rows * topk + 2 * n_experts - 1) // (2 * n_experts)), 16)

    small_piece = pad_to(
        jnp.concatenate([w_router, attn_gain[:, None], ffn_gain[:, None]], axis=1), 1, small
    )
    q_pieces = pad_rows(
        jnp.concatenate(
            [
                query_projection.reshape(w_rows, n_in, q_cols),
                key_projection.reshape(w_rows, n_in, HEAD_SIZE),
                value_projection.reshape(w_rows, n_in, HEAD_SIZE),
                jnp.broadcast_to(small_piece[:, None], (w_rows, n_in, small)),
            ],
            axis=2,
        ).transpose(1, 0, 2),
        1,
    )

    def hidden_piece(weight):
        piece = weight.reshape(w_rows, 2, n_out, hid_core).transpose(2, 0, 1, 3)
        return pad_to(piece.reshape(n_out, w_rows, hid), 2, hid_pad)

    gu_pieces = pad_rows(
        jnp.concatenate([hidden_piece(shared_gate), hidden_piece(shared_up)], axis=2), 1
    )
    out_piece = pad_rows(w_out, 0)
    down_piece = pad_rows(shared_down, 0)
    x_own = tokens.transpose(1, 0, 2)
    c_own = out_grad.transpose(1, 0, 2)
    cot = c_own.reshape(rows, width)

    def shift(block, amount):
        return lax.ppermute(
            block, "fsdp", [(f, (f + amount * n_in) % shards) for f in range(shards)]
        )

    def swap(block, step):
        return lax.ppermute(
            block, "fsdp", [(f, f // n_in * n_in + (f % n_in ^ step)) for f in range(shards)]
        )

    def out_rows(wires, o_ref, wo_ref):
        core, chip, outer, inner = place()
        to_inner = 2 * core + chip // half_chips
        slot = lax.rem(chip, half_chips)
        base = wires.take(half_chips)
        sends = wires.take(n_out)
        across_core = wires.take(1)
        first = inner // 2 == core

        def copy(k):
            to = (core, k * n_in + to_inner)
            return to[1] == chip, pltpu.make_async_remote_copy(
                src_ref=o_ref,
                dst_ref=wo_ref.at[slot],
                send_sem=wires.send_sems.at[sends + k],
                recv_sem=wires.recv_sems.at[base + slot],
                device_id=to,
                device_id_type=MESH,
            )

        def start(k):
            here, send = copy(k)
            pl.when(jnp.logical_not(here))(send.start)
            pl.when(here)(lambda: wires.local(o_ref, wo_ref.at[slot], base).start())

        def leave(k):
            here, send = copy(k)
            pl.when(jnp.logical_not(here))(send.wait_send)

        def come(i):
            origin = (core, half_chips * lax.rem(inner, 2) + i)
            here = origin[1] == chip
            place_of = wo_ref.at[i]
            pl.when(jnp.logical_not(here))(
                wires.remote(place_of, place_of, base + i, origin).wait_recv
            )
            pl.when(here)(lambda: wires.local(o_ref, place_of, base).wait())

        def hand_on():
            return wires.remote(wo_ref, wo_ref, across_core, (1 - core, chip))

        def arrive():
            @pl.when(first)
            def _():
                repeat(0, half_chips, come)
                hand_on().start()

        def settle():
            @pl.when(first)
            def _():
                hand_on().wait_send()

            @pl.when(jnp.logical_not(first))
            def _():
                hand_on().wait_recv()

        repeat(0, n_out, start)
        wires.leaving.append(lambda: repeat(0, n_out, leave))
        return arrive, settle

    own_rows = half_chips // 2
    line = n_out == 4

    def fetch(wires, ins, outs):
        x_ref, q_ref, o_ref = ins
        xs_ref, wq_ref, wo_ref = outs
        core = lax.axis_index("seq")
        q_in = wires.exchange(
            "chips", lambda r, d: q_ref.at[lax.rem(r, n_in)], lambda r, d: wq_ref.at[core, r]
        )
        x_in = wires.exchange("plane", lambda r, d: x_ref.at[r // n_in], lambda r, d: xs_ref.at[r])
        o_in, o_settle = out_rows(wires, o_ref, wo_ref)
        q_in()
        q_other = wires.sibling(wq_ref.at[core], wq_ref.at[core], wq_ref.at[1 - core])
        o_in()
        x_in()
        q_other()
        o_settle()

    down_half = lax.dynamic_slice_in_dim(expert_down[0], core * half_ff, half_ff, 0)
    expert_half = jnp.concatenate(
        [
            lax.dynamic_slice_in_dim(expert_gate[0], core * half_width, half_width, 0),
            lax.dynamic_slice_in_dim(expert_up[0], core * half_width, half_width, 0),
        ]
        + [down_half[:, k : k + ff] for k in range(0, width, ff)],
        axis=0,
    )
    if line:
        mixed, log_rows, kv_all, out_sum, h1, qkv, sgu, ws, wq, wo, side_x, side_y, *c_came = attend(
            1,
            shards,
            chunk,
            (x_own, q_pieces, out_piece, cot, expert_half, gu_pieces, down_piece),
            n_experts,
            out_rows,
        )
        c_parts = [cot] + c_came[0::2] + c_came[1::2]
    else:
        xs, wq, wo = transfer(
            "fetch",
            0,
            shards,
            ["all"],
            4 * shards + 16,
            fetch,
            [x_own, q_pieces, out_piece],
            [
                ((2 * n_in, seg, width), bf16),
                ((2, shards, w_pad, cols + small), bf16),
                ((half_chips, w_pad, width), bf16),
            ],
        )
        side_x = side_y = expert_half
    wq = wq[:, :, :w_rows].reshape(width, cols + small)
    wo = wo[:, :w_rows].reshape(q_cols, width)
    wq, small_w = wq[:, :cols], wq[:, cols:]
    router_w = small_w[:, :n_experts]
    gain_one = small_w[:, n_experts].astype(f32)
    gain_two = small_w[:, n_experts + 1].astype(f32)

    inputs = x_own.astype(f32)
    if line:
        residual = inputs + out_sum
    else:
        h1 = norm_rows(xs.reshape(2 * chunk, width).astype(f32), gain_one)[2].astype(bf16)
        qkv = nn(h1, wq).astype(bf16)
        mixed, log_rows, kv_all = attend(1, shards, chunk, (qkv,))
        mixed_low = mixed.astype(bf16)
        out_part = nn(mixed_low, wo).astype(bf16).reshape(2 * n_in, seg, width)

        def sum_out(wires, ins, outs):
            part_ref, gu_ref, s_ref = ins
            parts_ref, wgu_ref, ws_ref = outs
            gu_in, gu_settle, s_in, s_settle = spread_shared(wires, gu_ref, s_ref, wgu_ref, ws_ref)
            part_in = wires.exchange(
                "plane", lambda r, d: part_ref.at[r], lambda r, d: parts_ref.at[r]
            )
            gu_in()
            gu_settle.start()
            s_in()
            s_settle.start()
            part_in()
            gu_settle.wait()
            s_settle.wait()

        out_parts, sgu, ws = transfer(
            "sum_out",
            2,
            shards,
            ["all"],
            shards + 8 * n_in + 16,
            sum_out,
            [out_part, gu_pieces, down_piece],
            [
                ((2 * n_in, seg, width), bf16),
                ((2, shards, w_pad, 2 * hid_pad), bf16),
                ((2, n_in, d_pad, width), bf16),
            ],
        )
        c_parts = [cot] + [shift(cot, d) for d in range(1, n_out)]
        residual = inputs + jnp.sum(out_parts.astype(f32).reshape(2, n_in, seg, width), axis=1)
    sgu = sgu[:, :, :w_rows].reshape(width, 2 * hid_pad)
    ws = pad_to(ws[:, :, :d_rows].reshape(hid, width), 0, hid_pad)

    normed_two, inverse_two, scaled_two = norm_rows(residual, gain_two)
    hidden_two = scaled_two.astype(bf16).reshape(rows, width)
    logits = nn(hidden_two, router_w)
    flat_routes = routes.transpose(1, 0, 2).reshape(rows, topk)
    chooser = (flat_routes[:, :, None] == jnp.arange(n_experts, dtype=jnp.int32)).astype(f32)
    taken = jnp.sum(chooser, axis=1)
    chosen = jnp.where(taken > 0, logits, masked_score)
    exponent = jnp.where(
        taken > 0, jnp.exp(chosen - jnp.max(chosen, axis=-1, keepdims=True)), 0.0
    )
    gates = exponent / jnp.sum(exponent, axis=-1, keepdims=True)
    before = (
        lax.broadcasted_iota(jnp.int32, (rows, rows), 0)
        < lax.broadcasted_iota(jnp.int32, (rows, rows), 1)
    ).astype(bf16)
    slots = jnp.where(taken.T > 0, nn(taken.T.astype(bf16), before), -1.0)
    meta = jnp.concatenate(
        [gates.T.reshape(n_out, n_in, rows), slots.reshape(n_out, n_in, rows)], axis=1
    )

    run = functools.partial(experts_line if line else experts_split, room, hid_pad, shards)
    dhs, dgs, mix_part, e_mine, e_other, gu_mine, gus, sd_grad = run(
        3 if line else (3, 4),
        hidden_two,
        meta,
        c_parts,
        (expert_gate, expert_up, expert_down),
        (side_x, side_y),
        sgu,
        ws,
    )

    gu_half = (gu_mine.astype(f32) + gus.astype(f32)).astype(bf16)
    gu_half = pad_rows(gu_half.reshape(shards, w_rows, 2 * hid_pad), 1)
    sd_send = pad_rows(sd_grad[:hid].reshape(2 * n_in, d_rows, width), 1)

    grad_float = c_own.astype(f32)
    grad_gates = dgs[:, :n_in].reshape(n_experts, rows).T
    grad_logits = gates * (grad_gates - jnp.sum(gates * grad_gates, axis=-1, keepdims=True))
    router_grad = lax.dot_general(
        hidden_two.astype(f32),
        grad_logits,
        (((0,), (0,)), ((), ())),
        precision=lax.Precision.HIGHEST,
        preferred_element_type=f32,
    )
    grad_hidden_two = jnp.sum(dhs.astype(f32), axis=0) + lax.dot_general(
        grad_logits,
        router_w.astype(f32),
        (((1,), (1,)), ((), ())),
        precision=lax.Precision.HIGHEST,
        preferred_element_type=f32,
    )
    grad_norm_two, gain_two_grad = norm_back(
        grad_hidden_two.reshape(seqs, seg, width), normed_two, inverse_two, gain_two
    )
    grad_residual = grad_float + grad_norm_two
    grad_attn = grad_residual.astype(bf16)

    small_grad = pad_to(
        jnp.concatenate(
            [router_grad, jnp.zeros((width, 1), f32), gain_two_grad[:, None]], axis=1
        ),
        1,
        small,
    )
    if line:
        grad_hidden_one, wq_total, small_total, out_w_grad, down_w_grad, gus, *rest = finish(
            6,
            shards,
            chunk,
            n_experts,
            kv_all,
            wo,
            mixed,
            log_rows,
            h1,
            wq,
            gain_one[None],
            small_grad.astype(bf16),
            qkv,
            grad_attn,
            gu_half,
            sd_send,
            mix_part,
            (mix_part[1 % n_out], mix_part[(n_out - 1) % n_out]),
            e_mine,
            e_other,
        )
        *mix_third, e_total, _ = rest
        mixes = [mix_part[0].astype(f32)] + [
            jnp.where(inside, came.astype(f32), 0.0)
            for inside, came in zip((outer > 0, outer < n_out - 1), mix_third)
        ]
    else:
        mixes = [mix_part[0].astype(f32)] + [
            shift(mix_part[n_out - d], d).astype(f32) for d in range(1, n_out)
        ]

        def spread_grad(wires, ins, outs):
            second = wires.exchange("chips", lambda r, d: ins[1].at[r], lambda r, d: outs[1].at[r])
            first = wires.exchange(
                "plane", lambda r, d: ins[0].at[r // n_in], lambda r, d: outs[0].at[r]
            )
            first()
            second()

        grad_all, gus = transfer(
            "spread_grad",
            5,
            shards,
            ["all"],
            shards + 2 * n_in + 16,
            spread_grad,
            [grad_attn, gu_half],
            [((2 * n_in, seg, width), bf16), ((shards, w_pad, 2 * hid_pad), bf16)],
        )
        grad_all = grad_all.reshape(2 * chunk, width)
        e_sum = (e_mine.astype(f32) + e_other.astype(f32)).astype(bf16)
        grad_mixed = nt(grad_all, wo).astype(bf16)
        wo_grad = tn(mixed_low, grad_all).astype(bf16).reshape(half_chips, w_rows, width)
        wo_grad = pad_rows(wo_grad, 1)
        delta_rows = jnp.sum(
            (grad_mixed.astype(f32) * mixed).reshape(2, chunk, GROUP_MEMBERS, HEAD_SIZE), axis=-1
        ).transpose(2, 0, 1)
        dqkv, wos = attend_back(
            6,
            shards,
            chunk,
            qkv[:, :q_cols],
            kv_all,
            grad_mixed,
            log_rows,
            delta_rows,
            wo_grad,
        )
        wo_mine = lax.dynamic_slice_in_dim(wo_grad, core * own_rows, own_rows, 0)
        wo_half = (wo_mine.astype(f32) + wos.astype(f32)).astype(bf16)
        dh1_part = nt(dqkv, wq).astype(bf16).reshape(2 * n_in, seg, width)
        wq_send = pad_rows(tn(h1, dqkv).astype(bf16).reshape(2 * shards, w_rows, cols), 1)
        gain_one_grad = (
            jnp.sum(
                dh1_part.reshape(2 * chunk, width).astype(f32) * h1.astype(f32), axis=0
            )
            / gain_one
        )
        small_grad = small_grad.at[:, n_experts].set(gain_one_grad)
        small_send = pad_rows(small_grad.astype(bf16).reshape(2 * shards, w_rows, small), 1)

        def sum_first(wires, ins, outs):
            dh_ref, wq_ref, small_ref, s_ref, o_ref = ins
            dhs, wqs, smalls, sds, wos = outs
            waits = [
                out_rows_back(wires, shards, o_ref, wos),
                wires.exchange("all", lambda r, d: wq_ref.at[r], lambda r, d: wqs.at[r]),
                wires.exchange("plane", lambda r, d: dh_ref.at[r], lambda r, d: dhs.at[r]),
                wires.exchange("all", lambda r, d: small_ref.at[r], lambda r, d: smalls.at[r]),
                wires.exchange("plane", lambda r, d: s_ref.at[r], lambda r, d: sds.at[r]),
            ]
            for wait in waits:
                wait()

        dh1s, wq_parts, small_parts, sds, wos = transfer(
            "sum_first",
            7,
            shards,
            ["all"],
            4 * n_in + 6 * shards + 16,
            sum_first,
            [dh1_part, wq_send, small_send, sd_send, wo_half.reshape(own_rows * w_pad, width)],
            [
                ((2 * n_in, seg, width), bf16),
                ((2 * shards, w_pad, cols), bf16),
                ((2 * shards, w_pad, small), bf16),
                ((2 * n_in, d_pad, width), bf16),
                ((n_out, w_pad, width), bf16),
            ],
        )
        grad_hidden_one = jnp.sum(dh1s.astype(f32).reshape(2, n_in, seg, width), axis=1)
        wq_total = jnp.sum(
            wq_parts[:, :w_rows].astype(f32).reshape(2 * n_out, n_in, w_rows, cols), axis=0
        )
        down_w_grad = jnp.sum(sds[:, :d_rows].astype(f32), axis=0)
        out_w_grad = jnp.sum(wos[:, :w_rows].astype(f32), axis=0)
        small_total = jnp.sum(small_parts[:, :w_rows].astype(f32), axis=0)
        e_parts = [swap(e_sum[e], e) for e in range(1, n_in)]
        e_total = sum([part.astype(f32) for part in e_parts], e_sum[0].astype(f32)).astype(bf16)
        e_came = lax.ppermute(e_total, "seq", [(0, 1), (1, 0)])
        e_total = jnp.where(
            core == 0,
            jnp.concatenate([e_total, e_came], axis=0),
            jnp.concatenate([e_came, e_total], axis=0),
        )
    total_out = residual + sum(mixes).reshape(seqs, seg, width)
    normed_one, inverse_one, _ = norm_rows(inputs, gain_one)
    grad_norm_one = norm_back(grad_hidden_one, normed_one, inverse_one, gain_one)[0]
    tokens_grad = grad_residual + grad_norm_one

    wq_total = wq_total.transpose(1, 0, 2)
    query_grad = wq_total[:, :, :q_cols].reshape(w_rows, n_in * q_cols)
    key_grad = wq_total[:, :, q_cols : q_cols + HEAD_SIZE].reshape(w_rows, n_in * HEAD_SIZE)
    value_grad = wq_total[:, :, q_cols + HEAD_SIZE :].reshape(w_rows, n_in * HEAD_SIZE)
    gu_total = jnp.sum(
        gus[:, :w_rows].astype(f32).reshape(n_out, n_in, w_rows, 2 * hid_pad), axis=1
    )

    def hidden_whole(piece):
        piece = piece[:, :, :hid].reshape(n_out, w_rows, 2, hid_core)
        return piece.transpose(1, 2, 0, 3).reshape(w_rows, n_out * hid)

    gate_w_grad = hidden_whole(gu_total[:, :, :hid_pad])
    up_w_grad = hidden_whole(gu_total[:, :, hid_pad:])
    e_total = e_total.astype(f32)

    return (
        total_out.astype(bf16).transpose(1, 0, 2),
        tokens_grad.transpose(1, 0, 2),
        small_total[:, n_experts],
        small_total[:, n_experts + 1],
        query_grad,
        key_grad,
        value_grad,
        out_w_grad,
        small_total[:, :n_experts],
        gate_w_grad,
        up_w_grad,
        down_w_grad,
        e_total[:, :ff][None],
        e_total[:, ff : 2 * ff][None],
        e_total[:, 2 * ff :].T[None],
    )


def solution(mesh):
    rows = P(("seq", "fsdp"), None, None)
    matrix = P(("seq", "fsdp"), None)
    vector = P(("seq", "fsdp"))
    expert = P("fsdp", None, None)
    return jax.shard_map(
        body,
        mesh=mesh,
        in_specs=(rows,) * 3 + (vector,) * 2 + (matrix,) * 8 + (expert,) * 3,
        out_specs=(rows,) * 2 + (vector,) * 2 + (matrix,) * 8 + (expert,) * 3,
        check_vma=False,
    )
```

```python
import functools
import math

import jax
import jax.numpy as jnp
from jax import lax
from jax.experimental import pallas as pl
from jax.experimental.pallas import tpu as pltpu
from jax.sharding import PartitionSpec as P

QUERY_HEADS = 12
KEY_VALUE_HEADS = 4
HEAD_SIZE = 128
GROUP_MEMBERS = QUERY_HEADS // KEY_VALUE_HEADS

epsilon = 1e-06
masked_score = -1e30
MESH = pl.DeviceIdType.MESH
VMEM_LIMIT = 63 * 1024 * 1024
f32 = jnp.float32
bf16 = jnp.bfloat16


def round_up(number, step):
    return -(-number // step) * step


def nn(left, right):
    return lax.dot_general(left, right, (((1,), (0,)), ((), ())), preferred_element_type=f32)


def nt(left, right):
    return lax.dot_general(left, right, (((1,), (1,)), ((), ())), preferred_element_type=f32)


def tn(left, right):
    return lax.dot_general(left, right, (((0,), (0,)), ((), ())), preferred_element_type=f32)


def across(inner, step):
    low = lax.rem(inner + step, 2)
    high = lax.rem(inner // 2 + step // 2, 2)
    return low + 2 * high


def place():
    core = lax.axis_index("seq")
    chip = lax.axis_index("fsdp")
    return core, chip, chip // KEY_VALUE_HEADS, lax.rem(chip, KEY_VALUE_HEADS)


def group(kind, shards):
    core, chip, outer, inner = place()
    if kind == "plane":
        size = 2 * KEY_VALUE_HEADS
        return (
            size,
            core * KEY_VALUE_HEADS + inner,
            lambda r: (r // KEY_VALUE_HEADS, outer * KEY_VALUE_HEADS + lax.rem(r, KEY_VALUE_HEADS)),
        )
    if kind == "inner":
        return KEY_VALUE_HEADS, inner, lambda r: (core, outer * KEY_VALUE_HEADS + r)
    if kind == "outer":
        return shards // KEY_VALUE_HEADS, outer, lambda r: (core, r * KEY_VALUE_HEADS + inner)
    if kind == "chips":
        return shards, chip, lambda r: (core, r)
    if kind == "all":
        return 2 * shards, core * shards + chip, lambda r: (r // shards, lax.rem(r, shards))
    return 2, core, lambda r: (r, chip)


def repeat(first, last, step):
    if last - first <= 16:
        for index in range(first, last):
            step(index)
    else:

        def one(index, carry):
            step(index)
            return carry

        lax.fori_loop(first, last, one, 0)


class Wires:
    def __init__(self, shards, send_sems, recv_sems, local_sems):
        self.shards = shards
        self.send_sems, self.recv_sems, self.local_sems = send_sems, recv_sems, local_sems
        self.used = 0
        self.leaving = []

    def greet(self, kinds):
        barrier = pltpu.get_barrier_semaphore()
        total = 0
        for kind in kinds:
            size, me, device = group(kind, self.shards)

            def signal(d, size=size, me=me, device=device):
                pl.semaphore_signal(
                    barrier, inc=1, device_id=device(lax.rem(me + d, size)), device_id_type=MESH
                )

            repeat(1, size, signal)
            total += size - 1
        pl.semaphore_wait(barrier, total)

    def take(self, count):
        base = self.used
        self.used += count
        return base

    def remote(self, source, target, index, device):
        return pltpu.make_async_remote_copy(
            src_ref=source,
            dst_ref=target,
            send_sem=self.send_sems.at[index],
            recv_sem=self.recv_sems.at[index],
            device_id=device,
            device_id_type=MESH,
        )

    def local(self, source, target, index):
        return pltpu.make_async_copy(source, target, self.local_sems.at[index])

    def exchange(self, kind, source_for, target_from, own=True):
        size, me, device = group(kind, self.shards)
        base = self.take(size)

        def copy(d):
            to = lax.rem(me + d, size)
            return self.remote(source_for(to, d), target_from(me, d), base + d, device(to))

        repeat(1, size, lambda d: copy(d).start())
        if own:
            self.local(source_for(me, 0), target_from(me, 0), base).start()
        self.leaving.append(lambda: repeat(1, size, lambda d: copy(d).wait_send()))

        def arrive(then=None):
            def one(d):
                came = lax.rem(me - d + size, size)
                place_of = target_from(came, d)
                self.remote(place_of, place_of, base + d, device(came)).wait_recv()
                if then is not None:
                    then(d)

            repeat(1, size, one)
            if own:
                self.local(source_for(me, 0), target_from(me, 0), base).wait()

        return arrive

    def sibling(self, source, target, comes):
        core, chip, _, _ = place()
        device = (1 - core, chip)
        index = self.take(1)
        copy = self.remote(source, target, index, device)
        copy.start()
        self.leaving.append(copy.wait_send)
        return self.remote(comes, comes, index, device).wait_recv

    def finish(self):
        for leave in self.leaving:
            leave()


def transfer(name, collective, shards, kinds, sems, body, operands, outs, scratch=()):
    count = len(operands)

    def kernel(*refs):
        ins, results = refs[:count], refs[count : count + len(outs)]
        room, sem_refs = refs[count + len(outs) : -3], refs[-3:]
        wires = Wires(shards, *sem_refs)
        wires.greet(kinds)
        body(wires, ins, results, *room)
        wires.finish()

    return pl.pallas_call(
        kernel,
        out_shape=[jax.ShapeDtypeStruct(shape, kind) for shape, kind in outs],
        in_specs=[pl.BlockSpec(memory_space=pl.ANY)] * count,
        out_specs=[pl.BlockSpec(memory_space=pl.ANY)] * len(outs),
        scratch_shapes=[pltpu.VMEM(shape, kind) for shape, kind in scratch]
        + [pltpu.SemaphoreType.DMA((sems,))] * 3,
        compiler_params=pltpu.CompilerParams(
            collective_id=collective, has_side_effects=True, vmem_limit_bytes=VMEM_LIMIT
        ),
        name=name,
    )(*operands)


def add_pieces(wires, first, second, result, size, left, right, total):
    items, rows, _ = first.shape
    per_item = rows // size
    count = items * per_item
    load_base, store_base = wires.take(4), wires.take(2)

    def cut(i):
        return i // per_item, pl.ds(i % per_item * size, size)

    def loads(i):
        slot = i % 2
        return (
            wires.local(first.at[cut(i)], left(slot), load_base + 2 * slot),
            wires.local(second.at[cut(i)], right(slot), load_base + 2 * slot + 1),
        )

    def store(i):
        return wires.local(total(i % 2), result.at[cut(i)], store_base + i % 2)

    for copy in loads(0):
        copy.start()
    for i in range(count):
        if i + 1 < count:
            for copy in loads(i + 1):
                copy.start()
        for copy in loads(i):
            copy.wait()
        if i >= 2:
            store(i - 2).wait()
        slot = i % 2
        total(slot)[...] = (left(slot)[...].astype(f32) + right(slot)[...].astype(f32)).astype(bf16)
        store(i).start()
    for i in range(max(0, count - 2), count):
        store(i).wait()


def neighbours(wires, n, sources, targets, sends, comes):
    core, chip, outer, inner = place()
    base = wires.take(2)

    def copy(way):
        sign = (1, -1)[way]
        to = lax.rem(outer + sign + n, n)
        device = (core, to * KEY_VALUE_HEADS + inner)
        return wires.remote(sources[way], targets[way], base + way, device)

    def come(way):
        sign = (1, -1)[way]
        origin = lax.rem(outer - sign + n, n)
        device = (core, origin * KEY_VALUE_HEADS + inner)
        return wires.remote(targets[way], targets[way], base + way, device)

    def each(conditions, action):
        for way in range(2):
            pl.when(conditions[way])(lambda way=way: action(way))

    each(sends, lambda way: copy(way).start())
    wires.leaving.append(lambda: each(sends, lambda way: copy(way).wait_send()))
    return lambda: each(comes, lambda way: come(way).wait_recv())


def gather_step(wires, n, step, sources, targets):
    outer = place()[2]
    sends = ((outer >= step) & (outer < n - 1), (outer < n - step) & (outer > 0))
    comes = (outer > step, outer < n - 1 - step)
    return neighbours(wires, n, sources, targets, sends, comes)


def sum_step(wires, n, step, sources, targets):
    outer = place()[2]
    sends = (
        (outer <= step) & (outer < n - 1),
        (outer >= n - 1 - step) & (outer > 0),
    )
    comes = (
        (outer >= 1) & (outer <= step + 1),
        (outer <= n - 2) & (outer >= n - 2 - step),
    )
    return neighbours(wires, n, sources, targets, sends, comes)


def out_rows_back(wires, shards, grad_ref, sums_ref):
    core, chip, outer, inner = place()
    n_in, n_out, half_chips = KEY_VALUE_HEADS, shards // KEY_VALUE_HEADS, shards // 2
    own_rows = half_chips // 2
    rows = sums_ref.shape[1]
    from_inner = 2 * core + chip // half_chips
    from_core = lax.rem(chip, half_chips) // own_rows
    sends = wires.take(own_rows)
    base = wires.take(n_out)

    def copy(i):
        to = (inner // 2, half_chips * lax.rem(inner, 2) + core * own_rows + i)
        here = (to[0] == core) & (to[1] == chip)
        return here, pltpu.make_async_remote_copy(
            src_ref=grad_ref.at[pl.ds(i * rows, rows)],
            dst_ref=sums_ref.at[outer],
            send_sem=wires.send_sems.at[sends + i],
            recv_sem=wires.recv_sems.at[base + outer],
            device_id=to,
            device_id_type=MESH,
        )

    def start(i):
        here, send = copy(i)
        pl.when(jnp.logical_not(here))(send.start)
        pl.when(here)(lambda: wires.local(grad_ref.at[pl.ds(i * rows, rows)], sums_ref.at[outer], base).start())

    def leave(i):
        here, send = copy(i)
        pl.when(jnp.logical_not(here))(send.wait_send)

    def come(k):
        origin = (from_core, k * n_in + from_inner)
        here = (origin[0] == core) & (origin[1] == chip)
        place_of = sums_ref.at[k]
        pl.when(jnp.logical_not(here))(
            wires.remote(place_of, place_of, base + k, origin).wait_recv
        )
        pl.when(here)(lambda: wires.local(place_of, place_of, base).wait())

    repeat(0, own_rows, start)
    wires.leaving.append(lambda: repeat(0, own_rows, leave))
    return lambda: repeat(0, n_out, come)


class Line:
    def __init__(self, wires, source, every):
        self.wires, self.source, self.every = wires, source, every
        self.n = every.shape[0]
        self.core, _, self.outer, self.inner = place()
        self.bases = {1: wires.take(self.n), -1: wires.take(self.n)}

    def device(self, at):
        return self.core, at * KEY_VALUE_HEADS + self.inner

    def order(self):
        low = self.outer < self.n // 2
        return [
            lax.rem(jnp.where(low, self.outer + k, self.outer - k + self.n), self.n)
            for k in range(self.n)
        ]

    def hop(self, step, sign):
        to = lax.rem(self.outer + sign + self.n, self.n)
        block = lax.rem(self.outer - sign * step + 2 * self.n, self.n)
        source = self.source if step == 0 else self.every.at[block]
        index = self.bases[sign] + step
        return self.wires.remote(source, self.every.at[block], index, self.device(to))

    def sends(self, step, sign):
        to, block = self.outer + sign, self.outer - sign * step
        return (to >= 0) & (to < self.n) & (block >= 0) & (block < self.n)

    def start(self, step):
        for sign in (1, -1):
            pl.when(self.sends(step, sign))(lambda sign=sign: self.hop(step, sign).start())

    def arrive(self, step):
        for sign in (1, -1):
            come = self.outer - sign * (step + 1)

            def wait(sign=sign, come=come):
                block = self.every.at[lax.rem(come + self.n, self.n)]
                to = lax.rem(self.outer - sign + self.n, self.n)
                index = self.bases[sign] + step
                self.wires.remote(block, block, index, self.device(to)).wait_recv()

            pl.when((come >= 0) & (come < self.n))(wait)

    def leave(self):
        for step in range(self.n - 1):
            for sign in (1, -1):
                pl.when(self.sends(step, sign))(
                    lambda step=step, sign=sign: self.hop(step, sign).wait_send()
                )


def far_first(outer, n):
    low = outer < n // 2
    order = []
    for k in range(n - 1):
        down = n - 1 - k
        order.append(
            jnp.where(low, jnp.where(down <= outer, down - 1, down), jnp.where(k >= outer, k + 1, k))
        )
    return order


def causal(scores):
    key_at = lax.broadcasted_iota(jnp.int32, scores.shape, 0)
    query_at = lax.broadcasted_iota(jnp.int32, scores.shape, 1)
    return jnp.where(key_at <= query_at, scores, masked_score)


def each_pair(block, outer, own, pair):
    def some(head, carry):
        if own:
            pair(head, 0, block, 0, True)
            pair(head, 1, block, 0, False)
            pair(head, 1, block, 1, True)
        else:
            pair(head, 1, block, 0, False)

            @pl.when(block < outer)
            def _():
                pair(head, 0, block, 0, False)
                pair(head, 1, block, 1, False)

        return carry

    lax.fori_loop(0, GROUP_MEMBERS, some, 0)


def attend_kernel(shards, chunk, joined, gain_col, out_rows, *refs):
    if joined:
        x_ref, q_pieces, o_ref, cot_ref, expert_ref, gu_ref, s_ref, *refs = refs
    else:
        qkv_in, *refs = refs
    mixed_ref, log_ref, kv_out, *refs = refs
    if joined:
        out_ref, h1_ref, qkv_ref, wgu_ref, ws_ref, wq_out, wo_out, side_x, side_y, *refs = refs
        passes, refs = (refs[:2], refs[2:4], refs[4:6]), refs[6:]
        out_stage, out_recv, xs, wq, wo, *refs = refs
    else:
        qkv_ref, *refs = refs
    kv_all, largest, total, summed, send_sems, recv_sems, local_sems = refs
    core, chip, outer, inner = place()
    q_width = GROUP_MEMBERS * HEAD_SIZE
    cols = q_width + 2 * HEAD_SIZE
    wires = Wires(shards, send_sems, recv_sems, local_sems)
    factor = HEAD_SIZE**-0.5 * math.log2(math.e)
    if joined:
        wires.greet(["all"])
        q_in = wires.exchange(
            "chips",
            lambda r, d: q_pieces.at[lax.rem(r, KEY_VALUE_HEADS)],
            lambda r, d: wq.at[core, r],
        )
        x_in = wires.exchange(
            "plane", lambda r, d: x_ref.at[r // KEY_VALUE_HEADS], lambda r, d: xs.at[r]
        )
        o_in, o_settle = out_rows(wires, o_ref, wo)
        passed = gather_step(wires, kv_all.shape[0], 0, [cot_ref, cot_ref], passes[0])
        q_in()
        wires.sibling(wq.at[core], wq.at[core], wq.at[1 - core])()
        x_in()
        sides = [
            wires.remote(
                expert_ref,
                side,
                wires.take(1),
                (core, outer * KEY_VALUE_HEADS + across(inner, step)),
            )
            for step, side in ((1, side_x), (2, side_y))
        ]
        for side in sides:
            side.start()
        wide = xs.shape[2]
        small = wq[:, :, :, cols:].reshape(wide, wq.shape[3] - cols).astype(f32)
        gain = small.T[gain_col : gain_col + 1, :]
        seg = xs.shape[1]
        for r in range(xs.shape[0]):
            values = xs[r].astype(f32)
            inverse = lax.rsqrt(jnp.mean(values * values, axis=-1, keepdims=True) + epsilon)
            h1_ref[r * seg : (r + 1) * seg, :] = (values * inverse * gain).astype(bf16)
        projection = wq[:, :, :, 0:cols].reshape(wide, cols)
        for half in range(2):
            rows = pl.ds(half * chunk, chunk)
            part = nn(h1_ref[rows, :], projection).astype(bf16)
            qkv_ref[rows, :] = part
            kv_all[outer, rows, :] = part[:, q_width:]
    else:
        load = wires.local(qkv_in, qkv_ref, wires.take(1))
        load.start()
        load.wait()
        kv_all[outer] = qkv_ref[:, q_width:]
        wires.greet(["outer"])
    line = Line(wires, kv_all.at[outer], kv_all)
    line.start(0)
    largest[...] = jnp.full_like(largest, masked_score)
    total[...] = jnp.zeros_like(total)
    summed[...] = jnp.zeros_like(summed)

    def pair(head, half, block, key_half, masked):
        cols = pl.ds(pl.multiple_of(head * HEAD_SIZE, HEAD_SIZE), HEAD_SIZE)
        rows = pl.ds(key_half * chunk, chunk)
        query = qkv_ref[pl.ds(half * chunk, chunk), cols]
        scores = nt(kv_all[block, rows, 0:HEAD_SIZE], query)
        if masked:
            scores = causal(scores)
        before = largest[head, half]
        new = jnp.maximum(before, jnp.max(scores, axis=0, keepdims=True))
        weights = jnp.exp2((scores - new) * factor)
        shrink = jnp.exp2((before - new) * factor)
        largest[head, half] = new
        total[head, half] = total[head, half] * shrink + jnp.sum(weights, axis=0, keepdims=True)
        summed[head, half] = summed[head, half] * shrink + tn(
            kv_all[block, rows, HEAD_SIZE : 2 * HEAD_SIZE], weights.astype(bf16)
        )

    for k, block in enumerate(line.order()):
        if k > 0:
            line.arrive(k - 1)
            if k < line.n - 1:
                line.start(k)
        if joined and k == line.n - 2:
            passed()
            passed = gather_step(wires, line.n, 1, passes[0], passes[1])
            o_in()
            gu_in, gu_settle, s_in, s_settle = spread_shared(wires, gu_ref, s_ref, wgu_ref, ws_ref)
        each_pair(block, outer, k == 0, pair)
    keep = wires.local(kv_all, kv_out, wires.take(1))
    keep.start()
    for head in range(GROUP_MEMBERS):
        for half in range(2):
            mixed_ref[
                half * chunk : (half + 1) * chunk, head * HEAD_SIZE : (head + 1) * HEAD_SIZE
            ] = (summed[head, half] / total[head, half]).T
            log_ref[head, half : half + 1, :] = largest[head, half] * factor + jnp.log2(
                total[head, half]
            )
    if joined:
        o_settle()
        w_out = wo[...].reshape(q_width, wide)
        for half in range(2):
            rows = pl.ds(half * chunk, chunk)
            out_stage[rows, :] = nn(mixed_ref[rows, :].astype(bf16), w_out).astype(bf16)
        out_in = wires.exchange(
            "plane", lambda r, d: out_stage.at[pl.ds(r * seg, seg)], lambda r, d: out_recv.at[r]
        )
        passed()
        passed = gather_step(wires, line.n, 2, passes[1], passes[2])
        kept = [wires.local(wq, wq_out, wires.take(1)), wires.local(wo, wo_out, wires.take(1))]
        for copy in kept:
            copy.start()
        gu_in()
        gu_settle.start()
        s_in()
        s_settle.start()
        out_in()
        for half in range(2):
            parts = out_recv[half * KEY_VALUE_HEADS].astype(f32)
            for j in range(1, KEY_VALUE_HEADS):
                parts = parts + out_recv[half * KEY_VALUE_HEADS + j].astype(f32)
            out_ref[half] = parts
        gu_settle.wait()
        s_settle.wait()
        passed()
        for copy in sides + kept:
            copy.wait()
    line.leave()
    wires.finish()
    keep.wait()


def spread_shared(wires, gu_ref, s_ref, wgu_ref, ws_ref):
    core, chip, _, _ = place()
    sibling = (1 - core, chip)
    gu_in = wires.exchange(
        "chips",
        lambda r, d: gu_ref.at[r // KEY_VALUE_HEADS],
        lambda r, d: wgu_ref.at[core, r],
    )
    s_in = wires.exchange("inner", lambda r, d: s_ref, lambda r, d: ws_ref.at[core, r])
    gu_settle = wires.remote(wgu_ref.at[core], wgu_ref.at[core], wires.take(1), sibling)
    s_settle = wires.remote(ws_ref.at[core], ws_ref.at[core], wires.take(1), sibling)
    return gu_in, gu_settle, s_in, s_settle


def attend(collective, shards, chunk, operands, gain_col=None, out_rows=None):
    joined = out_rows is not None
    n_out = shards // KEY_VALUE_HEADS
    rows = 2 * chunk
    seg = chunk // KEY_VALUE_HEADS
    cols = (GROUP_MEMBERS + 2) * HEAD_SIZE
    more_outs, more_scratch = [], [pltpu.VMEM((rows, cols), bf16)]
    if joined:
        _, q_pieces, out_piece, cot, expert_half, gu, down = operands
        wide = out_piece.shape[1]
        wq_shape = (2, shards) + q_pieces.shape[1:]
        wo_shape = (shards // 2,) + out_piece.shape

        def array(shape, kind=bf16):
            return jax.ShapeDtypeStruct(shape, kind)

        more_outs = [
            array((2, seg, wide), f32),
            array((rows, wide)),
            array((rows, cols)),
            array((2, shards) + gu.shape[1:]),
            array((2, KEY_VALUE_HEADS) + down.shape),
            array(wq_shape),
            array(wo_shape),
            array(expert_half.shape),
            array(expert_half.shape),
        ] + [array(cot.shape)] * 6
        more_scratch = [
            pltpu.VMEM((rows, wide), bf16),
            pltpu.VMEM((2 * KEY_VALUE_HEADS, seg, wide), bf16),
            pltpu.VMEM((2 * KEY_VALUE_HEADS, seg, wide), bf16),
            pltpu.VMEM(wq_shape, bf16),
            pltpu.VMEM(wo_shape, bf16),
        ]
    kv_shape = (n_out, rows, 2 * HEAD_SIZE)
    vmem = pl.BlockSpec(memory_space=pltpu.VMEM)
    hbm = pl.BlockSpec(memory_space=pl.ANY)
    state = (GROUP_MEMBERS, 2, 1, chunk)
    return pl.pallas_call(
        functools.partial(attend_kernel, shards, chunk, joined, gain_col, out_rows),
        in_specs=[hbm] * len(operands),
        out_specs=[vmem, vmem, hbm] + ([vmem] * 3 + [hbm] * 12) * joined,
        out_shape=[
            jax.ShapeDtypeStruct((rows, GROUP_MEMBERS * HEAD_SIZE), f32),
            jax.ShapeDtypeStruct((GROUP_MEMBERS, 2, chunk), f32),
            jax.ShapeDtypeStruct(kv_shape, bf16),
        ]
        + more_outs,
        scratch_shapes=more_scratch
        + [
            pltpu.VMEM(kv_shape, bf16),
            pltpu.VMEM(state, f32),
            pltpu.VMEM(state, f32),
            pltpu.VMEM((GROUP_MEMBERS, 2, HEAD_SIZE, chunk), f32),
        ]
        + [pltpu.SemaphoreType.DMA((2 * n_out + 4 * shards + 64,))] * 3,
        compiler_params=pltpu.CompilerParams(
            collective_id=collective, has_side_effects=True, vmem_limit_bytes=VMEM_LIMIT
        ),
        name="attend",
    )(*operands)


def attend_back_kernel(shards, chunk, own_rows, *refs):
    q_ref, kv_ref, grad_ref, log_ref, delta_ref, wo_ref, *refs = refs
    dqkv_ref, wo_other, *refs = refs
    came, stage, sums, dq_sums, send_sems, recv_sems, local_sems = refs
    wires = Wires(shards, send_sems, recv_sems, local_sems)
    core, chip, outer, inner = place()
    n = kv_ref.shape[0]
    scale = HEAD_SIZE**-0.5
    factor = scale * math.log2(math.e)
    wires.greet(["outer", "core"])
    wo_in = wires.sibling(
        wo_ref.at[pl.ds((1 - core) * own_rows, own_rows)], wo_other, wo_other
    )
    send_base, recv_base = wires.take(n), wires.take(n)
    dq_sums[...] = jnp.zeros_like(dq_sums)

    def pair(head, half, block, key_half, masked):
        cols = pl.ds(pl.multiple_of(head * HEAD_SIZE, HEAD_SIZE), HEAD_SIZE)
        mine, rows = pl.ds(half * chunk, chunk), pl.ds(key_half * chunk, chunk)
        query, grad = q_ref[mine, cols], grad_ref[mine, cols]
        key = kv_ref[block, rows, 0:HEAD_SIZE]
        value = kv_ref[block, rows, HEAD_SIZE : 2 * HEAD_SIZE]
        scores = nt(key, query)
        if masked:
            scores = causal(scores)
        weights = jnp.exp2(scores * factor - log_ref[head, half : half + 1, :])
        grad_scores = (
            weights * (nt(value, grad) - delta_ref[head, half : half + 1, :])
        ).astype(bf16)
        sums[rows, 0:HEAD_SIZE] += nn(grad_scores, query)
        sums[rows, HEAD_SIZE : 2 * HEAD_SIZE] += nn(weights.astype(bf16), grad)
        dq_sums[mine, cols] += tn(grad_scores, key)

    def send(k, block):
        return pltpu.make_async_remote_copy(
            src_ref=stage.at[k],
            dst_ref=came.at[outer],
            send_sem=send_sems.at[send_base + k],
            recv_sem=recv_sems.at[recv_base + outer],
            device_id=(core, block * KEY_VALUE_HEADS + inner),
            device_id_type=MESH,
        )

    order = far_first(outer, n)
    for k, block in enumerate(order + [outer]):
        sums[...] = jnp.zeros_like(sums)
        each_pair(block, outer, k == n - 1, pair)
        if k < n - 1:
            stage[k] = sums[...].astype(bf16)
            send(k, block).start()
    width = GROUP_MEMBERS * HEAD_SIZE
    dqkv_ref[:, 0:width] = (dq_sums[...] * scale).astype(bf16)
    for d in range(1, n):
        origin = lax.rem(outer + d, n)
        pltpu.make_async_remote_copy(
            src_ref=came.at[origin],
            dst_ref=came.at[origin],
            send_sem=send_sems.at[send_base],
            recv_sem=recv_sems.at[recv_base + origin],
            device_id=(core, origin * KEY_VALUE_HEADS + inner),
            device_id_type=MESH,
        ).wait_recv()
        sums[...] += came[origin].astype(f32)
    dqkv_ref[:, width : width + HEAD_SIZE] = (sums[:, 0:HEAD_SIZE] * scale).astype(bf16)
    dqkv_ref[:, width + HEAD_SIZE :] = sums[:, HEAD_SIZE:].astype(bf16)
    for k, block in enumerate(order):
        send(k, block).wait_send()
    wo_in()
    wires.finish()


def attend_back(collective, shards, chunk, q, kv_all, grad_mixed, log_rows, delta_rows, wo_grad):
    n_out, rows, kv_cols = kv_all.shape
    own_rows = wo_grad.shape[0] // 2
    vmem = pl.BlockSpec(memory_space=pltpu.VMEM)
    hbm = pl.BlockSpec(memory_space=pl.ANY)
    width = GROUP_MEMBERS * HEAD_SIZE
    return pl.pallas_call(
        functools.partial(attend_back_kernel, shards, chunk, own_rows),
        in_specs=[vmem] * 5 + [hbm],
        out_specs=[vmem, hbm],
        out_shape=[
            jax.ShapeDtypeStruct((rows, width + kv_cols), bf16),
            jax.ShapeDtypeStruct((own_rows,) + wo_grad.shape[1:], bf16),
        ],
        scratch_shapes=[
            pltpu.VMEM(kv_all.shape, bf16),
            pltpu.VMEM(kv_all.shape, bf16),
            pltpu.VMEM((rows, kv_cols), f32),
            pltpu.VMEM((rows, width), f32),
        ]
        + [pltpu.SemaphoreType.DMA((2 * n_out + 8,))] * 3,
        compiler_params=pltpu.CompilerParams(
            collective_id=collective, has_side_effects=True, vmem_limit_bytes=VMEM_LIMIT
        ),
        name="attend_back",
    )(q, kv_all, grad_mixed, log_rows, delta_rows, wo_grad)


def finish_kernel(shards, chunk, gain_col, *refs):
    (
        kv_ref,
        wo_ref,
        mixed_ref,
        log_ref,
        h1_ref,
        wq_ref,
        gain_ref,
        small_ref,
        qkv_ref,
        grad_own,
        gu_ref,
        sd_ref,
        mix_ref,
        mix_up,
        mix_down,
        e_first_ref,
        e_second_ref,
        dh1_out,
        wq_out,
        small_out,
        wo_out,
        sd_out,
        gu_out,
        mix_up_out,
        mix_down_out,
        e_both,
        e_ref,
        q_ref,
        grad_all,
        dmixed,
        delta,
        came,
        stage,
        sums,
        dq_sums,
        dqkv,
        dwo,
        wo_came,
        wo_recv,
        dwq,
        wq_came,
        wq_recv,
        small_all,
        small_came,
        small_recv,
        dh_stage,
        dh_recv,
        sd_recv,
        mix_came,
        mix_term,
        mix_came_last,
        mix_term_last,
        e_came,
        e_term,
        e_last,
        e_own,
        send_sems,
        recv_sems,
        local_sems,
    ) = refs
    wires = Wires(shards, send_sems, recv_sems, local_sems)
    core, chip, outer, inner = place()
    n = kv_ref.shape[0]
    scale = HEAD_SIZE**-0.5
    factor = scale * math.log2(math.e)
    width = GROUP_MEMBERS * HEAD_SIZE
    wide = h1_ref.shape[1]
    half_wide = wide // 2
    w_rows = wq_recv.shape[1]
    seg = dh_recv.shape[1]
    mine, other = pl.ds(core * half_wide, half_wide), pl.ds((1 - core) * half_wide, half_wide)
    wires.greet(["all"])
    q_load = wires.local(qkv_ref.at[:, pl.ds(0, width)], q_ref, wires.take(1))
    q_load.start()
    grad_in = wires.exchange(
        "plane", lambda r, d: grad_own.at[r // KEY_VALUE_HEADS], lambda r, d: grad_all.at[r]
    )

    mix_steps = [sum_step(wires, n, 0, [mix_up, mix_down], [mix_came.at[0], mix_came.at[1]])]
    mix_loads = [
        wires.local(mix_ref.at[slot], target.at[way], wires.take(1))
        for target, slots in ((mix_term, (2 % n, (n - 2) % n)), (mix_term_last, (3 % n, (n - 3) % n)))
        for way, slot in enumerate(slots)
    ]
    for copy in mix_loads:
        copy.start()

    def mix_on(step, came, term, targets):
        mix_steps[-1]()
        for way in range(2):
            mix_loads[2 * (step - 1) + way].wait()
            inside = (outer > 0, outer < n - 1)[way]
            term[way] = (
                term[way].astype(f32) + jnp.where(inside, came[way].astype(f32), 0.0)
            ).astype(bf16)
        mix_steps.append(sum_step(wires, n, step, [term.at[0], term.at[1]], targets))

    add_pieces(
        wires,
        e_first_ref,
        e_second_ref,
        e_ref,
        half_wide // 3,
        lambda slot: dh_stage.at[pl.ds(slot * (half_wide // 3), half_wide // 3)],
        lambda slot: dh_stage.at[pl.ds((2 + slot) * (half_wide // 3), half_wide // 3)],
        lambda slot: e_own.at[pl.ds(slot * (half_wide // 3), half_wide // 3)],
    )

    e_cols = e_ref.shape[2] // 2
    e_cuts = (pl.ds(0, e_cols), pl.ds(e_cols, e_cols))
    e_sides = ((1, 2), (2, 1))

    def plane_device(step):
        return core, outer * KEY_VALUE_HEADS + across(inner, step)

    e_local, e_first, e_second = wires.take(3), wires.take(4), wires.take(2)
    e_loads = [wires.local(e_ref.at[0], e_own, e_local)]
    e_sends = []
    for way, (near, far) in enumerate(e_sides):
        e_loads.append(wires.local(e_ref.at[far, :, e_cuts[way]], e_term.at[way], e_local + 1 + way))
        for k, e in enumerate((near, 3)):
            e_sends.append(
                wires.remote(
                    e_ref.at[e, :, e_cuts[way]],
                    e_came.at[way, k],
                    e_first + 2 * way + k,
                    plane_device(near),
                )
            )
    grad_in()
    for copy in e_sends + e_loads:
        copy.start()
    gu_in = wires.exchange("chips", lambda r, d: gu_ref.at[r], lambda r, d: gu_out.at[r])
    sd_in = wires.exchange("plane", lambda r, d: sd_ref.at[r], lambda r, d: sd_recv.at[r])

    q_load.wait()
    mix_on(1, mix_came, mix_term, [mix_came_last.at[0], mix_came_last.at[1]])
    per_half = grad_all.shape[0] // 2
    for half in range(2):
        rows = pl.ds(half * chunk, chunk)
        grad = grad_all[pl.ds(half * per_half, per_half)].reshape(chunk, wide)
        part = nt(grad, wo_ref[...]).astype(bf16)
        dmixed[rows, :] = part
        weighted = part.astype(f32) * mixed_ref[rows, :]
        for head in range(GROUP_MEMBERS):
            cols = slice(head * HEAD_SIZE, (head + 1) * HEAD_SIZE)
            delta[head, half] = jnp.sum(weighted[:, cols].T, axis=0, keepdims=True)

    send_base, recv_base = wires.take(n), wires.take(n)
    dq_sums[...] = jnp.zeros_like(dq_sums)

    def pair(head, half, block, key_half, masked):
        cols = pl.ds(pl.multiple_of(head * HEAD_SIZE, HEAD_SIZE), HEAD_SIZE)
        here, rows = pl.ds(half * chunk, chunk), pl.ds(key_half * chunk, chunk)
        query, grad = q_ref[here, cols], dmixed[here, cols]
        key = kv_ref[block, rows, 0:HEAD_SIZE]
        value = kv_ref[block, rows, HEAD_SIZE : 2 * HEAD_SIZE]
        scores = nt(key, query)
        if masked:
            scores = causal(scores)
        weights = jnp.exp2(scores * factor - log_ref[head, half : half + 1, :])
        grad_scores = (weights * (nt(value, grad) - delta[head, half])).astype(bf16)
        sums[rows, 0:HEAD_SIZE] += nn(grad_scores, query)
        sums[rows, HEAD_SIZE : 2 * HEAD_SIZE] += nn(weights.astype(bf16), grad)
        dq_sums[here, cols] += tn(grad_scores, key)

    def send(k, block):
        return pltpu.make_async_remote_copy(
            src_ref=stage.at[k],
            dst_ref=came.at[outer],
            send_sem=send_sems.at[send_base + k],
            recv_sem=recv_sems.at[recv_base + outer],
            device_id=(core, block * KEY_VALUE_HEADS + inner),
            device_id_type=MESH,
        )

    order = far_first(outer, n)
    for k, block in enumerate(order + [outer]):
        sums[...] = jnp.zeros_like(sums)
        each_pair(block, outer, k == n - 1, pair)
        if k < n - 1:
            stage[k] = sums[...].astype(bf16)
            send(k, block).start()

    dqkv[:, 0:width] = (dq_sums[...] * scale).astype(bf16)
    dwo[...] = tn(
        mixed_ref[...].astype(bf16), grad_all[...].reshape(2 * chunk, wide)
    ).astype(bf16)
    wo_rows = wo_came.shape[0]
    wo_in = wires.sibling(dwo.at[pl.ds((1 - core) * wo_rows, wo_rows)], wo_came, wo_came)
    dwq[:, 0:width] = tn(h1_ref[...], dqkv[:, 0:width]).astype(bf16)
    q_cols = pl.ds(0, width)
    q_in = wires.sibling(dwq.at[other, q_cols], wq_came.at[:, q_cols], wq_came.at[:, q_cols])
    wo_in()
    wo_came[...] = (
        dwo[pl.ds(core * wo_rows, wo_rows), :].astype(f32) + wo_came[...].astype(f32)
    ).astype(bf16)
    wo_parts = out_rows_back(wires, shards, wo_came, wo_recv)
    q_in()
    wq_came[:, 0:width] = (
        dwq[mine, 0:width].astype(f32) + wq_came[:, 0:width].astype(f32)
    ).astype(bf16)

    def pieces(cols):
        return wires.exchange(
            "chips",
            lambda r, d: wq_came.at[pl.ds(r * w_rows, w_rows), cols],
            lambda r, d: wq_recv.at[r, :, cols],
        )

    q_parts = pieces(q_cols)

    for copy in e_sends:
        copy.wait()
    for copy in e_loads:
        copy.wait()
    e_passed = []
    for way, (near, far) in enumerate(e_sides):
        e_term[way] = (e_term[way].astype(f32) + e_came[way, 1].astype(f32)).astype(bf16)
        e_passed.append(
            wires.remote(e_term.at[way], e_last.at[way], e_second + way, plane_device(far))
        )
    for copy in e_passed:
        copy.start()

    for d in range(1, n):
        origin = lax.rem(outer + d, n)
        pltpu.make_async_remote_copy(
            src_ref=came.at[origin],
            dst_ref=came.at[origin],
            send_sem=send_sems.at[send_base],
            recv_sem=recv_sems.at[recv_base + origin],
            device_id=(core, origin * KEY_VALUE_HEADS + inner),
            device_id_type=MESH,
        ).wait_recv()
        sums[...] += came[origin].astype(f32)
    dqkv[:, width : width + HEAD_SIZE] = (sums[:, 0:HEAD_SIZE] * scale).astype(bf16)
    dqkv[:, width + HEAD_SIZE :] = sums[:, HEAD_SIZE:].astype(bf16)

    gain_sum = jnp.zeros((1, wide), f32)
    for half in range(2):
        rows = pl.ds(half * chunk, chunk)
        part = nt(dqkv[rows, :], wq_ref[...]).astype(bf16)
        dh_stage[rows, :] = part
        gain_sum = gain_sum + jnp.sum(
            part.astype(f32) * h1_ref[rows, :].astype(f32), axis=0, keepdims=True
        )
    dh_in = wires.exchange(
        "plane", lambda r, d: dh_stage.at[pl.ds(r * seg, seg)], lambda r, d: dh_recv.at[r]
    )
    dwq[:, width:] = tn(h1_ref[...], dqkv[:, width:]).astype(bf16)
    kv_cols = pl.ds(width, 2 * HEAD_SIZE)
    kv_in = wires.sibling(dwq.at[other, kv_cols], wq_came.at[:, kv_cols], wq_came.at[:, kv_cols])
    column = (gain_sum / gain_ref[...])
    columns = jnp.broadcast_to(column, (small_all.shape[1], wide)).T
    at_col = lax.broadcasted_iota(jnp.int32, columns.shape, 1)
    small_all[...] = jnp.where(at_col == gain_col, columns, small_ref[...].astype(f32)).astype(bf16)
    small_in = wires.sibling(small_all.at[other], small_came, small_came)
    kv_in()
    wq_came[:, width:] = (
        dwq[mine, width:].astype(f32) + wq_came[:, width:].astype(f32)
    ).astype(bf16)
    kv_parts = pieces(kv_cols)
    small_in()
    small_came[...] = (small_all[mine, :].astype(f32) + small_came[...].astype(f32)).astype(bf16)
    small_parts = wires.exchange(
        "chips",
        lambda r, d: small_came.at[pl.ds(r * w_rows, w_rows)],
        lambda r, d: small_recv.at[r],
    )
    mix_on(2, mix_came_last, mix_term_last, [mix_up_out, mix_down_out])

    for way, copy in enumerate(e_passed):
        copy.wait()
        e_own[:, e_cuts[way]] = (
            e_own[:, e_cuts[way]].astype(f32)
            + e_came[way, 0].astype(f32)
            + e_last[way].astype(f32)
        ).astype(bf16)
    e_keep = wires.local(e_own, e_both.at[mine], e_local)
    e_keep.start()
    e_in = wires.sibling(e_own, e_both.at[mine], e_both.at[other])
    sd_in()
    sd_out[...] = jnp.sum(sd_recv[...].astype(f32), axis=0)
    wo_parts()
    wo_out[...] = jnp.sum(wo_recv[...].astype(f32), axis=0)
    q_parts()
    kv_parts()
    for j in range(KEY_VALUE_HEADS):
        total = wq_recv[j].astype(f32)
        for k in range(1, n):
            total = total + wq_recv[k * KEY_VALUE_HEADS + j].astype(f32)
        wq_out[j] = total
    small_parts()
    small_out[...] = jnp.sum(small_recv[...].astype(f32), axis=0)
    dh_in()
    for core_half in range(2):
        total = dh_recv[core_half * KEY_VALUE_HEADS].astype(f32)
        for j in range(1, KEY_VALUE_HEADS):
            total = total + dh_recv[core_half * KEY_VALUE_HEADS + j].astype(f32)
        dh1_out[core_half] = total
    mix_steps[-1]()
    gu_in()
    e_in()
    e_keep.wait()
    for k, block in enumerate(order):
        send(k, block).wait_send()
    wires.finish()


def finish(
    collective,
    shards,
    chunk,
    gain_col,
    kv_all,
    wo,
    mixed,
    log_rows,
    h1,
    wq,
    gain_row,
    small_grad,
    qkv,
    grad_own,
    gu_half,
    sd_send,
    mix_part,
    mix_terms,
    e_mine,
    e_other,
):
    n, rows, kv_cols = kv_all.shape
    width, wide = wo.shape
    cols = wq.shape[1]
    small = small_grad.shape[1]
    n_in = KEY_VALUE_HEADS
    seg = rows // (2 * n_in)
    w_rows = wide // (2 * shards)
    d_rows = sd_send.shape[1]
    block = mix_part.shape[1:]
    vmem = pl.BlockSpec(memory_space=pltpu.VMEM)
    hbm = pl.BlockSpec(memory_space=pl.ANY)

    def array(shape, kind=bf16):
        return jax.ShapeDtypeStruct(shape, kind)

    e_rows, e_cols = e_mine.shape[1:]
    scratch = [
        ((rows, width), bf16),
        ((2 * n_in, seg, wide), bf16),
        ((rows, width), bf16),
        ((GROUP_MEMBERS, 2, 1, chunk), f32),
        (kv_all.shape, bf16),
        (kv_all.shape, bf16),
        ((rows, kv_cols), f32),
        ((rows, width), f32),
        ((rows, cols), bf16),
        ((width, wide), bf16),
        ((width // 2, wide), bf16),
        ((n, w_rows, wide), bf16),
        ((wide, cols), bf16),
        ((wide // 2, cols), bf16),
        ((shards, w_rows, cols), bf16),
        ((wide, small), bf16),
        ((wide // 2, small), bf16),
        ((shards, w_rows, small), bf16),
        ((rows, wide), bf16),
        ((2 * n_in, seg, wide), bf16),
        ((2 * n_in, d_rows, wide), bf16),
        ((2,) + block, bf16),
        ((2,) + block, bf16),
        ((2,) + block, bf16),
        ((2,) + block, bf16),
        ((2, 2, e_rows, e_cols // 2), bf16),
        ((2, e_rows, e_cols // 2), bf16),
        ((2, e_rows, e_cols // 2), bf16),
        ((e_rows, e_cols), bf16),
    ]
    return pl.pallas_call(
        functools.partial(finish_kernel, shards, chunk, gain_col),
        in_specs=[vmem] * 8 + [hbm] * 9,
        out_specs=[vmem] * 5 + [hbm] * 5,
        out_shape=[
            array((2, seg, wide), f32),
            array((n_in, w_rows, cols), f32),
            array((w_rows, small), f32),
            array((w_rows, wide), f32),
            array((d_rows, wide), f32),
            array(gu_half.shape),
            array(block),
            array(block),
            array((2 * e_rows, e_cols)),
            array(e_mine.shape),
        ],
        scratch_shapes=[pltpu.VMEM(shape, kind) for shape, kind in scratch]
        + [pltpu.SemaphoreType.DMA((6 * shards + 96,))] * 3,
        compiler_params=pltpu.CompilerParams(
            collective_id=collective, has_side_effects=True, vmem_limit_bytes=VMEM_LIMIT
        ),
        name="finish",
    )(
        kv_all,
        wo,
        mixed,
        log_rows,
        h1,
        wq,
        gain_row,
        small_grad,
        qkv,
        grad_own,
        gu_half,
        sd_send,
        mix_part,
        *mix_terms,
        e_mine,
        e_other,
    )


def swiglu_parts(gate_part, up_part):
    sigmoid = jax.nn.sigmoid(gate_part)
    active = gate_part * sigmoid
    slope = up_part * sigmoid * (1.0 + gate_part * (1.0 - sigmoid))
    return active * up_part, active, slope


def experts_kernel(
    room,
    hidden,
    h_ref,
    c_ref,
    meta_ref,
    wg_ref,
    wu_ref,
    wd_ref,
    sgu_ref,
    sd_ref,
    out_ref,
    dh_ref,
    dgate_ref,
    dw_ref,
    dsgu_ref,
    dsd_ref,
    sum_out,
    sum_dh,
    h_rows,
    c_rows,
    picks,
    gate_col,
):
    expert = pl.program_id(0)
    inner = lax.rem(lax.axis_index("fsdp"), KEY_VALUE_HEADS)
    at = across(inner, expert)
    blocks, rows, width = h_ref.shape

    @pl.when(expert == 0)
    def _():
        dgate_ref[...] = jnp.zeros_like(dgate_ref)
        hid = h_ref[...].reshape(blocks * rows, width)
        cot = c_ref[...].reshape(blocks * rows, width)
        gate_w, up_w, down_w = sgu_ref[:, 0:hidden], sgu_ref[:, hidden : 2 * hidden], sd_ref[...]
        both, active, slope = swiglu_parts(nn(hid, gate_w), nn(hid, up_w))
        act = both.astype(bf16)
        d_act = nt(cot, down_w)
        d_gate = (d_act * slope).astype(bf16)
        d_up = (d_act * active).astype(bf16)
        sum_out[...] = nn(act, down_w)
        sum_dh[...] = nt(d_gate, gate_w) + nt(d_up, up_w)
        dsgu_ref[:, 0:hidden] = tn(hid, d_gate).astype(bf16)
        dsgu_ref[:, hidden : 2 * hidden] = tn(hid, d_up).astype(bf16)
        dsd_ref[...] = tn(act, cot).astype(bf16)

    slots = lax.broadcasted_iota(jnp.int32, (room, rows), 0).astype(f32)
    for block in range(blocks):
        part = pl.ds(block * room, room)
        gate_row = meta_ref[block, pl.ds(at, 1), :]
        slot_row = meta_ref[block, pl.ds(at + KEY_VALUE_HEADS, 1), :]
        pick = (slots == slot_row).astype(f32)
        gate_col[part, :] = jnp.broadcast_to(
            jnp.sum(pick * gate_row, axis=1, keepdims=True), (room, gate_col.shape[1])
        )
        pick = pick.astype(bf16)
        picks[block] = pick
        h_rows[part, :] = nn(pick, h_ref[block]).astype(bf16)
        c_rows[part, :] = nn(pick, c_ref[block]).astype(bf16)
    gate = gate_col[:, 0:1]
    gate_w, up_w, down_w = wg_ref[0], wu_ref[0], wd_ref[0]
    both, active, slope = swiglu_parts(nn(h_rows[...], gate_w), nn(h_rows[...], up_w))
    act = both.astype(bf16)
    d_act = nt(c_rows[...], down_w)
    d_gates = jnp.sum(d_act * act.astype(f32), axis=1, keepdims=True)
    d_act = d_act * gate
    act = (act.astype(f32) * gate).astype(bf16)
    d_gate = (d_act * slope).astype(bf16)
    d_up = (d_act * active).astype(bf16)
    ff = act.shape[1]
    dw_ref[0, :, 0:ff] = tn(h_rows[...], d_gate).astype(bf16)
    dw_ref[0, :, ff : 2 * ff] = tn(h_rows[...], d_up).astype(bf16)
    dw_ref[0, :, 2 * ff : 3 * ff] = tn(c_rows[...], act).astype(bf16)
    result = nn(act, down_w).astype(bf16)
    d_rows = (nt(d_gate, gate_w) + nt(d_up, up_w)).astype(bf16)
    for block in range(blocks):
        pick = picks[block]
        part = slice(block * room, (block + 1) * room)
        here = pl.ds(block * rows, rows)
        sum_out[here, :] += tn(pick, result[part])
        sum_dh[here, :] += tn(pick, d_rows[part])
        dgate_ref[block, pl.ds(at, 1), :] = jnp.sum(
            pick.astype(f32) * d_gates[part], axis=0, keepdims=True
        )

    @pl.when(expert == pl.num_programs(0) - 1)
    def _():
        out_ref[...] = sum_out[...].astype(bf16).reshape(out_ref.shape)
        dh_ref[...] = sum_dh[...].astype(bf16).reshape(dh_ref.shape)


def experts(room, hidden, h_all, c_all, meta, wg, wu, wd, sgu, sd):
    blocks, rows, width = h_all.shape
    n_experts, _, inner = wg.shape

    def once(shape):
        return pl.BlockSpec(shape, lambda e: (0,) * len(shape), pipeline_mode=pl.Buffered(1))

    def each(shape, **kind):
        return pl.BlockSpec((1,) + shape[1:], lambda e: (e, 0, 0), **kind)

    single = dict(pipeline_mode=pl.Buffered(1))
    return pl.pallas_call(
        functools.partial(experts_kernel, room, hidden),
        grid=(n_experts,),
        in_specs=[
            once(h_all.shape),
            once(c_all.shape),
            once(meta.shape),
            each(wg.shape),
            each(wu.shape),
            each(wd.shape),
            once(sgu.shape),
            once(sd.shape),
        ],
        out_specs=[
            once(h_all.shape),
            once(h_all.shape),
            once(meta.shape),
            pl.BlockSpec((1, width, 3 * inner), lambda e: (e, 0, 0), **single),
            once(sgu.shape),
            once(sd.shape),
        ],
        out_shape=[
            jax.ShapeDtypeStruct(h_all.shape, bf16),
            jax.ShapeDtypeStruct(h_all.shape, bf16),
            jax.ShapeDtypeStruct(meta.shape, f32),
            jax.ShapeDtypeStruct((n_experts, width, 3 * inner), bf16),
            jax.ShapeDtypeStruct(sgu.shape, bf16),
            jax.ShapeDtypeStruct(sd.shape, bf16),
        ],
        scratch_shapes=[
            pltpu.VMEM((blocks * rows, width), f32),
            pltpu.VMEM((blocks * rows, width), f32),
            pltpu.VMEM((blocks * room, width), bf16),
            pltpu.VMEM((blocks * room, width), bf16),
            pltpu.VMEM((blocks, room, rows), bf16),
            pltpu.VMEM((blocks * room, 128), f32),
        ],
        compiler_params=pltpu.CompilerParams(vmem_limit_bytes=VMEM_LIMIT),
        name="experts",
    )(h_all, c_all, meta, wg, wu, wd, sgu, sd)


def experts_line_kernel(room, hidden, shards, refs):
    n = shards // KEY_VALUE_HEADS
    h_ref, meta_ref = refs[:2]
    c_refs = refs[2 : 1 + 2 * n]
    (
        wg_ref,
        wu_ref,
        wd_ref,
        side_x,
        side_y,
        sgu_ref,
        sd_ref,
        dh_out,
        dgate_out,
        mix_out,
        e_mine,
        e_other,
        gu_mine,
        gu_other,
        dsd_ref,
        h_all,
        c_all,
        metas,
        wgu,
        wd,
        picks,
        kept_gu,
        kept_act,
        kept_shared,
        row_a,
        row_b,
        own_a,
        own_b,
        dh_stage,
        mix_stage,
        dg_stage,
        down_stage,
        gu_stage,
        send_sems,
        recv_sems,
        local_sems,
    ) = refs[1 + 2 * n :]
    wires = Wires(shards, send_sems, recv_sems, local_sems)
    core, chip, outer, inner = place()
    rows, width = h_ref.shape
    ff = wd.shape[1]
    experts_here = KEY_VALUE_HEADS

    own_h = wires.local(h_ref, h_all.at[outer], wires.take(1))
    own_meta = wires.local(meta_ref.at[outer], metas.at[outer], wires.take(1))
    own_h.start()
    own_meta.start()
    c_own = wires.local(c_refs[0], c_all.at[outer], wires.take(1))
    c_base = wires.take(2 * n - 2)

    def c_each(action):
        for k in range(2 * n - 2):
            block = outer - 1 - k if k < n - 1 else outer + 1 + k - (n - 1)

            def one(k=k, block=block):
                at = lax.rem(block + n, n)
                action(wires.local(c_refs[1 + k], c_all.at[at], c_base + k))

            pl.when((block >= 0) & (block < n))(one)

    deep, tall = ff // 2, width // 2
    own_weights = (
        wires.local(wg_ref.at[0], wgu.at[0, :, pl.ds(0, ff)], wires.take(1)),
        wires.local(wu_ref.at[0], wgu.at[0, :, pl.ds(ff, ff)], wires.take(1)),
        wires.local(wd_ref.at[0], wd.at[0], wires.take(1)),
    )

    def half_places(e, first_col, cols, of_core):
        found = [
            wgu.at[e, pl.ds(of_core * tall, tall), pl.ds(k * ff + first_col, cols)]
            for k in range(2)
        ]
        found += [
            wd.at[e, pl.ds(of_core * deep, deep), pl.ds(k * ff + first_col, cols)]
            for k in range(width // ff)
        ]
        return found

    def half_sources(source, first_col, cols):
        starts = [(k * tall, tall) for k in range(2)]
        starts += [(2 * tall + k * deep, deep) for k in range(width // ff)]
        return [source.at[pl.ds(at, size), pl.ds(first_col, cols)] for at, size in starts]

    per_half = 2 + width // ff
    sides = ((1, side_x, 0, ff), (2, side_y, 0, ff), (3, side_x, 0, ff // 2), (3, side_y, ff // 2, ff // 2))
    half_sems = [wires.take(per_half) for _ in sides]
    cross_sems = [wires.take(per_half) for _ in range(2)]

    def half_local(which):
        e, source, first_col, cols = sides[which]
        return [
            wires.local(here, there, half_sems[which] + k)
            for k, (here, there) in enumerate(
                zip(half_sources(source, first_col, cols), half_places(e, first_col, cols, core))
            )
        ]

    def half_remote(which, of_core):
        e, source, first_col, cols = sides[which]
        places = half_places(e, first_col, cols, of_core)
        here = half_sources(source, first_col, cols) if which < 2 else places
        return [
            wires.remote(here[k], places[k], half_sems[which] + k, (1 - core, chip))
            for k in range(per_half)
        ]

    def cross_remote(which):
        _, source, first_col, cols = sides[2 + which]
        return [
            wires.remote(
                here,
                there,
                cross_sems[which] + k,
                (core, outer * KEY_VALUE_HEADS + across(inner, 2 - which)),
            )
            for k, (here, there) in enumerate(
                zip(half_sources(source, first_col, cols), half_places(3, first_col, cols, core))
            )
        ]

    c_own.start()
    for copy in own_weights:
        copy.start()
    for which in range(2):
        for copy in half_local(which):
            copy.start()
    c_each(lambda copy: copy.start())

    wires.greet(["outer", "plane"])

    line = Line(wires, h_ref, h_all)
    device = line.device
    line.start(0)
    for which in range(2):
        for copy in cross_remote(which):
            copy.start()
    for which in range(2):
        for copy in half_remote(which, core):
            copy.start()
    meta_in = wires.exchange(
        "outer", lambda r, d: meta_ref.at[r], lambda r, d: metas.at[r], own=False
    )

    dh_send, dh_recv = wires.take(n), wires.take(n)
    dg_send, dg_recv = wires.take(n), wires.take(n)

    def give_back(stage, target, k, block, sends, receives):
        return pltpu.make_async_remote_copy(
            src_ref=stage,
            dst_ref=target.at[outer],
            send_sem=send_sems.at[sends + k],
            recv_sem=recv_sems.at[receives + outer],
            device_id=device(block),
            device_id_type=MESH,
        )

    def take_back(target, origin, receives):
        return pltpu.make_async_remote_copy(
            src_ref=target.at[origin],
            dst_ref=target.at[origin],
            send_sem=send_sems.at[receives],
            recv_sem=recv_sems.at[receives + origin],
            device_id=device(origin),
            device_id_type=MESH,
        )

    dh_own = wires.local(dh_stage.at[n - 1], dh_out.at[outer], wires.take(1))
    dg_own = wires.local(dg_stage.at[n - 1], dgate_out.at[outer], wires.take(1))
    mix_base = wires.take(n)

    def mix_copy(k, block):
        return wires.local(
            mix_stage.at[k % 2], mix_out.at[lax.rem(outer - block + n, n)], mix_base + k
        )

    slots = lax.broadcasted_iota(jnp.int32, (room, rows), 0).astype(f32)
    order = line.order()
    gate_w, up_w, down_w = sgu_ref[:, 0:hidden], sgu_ref[:, hidden : 2 * hidden], sd_ref[...]

    def choose(k, block, left, right):
        for e in range(experts_here):
            at = across(inner, e)
            slot_row = metas[block, pl.ds(at + experts_here, 1), :]
            picks[block, pl.ds(e * room, room), :] = (slots == slot_row).astype(bf16)
        left[...] = nn(picks[block], h_all[block]).astype(bf16)
        right[...] = nn(picks[block], c_all[block]).astype(bf16)
        dg_stage[k] = jnp.zeros(dg_stage.shape[1:], f32)

    def one_expert(e, k, block, left, right):
        at = across(inner, e)
        part = pl.ds(pl.multiple_of(e * room, 16), room)
        pick = picks[block, part, :].astype(f32)
        gate = jnp.sum(pick * metas[block, pl.ds(at, 1), :], axis=1, keepdims=True)
        first = nn(left[part, :], wgu[e])
        both, active, slope = swiglu_parts(first[:, 0:ff], first[:, ff : 2 * ff])
        act = both.astype(bf16)
        d_act = nt(right[part, :], wd[e])
        d_gates = jnp.sum(d_act * act.astype(f32), axis=1, keepdims=True)
        dg_stage[k, pl.ds(at, 1), :] = jnp.sum(pick * d_gates, axis=0, keepdims=True)
        d_act = d_act * gate
        act = (act.astype(f32) * gate).astype(bf16)
        here = pl.ds(pl.multiple_of(block * room, 16), room)
        kept_act[e, here, :] = act
        kept_gu[e, here, 0:ff] = (d_act * slope).astype(bf16)
        kept_gu[e, here, ff : 2 * ff] = (d_act * active).astype(bf16)
        left[part, :] = nn(act, wd[e]).astype(bf16)
        right[part, :] = nt(kept_gu[e, here, :], wgu[e]).astype(bf16)

    def some_experts(begin, end, k, block, left, right):
        def one(e, carry):
            one_expert(e, k, block, left, right)
            return carry

        lax.fori_loop(begin, end, one, 0)

    order = order[1:] + order[:1]
    last = n - 1
    own_h.wait()
    own_meta.wait()
    c_own.wait()
    choose(last, outer, own_a, own_b)
    for copy in own_weights:
        copy.wait()
    one_expert(0, last, outer, own_a, own_b)
    for which in range(2):
        for copy in half_local(which):
            copy.wait()
        for copy in half_remote(which, 1 - core):
            copy.wait_recv()
    some_experts(1, experts_here - 1, last, outer, own_a, own_b)

    for k, block in enumerate(order):
        if k < last:
            line.arrive(k)
            if k < last - 1:
                line.start(k + 1)
        if k == 0:
            meta_in()
            c_each(lambda copy: copy.wait())
        left, right = (row_a, row_b) if k < last else (own_a, own_b)
        hid, cot = h_all[block], c_all[block]
        if k < last:
            choose(k, block, left, right)
        if k == 0:
            some_experts(0, experts_here - 1, k, block, left, right)
            for which in range(2):
                for copy in cross_remote(which):
                    copy.wait_recv()
                for copy in half_remote(2 + which, core):
                    copy.start()
            for which in range(2):
                for copy in half_remote(2 + which, 1 - core):
                    copy.wait_recv()
            some_experts(experts_here - 1, experts_here, k, block, left, right)
        elif k < last:
            some_experts(0, experts_here, k, block, left, right)
        else:
            some_experts(experts_here - 1, experts_here, k, block, left, right)
        both, active, slope = swiglu_parts(nn(hid, gate_w), nn(hid, up_w))
        act = both.astype(bf16)
        d_act = nt(cot, down_w)
        d_gate = (d_act * slope).astype(bf16)
        d_up = (d_act * active).astype(bf16)
        kept_shared[block, :, 0:hidden] = d_gate
        kept_shared[block, :, hidden : 2 * hidden] = d_up
        kept_shared[block, :, 2 * hidden : 3 * hidden] = act
        dh_stage[k] = (
            tn(picks[block], right[...]) + nt(d_gate, gate_w) + nt(d_up, up_w)
        ).astype(bf16)
        if k == n - 1:
            dh_own.start()
            dg_own.start()
        else:
            give_back(dh_stage.at[k], dh_out, k, block, dh_send, dh_recv).start()
            give_back(dg_stage.at[k], dgate_out, k, block, dg_send, dg_recv).start()
        if k >= 2:
            mix_copy(k - 2, order[k - 2]).wait()
        mix_stage[k % 2] = (tn(picks[block], left[...]) + nn(act, down_w)).astype(bf16)
        mix_copy(k, block).start()

    half = width // 2
    mine, other = pl.ds(core * half, half), pl.ds((1 - core) * half, half)
    sibling = (1 - core, chip)
    left, right = pl.ds(0, 2 * ff), pl.ds(2 * ff, ff)
    keep_base, give_base = wires.take(2 * experts_here + 1), wires.take(2 * experts_here + 1)

    def keep(e):
        return (
            wires.local(wgu.at[e, mine, :], e_mine.at[e, :, left], keep_base + 2 * e),
            wires.local(down_stage.at[e % 2, mine, :], e_mine.at[e, :, right], keep_base + 2 * e + 1),
        )

    def give(e):
        return (
            wires.remote(wgu.at[e, other, :], e_other.at[e, :, left], give_base + 2 * e, sibling),
            wires.remote(
                down_stage.at[e % 2, other, :],
                e_other.at[e, :, right],
                give_base + 2 * e + 1,
                sibling,
            ),
        )

    for which in (2, 3):
        for copy in half_remote(which, core):
            copy.wait_send()
    for e in range(experts_here):
        for block in range(n):
            part = pl.ds(block * room, room)
            pick = picks[block, pl.ds(e * room, room), :]
            row_a[part, :] = nn(pick, h_all[block]).astype(bf16)
            row_b[part, :] = nn(pick, c_all[block]).astype(bf16)
        wgu[e] = tn(row_a[...], kept_gu[e]).astype(bf16)
        if e >= 2:
            keep(e - 2)[1].wait()
            give(e - 2)[1].wait_send()
        down_stage[e % 2] = tn(row_b[...], kept_act[e]).astype(bf16)
        for copy in keep(e) + give(e):
            copy.start()
    hid_all = h_all[...].reshape(n * rows, width)
    shared = kept_shared[...].reshape(n * rows, 3 * hidden)
    gu_stage[...] = tn(hid_all, shared[:, 0 : 2 * hidden]).astype(bf16)
    gu_keep = wires.local(gu_stage.at[mine, :], gu_mine, keep_base + 2 * experts_here)
    gu_give = wires.remote(gu_stage.at[other, :], gu_other, give_base + 2 * experts_here, sibling)
    gu_keep.start()
    gu_give.start()
    dsd_ref[...] = tn(shared[:, 2 * hidden :], c_all[...].reshape(n * rows, width)).astype(bf16)

    def settle(e):
        for which, (kept, given) in enumerate(zip(keep(e), give(e))):
            if which == 0 or e >= experts_here - 2:
                kept.wait()
                given.wait_send()
            given.wait_recv()

    line.leave()
    for e in range(experts_here):
        settle(e)

    for which in range(2):
        for copy in half_remote(which, core):
            copy.wait_send()
    for which in range(2):
        for copy in cross_remote(which):
            copy.wait_send()
    dh_own.wait()
    dg_own.wait()
    for k in range(max(0, n - 2), n):
        mix_copy(k, order[k]).wait()
    for k in range(n - 1):
        give_back(dh_stage.at[k], dh_out, k, order[k], dh_send, dh_recv).wait_send()
        give_back(dg_stage.at[k], dgate_out, k, order[k], dg_send, dg_recv).wait_send()
    for d in range(1, n):
        origin = lax.rem(outer + d, n)
        take_back(dh_out, origin, dh_recv).wait_recv()
        take_back(dgate_out, origin, dg_recv).wait_recv()
    gu_keep.wait()
    gu_give.wait()
    wires.finish()


def experts_line(room, hidden, shards, collective, h_own, meta, c_parts, weights, sides, sgu, sd):
    n = shards // KEY_VALUE_HEADS
    rows, width = h_own.shape
    n_experts, ff = KEY_VALUE_HEADS, weights[0].shape[2]
    half = width // 2
    any_spec = pl.BlockSpec(memory_space=pl.ANY)
    vmem = pl.BlockSpec(memory_space=pltpu.VMEM)
    e_shape = (n_experts, half, 3 * ff)
    sems = 112 + 24 * n

    def kernel(*refs):
        experts_line_kernel(room, hidden, shards, refs)

    return pl.pallas_call(
        kernel,
        in_specs=[any_spec] * (2 + len(c_parts) + 3 + len(sides)) + [vmem] * 2,
        out_specs=[any_spec] * 7 + [vmem],
        out_shape=[
            jax.ShapeDtypeStruct((n, rows, width), bf16),
            jax.ShapeDtypeStruct(meta.shape, f32),
            jax.ShapeDtypeStruct((n, rows, width), bf16),
            jax.ShapeDtypeStruct(e_shape, bf16),
            jax.ShapeDtypeStruct(e_shape, bf16),
            jax.ShapeDtypeStruct((half, 2 * hidden), bf16),
            jax.ShapeDtypeStruct((half, 2 * hidden), bf16),
            jax.ShapeDtypeStruct(sd.shape, bf16),
        ],
        scratch_shapes=[
            pltpu.VMEM((n, rows, width), bf16),
            pltpu.VMEM((n, rows, width), bf16),
            pltpu.VMEM(meta.shape, f32),
            pltpu.VMEM((n_experts, width, 2 * ff), bf16),
            pltpu.VMEM((n_experts, ff, width), bf16),
            pltpu.VMEM((n, n_experts * room, rows), bf16),
            pltpu.VMEM((n_experts, n * room, 2 * ff), bf16),
            pltpu.VMEM((n_experts, n * room, ff), bf16),
            pltpu.VMEM((n, rows, 3 * hidden), bf16),
            pltpu.VMEM((n * room, width), bf16),
            pltpu.VMEM((n * room, width), bf16),
            pltpu.VMEM((n * room, width), bf16),
            pltpu.VMEM((n * room, width), bf16),
            pltpu.VMEM((n, rows, width), bf16),
            pltpu.VMEM((2, rows, width), bf16),
            pltpu.VMEM((n,) + meta.shape[1:], f32),
            pltpu.VMEM((2, width, ff), bf16),
            pltpu.VMEM((width, 2 * hidden), bf16),
        ]
        + [pltpu.SemaphoreType.DMA((sems,))] * 3,
        compiler_params=pltpu.CompilerParams(
            collective_id=collective, has_side_effects=True, vmem_limit_bytes=VMEM_LIMIT
        ),
        name="experts_line",
    )(h_own, meta, *c_parts, *weights, *sides, sgu, sd)


def experts_split(room, hidden, shards, collectives, h_own, meta, c_parts, weights, sides, sgu, sd):
    n_out, n_in = shards // KEY_VALUE_HEADS, KEY_VALUE_HEADS
    rows, width = h_own.shape
    core = lax.axis_index("seq")
    half = width // 2

    def spread_hidden(wires, ins, outs):
        waits = [
            wires.exchange("outer", lambda r, d: ins[0], lambda r, d: outs[0].at[d]),
            wires.exchange("outer", lambda r, d: ins[1].at[r], lambda r, d: outs[1].at[d]),
        ]
        waits += [
            wires.exchange(
                "inner",
                lambda r, d, k=k: ins[k].at[0],
                lambda r, d, k=k: outs[k].at[across(r, lax.rem(r + d, n_in))],
            )
            for k in range(2, 5)
        ]
        for wait in waits:
            wait()

    h_all, meta_all, wg, wu, wd = transfer(
        "spread_hidden",
        collectives[0],
        shards,
        ["outer", "inner"],
        2 * n_out + 3 * n_in,
        spread_hidden,
        [h_own, meta, *weights],
        [((n_out, rows, width), bf16), (meta.shape, f32)]
        + [((n_in,) + weight.shape[1:], bf16) for weight in weights],
    )
    c_all = jnp.stack(c_parts)
    at_once = math.gcd(n_out, 4)
    parts = [
        experts(
            room,
            hidden,
            h_all[i : i + at_once],
            c_all[i : i + at_once],
            meta_all[i : i + at_once],
            wg,
            wu,
            wd,
            sgu,
            sd,
        )
        for i in range(0, n_out, at_once)
    ]
    mix_part, dh_part, dgate_part = (
        jnp.concatenate([part[k] for part in parts], axis=0) for k in range(3)
    )
    e_grad, sgu_grad, sd_grad = (
        sum(part[k].astype(f32) for part in parts).astype(bf16) for k in range(3, 6)
    )

    def sum_hidden(wires, ins, outs):
        core = lax.axis_index("seq")
        dh_ref, dg_ref, e_ref, gu_ref = ins
        dhs, dgs, es, gus = outs
        other = pl.ds((1 - core) * half, half)
        waits = [
            wires.exchange(
                "outer", lambda r, d: dh_ref.at[(n_out - d) % n_out], lambda r, d: dhs.at[r]
            ),
            wires.exchange(
                "outer", lambda r, d: dg_ref.at[(n_out - d) % n_out], lambda r, d: dgs.at[r]
            ),
            wires.sibling(e_ref.at[:, other], es, es),
            wires.sibling(gu_ref.at[other], gus, gus),
        ]
        for wait in waits:
            wait()

    dhs, dgs, es, gus = transfer(
        "sum_hidden",
        collectives[1],
        shards,
        ["outer", "core"],
        2 * n_out + 8,
        sum_hidden,
        [dh_part, dgate_part, e_grad, sgu_grad],
        [
            ((n_out, rows, width), bf16),
            (meta.shape, f32),
            ((n_in, half, e_grad.shape[2]), bf16),
            ((half, 2 * hidden), bf16),
        ],
    )
    e_mine = lax.dynamic_slice_in_dim(e_grad, core * half, half, 1)
    gu_mine = lax.dynamic_slice_in_dim(sgu_grad, core * half, half, 0)
    return dhs, dgs, mix_part, e_mine, es, gu_mine, gus, sd_grad


def norm_rows(values, gain_vector):
    inverse = lax.rsqrt(jnp.mean(values * values, axis=-1, keepdims=True) + epsilon)
    normed = values * inverse
    return (normed, inverse, normed * gain_vector)


def norm_back(grad_hidden, normed, inverse, gain_vector):
    grad_normed = grad_hidden * gain_vector
    gain_grad = jnp.sum(grad_hidden * normed, axis=(0, 1))
    inner_mean = jnp.mean(grad_normed * normed, axis=-1, keepdims=True)
    return (inverse * (grad_normed - normed * inner_mean), gain_grad)


def pad_rows(array, axis):
    size = array.shape[axis]
    widths = [(0, 0)] * array.ndim
    widths[axis] = (0, round_up(size, 16) - size)
    return jnp.pad(array, widths) if widths[axis][1] else array


def pad_to(array, axis, size):
    widths = [(0, 0)] * array.ndim
    widths[axis] = (0, size - array.shape[axis])
    return jnp.pad(array, widths) if widths[axis][1] else array


def body(
    tokens,
    routes,
    out_grad,
    attn_gain,
    ffn_gain,
    query_projection,
    key_projection,
    value_projection,
    w_out,
    w_router,
    shared_gate,
    shared_up,
    shared_down,
    expert_gate,
    expert_up,
    expert_down,
):
    shards = lax.axis_size("fsdp")
    n_in = KEY_VALUE_HEADS
    n_out = shards // n_in
    core, chip, outer, inner = place()
    seg, seqs, width = tokens.shape
    rows = seg * seqs
    topk = routes.shape[2]
    n_experts = w_router.shape[1]
    w_rows = query_projection.shape[0]
    w_pad = round_up(w_rows, 16)
    d_rows = shared_down.shape[0]
    d_pad = round_up(d_rows, 16)
    half_chips = shards // 2
    q_cols = GROUP_MEMBERS * HEAD_SIZE
    cols = q_cols + 2 * HEAD_SIZE
    ff = expert_gate.shape[2]
    hid_core = n_in * d_rows
    hid = 2 * hid_core
    hid_pad = round_up(hid, 128)
    small = round_up(n_experts + 2, 128)
    chunk = n_in * seg
    half_width, half_ff = width // 2, ff // 2
    room = round_up(max(2, (3 * rows * topk + 2 * n_experts - 1) // (2 * n_experts)), 16)

    small_piece = pad_to(
        jnp.concatenate([w_router, attn_gain[:, None], ffn_gain[:, None]], axis=1), 1, small
    )
    q_pieces = pad_rows(
        jnp.concatenate(
            [
                query_projection.reshape(w_rows, n_in, q_cols),
                key_projection.reshape(w_rows, n_in, HEAD_SIZE),
                value_projection.reshape(w_rows, n_in, HEAD_SIZE),
                jnp.broadcast_to(small_piece[:, None], (w_rows, n_in, small)),
            ],
            axis=2,
        ).transpose(1, 0, 2),
        1,
    )

    def hidden_piece(weight):
        piece = weight.reshape(w_rows, 2, n_out, hid_core).transpose(2, 0, 1, 3)
        return pad_to(piece.reshape(n_out, w_rows, hid), 2, hid_pad)

    gu_pieces = pad_rows(
        jnp.concatenate([hidden_piece(shared_gate), hidden_piece(shared_up)], axis=2), 1
    )
    out_piece = pad_rows(w_out, 0)
    down_piece = pad_rows(shared_down, 0)
    x_own = tokens.transpose(1, 0, 2)
    c_own = out_grad.transpose(1, 0, 2)
    cot = c_own.reshape(rows, width)

    def shift(block, amount):
        return lax.ppermute(
            block, "fsdp", [(f, (f + amount * n_in) % shards) for f in range(shards)]
        )

    def swap(block, step):
        return lax.ppermute(
            block, "fsdp", [(f, f // n_in * n_in + (f % n_in ^ step)) for f in range(shards)]
        )

    def out_rows(wires, o_ref, wo_ref):
        core, chip, outer, inner = place()
        to_inner = 2 * core + chip // half_chips
        slot = lax.rem(chip, half_chips)
        base = wires.take(half_chips)
        sends = wires.take(n_out)
        across_core = wires.take(1)
        first = inner // 2 == core

        def copy(k):
            to = (core, k * n_in + to_inner)
            return to[1] == chip, pltpu.make_async_remote_copy(
                src_ref=o_ref,
                dst_ref=wo_ref.at[slot],
                send_sem=wires.send_sems.at[sends + k],
                recv_sem=wires.recv_sems.at[base + slot],
                device_id=to,
                device_id_type=MESH,
            )

        def start(k):
            here, send = copy(k)
            pl.when(jnp.logical_not(here))(send.start)
            pl.when(here)(lambda: wires.local(o_ref, wo_ref.at[slot], base).start())

        def leave(k):
            here, send = copy(k)
            pl.when(jnp.logical_not(here))(send.wait_send)

        def come(i):
            origin = (core, half_chips * lax.rem(inner, 2) + i)
            here = origin[1] == chip
            place_of = wo_ref.at[i]
            pl.when(jnp.logical_not(here))(
                wires.remote(place_of, place_of, base + i, origin).wait_recv
            )
            pl.when(here)(lambda: wires.local(o_ref, place_of, base).wait())

        def hand_on():
            return wires.remote(wo_ref, wo_ref, across_core, (1 - core, chip))

        def arrive():
            @pl.when(first)
            def _():
                repeat(0, half_chips, come)
                hand_on().start()

        def settle():
            @pl.when(first)
            def _():
                hand_on().wait_send()

            @pl.when(jnp.logical_not(first))
            def _():
                hand_on().wait_recv()

        repeat(0, n_out, start)
        wires.leaving.append(lambda: repeat(0, n_out, leave))
        return arrive, settle

    own_rows = half_chips // 2
    line = n_out == 4

    def fetch(wires, ins, outs):
        x_ref, q_ref, o_ref = ins
        xs_ref, wq_ref, wo_ref = outs
        core = lax.axis_index("seq")
        q_in = wires.exchange(
            "chips", lambda r, d: q_ref.at[lax.rem(r, n_in)], lambda r, d: wq_ref.at[core, r]
        )
        x_in = wires.exchange("plane", lambda r, d: x_ref.at[r // n_in], lambda r, d: xs_ref.at[r])
        o_in, o_settle = out_rows(wires, o_ref, wo_ref)
        q_in()
        q_other = wires.sibling(wq_ref.at[core], wq_ref.at[core], wq_ref.at[1 - core])
        o_in()
        x_in()
        q_other()
        o_settle()

    down_half = lax.dynamic_slice_in_dim(expert_down[0], core * half_ff, half_ff, 0)
    expert_half = jnp.concatenate(
        [
            lax.dynamic_slice_in_dim(expert_gate[0], core * half_width, half_width, 0),
            lax.dynamic_slice_in_dim(expert_up[0], core * half_width, half_width, 0),
        ]
        + [down_half[:, k : k + ff] for k in range(0, width, ff)],
        axis=0,
    )
    if line:
        mixed, log_rows, kv_all, out_sum, h1, qkv, sgu, ws, wq, wo, side_x, side_y, *c_came = attend(
            1,
            shards,
            chunk,
            (x_own, q_pieces, out_piece, cot, expert_half, gu_pieces, down_piece),
            n_experts,
            out_rows,
        )
        c_parts = [cot] + c_came[0::2] + c_came[1::2]
    else:
        xs, wq, wo = transfer(
            "fetch",
            0,
            shards,
            ["all"],
            4 * shards + 16,
            fetch,
            [x_own, q_pieces, out_piece],
            [
                ((2 * n_in, seg, width), bf16),
                ((2, shards, w_pad, cols + small), bf16),
                ((half_chips, w_pad, width), bf16),
            ],
        )
        side_x = side_y = expert_half
    wq = wq[:, :, :w_rows].reshape(width, cols + small)
    wo = wo[:, :w_rows].reshape(q_cols, width)
    wq, small_w = wq[:, :cols], wq[:, cols:]
    router_w = small_w[:, :n_experts]
    gain_one = small_w[:, n_experts].astype(f32)
    gain_two = small_w[:, n_experts + 1].astype(f32)

    inputs = x_own.astype(f32)
    if line:
        residual = inputs + out_sum
    else:
        h1 = norm_rows(xs.reshape(2 * chunk, width).astype(f32), gain_one)[2].astype(bf16)
        qkv = nn(h1, wq).astype(bf16)
        mixed, log_rows, kv_all = attend(1, shards, chunk, (qkv,))
        mixed_low = mixed.astype(bf16)
        out_part = nn(mixed_low, wo).astype(bf16).reshape(2 * n_in, seg, width)

        def sum_out(wires, ins, outs):
            part_ref, gu_ref, s_ref = ins
            parts_ref, wgu_ref, ws_ref = outs
            gu_in, gu_settle, s_in, s_settle = spread_shared(wires, gu_ref, s_ref, wgu_ref, ws_ref)
            part_in = wires.exchange(
                "plane", lambda r, d: part_ref.at[r], lambda r, d: parts_ref.at[r]
            )
            gu_in()
            gu_settle.start()
            s_in()
            s_settle.start()
            part_in()
            gu_settle.wait()
            s_settle.wait()

        out_parts, sgu, ws = transfer(
            "sum_out",
            2,
            shards,
            ["all"],
            shards + 8 * n_in + 16,
            sum_out,
            [out_part, gu_pieces, down_piece],
            [
                ((2 * n_in, seg, width), bf16),
                ((2, shards, w_pad, 2 * hid_pad), bf16),
                ((2, n_in, d_pad, width), bf16),
            ],
        )
        c_parts = [cot] + [shift(cot, d) for d in range(1, n_out)]
        residual = inputs + jnp.sum(out_parts.astype(f32).reshape(2, n_in, seg, width), axis=1)
    sgu = sgu[:, :, :w_rows].reshape(width, 2 * hid_pad)
    ws = pad_to(ws[:, :, :d_rows].reshape(hid, width), 0, hid_pad)

    normed_two, inverse_two, scaled_two = norm_rows(residual, gain_two)
    hidden_two = scaled_two.astype(bf16).reshape(rows, width)
    logits = nn(hidden_two, router_w)
    flat_routes = routes.transpose(1, 0, 2).reshape(rows, topk)
    chooser = (flat_routes[:, :, None] == jnp.arange(n_experts, dtype=jnp.int32)).astype(f32)
    taken = jnp.sum(chooser, axis=1)
    chosen = jnp.where(taken > 0, logits, masked_score)
    exponent = jnp.where(
        taken > 0, jnp.exp(chosen - jnp.max(chosen, axis=-1, keepdims=True)), 0.0
    )
    gates = exponent / jnp.sum(exponent, axis=-1, keepdims=True)
    before = (
        lax.broadcasted_iota(jnp.int32, (rows, rows), 0)
        < lax.broadcasted_iota(jnp.int32, (rows, rows), 1)
    ).astype(bf16)
    slots = jnp.where(taken.T > 0, nn(taken.T.astype(bf16), before), -1.0)
    meta = jnp.concatenate(
        [gates.T.reshape(n_out, n_in, rows), slots.reshape(n_out, n_in, rows)], axis=1
    )

    run = functools.partial(experts_line if line else experts_split, room, hid_pad, shards)
    dhs, dgs, mix_part, e_mine, e_other, gu_mine, gus, sd_grad = run(
        3 if line else (3, 4),
        hidden_two,
        meta,
        c_parts,
        (expert_gate, expert_up, expert_down),
        (side_x, side_y),
        sgu,
        ws,
    )

    gu_half = (gu_mine.astype(f32) + gus.astype(f32)).astype(bf16)
    gu_half = pad_rows(gu_half.reshape(shards, w_rows, 2 * hid_pad), 1)
    sd_send = pad_rows(sd_grad[:hid].reshape(2 * n_in, d_rows, width), 1)

    grad_float = c_own.astype(f32)
    grad_gates = dgs[:, :n_in].reshape(n_experts, rows).T
    grad_logits = gates * (grad_gates - jnp.sum(gates * grad_gates, axis=-1, keepdims=True))
    router_grad = lax.dot_general(
        hidden_two.astype(f32),
        grad_logits,
        (((0,), (0,)), ((), ())),
        precision=lax.Precision.HIGHEST,
        preferred_element_type=f32,
    )
    grad_hidden_two = jnp.sum(dhs.astype(f32), axis=0) + lax.dot_general(
        grad_logits,
        router_w.astype(f32),
        (((1,), (1,)), ((), ())),
        precision=lax.Precision.HIGHEST,
        preferred_element_type=f32,
    )
    grad_norm_two, gain_two_grad = norm_back(
        grad_hidden_two.reshape(seqs, seg, width), normed_two, inverse_two, gain_two
    )
    grad_residual = grad_float + grad_norm_two
    grad_attn = grad_residual.astype(bf16)

    small_grad = pad_to(
        jnp.concatenate(
            [router_grad, jnp.zeros((width, 1), f32), gain_two_grad[:, None]], axis=1
        ),
        1,
        small,
    )
    if line:
        grad_hidden_one, wq_total, small_total, out_w_grad, down_w_grad, gus, *rest = finish(
            6,
            shards,
            chunk,
            n_experts,
            kv_all,
            wo,
            mixed,
            log_rows,
            h1,
            wq,
            gain_one[None],
            small_grad.astype(bf16),
            qkv,
            grad_attn,
            gu_half,
            sd_send,
            mix_part,
            (mix_part[1 % n_out], mix_part[(n_out - 1) % n_out]),
            e_mine,
            e_other,
        )
        *mix_third, e_total, _ = rest
        mixes = [mix_part[0].astype(f32)] + [
            jnp.where(inside, came.astype(f32), 0.0)
            for inside, came in zip((outer > 0, outer < n_out - 1), mix_third)
        ]
    else:
        mixes = [mix_part[0].astype(f32)] + [
            shift(mix_part[n_out - d], d).astype(f32) for d in range(1, n_out)
        ]

        def spread_grad(wires, ins, outs):
            second = wires.exchange("chips", lambda r, d: ins[1].at[r], lambda r, d: outs[1].at[r])
            first = wires.exchange(
                "plane", lambda r, d: ins[0].at[r // n_in], lambda r, d: outs[0].at[r]
            )
            first()
            second()

        grad_all, gus = transfer(
            "spread_grad",
            5,
            shards,
            ["all"],
            shards + 2 * n_in + 16,
            spread_grad,
            [grad_attn, gu_half],
            [((2 * n_in, seg, width), bf16), ((shards, w_pad, 2 * hid_pad), bf16)],
        )
        grad_all = grad_all.reshape(2 * chunk, width)
        e_sum = (e_mine.astype(f32) + e_other.astype(f32)).astype(bf16)
        grad_mixed = nt(grad_all, wo).astype(bf16)
        wo_grad = tn(mixed_low, grad_all).astype(bf16).reshape(half_chips, w_rows, width)
        wo_grad = pad_rows(wo_grad, 1)
        delta_rows = jnp.sum(
            (grad_mixed.astype(f32) * mixed).reshape(2, chunk, GROUP_MEMBERS, HEAD_SIZE), axis=-1
        ).transpose(2, 0, 1)
        dqkv, wos = attend_back(
            6,
            shards,
            chunk,
            qkv[:, :q_cols],
            kv_all,
            grad_mixed,
            log_rows,
            delta_rows,
            wo_grad,
        )
        wo_mine = lax.dynamic_slice_in_dim(wo_grad, core * own_rows, own_rows, 0)
        wo_half = (wo_mine.astype(f32) + wos.astype(f32)).astype(bf16)
        dh1_part = nt(dqkv, wq).astype(bf16).reshape(2 * n_in, seg, width)
        wq_send = pad_rows(tn(h1, dqkv).astype(bf16).reshape(2 * shards, w_rows, cols), 1)
        gain_one_grad = (
            jnp.sum(
                dh1_part.reshape(2 * chunk, width).astype(f32) * h1.astype(f32), axis=0
            )
            / gain_one
        )
        small_grad = small_grad.at[:, n_experts].set(gain_one_grad)
        small_send = pad_rows(small_grad.astype(bf16).reshape(2 * shards, w_rows, small), 1)

        def sum_first(wires, ins, outs):
            dh_ref, wq_ref, small_ref, s_ref, o_ref = ins
            dhs, wqs, smalls, sds, wos = outs
            waits = [
                out_rows_back(wires, shards, o_ref, wos),
                wires.exchange("all", lambda r, d: wq_ref.at[r], lambda r, d: wqs.at[r]),
                wires.exchange("plane", lambda r, d: dh_ref.at[r], lambda r, d: dhs.at[r]),
                wires.exchange("all", lambda r, d: small_ref.at[r], lambda r, d: smalls.at[r]),
                wires.exchange("plane", lambda r, d: s_ref.at[r], lambda r, d: sds.at[r]),
            ]
            for wait in waits:
                wait()

        dh1s, wq_parts, small_parts, sds, wos = transfer(
            "sum_first",
            7,
            shards,
            ["all"],
            4 * n_in + 6 * shards + 16,
            sum_first,
            [dh1_part, wq_send, small_send, sd_send, wo_half.reshape(own_rows * w_pad, width)],
            [
                ((2 * n_in, seg, width), bf16),
                ((2 * shards, w_pad, cols), bf16),
                ((2 * shards, w_pad, small), bf16),
                ((2 * n_in, d_pad, width), bf16),
                ((n_out, w_pad, width), bf16),
            ],
        )
        grad_hidden_one = jnp.sum(dh1s.astype(f32).reshape(2, n_in, seg, width), axis=1)
        wq_total = jnp.sum(
            wq_parts[:, :w_rows].astype(f32).reshape(2 * n_out, n_in, w_rows, cols), axis=0
        )
        down_w_grad = jnp.sum(sds[:, :d_rows].astype(f32), axis=0)
        out_w_grad = jnp.sum(wos[:, :w_rows].astype(f32), axis=0)
        small_total = jnp.sum(small_parts[:, :w_rows].astype(f32), axis=0)
        e_parts = [swap(e_sum[e], e) for e in range(1, n_in)]
        e_total = sum([part.astype(f32) for part in e_parts], e_sum[0].astype(f32)).astype(bf16)
        e_came = lax.ppermute(e_total, "seq", [(0, 1), (1, 0)])
        e_total = jnp.where(
            core == 0,
            jnp.concatenate([e_total, e_came], axis=0),
            jnp.concatenate([e_came, e_total], axis=0),
        )
    total_out = residual + sum(mixes).reshape(seqs, seg, width)
    normed_one, inverse_one, _ = norm_rows(inputs, gain_one)
    grad_norm_one = norm_back(grad_hidden_one, normed_one, inverse_one, gain_one)[0]
    tokens_grad = grad_residual + grad_norm_one

    wq_total = wq_total.transpose(1, 0, 2)
    query_grad = wq_total[:, :, :q_cols].reshape(w_rows, n_in * q_cols)
    key_grad = wq_total[:, :, q_cols : q_cols + HEAD_SIZE].reshape(w_rows, n_in * HEAD_SIZE)
    value_grad = wq_total[:, :, q_cols + HEAD_SIZE :].reshape(w_rows, n_in * HEAD_SIZE)
    gu_total = jnp.sum(
        gus[:, :w_rows].astype(f32).reshape(n_out, n_in, w_rows, 2 * hid_pad), axis=1
    )

    def hidden_whole(piece):
        piece = piece[:, :, :hid].reshape(n_out, w_rows, 2, hid_core)
        return piece.transpose(1, 2, 0, 3).reshape(w_rows, n_out * hid)

    gate_w_grad = hidden_whole(gu_total[:, :, :hid_pad])
    up_w_grad = hidden_whole(gu_total[:, :, hid_pad:])
    e_total = e_total.astype(f32)

    return (
        total_out.astype(bf16).transpose(1, 0, 2),
        tokens_grad.transpose(1, 0, 2),
        small_total[:, n_experts],
        small_total[:, n_experts + 1],
        query_grad,
        key_grad,
        value_grad,
        out_w_grad,
        small_total[:, :n_experts],
        gate_w_grad,
        up_w_grad,
        down_w_grad,
        e_total[:, :ff][None],
        e_total[:, ff : 2 * ff][None],
        e_total[:, 2 * ff :].T[None],
    )


def solution(mesh):
    rows = P(("seq", "fsdp"), None, None)
    matrix = P(("seq", "fsdp"), None)
    vector = P(("seq", "fsdp"))
    expert = P("fsdp", None, None)
    return jax.shard_map(
        body,
        mesh=mesh,
        in_specs=(rows,) * 3 + (vector,) * 2 + (matrix,) * 8 + (expert,) * 3,
        out_specs=(rows,) * 2 + (vector,) * 2 + (matrix,) * 8 + (expert,) * 3,
        check_vma=False,
    )
```
